32 devices in a mesh: dp: 8 (over z, x), tensor: 4 (over y, core).
Axes of the slice: x: 2, y: 2, z: 4, core: 2. Of those that a mesh axis runs over, the one named last changes fastest.
Arguments:
- tokens: bfloat16 [1, 4096, 1280], P(None, 'dp'), may hold values from -6 to 6
- cotangent: bfloat16 [1, 4096, 1280], P(None, 'dp'), may hold values from -6 to 6
- norm1_gain: float32 [1280], replicated, may hold values from 0.5 to 1.5
- norm1_shift: float32 [1280], replicated, may hold values from -3 to 3
- qkv_weight: bfloat16 [1280, 3, 1280], P(None, None, 'tensor'), may hold values from -0.15625 to 0.15625
- qv_bias: float32 [2, 1280], P(None, 'tensor'), may hold values from -0.24 to 0.24
- proj_weight: bfloat16 [1280, 1280], P('tensor'), may hold values from -4 to 4
- proj_bias: float32 [1280], replicated, may hold values from -3 to 3
- table_rows: bfloat16 [127, 80], replicated, may hold values from -0.59765625 to 0.59765625
- table_cols: bfloat16 [127, 80], replicated, may hold values from -0.59765625 to 0.59765625
- norm2_gain: float32 [1280], replicated, may hold values from 0.5 to 1.5
- norm2_shift: float32 [1280], replicated, may hold values from -3 to 3
- fc1_weight: bfloat16 [1280, 5120], P(None, 'tensor'), may hold values from -0.15625 to 0.15625
- fc1_bias: float32 [5120], P('tensor'), may hold values from -3 to 3
- fc2_weight: bfloat16 [5120, 1280], P('tensor'), may hold values from -0.125 to 0.125
- fc2_bias: float32 [1280], replicated, may hold values from -3 to 3
- threshold: float32 [1], replicated, may hold values from 0.5 to 3
Outputs:
- output: bfloat16 [1, 4096, 1280], P(None, 'dp')
- grad_tokens: bfloat16 [1, 4096, 1280], P(None, 'dp')
- grad_norm1_gain: float32 [1280], replicated
- grad_norm1_shift: float32 [1280], replicated
- grad_qkv: float32 [1280, 3, 1280], P('dp', None, 'tensor')
- grad_qv_bias: float32 [2, 1280], P(None, 'tensor')
- grad_proj: float32 [1280, 1280], P('tensor', 'dp')
- grad_proj_bias: float32 [1280], replicated
- grad_table_rows: float32 [127, 80], replicated
- grad_table_cols: float32 [127, 80], replicated
- grad_norm2_gain: float32 [1280], replicated
- grad_norm2_shift: float32 [1280], replicated
- grad_fc1: float32 [1280, 5120], P('dp', 'tensor')
- grad_fc1_bias: float32 [5120], P('tensor')
- grad_fc2: float32 [5120, 1280], P('tensor', 'dp')
- grad_fc2_bias: float32 [1280], replicated
- clipped_qk: bfloat16 [1280, 2, 1280], P(None, None, 'tensor')
- clipped_q_bias: float32 [1280], P('tensor')
- head_peaks: float32 [16], P('tensor')
- clip_factors: float32 [16], P('tensor')
The draws below stay inside these ranges and needn't reach their ends.
All inputs are finite; a program needn't handle non-finite values.
Results may differ from the reference program's by a relative error of at most 0.02.
Values may be sent and summed in bfloat16 or wider, within the bound.
A program may use at most 192 MiB of HBM per device.

```python
import jax
import jax.numpy as jnp
from jax import lax

D = 1280
HEADS = 16
HEAD = 80
FF = 5120
SIDE = 64
IMAGES = 1
SEQ = 4096
REL = 127


def spiked(values, own_key, source, target, shards_of, factor):
    owner, partner = [(jnp.arange(values.shape[dim]) // (values.shape[dim] // shards_of)).reshape([-1 if axis == dim else 1 for axis in range(values.ndim)]) for dim in (source, target)]
    chosen = jax.random.permutation(own_key, shards_of)[partner]
    strong = (owner == chosen) | (owner == (partner + shards_of // 2) % shards_of)
    return jnp.where(strong, factor * values, values)


def level_of(stream_key, shape, pieces, least, top_value):
    gain, own = 1.0, jax.random.fold_in(stream_key, 6)
    for dim, parts in pieces:
        steps = jnp.exp(jax.random.uniform(jax.random.fold_in(own, dim), (parts,), jnp.float32, least / len(pieces), top_value / len(pieces)))
        gain = gain * jnp.repeat(steps, shape[dim] // parts).reshape([-1 if axis == dim else 1 for axis in range(len(shape))])
    return gain


def gaussian(rng, extent, scale, most, pieces=(), kind=jnp.bfloat16):
    drawn = jax.random.normal(rng, extent, jnp.float32) * scale
    if len(pieces) > 0:
        drawn = level_of(rng, extent, pieces, -0.22, 0.18) * drawn
    return jnp.clip(drawn, min=-most, max=most).astype(kind)


def noise_with(stream_key, extent, scale, reach, cuts, heavy, kind=jnp.bfloat16):
    drawn = scale * jax.random.normal(stream_key, extent, jnp.float32)
    if cuts:
        drawn = drawn * level_of(stream_key, extent, cuts, -0.22, 0.18)
    return jnp.clip(spiked(drawn, jax.random.fold_in(stream_key, 3), *heavy), -reach, reach).astype(kind)


def setup_inputs(seed: int = 0) -> dict:
    key_list = jax.random.split(jax.random.key(seed), 18)
    tokens = gaussian(key_list[0], (IMAGES, SEQ, D), 1.0, 6.0, ((1, 8),))
    cotangent = noise_with(key_list[1], (IMAGES, SEQ, D), 1.0, 6.0, ((1, 8),), (1, 2, 8, 2.0))
    norm1_gain = jnp.clip(1.0 + 0.1 * jax.random.normal(key_list[2], (D,), jnp.float32), 0.5, 1.5)
    norm1_shift = gaussian(key_list[3], (D,), 0.5, 3.0, (), jnp.float32)
    qkv_weight = gaussian(key_list[4], (D, 3, D), D ** -0.5, 0.15625, ((2, 4),))
    qv_bias = gaussian(key_list[5], (2, D), 0.04, 0.24, ((1, 4),), jnp.float32)
    proj_weight = gaussian(key_list[6], (D, D), 2 ** -0.5, 4.0, ((0, 4),))
    proj_bias = gaussian(key_list[7], (D,), 0.5, 3.0, (), jnp.float32)
    table_rows = gaussian(key_list[8], (REL, HEAD), 0.1, 0.59765625)
    table_cols = gaussian(key_list[9], (REL, HEAD), 0.1, 0.59765625)
    norm2_gain = jnp.clip(1.0 + 0.1 * jax.random.normal(key_list[10], (D,), jnp.float32), 0.5, 1.5)
    norm2_shift = gaussian(key_list[11], (D,), 0.5, 3.0, (), jnp.float32)
    fc1_weight = gaussian(key_list[12], (D, FF), D ** -0.5, 0.15625, ((1, 4),))
    fc1_bias = gaussian(key_list[13], (FF,), 0.5, 3.0, ((0, 4),), jnp.float32)
    fc2_weight = gaussian(key_list[14], (FF, D), (FF // 2) ** -0.5, 0.125, ((0, 4),))
    fc2_bias = gaussian(key_list[15], (D,), 0.5, 3.0, (), jnp.float32)
    threshold = jnp.clip(jax.random.uniform(key_list[16], (1,), jnp.float32, 0.5, 3.0), 0.5, 3.0)
    return dict(tokens=tokens, cotangent=cotangent, norm1_gain=norm1_gain, norm1_shift=norm1_shift, qkv_weight=qkv_weight, qv_bias=qv_bias, proj_weight=proj_weight, proj_bias=proj_bias, table_rows=table_rows, table_cols=table_cols, norm2_gain=norm2_gain, norm2_shift=norm2_shift, fc1_weight=fc1_weight, fc1_bias=fc1_bias, fc2_weight=fc2_weight, fc2_bias=fc2_bias, threshold=threshold)


HIGHEST = lax.Precision.HIGHEST
EPSILON = 1e-06

@jax.custom_vjp
def low(v):
    return lax.optimization_barrier(v.astype(jnp.bfloat16)).astype(jnp.float32)

@jax.custom_vjp
def low_back(v):
    return v

def low_keep(v):
    return (low(v), None)

def low_pass(kept, grad):
    return (grad,)

def back_keep(v):
    return (v, None)

def back_low(kept, grad):
    return (low(grad),)
low.defvjp(low_keep, low_pass)
low_back.defvjp(back_keep, back_low)

def layer_norm(values, norm_gain, norm_shift):
    center = values - lax.optimization_barrier(jnp.mean(values, axis=-1, keepdims=True))
    variance = lax.optimization_barrier(jnp.mean(center * center, axis=-1, keepdims=True))
    return center * lax.rsqrt(variance + EPSILON) * norm_gain + norm_shift

def attend_head(queries, key_rows, value_rows, table_rows, table_cols):
    positions = jnp.arange(SEQ)
    offsets = jnp.arange(SIDE)
    index_rows = ((positions // SIDE)[:, None] - offsets[None, :] + SIDE - 1).astype(jnp.int32)
    index_cols = ((positions % SIDE)[:, None] - offsets[None, :] + SIDE - 1).astype(jnp.int32)
    logits = jnp.dot(queries, key_rows.T, precision=HIGHEST) * HEAD ** (-0.5)
    bias_rows = jnp.take_along_axis(jnp.dot(queries, table_rows.T, precision=HIGHEST), index_rows, axis=1)
    bias_cols = jnp.take_along_axis(jnp.dot(queries, table_cols.T, precision=HIGHEST), index_cols, axis=1)
    scores = logits.reshape(SEQ, SIDE, SIDE) + bias_rows[:, :, None] + bias_cols[:, None, :]
    scores = low_back(scores.reshape(SEQ, SEQ))
    log_total = jax.nn.logsumexp(scores, axis=-1)
    weights = low(jnp.exp(scores - log_total[:, None]))
    attended = low(low_back(jnp.dot(weights, value_rows, precision=HIGHEST)))
    return (attended, jnp.max(logits))

def image_layer(one_image, norm1_gain, norm1_shift, qkv_weight, qv_bias, proj_weight, proj_bias, table_rows, table_cols, norm2_gain, norm2_shift, fc1_weight, fc1_bias, fc2_weight, fc2_bias):
    normed = low(layer_norm(one_image, norm1_gain, norm1_shift))
    triple = jnp.einsum('nd,dtc->ntc', normed, qkv_weight, precision=HIGHEST)
    queries = low(low_back(triple[:, 0] + qv_bias[0]))
    key_rows = low(low_back(triple[:, 1]))
    value_rows = low(low_back(triple[:, 2] + qv_bias[1]))

    def split_heads(flat_rows):
        return flat_rows.reshape(SEQ, HEADS, HEAD).transpose(1, 0, 2)

    def one_head(operands):
        return attend_head(operands[0], operands[1], operands[2], table_rows, table_cols)
    attended, head_peaks = lax.map(jax.checkpoint(one_head), (split_heads(queries), split_heads(key_rows), split_heads(value_rows)))
    attended = attended.transpose(1, 0, 2).reshape(SEQ, D)
    branch = low_back(jnp.dot(attended, proj_weight, precision=HIGHEST) + proj_bias)
    middle = one_image + branch
    normed2 = low(layer_norm(middle, norm2_gain, norm2_shift))
    hidden_pre = low_back(jnp.dot(normed2, fc1_weight, precision=HIGHEST) + fc1_bias)
    activated = low(jax.nn.gelu(hidden_pre, approximate=False))
    return (middle + jnp.dot(activated, fc2_weight, precision=HIGHEST) + fc2_bias, head_peaks)

def reference(tokens, cotangent, norm1_gain, norm1_shift, qkv_weight, qv_bias, proj_weight, proj_bias, table_rows, table_cols, norm2_gain, norm2_shift, fc1_weight, fc1_bias, fc2_weight, fc2_bias, threshold):
    params = tuple((weight_arg.astype(jnp.float32) for weight_arg in (norm1_gain, norm1_shift, qkv_weight, qv_bias, proj_weight, proj_bias, table_rows, table_cols, norm2_gain, norm2_shift, fc1_weight, fc1_bias, fc2_weight, fc2_bias)))

    def whole_layer(inputs, *weight_args):

        def per_image(one_image):
            return image_layer(one_image, *weight_args)
        outputs, peak_rows = lax.map(per_image, inputs)
        return (outputs, lax.optimization_barrier(jnp.max(peak_rows, axis=0)))
    output, pullback, head_peaks = jax.vjp(whole_layer, tokens.astype(jnp.float32), *params, has_aux=True)
    gradients = pullback(cotangent.astype(jnp.float32))
    limit = threshold[0]
    clip_factors = jnp.sqrt(limit / jnp.maximum(head_peaks, limit))
    spread = jnp.repeat(clip_factors, HEAD)
    clipped_qk = (qkv_weight[:, :2, :].astype(jnp.float32) * spread).astype(jnp.bfloat16)
    clipped_q_bias = qv_bias[0] * spread
    return (output.astype(jnp.bfloat16), gradients[0].astype(jnp.bfloat16), gradients[1], gradients[2], gradients[3], gradients[4], gradients[5], gradients[6], gradients[7], gradients[8], gradients[9], gradients[10], gradients[11], gradients[12], gradients[13], gradients[14], clipped_qk, clipped_q_bias, head_peaks, clip_factors)
```

```python
import functools
import math

import jax
import jax.numpy as jnp
from jax import lax
from jax.experimental import pallas as pl
from jax.experimental.pallas import tpu as pltpu
from jax.sharding import PartitionSpec as P

HEAD = 80
SIDE = 64

MESH = pl.DeviceIdType.MESH
LOW = jnp.bfloat16
F32 = jnp.float32
EPSILON = 1e-06
SCALE = HEAD**-0.5
EXP2_SCALE = SCALE * math.log2(math.e)
COLS_AT = HEAD
ROWS_AT = COLS_AT + 2 * SIDE
LSE_AT = ROWS_AT + 16
AUG = LSE_AT + 16
VMEM_LIMIT = 60 * 2**20


def nn(a, b):
    return lax.dot_general(a, b, (((1,), (0,)), ((), ())), preferred_element_type=F32)


def tn(a, b):
    return lax.dot_general(a, b, (((0,), (0,)), ((), ())), preferred_element_type=F32)


def nt(a, b):
    return lax.dot_general(a, b, (((1,), (1,)), ((), ())), preferred_element_type=F32)


def parts_of(values, count):
    pieces = []
    for _ in range(count):
        piece = values.astype(LOW).astype(F32)
        pieces.append(piece)
        values = values - piece
    return pieces


def send_dp(src, dst, send_sem, recv_sem, dev):
    return pltpu.make_async_remote_copy(
        src_ref=src,
        dst_ref=dst,
        send_sem=send_sem,
        recv_sem=recv_sem,
        device_id={"dp": dev},
        device_id_type=MESH,
    )


def shifts(rows, dev):
    spot = lax.broadcasted_iota(jnp.int32, (2 * SIDE, rows), 1)
    by_row = SIDE - 1 - (dev * (rows // SIDE) + lax.shift_right_logical(spot, 6))
    by_col = SIDE - 1 - (spot & (SIDE - 1))
    return by_row, by_col


def skew(values, shift):
    for bit in (32, 16, 8, 4, 2, 1):
        moved = pltpu.roll(values, 2 * SIDE - bit, 0)
        values = jnp.where((shift & bit) != 0, moved, values)
    return values[:SIDE]


def unskew(values, shift):
    values = jnp.concatenate([values, jnp.zeros_like(values)], axis=0)
    for bit in (32, 16, 8, 4, 2, 1):
        moved = pltpu.roll(values, bit, 0)
        values = jnp.where((shift & bit) != 0, moved, values)
    return values


def greet(peers):
    barrier = pltpu.get_barrier_semaphore()
    for peer in peers:
        pl.semaphore_signal(barrier, inc=1, device_id={"dp": peer}, device_id_type=MESH)
    pl.semaphore_wait(barrier, len(peers))


def key_onehots(rows, dev):
    spot = lax.broadcasted_iota(jnp.int32, (2 * SIDE, rows), 1)
    index = lax.broadcasted_iota(jnp.int32, (2 * SIDE, rows), 0)
    cols = jnp.where((index & (SIDE - 1)) == (spot & (SIDE - 1)), 1.0, 0.0)
    spot, index = spot[:16], index[:16]
    offset = lax.rem(dev * (rows // SIDE), 8)
    in_group = jnp.where((index & 7) == offset + lax.shift_right_logical(spot, 6), 1.0, 0.0)
    return cols, in_group


class Shape:
    def __init__(self, heads, group, rows):
        self.heads, self.group, self.rows = heads, group, rows
        self.queries = heads * rows
        self.block = min(512, self.queries)


def forward_kernel(
    shape, qkv, tables, att, qaug, bias_rows, kv_out, o_out, lse_out, peak_out,
    rq, rkv, kaug_t, kaug, vaug, oacc, mrow, lpk, att_s, att_r,
    q_send, q_recv, k_send, k_recv, x_send, x_recv, r_send, r_recv, o_sem,
):
    heads, group, rows, block = shape.heads, shape.group, shape.rows, shape.block
    me = lax.axis_index("dp")
    z, g = me // group, lax.rem(me, group)
    column = [lax.rem(z + k, heads) for k in range(1, heads)]
    mates = [lax.rem(g + k, group) for k in range(1, group)]
    greet([h * group + g for h in column] + [z * group + o for o in mates])
    sends = []
    for h in column:
        sends.append(send_dp(qkv.at[h, 0], rq.at[z], q_send.at[h], q_recv.at[z], h * group + g))
    for h in column:
        sends.append(
            send_dp(
                qkv.at[h, pl.ds(1, 2)], rkv.at[z, g], k_send.at[h], k_recv.at[z], h * group + g
            )
        )
    for copy in sends:
        copy.start()
    rq[z] = qkv[z, 0]
    rkv[z, g] = qkv[z, pl.ds(1, 2)]
    qaug[pl.ds(LSE_AT, 16), :] = jnp.zeros((16, shape.queries), LOW)
    kaug_t[pl.ds(LSE_AT, 16), :] = jnp.zeros((16, rows), LOW)
    vaug[pl.ds(HEAD, 16), :] = jnp.where(
        lax.broadcasted_iota(jnp.int32, (16, rows), 0) == 0, 1.0, 0.0
    ).astype(LOW)
    oacc[...] = jnp.zeros_like(oacc)
    mrow[...] = jnp.full_like(mrow, -jnp.inf)
    lpk[...] = jnp.full_like(lpk, -jnp.inf)

    def prepare(k, carry):
        source = lax.rem(z - k + heads, heads)
        span = pl.ds(pl.multiple_of(source * rows, rows), rows)

        @pl.when(k > 0)
        def _():
            send_dp(rq.at[source], rq.at[source], q_send.at[source], q_recv.at[source], me).wait_recv()

        query = rq[source]
        by_row, by_col = shifts(rows, source * group + g)
        along_rows = skew(nn(tables[0], query) * (1.0 / SCALE), by_row)
        along_cols = skew(nn(tables[1], query) * (1.0 / SCALE), by_col)
        qaug[pl.ds(0, HEAD), span] = query
        cols = parts_of(along_cols, 2)
        qaug[pl.ds(COLS_AT, 2 * SIDE), span] = jnp.concatenate(cols, axis=0).astype(LOW)
        high, rest = parts_of(along_rows, 2)
        for at in range(SIDE // 8):
            pair = jnp.concatenate([high[8 * at : 8 * at + 8], rest[8 * at : 8 * at + 8]], axis=0)
            bias_rows[at, :, span] = pair.astype(LOW)
        return carry

    lax.fori_loop(0, heads, prepare, 0)

    def chunk(source, mate):
        dev = source * group + mate
        cols, in_group = key_onehots(rows, dev)
        kaug_t[pl.ds(0, HEAD), :] = rkv[source, mate, 0]
        kaug_t[pl.ds(COLS_AT, 2 * SIDE), :] = cols.astype(LOW)
        kaug_t[pl.ds(ROWS_AT, 16), :] = in_group.astype(LOW)
        kaug[...] = kaug_t[...].T
        vaug[pl.ds(0, HEAD), :] = rkv[source, mate, 1]
        qaug[pl.ds(ROWS_AT, 16), :] = bias_rows[(dev * (rows // SIDE)) // 8]

        def one(i, carry):
            span = pl.ds(pl.multiple_of(i * block, block), block)
            logits = nn(kaug[:, :HEAD], qaug[pl.ds(0, HEAD), span])
            lpk[...] = jnp.maximum(lpk[...], jnp.max(logits.reshape(rows // 8, 8, block), axis=0))
            scores = nn(kaug[...], qaug[:, span])
            before = mrow[:, span]
            top = jnp.maximum(before, jnp.max(scores, axis=0, keepdims=True))
            mrow[:, span] = top
            weights = jnp.exp2(scores * EXP2_SCALE - top * EXP2_SCALE).astype(LOW)
            keep = jnp.exp2((before - top) * EXP2_SCALE)
            oacc[:, span] = oacc[:, span] * keep + nn(vaug[...], weights)
            return carry

        lax.fori_loop(0, shape.queries // block, one, 0)

    def column_step(k, carry):
        source = lax.rem(z - k + heads, heads)

        @pl.when(k > 0)
        def _():
            send_dp(rkv.at[source, g], rkv.at[source, g], k_send.at[source], k_recv.at[source], me).wait_recv()

        for n, mate in enumerate(mates):
            send_dp(
                rkv.at[source, g], rkv.at[source, g], x_send.at[source, n], x_recv.at[source, g],
                z * group + mate,
            ).start()
        chunk(source, g)

        def mate_step(n, inner):
            mate = lax.rem(g + n, group)
            send_dp(
                rkv.at[source, mate], rkv.at[source, mate], x_send.at[source, 0], x_recv.at[source, mate], me
            ).wait_recv()
            chunk(source, mate)
            return inner

        lax.fori_loop(1, group, mate_step, 0)
        return carry

    lax.fori_loop(0, heads, column_step, 0)
    keep_kv = pltpu.make_async_copy(rkv, kv_out, o_sem)
    keep_kv.start()

    def finish(source, carry):
        span = pl.ds(pl.multiple_of(source * rows, rows), rows)
        total = oacc[pl.ds(HEAD, 1), span]
        attended = oacc[pl.ds(0, HEAD), span] / total
        o_out[:, span] = attended
        lse_out[:, span] = mrow[:, span] + jnp.log2(total) * (1.0 / EXP2_SCALE)
        att_s[source] = attended.astype(LOW)

        @pl.when(source != z)
        def _():
            send_dp(
                att_s.at[source], att_r.at[z], r_send.at[source], r_recv.at[z], source * group + g
            ).start()

        return carry

    lax.fori_loop(0, heads, finish, 0)
    att[z] = att_s[z]
    peak_out[...] = jnp.full(peak_out.shape, jnp.max(lpk[...]) * SCALE, F32)
    for h in column:
        send_dp(att_s.at[h], att_r.at[h], r_send.at[h], r_recv.at[h], h * group + g).wait()
        att[h] = att_r[h]
    for copy in sends:
        copy.wait_send()
    for source in range(heads):
        for n, mate in enumerate(mates):
            send_dp(
                rkv.at[source, g], rkv.at[source, g], x_send.at[source, n], x_recv.at[source, g],
                z * group + mate,
            ).wait_send()
    keep_kv.wait()


def attend(shape, qkv, tables):
    heads, group, rows, queries = shape.heads, shape.group, shape.rows, shape.queries
    vmem = pl.BlockSpec(memory_space=pltpu.VMEM)
    hbm = pl.BlockSpec(memory_space=pl.ANY)
    dma = pltpu.SemaphoreType.DMA
    return pl.pallas_call(
        functools.partial(forward_kernel, shape),
        out_shape=(
            jax.ShapeDtypeStruct((heads, HEAD, rows), LOW),
            jax.ShapeDtypeStruct((AUG, queries), LOW),
            jax.ShapeDtypeStruct((SIDE // 8, 16, queries), LOW),
            jax.ShapeDtypeStruct((heads, group, 2, HEAD, rows), LOW),
            jax.ShapeDtypeStruct((HEAD, queries), F32),
            jax.ShapeDtypeStruct((1, queries), F32),
            jax.ShapeDtypeStruct((8, 128), F32),
        ),
        in_specs=[vmem, vmem],
        out_specs=(vmem, vmem, vmem, hbm, vmem, vmem, vmem),
        scratch_shapes=[
            pltpu.VMEM((heads, HEAD, rows), LOW),
            pltpu.VMEM((heads, group, 2, HEAD, rows), LOW),
            pltpu.VMEM((AUG, rows), LOW),
            pltpu.VMEM((rows, AUG), LOW),
            pltpu.VMEM((HEAD + 16, rows), LOW),
            pltpu.VMEM((HEAD + 16, queries), F32),
            pltpu.VMEM((1, queries), F32),
            pltpu.VMEM((8, shape.block), F32),
            pltpu.VMEM((heads, HEAD, rows), LOW),
            pltpu.VMEM((heads, HEAD, rows), LOW),
            dma((heads,)), dma((heads,)), dma((heads,)), dma((heads,)),
            dma((heads, group)), dma((heads, group)), dma((heads,)), dma((heads,)),
            dma,
        ],
        compiler_params=pltpu.CompilerParams(
            collective_id=1, has_side_effects=True, vmem_limit_bytes=VMEM_LIMIT
        ),
        name="attend",
    )(qkv, tables)


def backward_kernel(
    shape, ga, tables, qaug_in, bias_rows, rkv, o_in, lse_in, grads, table_grads,
    rdo, qaug, q_tok, do_aug, do_tok, kaug_t, kaug, vaug_t, vaug, kacc, vacc, dq, drow, dcol,
    part, xr, summed, gq_s, gq_r, gkv_r,
    d_send, d_recv, x_send, x_recv, kv_send, kv_recv, q_send, q_recv,
):
    heads, group, rows, block = shape.heads, shape.group, shape.rows, shape.block
    queries = shape.queries
    me = lax.axis_index("dp")
    z, g = me // group, lax.rem(me, group)
    column = [lax.rem(z + k, heads) for k in range(1, heads)]
    mates = [lax.rem(g + k, group) for k in range(1, group)]
    greet([h * group + g for h in column] + [z * group + o for o in mates])
    sends = []
    for h in column:
        copy = send_dp(ga.at[h], rdo.at[z], d_send.at[h], d_recv.at[z], h * group + g)
        copy.start()
        sends.append(copy)
    rdo[z] = ga[z]
    qaug[...] = qaug_in[...]
    ones = jnp.where(lax.broadcasted_iota(jnp.int32, (16, rows), 0) < 3, 1.0, 0.0).astype(LOW)
    kaug_t[pl.ds(LSE_AT, 16), :] = ones
    vaug_t[pl.ds(HEAD, 16), :] = ones
    vaug_t[pl.ds(HEAD + 16, 32), :] = jnp.zeros((32, rows), LOW)
    low_lse = parts_of(-lse_in[...], 3)
    qaug[pl.ds(LSE_AT, 16), :] = jnp.concatenate(
        low_lse + [jnp.zeros((13, queries), F32)], axis=0
    ).astype(LOW)
    dq[...] = jnp.zeros_like(dq)
    dcol[...] = jnp.zeros_like(dcol)
    drow[...] = jnp.zeros_like(drow)

    def prepare(k, carry):
        source = lax.rem(z - k + heads, heads)
        span = pl.ds(pl.multiple_of(source * rows, rows), rows)

        @pl.when(k > 0)
        def _():
            send_dp(rdo.at[source], rdo.at[source], d_send.at[source], d_recv.at[source], me).wait_recv()

        upstream = rdo[source]
        dots = jnp.sum(upstream.astype(F32) * o_in[:, span], axis=0, keepdims=True)
        low_dots = parts_of(-dots, 3)
        do_aug[pl.ds(0, HEAD), span] = upstream
        do_aug[pl.ds(HEAD, 16), span] = jnp.concatenate(
            low_dots + [jnp.zeros((13, rows), F32)], axis=0
        ).astype(LOW)
        do_aug[pl.ds(HEAD + 16, 32), span] = jnp.zeros((32, rows), LOW)
        do_tok[span, :] = do_aug[:, span].T
        q_tok[span, :] = qaug[pl.ds(0, 128), span].T
        return carry

    lax.fori_loop(0, heads, prepare, 0)

    def chunk(source, mate):
        dev = source * group + mate
        at = (dev * (rows // SIDE)) // 8
        cols, in_group = key_onehots(rows, dev)
        kaug_t[pl.ds(0, HEAD), :] = rkv[source, mate, 0]
        kaug_t[pl.ds(COLS_AT, 2 * SIDE), :] = cols.astype(LOW)
        kaug_t[pl.ds(ROWS_AT, 16), :] = in_group.astype(LOW)
        kaug[...] = kaug_t[...].T
        vaug_t[pl.ds(0, HEAD), :] = rkv[source, mate, 1]
        vaug[...] = vaug_t[...].T
        qaug[pl.ds(ROWS_AT, 16), :] = bias_rows[at]
        kacc[...] = jnp.zeros_like(kacc)
        vacc[...] = jnp.zeros_like(vacc)
        back = jnp.concatenate(
            [kaug_t[pl.ds(0, COLS_AT + SIDE), :], kaug_t[pl.ds(ROWS_AT, 16), :]], axis=0
        )

        def one(i, carry):
            span = pl.ds(pl.multiple_of(i * block, block), block)
            probs = jnp.exp2(nn(kaug[...], qaug[:, span]) * EXP2_SCALE)
            pulled = nn(vaug[...], do_aug[:, span])
            low_grads = (probs * pulled).astype(LOW)
            vacc[...] += nn(probs.astype(LOW), do_tok[span, :])
            kacc[...] += nn(low_grads, q_tok[span, :])
            found = nn(back, low_grads)
            dq[:, span] += found[:HEAD]
            dcol[:, span] += found[COLS_AT : COLS_AT + SIDE]
            drow[at, :, span] += found[COLS_AT + SIDE : COLS_AT + SIDE + 8]
            return carry

        lax.fori_loop(0, queries // block, one, 0)

    def put(where, extra):
        key_part = (kacc[...] * SCALE).T[:HEAD]
        value_part = vacc[...].T[:HEAD]
        for other in extra:
            key_part = key_part + other[0].astype(F32)
            value_part = value_part + other[1].astype(F32)
        where[0] = key_part.astype(LOW)
        where[1] = value_part.astype(LOW)

    def mate_copy(source, mate):
        return send_dp(
            part.at[source, mate], xr.at[source, g], x_send.at[source, mate], x_recv.at[source, g],
            z * group + mate,
        )

    def mates_step(k, carry):
        source = lax.rem(z + k, heads)

        def mate_step(n, inner):
            mate = lax.rem(g + n, group)
            chunk(source, mate)
            put(part.at[source, mate], [])
            mate_copy(source, mate).start()
            return inner

        lax.fori_loop(1, group, mate_step, 0)
        return carry

    lax.fori_loop(1, heads + 1, mates_step, 0)

    def own_step(k, carry):
        source = lax.rem(z + k, heads)
        chunk(source, g)
        extra = []
        for mate in mates:
            send_dp(
                xr.at[source, mate], xr.at[source, mate], x_send.at[source, mate], x_recv.at[source, mate], me
            ).wait_recv()
            extra.append(xr.at[source, mate])
        put(summed.at[source], extra)

        @pl.when(source != z)
        def _():
            send_dp(
                summed.at[source], gkv_r.at[z], kv_send.at[source], kv_recv.at[z], source * group + g
            ).start()

        return carry

    lax.fori_loop(1, heads + 1, own_step, 0)
    table_grads[...] = jnp.zeros_like(table_grads)

    def finish(k, carry):
        source = lax.rem(z + k, heads)
        span = pl.ds(pl.multiple_of(source * rows, rows), rows)
        by_row, by_col = shifts(rows, source * group + g)
        total = dq[:, span] * SCALE
        for n, held in enumerate((drow[:, :, span].reshape(SIDE, rows), dcol[:, span])):
            spread = unskew(held, by_col if n else by_row)
            for piece in parts_of(spread, 2):
                low_piece = piece.astype(LOW)
                total = total + tn(tables[n], low_piece)
                table_grads[n] += nn(low_piece, q_tok[span, :])
        gq_s[source] = total.astype(LOW)

        @pl.when(source != z)
        def _():
            send_dp(
                gq_s.at[source], gq_r.at[z], q_send.at[source], q_recv.at[z], source * group + g
            ).start()

        return carry

    lax.fori_loop(1, heads + 1, finish, 0)
    grads[z, 0] = gq_s[z]
    grads[z, pl.ds(1, 2)] = summed[z]
    for h in column:
        send_dp(summed.at[h], gkv_r.at[h], kv_send.at[h], kv_recv.at[h], h * group + g).wait()
        grads[h, pl.ds(1, 2)] = gkv_r[h]
    for h in column:
        send_dp(gq_s.at[h], gq_r.at[h], q_send.at[h], q_recv.at[h], h * group + g).wait()
        grads[h, 0] = gq_r[h]
    for copy in sends:
        copy.wait_send()
    for source in range(heads):
        for mate in mates:
            mate_copy(source, mate).wait_send()


def attend_back(shape, ga, tables, qaug, bias_rows, kv, o_rows, lse):
    heads, group, rows, queries = shape.heads, shape.group, shape.rows, shape.queries
    vmem = pl.BlockSpec(memory_space=pltpu.VMEM)
    dma = pltpu.SemaphoreType.DMA
    return pl.pallas_call(
        functools.partial(backward_kernel, shape),
        out_shape=(
            jax.ShapeDtypeStruct((heads, 3, HEAD, rows), LOW),
            jax.ShapeDtypeStruct((2, 2 * SIDE, 128), F32),
        ),
        in_specs=[vmem] * 7,
        out_specs=(vmem, vmem),
        scratch_shapes=[
            pltpu.VMEM((heads, HEAD, rows), LOW),
            pltpu.VMEM((AUG, queries), LOW),
            pltpu.VMEM((queries, 128), LOW),
            pltpu.VMEM((128, queries), LOW),
            pltpu.VMEM((queries, 128), LOW),
            pltpu.VMEM((AUG, rows), LOW),
            pltpu.VMEM((rows, AUG), LOW),
            pltpu.VMEM((128, rows), LOW),
            pltpu.VMEM((rows, 128), LOW),
            pltpu.VMEM((rows, 128), F32),
            pltpu.VMEM((rows, 128), F32),
            pltpu.VMEM((HEAD, queries), F32),
            pltpu.VMEM((SIDE // 8, 8, queries), F32),
            pltpu.VMEM((SIDE, queries), F32),
            pltpu.VMEM((heads, group, 2, HEAD, rows), LOW),
            pltpu.VMEM((heads, group, 2, HEAD, rows), LOW),
            pltpu.VMEM((heads, 2, HEAD, rows), LOW),
            pltpu.VMEM((heads, HEAD, rows), LOW),
            pltpu.VMEM((heads, HEAD, rows), LOW),
            pltpu.VMEM((heads, 2, HEAD, rows), LOW),
            dma((heads,)), dma((heads,)), dma((heads, group)), dma((heads, group)),
            dma((heads,)), dma((heads,)), dma((heads,)), dma((heads,)),
        ],
        compiler_params=pltpu.CompilerParams(
            collective_id=2, has_side_effects=True, vmem_limit_bytes=VMEM_LIMIT
        ),
        name="attend_back",
    )(ga, tables, qaug, bias_rows, kv, o_rows, lse)


def norm_forward(values, norm_gain, norm_shift):
    center = values - jnp.mean(values, axis=-1, keepdims=True)
    variance = jnp.mean(center * center, axis=-1, keepdims=True)
    inverse = lax.rsqrt(variance + EPSILON)
    scaled = center * inverse
    return (scaled * norm_gain + norm_shift, scaled, inverse)


def norm_backward(upstream, scaled, inverse, norm_gain):
    weighted = upstream * norm_gain
    centered_grad = weighted - jnp.mean(weighted, axis=-1, keepdims=True)
    centered_grad = centered_grad - scaled * jnp.mean(weighted * scaled, axis=-1, keepdims=True)
    return centered_grad * inverse


def gain_terms(upstream, scaled):
    return (jnp.sum(upstream * scaled, axis=0), jnp.sum(upstream, axis=0))


def rows_of(values, share_base, share_rows):
    return lax.dynamic_slice_in_dim(values, share_base, share_rows, 0)


def exact_gelu(values):
    return jax.nn.gelu(values, approximate=False)


def full_sum(values):
    return lax.psum(values.astype(jnp.bfloat16), "tensor").astype(jnp.float32)


def on_device(
    tokens,
    cotangent,
    norm1_gain,
    norm1_shift,
    qkv_weight,
    qv_bias,
    proj_weight,
    proj_bias,
    table_rows,
    table_cols,
    norm2_gain,
    norm2_shift,
    fc1_weight,
    fc1_bias,
    fc2_weight,
    fc2_bias,
    threshold,
):
    images, row_count, model_width = tokens.shape
    token_count = images * row_count
    local_width = qkv_weight.shape[2]
    local_heads = local_width // HEAD
    groups = lax.axis_size("tensor")
    share_rows = token_count // groups
    share_base = lax.axis_index("tensor") * share_rows
    residual_in = tokens.reshape(token_count, model_width).astype(jnp.float32)
    normed1, scaled1, inverse1 = norm_forward(residual_in, norm1_gain, norm1_shift)
    normed1_low = normed1.astype(jnp.bfloat16)
    shape = Shape(local_heads, lax.axis_size("dp") // local_heads, row_count)
    flipped = jnp.stack([table_rows, table_cols])[:, ::-1]
    flipped = jnp.pad(flipped, ((0, 0), (0, 1), (0, 0)))
    triple = jnp.einsum("dtc,nd->tcn", qkv_weight, normed1_low, preferred_element_type=jnp.float32)
    bias = jnp.stack([qv_bias[0], jnp.zeros_like(qv_bias[0]), qv_bias[1]])
    triple = (triple + bias[:, :, None]).astype(jnp.bfloat16)
    qkv = triple.reshape(3, local_heads, HEAD, row_count).transpose(1, 0, 2, 3)
    attended, qaug, bias_rows, kv, o_rows, lse, peak = attend(shape, qkv, flipped)
    attended_flat = attended.reshape(local_width, token_count)
    branch_part = jnp.einsum(
        "cn,cd->nd", attended_flat, proj_weight, preferred_element_type=jnp.float32
    )
    middle_rows = residual_in + full_sum(branch_part) + proj_bias
    normed2, scaled2, inverse2 = norm_forward(middle_rows, norm2_gain, norm2_shift)
    normed2_low = normed2.astype(jnp.bfloat16)
    up_value = jnp.dot(normed2_low, fc1_weight, preferred_element_type=jnp.float32) + fc1_bias
    activated, gelu_pull = jax.vjp(exact_gelu, up_value)
    activated_low = activated.astype(jnp.bfloat16)
    mlp_part = jnp.dot(activated_low, fc2_weight, preferred_element_type=jnp.float32)
    output = (middle_rows + (full_sum(mlp_part) + fc2_bias)).astype(jnp.bfloat16)
    grad_out = cotangent.reshape(token_count, model_width)
    grad_out_f = grad_out.astype(jnp.float32)
    grad_fc2 = jnp.einsum("nf,nd->fd", activated_low, grad_out, preferred_element_type=jnp.float32)
    grad_fc2_bias = jnp.sum(grad_out_f, axis=0)
    grad_activated = jnp.einsum(
        "nd,fd->nf", grad_out, fc2_weight, preferred_element_type=jnp.float32
    )
    grad_up = gelu_pull(grad_activated)[0].astype(jnp.bfloat16)
    grad_fc1 = jnp.einsum("nd,nf->df", normed2_low, grad_up, preferred_element_type=jnp.float32)
    grad_fc1_bias = jnp.sum(grad_up.astype(jnp.float32), axis=0)
    normed2_part = jnp.einsum("nf,df->nd", grad_up, fc1_weight, preferred_element_type=jnp.float32)
    grad_normed2 = full_sum(normed2_part)
    grad_norm2_gain, grad_norm2_shift = gain_terms(
        rows_of(grad_normed2, share_base, share_rows), rows_of(scaled2, share_base, share_rows)
    )
    grad_middle = grad_out_f + norm_backward(grad_normed2, scaled2, inverse2, norm2_gain)
    grad_branch = grad_middle.astype(jnp.bfloat16)
    grad_proj = jnp.einsum(
        "cn,nd->cd", attended_flat, grad_branch, preferred_element_type=jnp.float32
    )
    grad_proj_bias = jnp.sum(grad_branch.astype(jnp.float32), axis=0)
    grad_attended = jnp.einsum(
        "cd,nd->cn", proj_weight, grad_branch, preferred_element_type=jnp.float32
    ).astype(jnp.bfloat16)
    grad_heads = grad_attended.reshape(local_heads, HEAD, row_count)
    grad_triple, table_terms = attend_back(
        shape, grad_heads, flipped, qaug, bias_rows, kv, o_rows, lse
    )
    grad_triple = grad_triple.transpose(1, 0, 2, 3).reshape(3, local_width, token_count)
    grad_qkv = jnp.einsum(
        "nd,tcn->dtc", normed1_low, grad_triple, preferred_element_type=jnp.float32
    )
    grad_qv_bias = jnp.sum(grad_triple[0::2].astype(jnp.float32), axis=2)
    normed1_part = jnp.einsum(
        "tcn,dtc->nd", grad_triple, qkv_weight, preferred_element_type=jnp.float32
    )
    grad_normed1 = full_sum(normed1_part)
    grad_norm1_gain, grad_norm1_shift = gain_terms(
        rows_of(grad_normed1, share_base, share_rows), rows_of(scaled1, share_base, share_rows)
    )
    from_norm1 = norm_backward(grad_normed1, scaled1, inverse1, norm1_gain)
    grad_tokens = (grad_middle + from_norm1).astype(jnp.bfloat16)
    grad_tokens = grad_tokens.reshape(images, row_count, model_width)
    grad_qkv, grad_proj, grad_fc1, grad_fc2 = (
        lax.psum_scatter(
            grad_qkv.astype(jnp.bfloat16), "dp", scatter_dimension=0, tiled=True
        ).astype(jnp.float32),
        lax.psum_scatter(
            grad_proj.astype(jnp.bfloat16), "dp", scatter_dimension=1, tiled=True
        ).astype(jnp.float32),
        lax.psum_scatter(
            grad_fc1.astype(jnp.bfloat16), "dp", scatter_dimension=0, tiled=True
        ).astype(jnp.float32),
        lax.psum_scatter(
            grad_fc2.astype(jnp.bfloat16), "dp", scatter_dimension=1, tiled=True
        ).astype(jnp.float32),
    )
    grad_proj_bias, grad_fc2_bias, grad_qv_bias, grad_fc1_bias = lax.psum(
        (grad_proj_bias, grad_fc2_bias, grad_qv_bias, grad_fc1_bias), "dp"
    )
    table_terms = table_terms[:, 2 * SIDE - 2 :: -1, :HEAD]
    rows_term, cols_term = table_terms[0], table_terms[1]
    own_head = jnp.arange(local_heads) == lax.axis_index("dp") // shape.group
    local_peaks = jnp.where(own_head, peak[0, 0], -jnp.inf)
    head_peaks = lax.pmax(local_peaks, "dp")
    (
        grad_table_rows,
        grad_table_cols,
        grad_norm1_gain,
        grad_norm1_shift,
        grad_norm2_gain,
        grad_norm2_shift,
    ) = lax.psum(
        (
            rows_term,
            cols_term,
            grad_norm1_gain,
            grad_norm1_shift,
            grad_norm2_gain,
            grad_norm2_shift,
        ),
        ("dp", "tensor"),
    )
    limit = threshold[0]
    clip_factors = jnp.sqrt(limit / jnp.maximum(head_peaks, limit))
    spread_factors = jnp.repeat(clip_factors, HEAD)
    clipped_qk = (qkv_weight[:, :2, :].astype(jnp.float32) * spread_factors).astype(jnp.bfloat16)
    clipped_q_bias = qv_bias[0] * spread_factors
    output = output.reshape(images, row_count, model_width)
    return (
        output,
        grad_tokens,
        grad_norm1_gain,
        grad_norm1_shift,
        grad_qkv,
        grad_qv_bias,
        grad_proj,
        grad_proj_bias,
        grad_table_rows,
        grad_table_cols,
        grad_norm2_gain,
        grad_norm2_shift,
        grad_fc1,
        grad_fc1_bias,
        grad_fc2,
        grad_fc2_bias,
        clipped_qk,
        clipped_q_bias,
        head_peaks,
        clip_factors,
    )


def solution(mesh):
    in_specs = (
        P(None, "dp", None),
        P(None, "dp", None),
        P(),
        P(),
        P(None, None, "tensor"),
        P(None, "tensor"),
        P("tensor", None),
        P(),
        P(),
        P(),
        P(),
        P(),
        P(None, "tensor"),
        P("tensor"),
        P("tensor", None),
        P(),
        P(),
    )
    out_specs = (
        P(None, "dp", None),
        P(None, "dp", None),
        P(),
        P(),
        P("dp", None, "tensor"),
        P(None, "tensor"),
        P("tensor", "dp"),
        P(),
        P(),
        P(),
        P(),
        P(),
        P("dp", "tensor"),
        P("tensor"),
        P("tensor", "dp"),
        P(),
        P(None, None, "tensor"),
        P("tensor"),
        P("tensor"),
        P("tensor"),
    )
    return jax.shard_map(
        on_device, mesh=mesh, in_specs=in_specs, out_specs=out_specs, check_vma=False
    )
```

```python
import functools
import math

import jax
import jax.numpy as jnp
from jax import lax
from jax.experimental import pallas as pl
from jax.experimental.pallas import tpu as pltpu
from jax.sharding import PartitionSpec as P

HEAD = 80
SIDE = 64

MESH = pl.DeviceIdType.MESH
LOW = jnp.bfloat16
F32 = jnp.float32
EPSILON = 1e-06
SCALE = HEAD**-0.5
EXP2_SCALE = SCALE * math.log2(math.e)
COLS_AT = HEAD
ROWS_AT = COLS_AT + 2 * SIDE
LSE_AT = ROWS_AT + 16
AUG = LSE_AT + 16
VMEM_LIMIT = 60 * 2**20


def nn(a, b):
    return lax.dot_general(a, b, (((1,), (0,)), ((), ())), preferred_element_type=F32)


def tn(a, b):
    return lax.dot_general(a, b, (((0,), (0,)), ((), ())), preferred_element_type=F32)


def nt(a, b):
    return lax.dot_general(a, b, (((1,), (1,)), ((), ())), preferred_element_type=F32)


def parts_of(values, count):
    pieces = []
    for _ in range(count):
        piece = values.astype(LOW).astype(F32)
        pieces.append(piece)
        values = values - piece
    return pieces


def send_dp(src, dst, send_sem, recv_sem, dev):
    return pltpu.make_async_remote_copy(
        src_ref=src,
        dst_ref=dst,
        send_sem=send_sem,
        recv_sem=recv_sem,
        device_id={"dp": dev},
        device_id_type=MESH,
    )


def shifts(rows, dev):
    spot = lax.broadcasted_iota(jnp.int32, (2 * SIDE, rows), 1)
    by_row = SIDE - 1 - (dev * (rows // SIDE) + lax.shift_right_logical(spot, 6))
    by_col = SIDE - 1 - (spot & (SIDE - 1))
    return by_row, by_col


def skew(values, shift):
    for bit in (32, 16, 8, 4, 2, 1):
        moved = pltpu.roll(values, 2 * SIDE - bit, 0)
        values = jnp.where((shift & bit) != 0, moved, values)
    return values[:SIDE]


def unskew(values, shift):
    values = jnp.concatenate([values, jnp.zeros_like(values)], axis=0)
    for bit in (32, 16, 8, 4, 2, 1):
        moved = pltpu.roll(values, bit, 0)
        values = jnp.where((shift & bit) != 0, moved, values)
    return values


def greet(peers):
    barrier = pltpu.get_barrier_semaphore()
    for peer in peers:
        pl.semaphore_signal(barrier, inc=1, device_id={"dp": peer}, device_id_type=MESH)
    pl.semaphore_wait(barrier, len(peers))


def key_onehots(rows, dev):
    spot = lax.broadcasted_iota(jnp.int32, (2 * SIDE, rows), 1)
    index = lax.broadcasted_iota(jnp.int32, (2 * SIDE, rows), 0)
    cols = jnp.where((index & (SIDE - 1)) == (spot & (SIDE - 1)), 1.0, 0.0)
    spot, index = spot[:16], index[:16]
    offset = lax.rem(dev * (rows // SIDE), 8)
    in_group = jnp.where((index & 7) == offset + lax.shift_right_logical(spot, 6), 1.0, 0.0)
    return cols, in_group


class Shape:
    def __init__(self, heads, group, rows):
        self.heads, self.group, self.rows = heads, group, rows
        self.queries = heads * rows
        self.block = min(512, self.queries)


def forward_kernel(
    shape, qkv, tables, att, qaug, bias_rows, kv_out, o_out, lse_out, peak_out,
    rq, rkv, kaug_t, kaug, vaug, oacc, mrow, lpk, att_s, att_r,
    q_send, q_recv, k_send, k_recv, x_send, x_recv, r_send, r_recv, o_sem,
):
    heads, group, rows, block = shape.heads, shape.group, shape.rows, shape.block
    me = lax.axis_index("dp")
    z, g = me // group, lax.rem(me, group)
    column = [lax.rem(z + k, heads) for k in range(1, heads)]
    mates = [lax.rem(g + k, group) for k in range(1, group)]
    greet([h * group + g for h in column] + [z * group + o for o in mates])
    sends = []
    for h in column:
        sends.append(send_dp(qkv.at[h, 0], rq.at[z], q_send.at[h], q_recv.at[z], h * group + g))
    for h in column:
        sends.append(
            send_dp(
                qkv.at[h, pl.ds(1, 2)], rkv.at[z, g], k_send.at[h], k_recv.at[z], h * group + g
            )
        )
    for copy in sends:
        copy.start()
    rq[z] = qkv[z, 0]
    rkv[z, g] = qkv[z, pl.ds(1, 2)]
    qaug[pl.ds(LSE_AT, 16), :] = jnp.zeros((16, shape.queries), LOW)
    kaug_t[pl.ds(LSE_AT, 16), :] = jnp.zeros((16, rows), LOW)
    vaug[pl.ds(HEAD, 16), :] = jnp.where(
        lax.broadcasted_iota(jnp.int32, (16, rows), 0) == 0, 1.0, 0.0
    ).astype(LOW)
    oacc[...] = jnp.zeros_like(oacc)
    mrow[...] = jnp.full_like(mrow, -jnp.inf)
    lpk[...] = jnp.full_like(lpk, -jnp.inf)

    def prepare(k, carry):
        source = lax.rem(z - k + heads, heads)
        span = pl.ds(pl.multiple_of(source * rows, rows), rows)

        @pl.when(k > 0)
        def _():
            send_dp(rq.at[source], rq.at[source], q_send.at[source], q_recv.at[source], me).wait_recv()

        query = rq[source]
        by_row, by_col = shifts(rows, source * group + g)
        along_rows = skew(nn(tables[0], query) * (1.0 / SCALE), by_row)
        along_cols = skew(nn(tables[1], query) * (1.0 / SCALE), by_col)
        qaug[pl.ds(0, HEAD), span] = query
        cols = parts_of(along_cols, 2)
        qaug[pl.ds(COLS_AT, 2 * SIDE), span] = jnp.concatenate(cols, axis=0).astype(LOW)
        high, rest = parts_of(along_rows, 2)
        for at in range(SIDE // 8):
            pair = jnp.concatenate([high[8 * at : 8 * at + 8], rest[8 * at : 8 * at + 8]], axis=0)
            bias_rows[at, :, span] = pair.astype(LOW)
        return carry

    lax.fori_loop(0, heads, prepare, 0)

    def chunk(source, mate):
        dev = source * group + mate
        cols, in_group = key_onehots(rows, dev)
        kaug_t[pl.ds(0, HEAD), :] = rkv[source, mate, 0]
        kaug_t[pl.ds(COLS_AT, 2 * SIDE), :] = cols.astype(LOW)
        kaug_t[pl.ds(ROWS_AT, 16), :] = in_group.astype(LOW)
        kaug[...] = kaug_t[...].T
        vaug[pl.ds(0, HEAD), :] = rkv[source, mate, 1]
        qaug[pl.ds(ROWS_AT, 16), :] = bias_rows[(dev * (rows // SIDE)) // 8]

        def one(i, carry):
            span = pl.ds(pl.multiple_of(i * block, block), block)
            logits = nn(kaug[:, :HEAD], qaug[pl.ds(0, HEAD), span])
            lpk[...] = jnp.maximum(lpk[...], jnp.max(logits.reshape(rows // 8, 8, block), axis=0))
            scores = nn(kaug[...], qaug[:, span])
            before = mrow[:, span]
            top = jnp.maximum(before, jnp.max(scores, axis=0, keepdims=True))
            mrow[:, span] = top
            weights = jnp.exp2(scores * EXP2_SCALE - top * EXP2_SCALE).astype(LOW)
            keep = jnp.exp2((before - top) * EXP2_SCALE)
            oacc[:, span] = oacc[:, span] * keep + nn(vaug[...], weights)
            return carry

        lax.fori_loop(0, shape.queries // block, one, 0)

    def column_step(k, carry):
        source = lax.rem(z - k + heads, heads)

        @pl.when(k > 0)
        def _():
            send_dp(rkv.at[source, g], rkv.at[source, g], k_send.at[source], k_recv.at[source], me).wait_recv()

        for n, mate in enumerate(mates):
            send_dp(
                rkv.at[source, g], rkv.at[source, g], x_send.at[source, n], x_recv.at[source, g],
                z * group + mate,
            ).start()
        chunk(source, g)

        def mate_step(n, inner):
            mate = lax.rem(g + n, group)
            send_dp(
                rkv.at[source, mate], rkv.at[source, mate], x_send.at[source, 0], x_recv.at[source, mate], me
            ).wait_recv()
            chunk(source, mate)
            return inner

        lax.fori_loop(1, group, mate_step, 0)
        return carry

    lax.fori_loop(0, heads, column_step, 0)
    keep_kv = pltpu.make_async_copy(rkv, kv_out, o_sem)
    keep_kv.start()

    def finish(source, carry):
        span = pl.ds(pl.multiple_of(source * rows, rows), rows)
        total = oacc[pl.ds(HEAD, 1), span]
        attended = oacc[pl.ds(0, HEAD), span] / total
        o_out[:, span] = attended
        lse_out[:, span] = mrow[:, span] + jnp.log2(total) * (1.0 / EXP2_SCALE)
        att_s[source] = attended.astype(LOW)

        @pl.when(source != z)
        def _():
            send_dp(
                att_s.at[source], att_r.at[z], r_send.at[source], r_recv.at[z], source * group + g
            ).start()

        return carry

    lax.fori_loop(0, heads, finish, 0)
    att[z] = att_s[z]
    peak_out[...] = jnp.full(peak_out.shape, jnp.max(lpk[...]) * SCALE, F32)
    for h in column:
        send_dp(att_s.at[h], att_r.at[h], r_send.at[h], r_recv.at[h], h * group + g).wait()
        att[h] = att_r[h]
    for copy in sends:
        copy.wait_send()
    for source in range(heads):
        for n, mate in enumerate(mates):
            send_dp(
                rkv.at[source, g], rkv.at[source, g], x_send.at[source, n], x_recv.at[source, g],
                z * group + mate,
            ).wait_send()
    keep_kv.wait()


def attend(shape, qkv, tables):
    heads, group, rows, queries = shape.heads, shape.group, shape.rows, shape.queries
    vmem = pl.BlockSpec(memory_space=pltpu.VMEM)
    hbm = pl.BlockSpec(memory_space=pl.ANY)
    dma = pltpu.SemaphoreType.DMA
    return pl.pallas_call(
        functools.partial(forward_kernel, shape),
        out_shape=(
            jax.ShapeDtypeStruct((heads, HEAD, rows), LOW),
            jax.ShapeDtypeStruct((AUG, queries), LOW),
            jax.ShapeDtypeStruct((SIDE // 8, 16, queries), LOW),
            jax.ShapeDtypeStruct((heads, group, 2, HEAD, rows), LOW),
            jax.ShapeDtypeStruct((HEAD, queries), F32),
            jax.ShapeDtypeStruct((1, queries), F32),
            jax.ShapeDtypeStruct((8, 128), F32),
        ),
        in_specs=[vmem, vmem],
        out_specs=(vmem, vmem, vmem, hbm, vmem, vmem, vmem),
        scratch_shapes=[
            pltpu.VMEM((heads, HEAD, rows), LOW),
            pltpu.VMEM((heads, group, 2, HEAD, rows), LOW),
            pltpu.VMEM((AUG, rows), LOW),
            pltpu.VMEM((rows, AUG), LOW),
            pltpu.VMEM((HEAD + 16, rows), LOW),
            pltpu.VMEM((HEAD + 16, queries), F32),
            pltpu.VMEM((1, queries), F32),
            pltpu.VMEM((8, shape.block), F32),
            pltpu.VMEM((heads, HEAD, rows), LOW),
            pltpu.VMEM((heads, HEAD, rows), LOW),
            dma((heads,)), dma((heads,)), dma((heads,)), dma((heads,)),
            dma((heads, group)), dma((heads, group)), dma((heads,)), dma((heads,)),
            dma,
        ],
        compiler_params=pltpu.CompilerParams(
            collective_id=1, has_side_effects=True, vmem_limit_bytes=VMEM_LIMIT
        ),
        name="attend",
    )(qkv, tables)


def backward_kernel(
    shape, ga, tables, qaug_in, bias_rows, rkv, o_in, lse_in, grads, table_grads,
    rdo, qaug, q_tok, do_aug, do_tok, kaug_t, kaug, vaug_t, vaug, kacc, vacc, dq, drow, dcol,
    part, xr, summed, gq_s, gq_r, gkv_r,
    d_send, d_recv, x_send, x_recv, kv_send, kv_recv, q_send, q_recv,
):
    heads, group, rows, block = shape.heads, shape.group, shape.rows, shape.block
    queries = shape.queries
    me = lax.axis_index("dp")
    z, g = me // group, lax.rem(me, group)
    column = [lax.rem(z + k, heads) for k in range(1, heads)]
    mates = [lax.rem(g + k, group) for k in range(1, group)]
    greet([h * group + g for h in column] + [z * group + o for o in mates])
    sends = []
    for h in column:
        copy = send_dp(ga.at[h], rdo.at[z], d_send.at[h], d_recv.at[z], h * group + g)
        copy.start()
        sends.append(copy)
    rdo[z] = ga[z]
    qaug[...] = qaug_in[...]
    ones = jnp.where(lax.broadcasted_iota(jnp.int32, (16, rows), 0) < 3, 1.0, 0.0).astype(LOW)
    kaug_t[pl.ds(LSE_AT, 16), :] = ones
    vaug_t[pl.ds(HEAD, 16), :] = ones
    vaug_t[pl.ds(HEAD + 16, 32), :] = jnp.zeros((32, rows), LOW)
    low_lse = parts_of(-lse_in[...], 3)
    qaug[pl.ds(LSE_AT, 16), :] = jnp.concatenate(
        low_lse + [jnp.zeros((13, queries), F32)], axis=0
    ).astype(LOW)
    dq[...] = jnp.zeros_like(dq)
    dcol[...] = jnp.zeros_like(dcol)
    drow[...] = jnp.zeros_like(drow)

    def prepare(k, carry):
        source = lax.rem(z - k + heads, heads)
        span = pl.ds(pl.multiple_of(source * rows, rows), rows)

        @pl.when(k > 0)
        def _():
            send_dp(rdo.at[source], rdo.at[source], d_send.at[source], d_recv.at[source], me).wait_recv()

        upstream = rdo[source]
        dots = jnp.sum(upstream.astype(F32) * o_in[:, span], axis=0, keepdims=True)
        low_dots = parts_of(-dots, 3)
        do_aug[pl.ds(0, HEAD), span] = upstream
        do_aug[pl.ds(HEAD, 16), span] = jnp.concatenate(
            low_dots + [jnp.zeros((13, rows), F32)], axis=0
        ).astype(LOW)
        do_aug[pl.ds(HEAD + 16, 32), span] = jnp.zeros((32, rows), LOW)
        do_tok[span, :] = do_aug[:, span].T
        q_tok[span, :] = qaug[pl.ds(0, 128), span].T
        return carry

    lax.fori_loop(0, heads, prepare, 0)

    def chunk(source, mate):
        dev = source * group + mate
        at = (dev * (rows // SIDE)) // 8
        cols, in_group = key_onehots(rows, dev)
        kaug_t[pl.ds(0, HEAD), :] = rkv[source, mate, 0]
        kaug_t[pl.ds(COLS_AT, 2 * SIDE), :] = cols.astype(LOW)
        kaug_t[pl.ds(ROWS_AT, 16), :] = in_group.astype(LOW)
        kaug[...] = kaug_t[...].T
        vaug_t[pl.ds(0, HEAD), :] = rkv[source, mate, 1]
        vaug[...] = vaug_t[...].T
        qaug[pl.ds(ROWS_AT, 16), :] = bias_rows[at]
        kacc[...] = jnp.zeros_like(kacc)
        vacc[...] = jnp.zeros_like(vacc)
        back = jnp.concatenate(
            [kaug_t[pl.ds(0, COLS_AT + SIDE), :], kaug_t[pl.ds(ROWS_AT, 16), :]], axis=0
        )

        def one(i, carry):
            span = pl.ds(pl.multiple_of(i * block, block), block)
            probs = jnp.exp2(nn(kaug[...], qaug[:, span]) * EXP2_SCALE)
            pulled = nn(vaug[...], do_aug[:, span])
            low_grads = (probs * pulled).astype(LOW)
            vacc[...] += nn(probs.astype(LOW), do_tok[span, :])
            kacc[...] += nn(low_grads, q_tok[span, :])
            found = nn(back, low_grads)
            dq[:, span] += found[:HEAD]
            dcol[:, span] += found[COLS_AT : COLS_AT + SIDE]
            drow[at, :, span] += found[COLS_AT + SIDE : COLS_AT + SIDE + 8]
            return carry

        lax.fori_loop(0, queries // block, one, 0)

    def put(where, extra):
        key_part = (kacc[...] * SCALE).T[:HEAD]
        value_part = vacc[...].T[:HEAD]
        for other in extra:
            key_part = key_part + other[0].astype(F32)
            value_part = value_part + other[1].astype(F32)
        where[0] = key_part.astype(LOW)
        where[1] = value_part.astype(LOW)

    def mate_copy(source, mate):
        return send_dp(
            part.at[source, mate], xr.at[source, g], x_send.at[source, mate], x_recv.at[source, g],
            z * group + mate,
        )

    def mates_step(k, carry):
        source = lax.rem(z + k, heads)

        def mate_step(n, inner):
            mate = lax.rem(g + n, group)
            chunk(source, mate)
            put(part.at[source, mate], [])
            mate_copy(source, mate).start()
            return inner

        lax.fori_loop(1, group, mate_step, 0)
        return carry

    lax.fori_loop(1, heads + 1, mates_step, 0)

    def own_step(k, carry):
        source = lax.rem(z + k, heads)
        chunk(source, g)
        extra = []
        for mate in mates:
            send_dp(
                xr.at[source, mate], xr.at[source, mate], x_send.at[source, mate], x_recv.at[source, mate], me
            ).wait_recv()
            extra.append(xr.at[source, mate])
        put(summed.at[source], extra)

        @pl.when(source != z)
        def _():
            send_dp(
                summed.at[source], gkv_r.at[z], kv_send.at[source], kv_recv.at[z], source * group + g
            ).start()

        return carry

    lax.fori_loop(1, heads + 1, own_step, 0)
    table_grads[...] = jnp.zeros_like(table_grads)

    def finish(k, carry):
        source = lax.rem(z + k, heads)
        span = pl.ds(pl.multiple_of(source * rows, rows), rows)
        by_row, by_col = shifts(rows, source * group + g)
        total = dq[:, span] * SCALE
        for n, held in enumerate((drow[:, :, span].reshape(SIDE, rows), dcol[:, span])):
            spread = unskew(held, by_col if n else by_row)
            for piece in parts_of(spread, 2):
                low_piece = piece.astype(LOW)
                total = total + tn(tables[n], low_piece)
                table_grads[n] += nn(low_piece, q_tok[span, :])
        gq_s[source] = total.astype(LOW)

        @pl.when(source != z)
        def _():
            send_dp(
                gq_s.at[source], gq_r.at[z], q_send.at[source], q_recv.at[z], source * group + g
            ).start()

        return carry

    lax.fori_loop(1, heads + 1, finish, 0)
    grads[z, 0] = gq_s[z]
    grads[z, pl.ds(1, 2)] = summed[z]
    for h in column:
        send_dp(summed.at[h], gkv_r.at[h], kv_send.at[h], kv_recv.at[h], h * group + g).wait()
        grads[h, pl.ds(1, 2)] = gkv_r[h]
    for h in column:
        send_dp(gq_s.at[h], gq_r.at[h], q_send.at[h], q_recv.at[h], h * group + g).wait()
        grads[h, 0] = gq_r[h]
    for copy in sends:
        copy.wait_send()
    for source in range(heads):
        for mate in mates:
            mate_copy(source, mate).wait_send()


def attend_back(shape, ga, tables, qaug, bias_rows, kv, o_rows, lse):
    heads, group, rows, queries = shape.heads, shape.group, shape.rows, shape.queries
    vmem = pl.BlockSpec(memory_space=pltpu.VMEM)
    dma = pltpu.SemaphoreType.DMA
    return pl.pallas_call(
        functools.partial(backward_kernel, shape),
        out_shape=(
            jax.ShapeDtypeStruct((heads, 3, HEAD, rows), LOW),
            jax.ShapeDtypeStruct((2, 2 * SIDE, 128), F32),
        ),
        in_specs=[vmem] * 7,
        out_specs=(vmem, vmem),
        scratch_shapes=[
            pltpu.VMEM((heads, HEAD, rows), LOW),
            pltpu.VMEM((AUG, queries), LOW),
            pltpu.VMEM((queries, 128), LOW),
            pltpu.VMEM((128, queries), LOW),
            pltpu.VMEM((queries, 128), LOW),
            pltpu.VMEM((AUG, rows), LOW),
            pltpu.VMEM((rows, AUG), LOW),
            pltpu.VMEM((128, rows), LOW),
            pltpu.VMEM((rows, 128), LOW),
            pltpu.VMEM((rows, 128), F32),
            pltpu.VMEM((rows, 128), F32),
            pltpu.VMEM((HEAD, queries), F32),
            pltpu.VMEM((SIDE // 8, 8, queries), F32),
            pltpu.VMEM((SIDE, queries), F32),
            pltpu.VMEM((heads, group, 2, HEAD, rows), LOW),
            pltpu.VMEM((heads, group, 2, HEAD, rows), LOW),
            pltpu.VMEM((heads, 2, HEAD, rows), LOW),
            pltpu.VMEM((heads, HEAD, rows), LOW),
            pltpu.VMEM((heads, HEAD, rows), LOW),
            pltpu.VMEM((heads, 2, HEAD, rows), LOW),
            dma((heads,)), dma((heads,)), dma((heads, group)), dma((heads, group)),
            dma((heads,)), dma((heads,)), dma((heads,)), dma((heads,)),
        ],
        compiler_params=pltpu.CompilerParams(
            collective_id=2, has_side_effects=True, vmem_limit_bytes=VMEM_LIMIT
        ),
        name="attend_back",
    )(ga, tables, qaug, bias_rows, kv, o_rows, lse)


def send_tensor(src, dst, send_sem, recv_sem, dev):
    return pltpu.make_async_remote_copy(
        src_ref=src,
        dst_ref=dst,
        send_sem=send_sem,
        recv_sem=recv_sem,
        device_id={"tensor": dev},
        device_id_type=MESH,
    )


def tensor_place():
    me = lax.axis_index("tensor")
    return lax.rem(me, 2), me // 2, lax.axis_size("tensor") // 2


def tensor_peers():
    core, line, lines = tensor_place()
    far = [lax.rem(line + k, lines) * 2 + core for k in range(1, lines)]
    return far + [line * 2 + 1 - core]


def part_bufs(lines, share, width):
    dma = pltpu.SemaphoreType.DMA
    return [pltpu.VMEM((lines, share, width), LOW)] * 3 + [dma((lines,))] * 4


class Reduce:
    def __init__(self, part, mate_in, passed, line_in, m_send, m_recv, l_send, l_recv):
        self.part, self.mate_in, self.passed, self.line_in = part, mate_in, passed, line_in
        self.sems = m_send, m_recv, l_send, l_recv
        self.core, self.line, self.lines = tensor_place()

    def mate_copy(self, to):
        m_send, m_recv, _, _ = self.sems
        return send_tensor(
            self.part.at[to * 2 + 1 - self.core], self.mate_in.at[to],
            m_send.at[to], m_recv.at[to], self.line * 2 + 1 - self.core,
        )

    def line_copy(self, to, slot):
        _, _, l_send, l_recv = self.sems
        return send_tensor(
            self.passed.at[to], self.line_in.at[slot], l_send.at[to], l_recv.at[slot],
            to * 2 + self.core,
        )

    def give(self, to):
        self.mate_copy(to).start()

    def pass_on(self, to):
        self.mate_copy(to).wait_recv()
        both = self.part[to * 2 + self.core].astype(F32) + self.mate_in[to].astype(F32)
        self.passed[to] = both.astype(LOW)
        self.line_copy(to, self.line).start()

    def others(self):
        return [lax.rem(self.line + k, self.lines) for k in range(1, self.lines)]

    def total(self):
        self.mate_copy(self.line).wait_recv()
        total = self.part[self.line * 2 + self.core].astype(F32) + self.mate_in[self.line].astype(F32)
        for other in self.others():
            self.line_copy(other, other).wait_recv()
            total = total + self.line_in[other].astype(F32)
        return total

    def finish(self):
        self.mate_copy(self.line).wait_send()
        for other in self.others():
            self.mate_copy(other).wait_send()
            self.line_copy(other, self.line).wait_send()


def gather_sems(lines):
    dma = pltpu.SemaphoreType.DMA
    return [dma((lines,)), dma((lines,)), dma((2 * lines,))]


class Gather:
    def __init__(self, whole, l_send, m_send, recv):
        self.whole, self.sems = whole, (l_send, m_send, recv)
        self.core, self.line, self.lines = tensor_place()

    def line_copy(self, to):
        l_send, _, recv = self.sems
        own = self.line * 2 + self.core
        return send_tensor(
            self.whole.at[own], self.whole.at[own], l_send.at[to], recv.at[own], to * 2 + self.core
        )

    def mate_copy(self, at):
        _, m_send, recv = self.sems
        part = at * 2 + self.core
        return send_tensor(
            self.whole.at[part], self.whole.at[part], m_send.at[at], recv.at[part],
            self.line * 2 + 1 - self.core,
        )

    def arrived(self, part):
        l_send, _, recv = self.sems
        send_tensor(
            self.whole.at[part], self.whole.at[part], l_send.at[0], recv.at[part], part
        ).wait_recv()

    def others(self):
        return [lax.rem(self.line + k, self.lines) for k in range(1, self.lines)]

    def start(self):
        for other in self.others():
            self.line_copy(other).start()
        self.mate_copy(self.line).start()

    def forward(self, at):
        self.arrived(at * 2 + self.core)
        self.mate_copy(at).start()

    def take(self, at):
        self.arrived(at * 2 + 1 - self.core)

    def finish(self):
        self.mate_copy(self.line).wait_send()
        for other in self.others():
            self.mate_copy(other).wait_send()
            self.line_copy(other).wait_send()


def normed(values):
    center = values - jnp.mean(values, axis=-1, keepdims=True)
    variance = jnp.mean(center * center, axis=-1, keepdims=True)
    inverse = lax.rsqrt(variance + EPSILON)
    return center * inverse, inverse


def normed_back(upstream, scaled, inverse, gain):
    weighted = upstream * gain
    centered = weighted - jnp.mean(weighted, axis=-1, keepdims=True)
    return (centered - scaled * jnp.mean(weighted * scaled, axis=-1, keepdims=True)) * inverse


def tile_of(width):
    return 256 if width % 256 == 0 else 128


def middle_kernel(
    att, proj_w, tokens, cot, fc1_hbm, fc2_hbm, fc1_bias, vectors,
    output, branch_out, middle_out, fc1_out, fc2_out, proj_out, ga_out, fc1_bias_out, sums_out,
    fc1, fc2, att_tok, branch, mlp, back, n2, act, gu, gb, outs, held, spread,
    load1, load2, *rest,
):
    core, line, lines = tensor_place()
    me = lax.axis_index("tensor")
    _, share, width = tokens.shape
    rows = tokens.shape[0] * share
    hidden = fc1_hbm.shape[1]
    step, dstep = tile_of(hidden), tile_of(width)
    in_fc1 = pltpu.make_async_copy(fc1_hbm, fc1, load1)
    in_fc2 = pltpu.make_async_copy(fc2_hbm, fc2, load2)
    in_fc1.start()
    in_fc2.start()
    greet_tensor()
    sum_branch = Reduce(branch, *rest[0:7])
    sum_mlp = Reduce(mlp, *rest[7:14])
    sum_back = Reduce(back, *rest[14:21])
    all_n2 = Gather(n2, *rest[21:24])
    all_gb = Gather(gb, *rest[24:27])
    all_out = Gather(outs, *rest[27:30])
    att_tok[...] = att[...].T.reshape(att_tok.shape)

    def project(k, carry):
        to = lax.rem(line + 1 + lax.rem(k, lines), lines)
        part = to * 2 + jnp.where(k < lines, 1 - core, core)
        branch[part] = nn(att_tok[part], proj_w[...]).astype(LOW)

        @pl.when(k < lines)
        def _():
            sum_branch.give(to)

        return carry

    lax.fori_loop(0, 2 * lines, project, 0)
    for other in sum_branch.others():
        sum_branch.pass_on(other)
    middle = tokens[me].astype(F32) + vectors[0:1]
    middle = middle + sum_branch.total()
    scaled, inverse = normed(middle)
    n2[me] = (scaled * vectors[1:2] + vectors[2:3]).astype(LOW)
    all_n2.start()
    held[0] = middle
    held[1] = scaled
    spread[...] = jnp.broadcast_to(inverse, spread.shape)
    fc1_bias_out[...] = jnp.zeros_like(fc1_bias_out)
    in_fc1.wait()
    in_fc2.wait()

    def hidden_part(k, carry):
        at = lax.rem(line + k, lines)

        @pl.when(k > 0)
        def _():
            all_n2.forward(at)

        all_n2.take(at)
        pair = pl.ds(at * 2, 2)
        inputs = n2[pair].reshape(2 * share, width)
        pulls = cot[pair].reshape(2 * share, width)

        def tile(n, inner):
            span = pl.ds(pl.multiple_of(n * step, step), step)
            up = nn(inputs, fc1[:, span]) + fc1_bias[:, span]
            phi = 0.5 + 0.5 * lax.erf(up * math.sqrt(0.5))
            slope = phi + up * (jnp.exp(-0.5 * up * up) * (2 * math.pi) ** -0.5)
            act[pair, :, span] = (up * phi).astype(LOW).reshape(2, share, step)
            grad_up = (nt(pulls, fc2[span, :]) * slope).astype(LOW)
            gu[pair, :, span] = grad_up.reshape(2, share, step)
            fc1_bias_out[:, span] += jnp.sum(grad_up.astype(F32), axis=0, keepdims=True)
            return inner

        lax.fori_loop(0, hidden // step, tile, 0)

        def tile_back(n, inner):
            span = pl.ds(pl.multiple_of(n * dstep, dstep), dstep)
            found = nt(gu[pair].reshape(2 * share, hidden), fc1[span, :])
            back[pair, :, span] = found.astype(LOW).reshape(2, share, dstep)
            return inner

        lax.fori_loop(0, width // dstep, tile_back, 0)
        sum_back.give(at)

        def tile_out(n, inner):
            span = pl.ds(pl.multiple_of(n * dstep, dstep), dstep)
            found = nn(act[pair].reshape(2 * share, hidden), fc2[:, span])
            mlp[pair, :, span] = found.astype(LOW).reshape(2, share, dstep)
            return inner

        lax.fori_loop(0, width // dstep, tile_out, 0)
        sum_mlp.give(at)
        return carry

    lax.fori_loop(0, lines, hidden_part, 0)
    for other in sum_back.others():
        sum_back.pass_on(other)
    for other in sum_mlp.others():
        sum_mlp.pass_on(other)

    def weights2(n, carry):
        span = pl.ds(pl.multiple_of(n * dstep, dstep), dstep)
        found = tn(cot[:, :, span].reshape(rows, dstep), act[...].reshape(rows, hidden))
        fc2_out[span, :] = found.astype(LOW)
        return carry

    lax.fori_loop(0, width // dstep, weights2, 0)
    upstream = sum_back.total()
    sums_out[0:1] = jnp.sum(upstream * held[1], axis=0, keepdims=True)
    sums_out[1:2] = jnp.sum(upstream, axis=0, keepdims=True)
    grad_middle = cot[me].astype(F32) + normed_back(
        upstream, held[1], spread[:, :1], vectors[1:2]
    )
    middle_out[...] = grad_middle
    gb[me] = grad_middle.astype(LOW)
    all_gb.start()
    outs[me] = (held[0] + sum_mlp.total() + vectors[3:4]).astype(LOW)
    all_out.start()

    def weights1(n, carry):
        span = pl.ds(pl.multiple_of(n * dstep, dstep), dstep)
        found = tn(n2[:, :, span].reshape(rows, dstep), gu[...].reshape(rows, hidden))
        fc1_out[span, :] = found.astype(LOW)
        return carry

    lax.fori_loop(0, width // dstep, weights1, 0)
    sums_out[2:3] = jnp.sum(cot[...].astype(F32).reshape(rows, width), axis=0, keepdims=True)
    for other in all_gb.others():
        all_gb.forward(other)
    for other in all_out.others():
        all_out.forward(other)
    all_gb.take(line)
    for other in all_gb.others():
        all_gb.take(other)
    whole = gb[...].reshape(rows, width)
    sums_out[3:4] = jnp.sum(whole.astype(F32), axis=0, keepdims=True)
    ga_out[...] = nt(proj_w[...], whole).astype(LOW)

    def weights0(n, carry):
        span = pl.ds(pl.multiple_of(n * dstep, dstep), dstep)
        found = tn(gb[:, :, span].reshape(rows, dstep), att_tok[...].reshape(rows, -1))
        proj_out[span, :] = found.astype(LOW)
        return carry

    lax.fori_loop(0, width // dstep, weights0, 0)
    branch_out[...] = gb[...]
    all_out.take(line)
    for other in all_out.others():
        all_out.take(other)
    output[...] = outs[...]
    for each in (sum_branch, sum_mlp, sum_back, all_n2, all_gb, all_out):
        each.finish()


def middle_block(att, proj_w, tokens, cot, fc1, fc2, fc1_bias, vectors):
    count = lax.axis_size("tensor")
    lines = count // 2
    local, width = proj_w.shape
    rows = tokens.shape[0]
    share = rows // count
    hidden = fc1.shape[1]
    vmem = pl.BlockSpec(memory_space=pltpu.VMEM)
    hbm = pl.BlockSpec(memory_space=pl.ANY)
    dma = pltpu.SemaphoreType.DMA
    whole = (count, share, width)
    scratch = [
        pltpu.VMEM((width, hidden), LOW),
        pltpu.VMEM((hidden, width), LOW),
        pltpu.VMEM((count, share, local), LOW),
        pltpu.VMEM(whole, LOW),
        pltpu.VMEM(whole, LOW),
        pltpu.VMEM(whole, LOW),
        pltpu.VMEM(whole, LOW),
        pltpu.VMEM((count, share, hidden), LOW),
        pltpu.VMEM((count, share, hidden), LOW),
        pltpu.VMEM(whole, LOW),
        pltpu.VMEM(whole, LOW),
        pltpu.VMEM((2, share, width), F32),
        pltpu.VMEM((share, 128), F32),
        dma,
        dma,
    ]
    scratch += part_bufs(lines, share, width) * 3 + gather_sems(lines) * 3
    return pl.pallas_call(
        middle_kernel,
        out_shape=(
            jax.ShapeDtypeStruct(whole, LOW),
            jax.ShapeDtypeStruct(whole, LOW),
            jax.ShapeDtypeStruct((share, width), F32),
            jax.ShapeDtypeStruct((width, hidden), LOW),
            jax.ShapeDtypeStruct((width, hidden), LOW),
            jax.ShapeDtypeStruct((width, local), LOW),
            jax.ShapeDtypeStruct((local, rows), LOW),
            jax.ShapeDtypeStruct((1, hidden), F32),
            jax.ShapeDtypeStruct((8, width), F32),
        ),
        in_specs=[vmem] * 4 + [hbm] * 2 + [vmem] * 2,
        out_specs=(vmem,) * 9,
        scratch_shapes=scratch,
        compiler_params=pltpu.CompilerParams(
            collective_id=3, has_side_effects=True, vmem_limit_bytes=VMEM_LIMIT
        ),
        name="middle",
    )(
        att, proj_w, tokens.reshape(whole), cot.reshape(whole), fc1, fc2,
        fc1_bias.reshape(1, hidden), vectors,
    )


def greet_tensor():
    peers = tensor_peers()
    barrier = pltpu.get_barrier_semaphore()
    for peer in peers:
        pl.semaphore_signal(barrier, inc=1, device_id={"tensor": peer}, device_id_type=MESH)
    pl.semaphore_wait(barrier, len(peers))


class Ring:
    def __init__(self, heads):
        self.heads, self.group = heads, lax.axis_size("dp") // heads
        me = lax.axis_index("dp")
        self.z, self.g = me // self.group, lax.rem(me, self.group)

    def column(self):
        return [lax.rem(self.z + k, self.heads) for k in range(1, self.heads)]

    def mates(self):
        return [lax.rem(self.g + k, self.group) for k in range(1, self.group)]

    def peers(self):
        far = [h * self.group + self.g for h in self.column()]
        return far + [self.z * self.group + o for o in self.mates()]


def greet_all(ring):
    barrier = pltpu.get_barrier_semaphore()
    near, far = tensor_peers(), ring.peers()
    for peer in near:
        pl.semaphore_signal(barrier, inc=1, device_id={"tensor": peer}, device_id_type=MESH)
    for peer in far:
        pl.semaphore_signal(barrier, inc=1, device_id={"dp": peer}, device_id_type=MESH)
    pl.semaphore_wait(barrier, len(near) + len(far))


def scatter_bufs(heads, share, width):
    group = lax.axis_size("dp") // heads
    dma = pltpu.SemaphoreType.DMA
    block = (heads, share, width)
    return [
        pltpu.VMEM(block, LOW), pltpu.VMEM((group,) + block, LOW), pltpu.VMEM(block, LOW),
        pltpu.VMEM(block, LOW), dma((heads, group)), dma((heads, group)),
        dma((heads,)), dma((heads,)), dma((heads,)),
    ]


SCATTER_BUFS = 9


class Scatter:
    def __init__(self, ring, source, mine, mate_in, passed, far_in, m_send, m_recv, f_send, f_recv, load):
        self.ring, self.source, self.mine = ring, source, mine
        self.mate_in, self.passed, self.far_in = mate_in, passed, far_in
        self.sems = m_send, m_recv, f_send, f_recv, load

    def load_copy(self, at):
        ring = self.ring
        return pltpu.make_async_copy(
            self.source.at[at * ring.group + ring.g], self.mine.at[at], self.sems[4].at[at]
        )

    def mate_copy(self, at, mate, slot):
        ring = self.ring
        return send_dp(
            self.source.at[at * ring.group + mate], self.mate_in.at[slot, at],
            self.sems[0].at[at, mate], self.sems[1].at[at, slot], ring.z * ring.group + mate,
        )

    def far_copy(self, at, slot):
        ring = self.ring
        return send_dp(
            self.passed.at[at], self.far_in.at[slot], self.sems[2].at[at], self.sems[3].at[slot],
            at * ring.group + ring.g,
        )

    def give(self, at):
        self.load_copy(at).start()
        for mate in self.ring.mates():
            self.mate_copy(at, mate, self.ring.g).start()

    def give_all(self):
        for at in self.ring.column() + [self.ring.z]:
            self.give(at)

    def near_sum(self, at):
        self.load_copy(at).wait()
        total = self.mine[at].astype(F32)
        for mate in self.ring.mates():
            self.mate_copy(at, mate, mate).wait_recv()
            total = total + self.mate_in[mate, at].astype(F32)
        return total

    def pass_on(self, at):
        self.passed[at] = self.near_sum(at).astype(LOW)
        self.far_copy(at, self.ring.z).start()

    def pass_all(self):
        def step(k, carry):
            self.pass_on(lax.rem(self.ring.z + k, self.ring.heads))
            return carry

        lax.fori_loop(1, self.ring.heads, step, 0)

    def total(self):
        total = self.near_sum(self.ring.z)
        for other in self.ring.column():
            self.far_copy(other, other).wait_recv()
            total = total + self.far_in[other].astype(F32)
        return total

    def finish(self):
        for at in self.ring.column() + [self.ring.z]:
            for mate in self.ring.mates():
                self.mate_copy(at, mate, self.ring.g).wait_send()
        for other in self.ring.column():
            self.far_copy(other, self.ring.z).wait_send()


def small_bufs(heads, stages, shape):
    group, lines = lax.axis_size("dp") // heads, lax.axis_size("tensor") // 2
    dma = pltpu.SemaphoreType.DMA
    found = []
    for stage in stages:
        count = {"core": 2, "line": lines, "mate": group, "far": heads}[stage]
        found += [
            pltpu.VMEM(shape, F32), pltpu.VMEM((count,) + shape, F32), dma((count,)), dma((count,))
        ]
    return found


class Small:
    def __init__(self, ring, stages, merge, *bufs):
        self.ring, self.stages, self.merge = ring, stages, merge
        self.bufs = [bufs[4 * n : 4 * n + 4] for n in range(len(stages))]
        core, line, lines = tensor_place()
        self.peers = {
            "core": (core, [(1 - core, line * 2 + 1 - core)]),
            "line": (line, [(o, o * 2 + core) for o in [lax.rem(line + k, lines) for k in range(1, lines)]]),
            "mate": (ring.g, [(o, ring.z * ring.group + o) for o in ring.mates()]),
            "far": (ring.z, [(o, o * ring.group + ring.g) for o in ring.column()]),
        }

    def copy(self, n, slot, other, dev):
        value, held, send, recv = self.bufs[n]
        call = send_tensor if self.stages[n] in ("core", "line") else send_dp
        return call(value, held.at[slot], send.at[other], recv.at[slot], dev)

    def start(self, n, value):
        own, peers = self.peers[self.stages[n]]
        self.bufs[n][0][...] = value
        for other, dev in peers:
            self.copy(n, own, other, dev).start()

    def take(self, n):
        _, peers = self.peers[self.stages[n]]
        total = self.bufs[n][0][...]
        for other, dev in peers:
            self.copy(n, other, other, dev).wait_recv()
            total = self.merge(total, self.bufs[n][1][other])
        return total

    def run(self, upto=None):
        for n in range(len(self.stages)):
            value = self.take(n)
            if n + 1 < len(self.stages):
                self.start(n + 1, value)
        return value

    def finish(self):
        for n in range(len(self.stages)):
            own, peers = self.peers[self.stages[n]]
            for other, dev in peers:
                self.copy(n, own, other, dev).wait_send()


EVERY = ("core", "line", "mate", "far")
OVER_DP = ("mate", "far")


def add_peaks(a, b):
    row = lax.broadcasted_iota(jnp.int32, a.shape, 0)
    return jnp.where(row == 2, jnp.maximum(a, b), a + b)


def widen(row, width):
    if row.shape[1] == width:
        return row
    return jnp.concatenate([row, jnp.zeros((1, width - row.shape[1]), F32)], axis=1)


def tail_kernel(
    heads, grads, qkv_w, n1_t, tokens, grad_middle, vectors, tables, sums, fc1_bias, peak,
    fc1, fc2, proj,
    tokens_out, fc1_out, fc2_out, proj_out, qkv_out, tables_out, sums_out, late_out, dp_out,
    g_all, g_tok, part, gt, gq, *rest,
):
    ring = Ring(heads)
    core, line, lines = tensor_place()
    me = lax.axis_index("tensor")
    count, share, width = tokens.shape
    rows = count * share
    local = heads * HEAD
    dstep = tile_of(width)
    rest = list(rest)

    def taken(number):
        found, rest[:] = rest[:number], rest[number:]
        return found

    greet_all(ring)
    moved2 = Scatter(ring, fc2, *taken(SCATTER_BUFS))
    moved1 = Scatter(ring, fc1, *taken(SCATTER_BUFS))
    moved0 = Scatter(ring, proj, *taken(SCATTER_BUFS))
    moved3 = Scatter(ring, gq, *taken(SCATTER_BUFS))
    sum_part = Reduce(part, *taken(7))
    all_gt = Gather(gt, *taken(3))
    small_tables = Small(ring, EVERY, lax.add, *taken(16))
    small_sums = Small(ring, EVERY, lax.add, *taken(16))
    small_late = Small(ring, EVERY, lax.add, *taken(16))
    small_dp = Small(ring, OVER_DP, add_peaks, *taken(8))
    moved2.give_all()
    moved1.give_all()
    moved0.give_all()
    small_tables.start(0, tables[...].reshape(4 * SIDE, 128))
    small_sums.start(0, sums[...])
    for t in range(3):
        for h in range(heads):
            g_all[pl.ds(t * local + h * HEAD, HEAD), :] = grads[h, t]
    g_tok[...] = g_all[...].T.reshape(g_tok.shape)
    whole = g_tok[...].reshape(rows, 3 * local)
    lane = lax.broadcasted_iota(jnp.int32, (1, width), 1)
    peaks = jnp.where(lane == ring.z, peak[0:1, 0:1], -jnp.inf)
    bias_sums = jnp.sum(whole.astype(F32), axis=0, keepdims=True)
    dp_rows = [widen(fc1_bias[...], width), widen(bias_sums, width), peaks]
    small_dp.start(0, jnp.concatenate(dp_rows + [jnp.zeros((5, width), F32)], axis=0))

    def norm_part(k, carry):
        at = lax.rem(line + 1 + k, lines)
        pair = pl.ds(at * 2, 2)

        def tile(n, inner):
            span = pl.ds(pl.multiple_of(n * dstep, dstep), dstep)
            found = nt(g_tok[pair].reshape(2 * share, 3 * local), qkv_w[span, :])
            part[pair, :, span] = found.astype(LOW).reshape(2, share, dstep)
            return inner

        lax.fori_loop(0, width // dstep, tile, 0)
        sum_part.give(at)
        return carry

    lax.fori_loop(0, lines, norm_part, 0)
    for other in sum_part.others():
        sum_part.pass_on(other)

    def weight_part(k, carry):
        at = lax.rem(ring.z + 1 + k // ring.group, heads)
        dev = at * ring.group + lax.rem(ring.g + 1 + lax.rem(k, ring.group), ring.group)
        gq[dev] = nn(n1_t[dev], g_tok[...].reshape(rows, 3 * local)).astype(LOW)

        @pl.when(lax.rem(k, ring.group) == ring.group - 1)
        def _():
            moved3.give(at)

        return carry

    lax.fori_loop(0, heads * ring.group, weight_part, 0)
    scaled, inverse = normed(tokens[me].astype(F32))
    upstream = sum_part.total()
    late = [
        jnp.sum(upstream * scaled, axis=0, keepdims=True),
        jnp.sum(upstream, axis=0, keepdims=True),
        jnp.zeros((6, width), F32),
    ]
    small_late.start(0, jnp.concatenate(late, axis=0))
    found = grad_middle[...] + normed_back(upstream, scaled, inverse, vectors[0:1])
    gt[me] = found.astype(LOW)
    all_gt.start()
    moved2.pass_all()
    for other in all_gt.others():
        all_gt.forward(other)
    dp_out[...] = small_dp.run()
    sums_out[...] = small_sums.run()
    moved1.pass_all()
    tables_out[...] = small_tables.run()
    moved0.pass_all()
    all_gt.take(line)
    for other in all_gt.others():
        all_gt.take(other)
    tokens_out[...] = gt[...]
    late_out[...] = small_late.run()
    moved3.pass_all()
    fc2_out[...] = moved2.total().T
    fc1_out[...] = moved1.total()
    proj_out[...] = moved0.total().T
    qkv_out[...] = moved3.total()
    for each in (
        moved0, moved1, moved2, moved3, sum_part, all_gt,
        small_tables, small_sums, small_late, small_dp,
    ):
        each.finish()


def tail(heads, grads, qkv_w, n1_t, tokens, grad_middle, vectors, tables, sums, fc1_bias, peak, fc1, fc2, proj):
    count = lax.axis_size("tensor")
    lines = count // 2
    local = heads * HEAD
    devices, owned, rows = n1_t.shape
    width = devices * owned
    share = rows // count
    hidden = fc1.shape[1]
    vmem = pl.BlockSpec(memory_space=pltpu.VMEM)
    hbm = pl.BlockSpec(memory_space=pl.ANY)
    whole = (count, share, width)
    scratch = [
        pltpu.VMEM((3 * local, rows), LOW),
        pltpu.VMEM((count, share, 3 * local), LOW),
        pltpu.VMEM(whole, LOW),
        pltpu.VMEM(whole, LOW),
        pltpu.VMEM((devices, owned, 3 * local), LOW),
    ]
    for columns in (hidden, hidden, local, 3 * local):
        scratch += scatter_bufs(heads, owned, columns)
    scratch += part_bufs(lines, share, width) + gather_sems(lines)
    scratch += small_bufs(heads, EVERY, (4 * SIDE, 128))
    scratch += small_bufs(heads, EVERY, (8, width)) * 2
    scratch += small_bufs(heads, OVER_DP, (8, width))
    return pl.pallas_call(
        functools.partial(tail_kernel, heads),
        out_shape=(
            jax.ShapeDtypeStruct(whole, LOW),
            jax.ShapeDtypeStruct((owned, hidden), F32),
            jax.ShapeDtypeStruct((hidden, owned), F32),
            jax.ShapeDtypeStruct((local, owned), F32),
            jax.ShapeDtypeStruct((owned, 3 * local), F32),
            jax.ShapeDtypeStruct((4 * SIDE, 128), F32),
            jax.ShapeDtypeStruct((8, width), F32),
            jax.ShapeDtypeStruct((8, width), F32),
            jax.ShapeDtypeStruct((8, width), F32),
        ),
        in_specs=[vmem] * 10 + [hbm] * 3,
        out_specs=(vmem,) * 9,
        scratch_shapes=scratch,
        compiler_params=pltpu.CompilerParams(
            collective_id=4, has_side_effects=True, vmem_limit_bytes=VMEM_LIMIT
        ),
        name="tail",
    )(
        grads, qkv_w, n1_t, tokens.reshape(whole), grad_middle, vectors, tables, sums, fc1_bias, peak,
        fc1.reshape(devices, owned, hidden), fc2.reshape(devices, owned, hidden),
        proj.reshape(devices, owned, local),
    )


def on_device(
    tokens,
    cotangent,
    norm1_gain,
    norm1_shift,
    qkv_weight,
    qv_bias,
    proj_weight,
    proj_bias,
    table_rows,
    table_cols,
    norm2_gain,
    norm2_shift,
    fc1_weight,
    fc1_bias,
    fc2_weight,
    fc2_bias,
    threshold,
):
    images, row_count, model_width = tokens.shape
    token_count = images * row_count
    local_width = qkv_weight.shape[2]
    local_heads = local_width // HEAD
    groups = lax.axis_size("tensor")
    residual_in = tokens.reshape(token_count, model_width).astype(jnp.float32)
    scaled1, _ = normed(residual_in)
    normed1_low = (scaled1 * norm1_gain + norm1_shift).astype(jnp.bfloat16)
    shape = Shape(local_heads, lax.axis_size("dp") // local_heads, row_count)
    flipped = jnp.stack([table_rows, table_cols])[:, ::-1]
    flipped = jnp.pad(flipped, ((0, 0), (0, 1), (0, 0)))
    triple = jnp.einsum("dtc,nd->tcn", qkv_weight, normed1_low, preferred_element_type=jnp.float32)
    bias = jnp.stack([qv_bias[0], jnp.zeros_like(qv_bias[0]), qv_bias[1]])
    triple = (triple + bias[:, :, None]).astype(jnp.bfloat16)
    qkv = triple.reshape(3, local_heads, HEAD, row_count).transpose(1, 0, 2, 3)
    attended, qaug, bias_rows, kv, o_rows, lse, peak = attend(shape, qkv, flipped)
    grad_out = cotangent.reshape(token_count, model_width)
    vectors = jnp.stack([proj_bias, norm2_gain, norm2_shift, fc2_bias])
    vectors = jnp.pad(vectors, ((0, 4), (0, 0)))
    (
        output,
        grad_branch,
        grad_middle,
        grad_fc1,
        grad_fc2,
        grad_proj,
        grad_attended,
        grad_fc1_bias,
        sums,
    ) = middle_block(
        attended.reshape(local_width, token_count),
        proj_weight,
        tokens.reshape(token_count, model_width),
        grad_out,
        fc1_weight,
        fc2_weight,
        fc1_bias,
        vectors,
    )
    grad_heads = grad_attended.reshape(local_heads, HEAD, row_count)
    grad_triple, table_terms = attend_back(
        shape, grad_heads, flipped, qaug, bias_rows, kv, o_rows, lse
    )
    devices = lax.axis_size("dp")
    tail_vectors = jnp.pad(norm1_gain[None], ((0, 7), (0, 0)))
    (
        grad_tokens,
        grad_fc1,
        grad_fc2,
        grad_proj,
        grad_qkv,
        table_sums,
        sums,
        late,
        dp_sums,
    ) = tail(
        local_heads,
        grad_triple,
        qkv_weight.reshape(model_width, 3 * local_width),
        normed1_low.T.reshape(devices, model_width // devices, token_count),
        tokens.reshape(token_count, model_width),
        grad_middle,
        tail_vectors,
        table_terms,
        sums,
        grad_fc1_bias,
        peak,
        grad_fc1,
        grad_fc2,
        grad_proj,
    )
    grad_tokens = grad_tokens.reshape(images, row_count, model_width)
    grad_qkv = grad_qkv.reshape(model_width // devices, 3, local_width)
    table_sums = table_sums.reshape(2, 2 * SIDE, 128)[:, 2 * SIDE - 2 :: -1, :HEAD]
    grad_table_rows, grad_table_cols = table_sums[0], table_sums[1]
    grad_norm2_gain, grad_norm2_shift = sums[0], sums[1]
    grad_fc2_bias, grad_proj_bias = sums[2] / groups, sums[3] / groups
    grad_norm1_gain, grad_norm1_shift = late[0], late[1]
    grad_fc1_bias = dp_sums[0, : fc1_bias.shape[0]]
    grad_qv_bias = dp_sums[1, : 3 * local_width].reshape(3, local_width)[0::2]
    head_peaks = dp_sums[2, :local_heads]
    limit = threshold[0]
    clip_factors = jnp.sqrt(limit / jnp.maximum(head_peaks, limit))
    spread_factors = jnp.repeat(clip_factors, HEAD)
    clipped_qk = (qkv_weight[:, :2, :].astype(jnp.float32) * spread_factors).astype(jnp.bfloat16)
    clipped_q_bias = qv_bias[0] * spread_factors
    output = output.reshape(images, row_count, model_width)
    return (
        output,
        grad_tokens,
        grad_norm1_gain,
        grad_norm1_shift,
        grad_qkv,
        grad_qv_bias,
        grad_proj,
        grad_proj_bias,
        grad_table_rows,
        grad_table_cols,
        grad_norm2_gain,
        grad_norm2_shift,
        grad_fc1,
        grad_fc1_bias,
        grad_fc2,
        grad_fc2_bias,
        clipped_qk,
        clipped_q_bias,
        head_peaks,
        clip_factors,
    )


def solution(mesh):
    in_specs = (
        P(None, "dp", None),
        P(None, "dp", None),
        P(),
        P(),
        P(None, None, "tensor"),
        P(None, "tensor"),
        P("tensor", None),
        P(),
        P(),
        P(),
        P(),
        P(),
        P(None, "tensor"),
        P("tensor"),
        P("tensor", None),
        P(),
        P(),
    )
    out_specs = (
        P(None, "dp", None),
        P(None, "dp", None),
        P(),
        P(),
        P("dp", None, "tensor"),
        P(None, "tensor"),
        P("tensor", "dp"),
        P(),
        P(),
        P(),
        P(),
        P(),
        P("dp", "tensor"),
        P("tensor"),
        P("tensor", "dp"),
        P(),
        P(None, None, "tensor"),
        P("tensor"),
        P("tensor"),
        P("tensor"),
    )
    return jax.shard_map(
        on_device, mesh=mesh, in_specs=in_specs, out_specs=out_specs, check_vma=False
    )
```

```python
import functools
import math

import jax
import jax.numpy as jnp
from jax import lax
from jax.experimental import pallas as pl
from jax.experimental.pallas import tpu as pltpu
from jax.sharding import PartitionSpec as P

HEAD = 80
SIDE = 64

MESH = pl.DeviceIdType.MESH
LOW = jnp.bfloat16
F32 = jnp.float32
EPSILON = 1e-06
SCALE = HEAD**-0.5
EXP2_SCALE = SCALE * math.log2(math.e)
COLS_AT = HEAD
ROWS_AT = COLS_AT + 2 * SIDE
LSE_AT = ROWS_AT + 16
AUG = LSE_AT + 16
VMEM_LIMIT = 60 * 2**20


def nn(a, b):
    return lax.dot_general(a, b, (((1,), (0,)), ((), ())), preferred_element_type=F32)


def tn(a, b):
    return lax.dot_general(a, b, (((0,), (0,)), ((), ())), preferred_element_type=F32)


def nt(a, b):
    return lax.dot_general(a, b, (((1,), (1,)), ((), ())), preferred_element_type=F32)


def parts_of(values, count):
    pieces = []
    for _ in range(count):
        piece = values.astype(LOW).astype(F32)
        pieces.append(piece)
        values = values - piece
    return pieces


def send_dp(src, dst, send_sem, recv_sem, dev):
    return pltpu.make_async_remote_copy(
        src_ref=src,
        dst_ref=dst,
        send_sem=send_sem,
        recv_sem=recv_sem,
        device_id={"dp": dev},
        device_id_type=MESH,
    )


def shifts(rows, dev):
    spot = lax.broadcasted_iota(jnp.int32, (2 * SIDE, rows), 1)
    by_row = SIDE - 1 - (dev * (rows // SIDE) + lax.shift_right_logical(spot, 6))
    by_col = SIDE - 1 - (spot & (SIDE - 1))
    return by_row, by_col


def skew(values, shift):
    for bit in (32, 16, 8, 4, 2, 1):
        moved = pltpu.roll(values, 2 * SIDE - bit, 0)
        values = jnp.where((shift & bit) != 0, moved, values)
    return values[:SIDE]


def unskew(values, shift):
    values = jnp.concatenate([values, jnp.zeros_like(values)], axis=0)
    for bit in (32, 16, 8, 4, 2, 1):
        moved = pltpu.roll(values, bit, 0)
        values = jnp.where((shift & bit) != 0, moved, values)
    return values


def greet(peers):
    barrier = pltpu.get_barrier_semaphore()
    for peer in peers:
        pl.semaphore_signal(barrier, inc=1, device_id={"dp": peer}, device_id_type=MESH)
    pl.semaphore_wait(barrier, len(peers))


def key_onehots(rows, dev):
    spot = lax.broadcasted_iota(jnp.int32, (2 * SIDE, rows), 1)
    index = lax.broadcasted_iota(jnp.int32, (2 * SIDE, rows), 0)
    cols = jnp.where((index & (SIDE - 1)) == (spot & (SIDE - 1)), 1.0, 0.0)
    spot, index = spot[:16], index[:16]
    offset = lax.rem(dev * (rows // SIDE), 8)
    in_group = jnp.where((index & 7) == offset + lax.shift_right_logical(spot, 6), 1.0, 0.0)
    return cols, in_group


class Shape:
    def __init__(self, heads, group, rows):
        self.heads, self.group, self.rows = heads, group, rows
        self.queries = heads * rows
        self.block = min(1024, self.queries)


def forward_kernel(
    shape, qkv, tables, att, qaug, bias_rows, kv_out, o_out, lse_out, peak_out,
    rq, rkv, kaug_t, kaug, vaug, oacc, mrow, lpk, att_s, att_r,
    q_send, q_recv, k_send, k_recv, x_send, x_recv, r_send, r_recv, o_sem,
):
    heads, group, rows, block = shape.heads, shape.group, shape.rows, shape.block
    me = lax.axis_index("dp")
    z, g = me // group, lax.rem(me, group)
    column = [lax.rem(z + k, heads) for k in range(1, heads)]
    mates = [lax.rem(g + k, group) for k in range(1, group)]
    greet([h * group + g for h in column] + [z * group + o for o in mates])
    sends = []
    for h in column:
        sends.append(send_dp(qkv.at[h, 0], rq.at[z], q_send.at[h], q_recv.at[z], h * group + g))
    for h in column:
        sends.append(
            send_dp(
                qkv.at[h, pl.ds(1, 2)], rkv.at[z, g], k_send.at[h], k_recv.at[z], h * group + g
            )
        )
    for copy in sends:
        copy.start()
    rq[z] = qkv[z, 0]
    rkv[z, g] = qkv[z, pl.ds(1, 2)]
    qaug[pl.ds(LSE_AT, 16), :] = jnp.zeros((16, shape.queries), LOW)
    kaug_t[pl.ds(LSE_AT, 16), :] = jnp.zeros((16, rows), LOW)
    vaug[pl.ds(HEAD, 16), :] = jnp.where(
        lax.broadcasted_iota(jnp.int32, (16, rows), 0) == 0, 1.0, 0.0
    ).astype(LOW)
    oacc[...] = jnp.zeros_like(oacc)
    mrow[...] = jnp.full_like(mrow, -jnp.inf)
    lpk[...] = jnp.full_like(lpk, -jnp.inf)

    def prepare(k, carry):
        source = lax.rem(z - k + heads, heads)
        span = pl.ds(pl.multiple_of(source * rows, rows), rows)

        @pl.when(k > 0)
        def _():
            send_dp(rq.at[source], rq.at[source], q_send.at[source], q_recv.at[source], me).wait_recv()

        query = rq[source]
        by_row, by_col = shifts(rows, source * group + g)
        along_rows = skew(nn(tables[0], query) * (1.0 / SCALE), by_row)
        along_cols = skew(nn(tables[1], query) * (1.0 / SCALE), by_col)
        qaug[pl.ds(0, HEAD), span] = query
        cols = parts_of(along_cols, 2)
        qaug[pl.ds(COLS_AT, 2 * SIDE), span] = jnp.concatenate(cols, axis=0).astype(LOW)
        high, rest = parts_of(along_rows, 2)
        for at in range(SIDE // 8):
            pair = jnp.concatenate([high[8 * at : 8 * at + 8], rest[8 * at : 8 * at + 8]], axis=0)
            bias_rows[at, :, span] = pair.astype(LOW)
        return carry

    lax.fori_loop(0, heads, prepare, 0)

    def chunk(source, mate):
        dev = source * group + mate
        cols, in_group = key_onehots(rows, dev)
        kaug_t[pl.ds(0, HEAD), :] = rkv[source, mate, 0]
        kaug_t[pl.ds(COLS_AT, 2 * SIDE), :] = cols.astype(LOW)
        kaug_t[pl.ds(ROWS_AT, 16), :] = in_group.astype(LOW)
        kaug[...] = kaug_t[...].T
        vaug[pl.ds(0, HEAD), :] = rkv[source, mate, 1]
        qaug[pl.ds(ROWS_AT, 16), :] = bias_rows[(dev * (rows // SIDE)) // 8]

        def one(i, carry):
            span = pl.ds(pl.multiple_of(i * block, block), block)
            logits = nn(kaug[:, :HEAD], qaug[pl.ds(0, HEAD), span])
            lpk[...] = jnp.maximum(lpk[...], jnp.max(logits.reshape(rows // 8, 8, block), axis=0))
            scores = nn(kaug[...], qaug[:, span])
            before = mrow[:, span]
            top = jnp.maximum(before, jnp.max(scores, axis=0, keepdims=True))
            mrow[:, span] = top
            weights = jnp.exp2(scores * EXP2_SCALE - top * EXP2_SCALE).astype(LOW)
            keep = jnp.exp2((before - top) * EXP2_SCALE)
            oacc[:, span] = oacc[:, span] * keep + nn(vaug[...], weights)
            return carry

        lax.fori_loop(0, shape.queries // block, one, 0)

    def column_step(k, carry):
        source = lax.rem(z - k + heads, heads)

        @pl.when(k > 0)
        def _():
            send_dp(rkv.at[source, g], rkv.at[source, g], k_send.at[source], k_recv.at[source], me).wait_recv()

        for n, mate in enumerate(mates):
            send_dp(
                rkv.at[source, g], rkv.at[source, g], x_send.at[source, n], x_recv.at[source, g],
                z * group + mate,
            ).start()
        chunk(source, g)

        def mate_step(n, inner):
            mate = lax.rem(g + n, group)
            send_dp(
                rkv.at[source, mate], rkv.at[source, mate], x_send.at[source, 0], x_recv.at[source, mate], me
            ).wait_recv()
            chunk(source, mate)
            return inner

        lax.fori_loop(1, group, mate_step, 0)
        return carry

    lax.fori_loop(0, heads, column_step, 0)
    keep_kv = pltpu.make_async_copy(rkv, kv_out, o_sem)
    keep_kv.start()

    def finish(source, carry):
        span = pl.ds(pl.multiple_of(source * rows, rows), rows)
        total = oacc[pl.ds(HEAD, 1), span]
        attended = oacc[pl.ds(0, HEAD), span] / total
        o_out[:, span] = attended
        lse_out[:, span] = mrow[:, span] + jnp.log2(total) * (1.0 / EXP2_SCALE)
        att_s[source] = attended.astype(LOW)

        @pl.when(source != z)
        def _():
            send_dp(
                att_s.at[source], att_r.at[z], r_send.at[source], r_recv.at[z], source * group + g
            ).start()

        return carry

    lax.fori_loop(0, heads, finish, 0)
    att[z] = att_s[z]
    peak_out[...] = jnp.full(peak_out.shape, jnp.max(lpk[...]) * SCALE, F32)
    for h in column:
        send_dp(att_s.at[h], att_r.at[h], r_send.at[h], r_recv.at[h], h * group + g).wait()
        att[h] = att_r[h]
    for copy in sends:
        copy.wait_send()
    for source in range(heads):
        for n, mate in enumerate(mates):
            send_dp(
                rkv.at[source, g], rkv.at[source, g], x_send.at[source, n], x_recv.at[source, g],
                z * group + mate,
            ).wait_send()
    keep_kv.wait()


def attend(shape, qkv, tables):
    heads, group, rows, queries = shape.heads, shape.group, shape.rows, shape.queries
    vmem = pl.BlockSpec(memory_space=pltpu.VMEM)
    hbm = pl.BlockSpec(memory_space=pl.ANY)
    dma = pltpu.SemaphoreType.DMA
    return pl.pallas_call(
        functools.partial(forward_kernel, shape),
        out_shape=(
            jax.ShapeDtypeStruct((heads, HEAD, rows), LOW),
            jax.ShapeDtypeStruct((AUG, queries), LOW),
            jax.ShapeDtypeStruct((SIDE // 8, 16, queries), LOW),
            jax.ShapeDtypeStruct((heads, group, 2, HEAD, rows), LOW),
            jax.ShapeDtypeStruct((HEAD, queries), F32),
            jax.ShapeDtypeStruct((1, queries), F32),
            jax.ShapeDtypeStruct((8, 128), F32),
        ),
        in_specs=[vmem, vmem],
        out_specs=(vmem, vmem, vmem, hbm, vmem, vmem, vmem),
        scratch_shapes=[
            pltpu.VMEM((heads, HEAD, rows), LOW),
            pltpu.VMEM((heads, group, 2, HEAD, rows), LOW),
            pltpu.VMEM((AUG, rows), LOW),
            pltpu.VMEM((rows, AUG), LOW),
            pltpu.VMEM((HEAD + 16, rows), LOW),
            pltpu.VMEM((HEAD + 16, queries), F32),
            pltpu.VMEM((1, queries), F32),
            pltpu.VMEM((8, shape.block), F32),
            pltpu.VMEM((heads, HEAD, rows), LOW),
            pltpu.VMEM((heads, HEAD, rows), LOW),
            dma((heads,)), dma((heads,)), dma((heads,)), dma((heads,)),
            dma((heads, group)), dma((heads, group)), dma((heads,)), dma((heads,)),
            dma,
        ],
        compiler_params=pltpu.CompilerParams(
            collective_id=1, has_side_effects=True, vmem_limit_bytes=VMEM_LIMIT
        ),
        name="attend",
    )(qkv, tables)


def backward_kernel(
    shape, ga, tables, qaug_in, bias_rows, rkv, o_in, lse_in, fc2_state, fc1, fc2,
    grads, table_grads, fc1_out, fc2_out,
    rdo, qaug, q_tok, do_aug, do_tok, kaug_t, kaug, vaug_t, vaug, kacc, vacc, dq, drow, dcol,
    part, xr, summed, gq_s, gq_r, gkv_r,
    d_send, d_recv, x_send, x_recv, kv_send, kv_recv, q_send, q_recv, *rest,
):
    chunks = fc1.shape[1]
    rest = list(rest)

    def taken(number):
        found, rest[:] = rest[:number], rest[number:]
        return found

    whole_bufs = 2 + 3 * halve_bits()
    moved2 = [Halve(near_first(), fc2_state, taken(3 * (halve_bits() - 1)), first=1)]
    moved1 = [Halve(near_first(), fc1.at[:, 0], taken(whole_bufs), own=True)]
    if chunks > 1:
        moved2 += [Halve(near_first(), fc2.at[:, 1], taken(whole_bufs), own=True)]
        moved1 += [Halve(far_first(shape.group), fc1.at[:, 1], taken(whole_bufs), own=True)]
    heads, group, rows, block = shape.heads, shape.group, shape.rows, shape.block
    queries = shape.queries
    me = lax.axis_index("dp")
    z, g = me // group, lax.rem(me, group)
    column = [lax.rem(z + k, heads) for k in range(1, heads)]
    mates = [lax.rem(g + k, group) for k in range(1, group)]
    greet([h * group + g for h in column] + [z * group + o for o in mates])
    sends = []
    for h in column:
        copy = send_dp(ga.at[h], rdo.at[z], d_send.at[h], d_recv.at[z], h * group + g)
        copy.start()
        sends.append(copy)
    if chunks > 1:
        moved2[1].start()
        moved2[1].load()
        moved1[1].load()
    moved1[0].load()
    rdo[z] = ga[z]
    qaug[...] = qaug_in[...]
    ones = jnp.where(lax.broadcasted_iota(jnp.int32, (16, rows), 0) < 3, 1.0, 0.0).astype(LOW)
    kaug_t[pl.ds(LSE_AT, 16), :] = ones
    vaug_t[pl.ds(HEAD, 16), :] = ones
    vaug_t[pl.ds(HEAD + 16, 32), :] = jnp.zeros((32, rows), LOW)
    low_lse = parts_of(-lse_in[...], 3)
    qaug[pl.ds(LSE_AT, 16), :] = jnp.concatenate(
        low_lse + [jnp.zeros((13, queries), F32)], axis=0
    ).astype(LOW)
    dq[...] = jnp.zeros_like(dq)
    dcol[...] = jnp.zeros_like(dcol)
    drow[...] = jnp.zeros_like(drow)

    def prepare(k, carry):
        source = lax.rem(z - k + heads, heads)
        span = pl.ds(pl.multiple_of(source * rows, rows), rows)

        @pl.when(k > 0)
        def _():
            send_dp(rdo.at[source], rdo.at[source], d_send.at[source], d_recv.at[source], me).wait_recv()

        upstream = rdo[source]
        dots = jnp.sum(upstream.astype(F32) * o_in[:, span], axis=0, keepdims=True)
        low_dots = parts_of(-dots, 3)
        do_aug[pl.ds(0, HEAD), span] = upstream
        do_aug[pl.ds(HEAD, 16), span] = jnp.concatenate(
            low_dots + [jnp.zeros((13, rows), F32)], axis=0
        ).astype(LOW)
        do_aug[pl.ds(HEAD + 16, 32), span] = jnp.zeros((32, rows), LOW)
        do_tok[span, :] = do_aug[:, span].T
        q_tok[span, :] = qaug[pl.ds(0, 128), span].T
        return carry

    lax.fori_loop(0, heads, prepare, 0)
    moved2[0].start()
    if chunks > 1:
        moved1[1].start()

    def chunk(source, mate):
        dev = source * group + mate
        at = (dev * (rows // SIDE)) // 8
        cols, in_group = key_onehots(rows, dev)
        kaug_t[pl.ds(0, HEAD), :] = rkv[source, mate, 0]
        kaug_t[pl.ds(COLS_AT, 2 * SIDE), :] = cols.astype(LOW)
        kaug_t[pl.ds(ROWS_AT, 16), :] = in_group.astype(LOW)
        kaug[...] = kaug_t[...].T
        vaug_t[pl.ds(0, HEAD), :] = rkv[source, mate, 1]
        vaug[...] = vaug_t[...].T
        qaug[pl.ds(ROWS_AT, 16), :] = bias_rows[at]
        kacc[...] = jnp.zeros_like(kacc)
        vacc[...] = jnp.zeros_like(vacc)
        back = jnp.concatenate(
            [kaug_t[pl.ds(0, COLS_AT + SIDE), :], kaug_t[pl.ds(ROWS_AT, 16), :]], axis=0
        )

        def one(i, carry):
            span = pl.ds(pl.multiple_of(i * block, block), block)
            probs = jnp.exp2(nn(kaug[...], qaug[:, span]) * EXP2_SCALE)
            pulled = nn(vaug[...], do_aug[:, span])
            low_grads = (probs * pulled).astype(LOW)
            vacc[...] += nn(probs.astype(LOW), do_tok[span, :])
            kacc[...] += nn(low_grads, q_tok[span, :])
            found = nn(back, low_grads)
            dq[:, span] += found[:HEAD]
            dcol[:, span] += found[COLS_AT : COLS_AT + SIDE]
            drow[at, :, span] += found[COLS_AT + SIDE : COLS_AT + SIDE + 8]
            return carry

        lax.fori_loop(0, queries // block, one, 0)

    def put(where, extra):
        key_part = (kacc[...] * SCALE).T[:HEAD]
        value_part = vacc[...].T[:HEAD]
        for other in extra:
            key_part = key_part + other[0].astype(F32)
            value_part = value_part + other[1].astype(F32)
        where[0] = key_part.astype(LOW)
        where[1] = value_part.astype(LOW)

    def mate_copy(source, mate):
        return send_dp(
            part.at[source, mate], xr.at[source, g], x_send.at[source, mate], x_recv.at[source, g],
            z * group + mate,
        )

    def mates_step(k, carry):
        source = lax.rem(z + k, heads)

        def mate_step(n, inner):
            mate = lax.rem(g + n, group)
            chunk(source, mate)
            put(part.at[source, mate], [])
            mate_copy(source, mate).start()
            return inner

        lax.fori_loop(1, group, mate_step, 0)

        @pl.when(k == 2)
        def _():
            moved2[0].run(1)

        return carry

    lax.fori_loop(1, heads + 1, mates_step, 0)
    moved1[0].start()
    if chunks > 1:
        moved2[1].loaded()
        moved2[1].run(0)

    def own_step(k, carry):
        source = lax.rem(z + k, heads)
        chunk(source, g)
        extra = []
        for mate in mates:
            send_dp(
                xr.at[source, mate], xr.at[source, mate], x_send.at[source, mate], x_recv.at[source, mate], me
            ).wait_recv()
            extra.append(xr.at[source, mate])
        put(summed.at[source], extra)

        @pl.when(source != z)
        def _():
            send_dp(
                summed.at[source], gkv_r.at[z], kv_send.at[source], kv_recv.at[z], source * group + g
            ).start()

        @pl.when(k == 1)
        def _():
            if chunks > 1:
                moved1[1].loaded()
                moved1[1].run(0)

        @pl.when(k == 2)
        def _():
            if chunks > 1:
                moved2[1].run(1)

        return carry

    lax.fori_loop(1, heads + 1, own_step, 0)
    moved1[0].loaded()
    moved1[0].run(0)
    table_grads[...] = jnp.zeros_like(table_grads)

    def finish(k, carry):
        source = lax.rem(z + k, heads)
        span = pl.ds(pl.multiple_of(source * rows, rows), rows)
        by_row, by_col = shifts(rows, source * group + g)
        total = dq[:, span] * SCALE
        for n, held in enumerate((drow[:, :, span].reshape(SIDE, rows), dcol[:, span])):
            spread = unskew(held, by_col if n else by_row)
            for piece in parts_of(spread, 2):
                low_piece = piece.astype(LOW)
                total = total + tn(tables[n], low_piece)
                table_grads[n] += nn(low_piece, q_tok[span, :])
        gq_s[source] = total.astype(LOW)

        @pl.when(source != z)
        def _():
            send_dp(
                gq_s.at[source], gq_r.at[z], q_send.at[source], q_recv.at[z], source * group + g
            ).start()

        return carry

    lax.fori_loop(1, heads + 1, finish, 0)
    if chunks > 1:
        moved1[1].run(1)
    for other in range(2, halve_bits() - 1):
        for each in moved2:
            each.run(other)
    found = [each.total() for each in moved2]
    fc2_out[...] = (jnp.concatenate(found, axis=0) if chunks > 1 else found[0]).T
    for other in range(1, halve_bits() - 1):
        moved1[0].run(other)
        if chunks > 1 and other > 1:
            moved1[1].run(other)
    owned = fc1_out.shape[0] // chunks
    for n, each in enumerate(moved1):
        fc1_out[pl.ds(n * owned, owned), :] = each.total()
    grads[z, 0] = gq_s[z]
    grads[z, pl.ds(1, 2)] = summed[z]
    for h in column:
        send_dp(summed.at[h], gkv_r.at[h], kv_send.at[h], kv_recv.at[h], h * group + g).wait()
        grads[h, pl.ds(1, 2)] = gkv_r[h]
    for h in column:
        send_dp(gq_s.at[h], gq_r.at[h], q_send.at[h], q_recv.at[h], h * group + g).wait()
        grads[h, 0] = gq_r[h]
    for copy in sends:
        copy.wait_send()
    for source in range(heads):
        for mate in mates:
            mate_copy(source, mate).wait_send()
    for each in moved1 + moved2:
        each.finish()


def attend_back(shape, ga, tables, qaug, bias_rows, kv, o_rows, lse, fc2_state, fc1, fc2):
    devices, chunks, owned, hidden = fc1.shape
    hbm = pl.BlockSpec(memory_space=pl.ANY)
    moving = halve_bufs(owned, hidden, first=1)
    moving += halve_bufs(owned, hidden, own=True) * (3 if chunks > 1 else 1)
    heads, group, rows, queries = shape.heads, shape.group, shape.rows, shape.queries
    vmem = pl.BlockSpec(memory_space=pltpu.VMEM)
    dma = pltpu.SemaphoreType.DMA
    return pl.pallas_call(
        functools.partial(backward_kernel, shape),
        out_shape=(
            jax.ShapeDtypeStruct((heads, 3, HEAD, rows), LOW),
            jax.ShapeDtypeStruct((2, 2 * SIDE, 128), F32),
            jax.ShapeDtypeStruct((chunks * owned, hidden), F32),
            jax.ShapeDtypeStruct((hidden, chunks * owned), F32),
        ),
        in_specs=[vmem] * 8 + [hbm] * 2,
        out_specs=(vmem,) * 4,
        scratch_shapes=[
            pltpu.VMEM((heads, HEAD, rows), LOW),
            pltpu.VMEM((AUG, queries), LOW),
            pltpu.VMEM((queries, 128), LOW),
            pltpu.VMEM((128, queries), LOW),
            pltpu.VMEM((queries, 128), LOW),
            pltpu.VMEM((AUG, rows), LOW),
            pltpu.VMEM((rows, AUG), LOW),
            pltpu.VMEM((128, rows), LOW),
            pltpu.VMEM((rows, 128), LOW),
            pltpu.VMEM((rows, 128), F32),
            pltpu.VMEM((rows, 128), F32),
            pltpu.VMEM((HEAD, queries), F32),
            pltpu.VMEM((SIDE // 8, 8, queries), F32),
            pltpu.VMEM((SIDE, queries), F32),
            pltpu.VMEM((heads, group, 2, HEAD, rows), LOW),
            pltpu.VMEM((heads, group, 2, HEAD, rows), LOW),
            pltpu.VMEM((heads, 2, HEAD, rows), LOW),
            pltpu.VMEM((heads, HEAD, rows), LOW),
            pltpu.VMEM((heads, HEAD, rows), LOW),
            pltpu.VMEM((heads, 2, HEAD, rows), LOW),
            dma((heads,)), dma((heads,)), dma((heads, group)), dma((heads, group)),
            dma((heads,)), dma((heads,)), dma((heads,)), dma((heads,)),
        ] + moving,
        compiler_params=pltpu.CompilerParams(
            collective_id=2, has_side_effects=True, vmem_limit_bytes=VMEM_LIMIT
        ),
        name="attend_back",
    )(ga, tables, qaug, bias_rows, kv, o_rows, lse, fc2_state, fc1, fc2)


def send_tensor(src, dst, send_sem, recv_sem, dev):
    return pltpu.make_async_remote_copy(
        src_ref=src,
        dst_ref=dst,
        send_sem=send_sem,
        recv_sem=recv_sem,
        device_id={"tensor": dev},
        device_id_type=MESH,
    )


def tensor_place():
    me = lax.axis_index("tensor")
    return lax.rem(me, 2), me // 2, lax.axis_size("tensor") // 2


def tensor_peers():
    core, line, lines = tensor_place()
    far = [lax.rem(line + k, lines) * 2 + core for k in range(1, lines)]
    return far + [line * 2 + 1 - core]


def part_bufs(lines, share, width):
    dma = pltpu.SemaphoreType.DMA
    return [pltpu.VMEM((lines, share, width), LOW)] * 3 + [dma((lines,))] * 4


class Reduce:
    def __init__(self, part, mate_in, passed, line_in, m_send, m_recv, l_send, l_recv):
        self.part, self.mate_in, self.passed, self.line_in = part, mate_in, passed, line_in
        self.sems = m_send, m_recv, l_send, l_recv
        self.core, self.line, self.lines = tensor_place()

    def mate_copy(self, to):
        m_send, m_recv, _, _ = self.sems
        return send_tensor(
            self.part.at[to * 2 + 1 - self.core], self.mate_in.at[to],
            m_send.at[to], m_recv.at[to], self.line * 2 + 1 - self.core,
        )

    def line_copy(self, to, slot):
        _, _, l_send, l_recv = self.sems
        return send_tensor(
            self.passed.at[to], self.line_in.at[slot], l_send.at[to], l_recv.at[slot],
            to * 2 + self.core,
        )

    def give(self, to):
        self.mate_copy(to).start()

    def pass_on(self, to):
        self.mate_copy(to).wait_recv()
        both = self.part[to * 2 + self.core].astype(F32) + self.mate_in[to].astype(F32)
        self.passed[to] = both.astype(LOW)
        self.line_copy(to, self.line).start()

    def others(self):
        return [lax.rem(self.line + k, self.lines) for k in range(1, self.lines)]

    def total(self):
        self.mate_copy(self.line).wait_recv()
        total = self.part[self.line * 2 + self.core].astype(F32) + self.mate_in[self.line].astype(F32)
        for other in self.others():
            self.line_copy(other, other).wait_recv()
            total = total + self.line_in[other].astype(F32)
        return total

    def finish(self):
        self.mate_copy(self.line).wait_send()
        for other in self.others():
            self.mate_copy(other).wait_send()
            self.line_copy(other, self.line).wait_send()


def gather_sems(lines):
    dma = pltpu.SemaphoreType.DMA
    return [dma((lines,)), dma((lines,)), dma((2 * lines,))]


class Gather:
    def __init__(self, whole, l_send, m_send, recv):
        self.whole, self.sems = whole, (l_send, m_send, recv)
        self.core, self.line, self.lines = tensor_place()

    def line_copy(self, to):
        l_send, _, recv = self.sems
        own = self.line * 2 + self.core
        return send_tensor(
            self.whole.at[own], self.whole.at[own], l_send.at[to], recv.at[own], to * 2 + self.core
        )

    def mate_copy(self, at):
        _, m_send, recv = self.sems
        part = at * 2 + self.core
        return send_tensor(
            self.whole.at[part], self.whole.at[part], m_send.at[at], recv.at[part],
            self.line * 2 + 1 - self.core,
        )

    def arrived(self, part):
        l_send, _, recv = self.sems
        send_tensor(
            self.whole.at[part], self.whole.at[part], l_send.at[0], recv.at[part], part
        ).wait_recv()

    def others(self):
        return [lax.rem(self.line + k, self.lines) for k in range(1, self.lines)]

    def start(self):
        for other in self.others():
            self.line_copy(other).start()
        self.mate_copy(self.line).start()

    def forward(self, at):
        self.arrived(at * 2 + self.core)
        self.mate_copy(at).start()

    def take(self, at):
        self.arrived(at * 2 + 1 - self.core)

    def finish(self):
        self.mate_copy(self.line).wait_send()
        for other in self.others():
            self.mate_copy(other).wait_send()
            self.line_copy(other).wait_send()


def normed(values):
    center = values - jnp.mean(values, axis=-1, keepdims=True)
    variance = jnp.mean(center * center, axis=-1, keepdims=True)
    inverse = lax.rsqrt(variance + EPSILON)
    return center * inverse, inverse


def normed_back(upstream, scaled, inverse, gain):
    weighted = upstream * gain
    centered = weighted - jnp.mean(weighted, axis=-1, keepdims=True)
    return (centered - scaled * jnp.mean(weighted * scaled, axis=-1, keepdims=True)) * inverse


def tile_of(width):
    return 256 if width % 256 == 0 else 128


class Ring:
    def __init__(self, heads):
        self.heads, self.group = heads, lax.axis_size("dp") // heads
        me = lax.axis_index("dp")
        self.z, self.g = me // self.group, lax.rem(me, self.group)

    def column(self):
        return [lax.rem(self.z + k, self.heads) for k in range(1, self.heads)]

    def mates(self):
        return [lax.rem(self.g + k, self.group) for k in range(1, self.group)]

    def peers(self):
        far = [h * self.group + self.g for h in self.column()]
        return far + [self.z * self.group + o for o in self.mates()]


def greet_all(ring):
    barrier = pltpu.get_barrier_semaphore()
    near, far = tensor_peers(), ring.peers()
    for peer in near:
        pl.semaphore_signal(barrier, inc=1, device_id={"tensor": peer}, device_id_type=MESH)
    for peer in far:
        pl.semaphore_signal(barrier, inc=1, device_id={"dp": peer}, device_id_type=MESH)
    pl.semaphore_wait(barrier, len(near) + len(far))


def halve_bits():
    return (lax.axis_size("dp") - 1).bit_length()


def near_first():
    return tuple(range(halve_bits()))


def far_first(group):
    first = group.bit_length() - 1
    return (first,) + tuple(bit for bit in range(halve_bits()) if bit != first)


def halve_bufs(share, width, first=0, last=None, own=False):
    bits = halve_bits()
    last = bits - 1 if last is None else last
    dma = pltpu.SemaphoreType.DMA
    found = []
    if own:
        found += [pltpu.VMEM((1 << (bits - 1), share, width), LOW), dma]
    for stage in range(first, last + 1):
        count = 1 << (bits - 1 - stage)
        found += [pltpu.VMEM((count, share, width), LOW), dma((count,)), dma((count,))]
    return found


class Halve:
    def __init__(self, order, source, bufs, first=0, last=None, own=False):
        self.order, self.source, self.first = order, source, first
        self.last = len(order) - 1 if last is None else last
        bufs = list(bufs)
        self.own = bufs[0:2] if own else None
        bufs = bufs[2:] if own else bufs
        self.stages = {first + n: bufs[3 * n : 3 * n + 3] for n in range(len(bufs) // 3)}
        self.me = lax.axis_index("dp")

    def bit(self, stage):
        return lax.rem(self.me // (1 << self.order[stage]), 2)

    def count(self, stage):
        return 1 << (len(self.order) - 1 - stage)

    def index(self, stage, at, bit):
        if stage > 0:
            return at * 2 + bit
        place = bit * (1 << self.order[0])
        for n, other in enumerate(self.order[1:]):
            place = place + lax.rem(at // (1 << n), 2) * (1 << other)
        return place

    def held(self, stage):
        return self.source if stage == self.first else self.stages[stage - 1][0]

    def copy(self, stage, at):
        bit = self.bit(stage)
        into, send, recv = self.stages[stage]
        return send_dp(
            self.held(stage).at[self.index(stage, at, 1 - bit)], into.at[at],
            send.at[at], recv.at[at], self.me + (1 - 2 * bit) * (1 << self.order[stage]),
        )

    def spots(self, stage):
        if stage == len(self.order) - 1:
            return [0]
        bit, half = self.bit(stage + 1), self.count(stage) // 2
        return [n * 2 + 1 - bit for n in range(half)] + [n * 2 + bit for n in range(half)]

    def load(self):
        for at in range(self.count(0)):
            pltpu.make_async_copy(
                self.source.at[self.index(0, at, self.bit(0))], self.own[0].at[at], self.own[1]
            ).start()

    def loaded(self):
        pltpu.make_async_copy(
            self.source.at[pl.ds(0, self.count(0))], self.own[0], self.own[1]
        ).wait()

    def start(self):
        for at in self.spots(self.first):
            self.copy(self.first, at).start()

    def kept(self, stage, at):
        if stage == self.first and self.own is not None:
            return self.own[0][at].astype(F32)
        return self.held(stage)[self.index(stage, at, self.bit(stage))].astype(F32)

    def sum_at(self, stage, at):
        self.copy(stage, at).wait_recv()
        return self.kept(stage, at) + self.stages[stage][0][at].astype(F32)

    def run(self, stage):
        for n, at in enumerate(self.spots(stage)):
            self.stages[stage][0][at] = self.sum_at(stage, at).astype(LOW)
            if stage < self.last and n < self.count(stage) // 2:
                self.copy(stage + 1, n).start()

    def total(self):
        return self.sum_at(self.last, 0)

    def finish(self):
        for stage in self.stages:
            for at in range(self.count(stage)):
                self.copy(stage, at).wait_send()


def middle_kernel(
    heads, att, proj_w, tokens, cot, fc1_hbm, fc2_hbm, fc1_bias, vectors,
    output, middle_out, fc1_out, fc2_out, proj_out, ga_out, fc1_bias_out, sums_out, fc2_state,
    fc1, fc2, att_tok, branch, mlp, back, n2, act, gu, gb, outs, held, spread,
    wide, load1, load2, *rest,
):
    core, line, lines = tensor_place()
    me = lax.axis_index("tensor")
    _, share, width = tokens.shape
    rows = tokens.shape[0] * share
    local, hidden = proj_w.shape[0], fc1_hbm.shape[1]
    step, dstep = tile_of(hidden), tile_of(width)
    in_fc1 = pltpu.make_async_copy(fc1_hbm, fc1, load1)
    in_fc2 = pltpu.make_async_copy(fc2_hbm, fc2, load2)
    in_fc1.start()
    in_fc2.start()
    greet_all(Ring(heads))
    sum_branch = Reduce(branch, *rest[0:7])
    sum_mlp = Reduce(mlp, *rest[7:14])
    sum_back = Reduce(back, *rest[14:21])
    all_n2 = Gather(n2, *rest[21:24])
    all_gb = Gather(gb, *rest[24:27])
    all_out = Gather(outs, *rest[27:30])
    devices, chunks, owned, _ = fc2_out.shape
    blocks = rest[30]
    moved = Halve(near_first(), blocks, rest[31:], last=0)
    att_tok[...] = att[...].T.reshape(att_tok.shape)

    def project(k, carry):
        to = lax.rem(line + 1 + lax.rem(k, lines), lines)
        part = to * 2 + jnp.where(k < lines, 1 - core, core)
        branch[part] = nn(att_tok[part], proj_w[...]).astype(LOW)

        @pl.when(k < lines)
        def _():
            sum_branch.give(to)

        return carry

    lax.fori_loop(0, 2 * lines, project, 0)
    for other in sum_branch.others():
        sum_branch.pass_on(other)
    middle = tokens[me].astype(F32) + vectors[0:1]
    middle = middle + sum_branch.total()
    scaled, inverse = normed(middle)
    n2[me] = (scaled * vectors[1:2] + vectors[2:3]).astype(LOW)
    all_n2.start()
    held[0] = middle
    held[1] = scaled
    spread[...] = jnp.broadcast_to(inverse, spread.shape)
    fc1_bias_out[...] = jnp.zeros_like(fc1_bias_out)
    in_fc1.wait()
    in_fc2.wait()

    def hidden_part(k, carry):
        at = lax.rem(line + k, lines)

        @pl.when(k > 0)
        def _():
            all_n2.forward(at)

        all_n2.take(at)
        pair = pl.ds(at * 2, 2)
        inputs = n2[pair].reshape(2 * share, width)
        pulls = cot[pair].reshape(2 * share, width)

        def tile(n, inner):
            span = pl.ds(pl.multiple_of(n * step, step), step)
            up = nn(inputs, fc1[:, span]) + fc1_bias[:, span]
            phi = 0.5 + 0.5 * lax.erf(up * math.sqrt(0.5))
            slope = phi + up * (jnp.exp(-0.5 * up * up) * (2 * math.pi) ** -0.5)
            act[pair, :, span] = (up * phi).astype(LOW).reshape(2, share, step)
            grad_up = (nt(pulls, fc2[span, :]) * slope).astype(LOW)
            gu[pair, :, span] = grad_up.reshape(2, share, step)
            fc1_bias_out[:, span] += jnp.sum(grad_up.astype(F32), axis=0, keepdims=True)
            return inner

        lax.fori_loop(0, hidden // step, tile, 0)

        def tile_back(n, inner):
            span = pl.ds(pl.multiple_of(n * dstep, dstep), dstep)
            found = nt(gu[pair].reshape(2 * share, hidden), fc1[span, :])
            back[pair, :, span] = found.astype(LOW).reshape(2, share, dstep)
            return inner

        lax.fori_loop(0, width // dstep, tile_back, 0)
        sum_back.give(at)

        def tile_out(n, inner):
            span = pl.ds(pl.multiple_of(n * dstep, dstep), dstep)
            found = nn(act[pair].reshape(2 * share, hidden), fc2[:, span])
            mlp[pair, :, span] = found.astype(LOW).reshape(2, share, dstep)
            return inner

        lax.fori_loop(0, width // dstep, tile_out, 0)
        sum_mlp.give(at)
        return carry

    lax.fori_loop(0, lines, hidden_part, 0)
    for other in sum_back.others():
        sum_back.pass_on(other)

    def weights2(n, carry):
        span = pl.ds(pl.multiple_of(n * dstep, dstep), dstep)
        found = tn(cot[:, :, span].reshape(rows, dstep), act[...].reshape(rows, hidden))
        wide[span, :] = found.astype(LOW)
        return carry

    lax.fori_loop(0, width // dstep, weights2, 0)
    for dev in range(devices):
        for chunk in range(chunks):
            at = (dev * chunks + chunk) * owned
            fc2_out[dev, chunk] = wide[pl.ds(at, owned), :]
        blocks[dev] = wide[pl.ds(dev * chunks * owned, owned), :]
    moved.start()
    for other in sum_mlp.others():
        sum_mlp.pass_on(other)
    upstream = sum_back.total()
    sums_out[0:1] = jnp.sum(upstream * held[1], axis=0, keepdims=True)
    sums_out[1:2] = jnp.sum(upstream, axis=0, keepdims=True)
    grad_middle = cot[me].astype(F32) + normed_back(
        upstream, held[1], spread[:, :1], vectors[1:2]
    )
    middle_out[...] = grad_middle
    gb[me] = grad_middle.astype(LOW)
    all_gb.start()
    outs[me] = (held[0] + sum_mlp.total() + vectors[3:4]).astype(LOW)
    all_out.start()

    def weights1(n, carry):
        span = pl.ds(pl.multiple_of(n * dstep, dstep), dstep)
        found = tn(n2[:, :, span].reshape(rows, dstep), gu[...].reshape(rows, hidden))
        wide[span, :] = found.astype(LOW)
        return carry

    lax.fori_loop(0, width // dstep, weights1, 0)
    for dev in range(devices):
        for chunk in range(chunks):
            at = (dev * chunks + chunk) * owned
            fc1_out[dev, chunk] = wide[pl.ds(at, owned), :]
    sums_out[2:3] = jnp.sum(cot[...].astype(F32).reshape(rows, width), axis=0, keepdims=True)
    for other in all_gb.others():
        all_gb.forward(other)
    for other in all_out.others():
        all_out.forward(other)
    all_gb.take(line)
    for other in all_gb.others():
        all_gb.take(other)
    whole = gb[...].reshape(rows, width)
    sums_out[3:4] = jnp.sum(whole.astype(F32), axis=0, keepdims=True)
    ga_out[...] = nt(proj_w[...], whole).astype(LOW)

    def weights0(n, carry):
        span = pl.ds(pl.multiple_of(n * dstep, dstep), dstep)
        found = tn(gb[:, :, span].reshape(rows, dstep), att_tok[...].reshape(rows, -1))
        wide[span, :local] = found.astype(LOW)
        return carry

    lax.fori_loop(0, width // dstep, weights0, 0)
    for dev in range(devices):
        proj_out[dev] = wide[pl.ds(dev * chunks * owned, chunks * owned), :local]
    all_out.take(line)
    for other in all_out.others():
        all_out.take(other)
    output[...] = outs[...]
    moved.run(0)
    fc2_state[...] = moved.stages[0][0][...]
    for each in (sum_branch, sum_mlp, sum_back, all_n2, all_gb, all_out, moved):
        each.finish()


def middle_block(heads, att, proj_w, tokens, cot, fc1, fc2, fc1_bias, vectors):
    count = lax.axis_size("tensor")
    lines = count // 2
    local, width = proj_w.shape
    rows = tokens.shape[0]
    share = rows // count
    hidden = fc1.shape[1]
    vmem = pl.BlockSpec(memory_space=pltpu.VMEM)
    hbm = pl.BlockSpec(memory_space=pl.ANY)
    dma = pltpu.SemaphoreType.DMA
    whole = (count, share, width)
    devices = lax.axis_size("dp")
    owned = width // devices
    chunks = 2 if owned % 32 == 0 else 1
    weights = (devices, chunks, owned // chunks, hidden)
    scratch = [
        pltpu.VMEM((width, hidden), LOW),
        pltpu.VMEM((hidden, width), LOW),
        pltpu.VMEM((count, share, local), LOW),
        pltpu.VMEM(whole, LOW),
        pltpu.VMEM(whole, LOW),
        pltpu.VMEM(whole, LOW),
        pltpu.VMEM(whole, LOW),
        pltpu.VMEM((count, share, hidden), LOW),
        pltpu.VMEM((count, share, hidden), LOW),
        pltpu.VMEM(whole, LOW),
        pltpu.VMEM(whole, LOW),
        pltpu.VMEM((2, share, width), F32),
        pltpu.VMEM((share, 128), F32),
        pltpu.VMEM((width, hidden), LOW),
        dma,
        dma,
    ]
    scratch += part_bufs(lines, share, width) * 3 + gather_sems(lines) * 3
    scratch += [pltpu.VMEM((devices, owned // chunks, hidden), LOW)]
    scratch += halve_bufs(owned // chunks, hidden, last=0)
    return pl.pallas_call(
        functools.partial(middle_kernel, heads),
        out_shape=(
            jax.ShapeDtypeStruct(whole, LOW),
            jax.ShapeDtypeStruct((share, width), F32),
            jax.ShapeDtypeStruct(weights, LOW),
            jax.ShapeDtypeStruct(weights, LOW),
            jax.ShapeDtypeStruct((devices, owned, local), LOW),
            jax.ShapeDtypeStruct((local, rows), LOW),
            jax.ShapeDtypeStruct((1, hidden), F32),
            jax.ShapeDtypeStruct((8, width), F32),
            jax.ShapeDtypeStruct((devices // 2, owned // chunks, hidden), LOW),
        ),
        in_specs=[vmem] * 4 + [hbm] * 2 + [vmem] * 2,
        out_specs=(vmem,) * 9,
        scratch_shapes=scratch,
        compiler_params=pltpu.CompilerParams(
            collective_id=3, has_side_effects=True, vmem_limit_bytes=VMEM_LIMIT
        ),
        name="middle",
    )(
        att, proj_w, tokens.reshape(whole), cot.reshape(whole), fc1, fc2,
        fc1_bias.reshape(1, hidden), vectors,
    )


def small_bufs(heads, stages, shape):
    group, lines = lax.axis_size("dp") // heads, lax.axis_size("tensor") // 2
    dma = pltpu.SemaphoreType.DMA
    found = []
    for stage in stages:
        count = {"core": 2, "line": lines, "mate": group, "far": heads}[stage]
        found += [
            pltpu.VMEM(shape, F32), pltpu.VMEM((count,) + shape, F32), dma((count,)), dma((count,))
        ]
    return found


class Small:
    def __init__(self, ring, stages, merge, *bufs):
        self.ring, self.stages, self.merge = ring, stages, merge
        self.bufs = [bufs[4 * n : 4 * n + 4] for n in range(len(stages))]
        core, line, lines = tensor_place()
        self.peers = {
            "core": (core, [(1 - core, line * 2 + 1 - core)]),
            "line": (line, [(o, o * 2 + core) for o in [lax.rem(line + k, lines) for k in range(1, lines)]]),
            "mate": (ring.g, [(o, ring.z * ring.group + o) for o in ring.mates()]),
            "far": (ring.z, [(o, o * ring.group + ring.g) for o in ring.column()]),
        }

    def copy(self, n, slot, other, dev):
        value, held, send, recv = self.bufs[n]
        call = send_tensor if self.stages[n] in ("core", "line") else send_dp
        return call(value, held.at[slot], send.at[other], recv.at[slot], dev)

    def start(self, n, value):
        own, peers = self.peers[self.stages[n]]
        self.bufs[n][0][...] = value
        for other, dev in peers:
            self.copy(n, own, other, dev).start()

    def take(self, n):
        _, peers = self.peers[self.stages[n]]
        total = self.bufs[n][0][...]
        for other, dev in peers:
            self.copy(n, other, other, dev).wait_recv()
            total = self.merge(total, self.bufs[n][1][other])
        return total

    def step(self, n):
        self.start(n + 1, self.take(n))

    def finish(self):
        for n in range(len(self.stages)):
            own, peers = self.peers[self.stages[n]]
            for other, dev in peers:
                self.copy(n, own, other, dev).wait_send()


EVERY = ("core", "line", "mate", "far")
OVER_DP = ("mate", "far")


def add_peaks(a, b):
    row = lax.broadcasted_iota(jnp.int32, a.shape, 0)
    return jnp.where(row == 2, jnp.maximum(a, b), a + b)


def widen(row, width):
    if row.shape[1] == width:
        return row
    return jnp.concatenate([row, jnp.zeros((1, width - row.shape[1]), F32)], axis=1)


def tail_kernel(
    heads, grads, qkv_w, n1_t, tokens, grad_middle, vectors, tables, sums, fc1_bias, peak, proj,
    tokens_out, proj_out, qkv_out, tables_out, sums_out, late_out, dp_out,
    g_all, g_tok, part, gt, *rest,
):
    ring = Ring(heads)
    core, line, lines = tensor_place()
    me = lax.axis_index("tensor")
    count, share, width = tokens.shape
    rows = count * share
    local = heads * HEAD
    dstep = tile_of(width)
    devices, chunks, _, _ = n1_t.shape
    rest = list(rest)

    def taken(number):
        found, rest[:] = rest[:number], rest[number:]
        return found

    greet_all(ring)
    blocks = [taken(1)[0] for _ in range(chunks)]
    orders = [near_first(), far_first(ring.group)]
    moved3 = [Halve(orders[n], blocks[n], taken(3 * halve_bits())) for n in range(chunks)]
    moved0 = Halve(near_first(), proj, taken(3 * halve_bits()))
    sum_part = Reduce(part, *taken(7))
    all_gt = Gather(gt, *taken(3))
    small_tables = Small(ring, EVERY, lax.add, *taken(16))
    small_sums = Small(ring, EVERY, lax.add, *taken(16))
    small_late = Small(ring, EVERY, lax.add, *taken(16))
    small_dp = Small(ring, OVER_DP, add_peaks, *taken(8))
    small_tables.start(0, tables[...].reshape(4 * SIDE, 128))
    small_sums.start(0, sums[...])
    moved0.start()
    for t in range(3):
        for h in range(heads):
            g_all[pl.ds(t * local + h * HEAD, HEAD), :] = grads[h, t]
    g_tok[...] = g_all[...].T.reshape(g_tok.shape)
    whole = g_tok[...].reshape(rows, 3 * local)
    lane = lax.broadcasted_iota(jnp.int32, (1, width), 1)
    peaks = jnp.where(lane == ring.z, peak[0:1, 0:1], -jnp.inf)
    bias_sums = jnp.sum(whole.astype(F32), axis=0, keepdims=True)
    dp_rows = [widen(fc1_bias[...], width), widen(bias_sums, width), peaks]
    small_dp.start(0, jnp.concatenate(dp_rows + [jnp.zeros((5, width), F32)], axis=0))

    def norm_part(k, carry):
        at = lax.rem(line + 1 + k, lines)
        pair = pl.ds(at * 2, 2)

        def tile(n, inner):
            span = pl.ds(pl.multiple_of(n * dstep, dstep), dstep)
            found = nt(g_tok[pair].reshape(2 * share, 3 * local), qkv_w[span, :])
            part[pair, :, span] = found.astype(LOW).reshape(2, share, dstep)
            return inner

        lax.fori_loop(0, width // dstep, tile, 0)
        sum_part.give(at)
        return carry

    lax.fori_loop(0, lines, norm_part, 0)
    for other in sum_part.others():
        sum_part.pass_on(other)

    for n in range(chunks):

        def weight_part(dev, carry):
            found = nn(n1_t[dev, n], g_tok[...].reshape(rows, 3 * local))
            blocks[n][dev] = found.astype(LOW)
            return carry

        lax.fori_loop(0, devices, weight_part, 0)
        moved3[n].start()
    small_tables.step(0)
    small_sums.step(0)
    scaled, inverse = normed(tokens[me].astype(F32))
    upstream = sum_part.total()
    late = [
        jnp.sum(upstream * scaled, axis=0, keepdims=True),
        jnp.sum(upstream, axis=0, keepdims=True),
        jnp.zeros((6, width), F32),
    ]
    small_late.start(0, jnp.concatenate(late, axis=0))
    found = grad_middle[...] + normed_back(upstream, scaled, inverse, vectors[0:1])
    gt[me] = found.astype(LOW)
    all_gt.start()
    small_tables.step(1)
    small_sums.step(1)
    small_late.step(0)
    small_dp.step(0)
    moved0.run(0)
    small_late.step(1)
    for other in all_gt.others():
        all_gt.forward(other)
    for each in moved3:
        each.run(0)
    small_tables.step(2)
    small_sums.step(2)
    small_late.step(2)
    for stage in range(1, halve_bits() - 1):
        moved0.run(stage)
        for each in moved3:
            each.run(stage)
    all_gt.take(line)
    for other in all_gt.others():
        all_gt.take(other)
    tokens_out[...] = gt[...]
    dp_out[...] = small_dp.take(1)
    tables_out[...] = small_tables.take(3)
    sums_out[...] = small_sums.take(3)
    late_out[...] = small_late.take(3)
    proj_out[...] = moved0.total().T
    for n, each in enumerate(moved3):
        qkv_out[n] = each.total()
    for each in [moved0, sum_part, all_gt, small_tables, small_sums, small_late, small_dp] + moved3:
        each.finish()


def tail(heads, grads, qkv_w, n1_t, tokens, grad_middle, vectors, tables, sums, fc1_bias, peak, proj):
    count = lax.axis_size("tensor")
    lines = count // 2
    local = heads * HEAD
    devices, chunks, owned, rows = n1_t.shape
    width = devices * chunks * owned
    share = rows // count
    vmem = pl.BlockSpec(memory_space=pltpu.VMEM)
    whole = (count, share, width)
    scratch = [
        pltpu.VMEM((3 * local, rows), LOW),
        pltpu.VMEM((count, share, 3 * local), LOW),
        pltpu.VMEM(whole, LOW),
        pltpu.VMEM(whole, LOW),
    ]
    scratch += [pltpu.VMEM((devices, owned, 3 * local), LOW)] * chunks
    scratch += halve_bufs(owned, 3 * local) * chunks
    scratch += halve_bufs(chunks * owned, local)
    scratch += part_bufs(lines, share, width) + gather_sems(lines)
    scratch += small_bufs(heads, EVERY, (4 * SIDE, 128))
    scratch += small_bufs(heads, EVERY, (8, width)) * 2
    scratch += small_bufs(heads, OVER_DP, (8, width))
    return pl.pallas_call(
        functools.partial(tail_kernel, heads),
        out_shape=(
            jax.ShapeDtypeStruct(whole, LOW),
            jax.ShapeDtypeStruct((local, chunks * owned), F32),
            jax.ShapeDtypeStruct((chunks, owned, 3 * local), F32),
            jax.ShapeDtypeStruct((4 * SIDE, 128), F32),
            jax.ShapeDtypeStruct((8, width), F32),
            jax.ShapeDtypeStruct((8, width), F32),
            jax.ShapeDtypeStruct((8, width), F32),
        ),
        in_specs=[vmem] * 11,
        out_specs=(vmem,) * 7,
        scratch_shapes=scratch,
        compiler_params=pltpu.CompilerParams(
            collective_id=4, has_side_effects=True, vmem_limit_bytes=VMEM_LIMIT
        ),
        name="tail",
    )(
        grads, qkv_w, n1_t, tokens.reshape(whole), grad_middle, vectors, tables, sums, fc1_bias,
        peak, proj,
    )


def on_device(
    tokens,
    cotangent,
    norm1_gain,
    norm1_shift,
    qkv_weight,
    qv_bias,
    proj_weight,
    proj_bias,
    table_rows,
    table_cols,
    norm2_gain,
    norm2_shift,
    fc1_weight,
    fc1_bias,
    fc2_weight,
    fc2_bias,
    threshold,
):
    images, row_count, model_width = tokens.shape
    token_count = images * row_count
    local_width = qkv_weight.shape[2]
    local_heads = local_width // HEAD
    groups = lax.axis_size("tensor")
    residual_in = tokens.reshape(token_count, model_width).astype(jnp.float32)
    scaled1, _ = normed(residual_in)
    normed1_low = (scaled1 * norm1_gain + norm1_shift).astype(jnp.bfloat16)
    shape = Shape(local_heads, lax.axis_size("dp") // local_heads, row_count)
    flipped = jnp.stack([table_rows, table_cols])[:, ::-1]
    flipped = jnp.pad(flipped, ((0, 0), (0, 1), (0, 0)))
    triple = jnp.einsum("dtc,nd->tcn", qkv_weight, normed1_low, preferred_element_type=jnp.float32)
    bias = jnp.stack([qv_bias[0], jnp.zeros_like(qv_bias[0]), qv_bias[1]])
    triple = (triple + bias[:, :, None]).astype(jnp.bfloat16)
    qkv = triple.reshape(3, local_heads, HEAD, row_count).transpose(1, 0, 2, 3)
    attended, qaug, bias_rows, kv, o_rows, lse, peak = attend(shape, qkv, flipped)
    grad_out = cotangent.reshape(token_count, model_width)
    vectors = jnp.stack([proj_bias, norm2_gain, norm2_shift, fc2_bias])
    vectors = jnp.pad(vectors, ((0, 4), (0, 0)))
    (
        output,
        grad_middle,
        grad_fc1,
        grad_fc2,
        grad_proj,
        grad_attended,
        grad_fc1_bias,
        sums,
        fc2_state,
    ) = middle_block(
        local_heads,
        attended.reshape(local_width, token_count),
        proj_weight,
        tokens.reshape(token_count, model_width),
        grad_out,
        fc1_weight,
        fc2_weight,
        fc1_bias,
        vectors,
    )
    grad_heads = grad_attended.reshape(local_heads, HEAD, row_count)
    devices, chunks, owned, _ = grad_fc1.shape
    grad_triple, table_terms, grad_fc1, grad_fc2 = attend_back(
        shape, grad_heads, flipped, qaug, bias_rows, kv, o_rows, lse, fc2_state, grad_fc1, grad_fc2
    )
    tail_vectors = jnp.pad(norm1_gain[None], ((0, 7), (0, 0)))
    (
        grad_tokens,
        grad_proj,
        grad_qkv,
        table_sums,
        sums,
        late,
        dp_sums,
    ) = tail(
        local_heads,
        grad_triple,
        qkv_weight.reshape(model_width, 3 * local_width),
        normed1_low.T.reshape(devices, chunks, owned, token_count),
        tokens.reshape(token_count, model_width),
        grad_middle,
        tail_vectors,
        table_terms,
        sums,
        grad_fc1_bias,
        peak,
        grad_proj,
    )
    grad_tokens = grad_tokens.reshape(images, row_count, model_width)
    grad_qkv = grad_qkv.reshape(model_width // devices, 3, local_width)
    table_sums = table_sums.reshape(2, 2 * SIDE, 128)[:, 2 * SIDE - 2 :: -1, :HEAD]
    grad_table_rows, grad_table_cols = table_sums[0], table_sums[1]
    grad_norm2_gain, grad_norm2_shift = sums[0], sums[1]
    grad_fc2_bias, grad_proj_bias = sums[2] / groups, sums[3] / groups
    grad_norm1_gain, grad_norm1_shift = late[0], late[1]
    grad_fc1_bias = dp_sums[0, : fc1_bias.shape[0]]
    grad_qv_bias = dp_sums[1, : 3 * local_width].reshape(3, local_width)[0::2]
    head_peaks = dp_sums[2, :local_heads]
    limit = threshold[0]
    clip_factors = jnp.sqrt(limit / jnp.maximum(head_peaks, limit))
    spread_factors = jnp.repeat(clip_factors, HEAD)
    clipped_qk = (qkv_weight[:, :2, :].astype(jnp.float32) * spread_factors).astype(jnp.bfloat16)
    clipped_q_bias = qv_bias[0] * spread_factors
    output = output.reshape(images, row_count, model_width)
    return (
        output,
        grad_tokens,
        grad_norm1_gain,
        grad_norm1_shift,
        grad_qkv,
        grad_qv_bias,
        grad_proj,
        grad_proj_bias,
        grad_table_rows,
        grad_table_cols,
        grad_norm2_gain,
        grad_norm2_shift,
        grad_fc1,
        grad_fc1_bias,
        grad_fc2,
        grad_fc2_bias,
        clipped_qk,
        clipped_q_bias,
        head_peaks,
        clip_factors,
    )


def solution(mesh):
    in_specs = (
        P(None, "dp", None),
        P(None, "dp", None),
        P(),
        P(),
        P(None, None, "tensor"),
        P(None, "tensor"),
        P("tensor", None),
        P(),
        P(),
        P(),
        P(),
        P(),
        P(None, "tensor"),
        P("tensor"),
        P("tensor", None),
        P(),
        P(),
    )
    out_specs = (
        P(None, "dp", None),
        P(None, "dp", None),
        P(),
        P(),
        P("dp", None, "tensor"),
        P(None, "tensor"),
        P("tensor", "dp"),
        P(),
        P(),
        P(),
        P(),
        P(),
        P("dp", "tensor"),
        P("tensor"),
        P("tensor", "dp"),
        P(),
        P(None, None, "tensor"),
        P("tensor"),
        P("tensor"),
        P("tensor"),
    )
    return jax.shard_map(
        on_device, mesh=mesh, in_specs=in_specs, out_specs=out_specs, check_vma=False
    )
```

```python
import functools
import math

import jax
import jax.numpy as jnp
from jax import lax
from jax.experimental import pallas as pl
from jax.experimental.pallas import tpu as pltpu
from jax.sharding import PartitionSpec as P

HEAD = 80
SIDE = 64

MESH = pl.DeviceIdType.MESH
LOW = jnp.bfloat16
F32 = jnp.float32
EPSILON = 1e-06
SCALE = HEAD**-0.5
EXP2_SCALE = SCALE * math.log2(math.e)
COLS_AT = HEAD
ROWS_AT = COLS_AT + 2 * SIDE
LSE_AT = ROWS_AT + 16
AUG = LSE_AT + 16
VMEM_LIMIT = {
    "attend": 60 * 2**20,
    "middle": 40 * 2**20,
    "attend_back": 24 * 2**20,
    "tail": 24 * 2**20,
    "finish": 12 * 2**20,
}


def nn(a, b):
    return lax.dot_general(a, b, (((1,), (0,)), ((), ())), preferred_element_type=F32)


def tn(a, b):
    return lax.dot_general(a, b, (((0,), (0,)), ((), ())), preferred_element_type=F32)


def nt(a, b):
    return lax.dot_general(a, b, (((1,), (1,)), ((), ())), preferred_element_type=F32)


def parts_of(values, count):
    pieces = []
    for _ in range(count):
        piece = values.astype(LOW).astype(F32)
        pieces.append(piece)
        values = values - piece
    return pieces


def send_dp(src, dst, send_sem, recv_sem, dev):
    return pltpu.make_async_remote_copy(
        src_ref=src,
        dst_ref=dst,
        send_sem=send_sem,
        recv_sem=recv_sem,
        device_id={"dp": dev},
        device_id_type=MESH,
    )


def paired(place, k, count):
    found, bit = 0, 1
    while bit < count:
        found = found + bit * lax.rem(place // bit + k // bit, 2)
        bit *= 2
    return found


def turned(count):
    row = lax.broadcasted_iota(jnp.int32, (count, count), 0)
    column = lax.broadcasted_iota(jnp.int32, (count, count), 1)
    return jnp.where(row + column == count - 2, 1.0, 0.0).astype(LOW)


def shifts(rows, dev):
    spot = lax.broadcasted_iota(jnp.int32, (2 * SIDE, rows), 1)
    by_row = SIDE - 1 - (dev * (rows // SIDE) + lax.shift_right_logical(spot, 6))
    by_col = SIDE - 1 - (spot & (SIDE - 1))
    return by_row, by_col


def skew(values, shift):
    for bit in (32, 16, 8, 4, 2, 1):
        moved = pltpu.roll(values, 2 * SIDE - bit, 0)
        values = jnp.where((shift & bit) != 0, moved, values)
    return values[:SIDE]


def unskew(values, shift):
    values = jnp.concatenate([values, jnp.zeros_like(values)], axis=0)
    for bit in (32, 16, 8, 4, 2, 1):
        moved = pltpu.roll(values, bit, 0)
        values = jnp.where((shift & bit) != 0, moved, values)
    return values


def greet(peers):
    barrier = pltpu.get_barrier_semaphore()
    for peer in peers:
        pl.semaphore_signal(barrier, inc=1, device_id={"dp": peer}, device_id_type=MESH)
    pl.semaphore_wait(barrier, len(peers))


def key_onehots(rows, dev):
    spot = lax.broadcasted_iota(jnp.int32, (2 * SIDE, rows), 1)
    index = lax.broadcasted_iota(jnp.int32, (2 * SIDE, rows), 0)
    cols = jnp.where((index & (SIDE - 1)) == (spot & (SIDE - 1)), 1.0, 0.0)
    spot, index = spot[:16], index[:16]
    offset = lax.rem(dev * (rows // SIDE), 8)
    in_group = jnp.where((index & 7) == offset + lax.shift_right_logical(spot, 6), 1.0, 0.0)
    return cols, in_group


class Shape:
    def __init__(self, heads, group, rows):
        self.heads, self.group, self.rows = heads, group, rows
        self.queries = heads * rows
        self.block = min(1024, self.queries)


def forward_kernel(shape, count, outs, *refs):
    held = refs[count + outs : 2 * count + outs]
    load = refs[2 * count + outs]
    copies = [
        pltpu.make_async_copy(a, b, load.at[n]) for n, (a, b) in enumerate(zip(refs[:count], held))
    ]
    for copy in copies[2:] + copies[:2]:
        copy.start()
    forward_body(
        shape, copies, *held, *refs[count : count + outs], *refs[2 * count + outs + 1 :]
    )


def forward_body(
    shape, copies, tokens, weights, proj_bias, gain2, shift2, fc2_bias, gain1, shift1, fc1_bias,
    qv_bias, threshold, rows_t, cols_t,
    att, qaug, bias_rows, kv_out, o_out, lse_out, peak_out, n1_out, tables, vectors,
    n1, qkv, wide_t, rq, rkv, kaug_t, kaug, vaug, oacc, mrow, lpk, att_s, att_r,
    q_send, q_recv, k_send, k_recv, x_send, x_recv, r_send, r_recv, o_sem,
):
    heads, group, rows, block = shape.heads, shape.group, shape.rows, shape.block
    local = heads * HEAD
    me = lax.axis_index("dp")
    z, g = me // group, lax.rem(me, group)
    column = [paired(z, k, heads) for k in range(1, heads)]
    mates = [lax.rem(g + k, group) for k in range(1, group)]
    greet([h * group + g for h in column] + [z * group + o for o in mates])
    width = tokens.shape[1]
    vectors[...] = jnp.zeros_like(vectors)
    for copy in copies[2:] + copies[:1]:
        copy.wait()
    listed = (proj_bias, gain2, shift2, fc2_bias, gain1, shift1, fc1_bias)
    for n, each in enumerate(listed):
        vectors[n : n + 1, : each.shape[0]] = each[...].reshape(1, each.shape[0])
    vectors[7:9, :local] = qv_bias[...]
    vectors[9:10] = jnp.broadcast_to(threshold[...].reshape(1, 1), (1, width))
    scaled, _ = normed(tokens[...].astype(F32))
    n1[...] = (scaled * vectors[4:5] + vectors[5:6]).astype(LOW)
    biases = vectors[7:9].astype(F32)
    biases = jnp.concatenate([biases, jnp.zeros((6, biases.shape[1]), F32)], axis=0).T

    def project(t):
        found = nt(weights[pl.ds(t * local, local), :], n1[...])
        if t != 1:
            found = found + biases[:local, t // 2 : t // 2 + 1]
        qkv[t] = found.astype(LOW)

    sends = []
    copies[1].wait()
    project(0)
    for h in column:
        mine = pl.ds(pl.multiple_of(h * HEAD, 16), HEAD)
        copy = send_dp(qkv.at[0, mine], rq.at[z], q_send.at[h], q_recv.at[z], h * group + g)
        copy.start()
        sends.append(copy)
    project(1)
    project(2)
    for h in column:
        mine = pl.ds(pl.multiple_of(h * HEAD, 16), HEAD)
        copy = send_dp(
            qkv.at[pl.ds(1, 2), mine], rkv.at[z, g], k_send.at[h], k_recv.at[z], h * group + g
        )
        copy.start()
        sends.append(copy)
    mine = pl.ds(pl.multiple_of(z * HEAD, 16), HEAD)
    rq[z] = qkv[0, mine]
    rkv[z, g] = qkv[pl.ds(1, 2), mine]
    for n, mate in enumerate(mates):
        send_dp(
            rkv.at[z, g], rkv.at[z, g], x_send.at[z, n], x_recv.at[z, g], z * group + mate
        ).start()
    n1_out[...] = n1[...].T
    wide_t[...] = jnp.zeros_like(wide_t)
    for n, held in enumerate((rows_t, cols_t)):
        wide_t[n, :HEAD, : held.shape[1]] = held[...]
        tables[n] = nn(wide_t[n], turned(2 * SIDE)).T[:, :HEAD].astype(LOW)
    qaug[pl.ds(LSE_AT, 16), :] = jnp.zeros((16, shape.queries), LOW)
    kaug_t[pl.ds(LSE_AT, 16), :] = jnp.zeros((16, rows), LOW)
    vaug[pl.ds(HEAD, 16), :] = jnp.where(
        lax.broadcasted_iota(jnp.int32, (16, rows), 0) == 0, 1.0, 0.0
    ).astype(LOW)
    oacc[...] = jnp.zeros_like(oacc)
    mrow[...] = jnp.full_like(mrow, -jnp.inf)
    lpk[...] = jnp.full_like(lpk, -jnp.inf)

    def prepare(k, carry):
        source = paired(z, k, heads)
        span = pl.ds(pl.multiple_of(source * rows, rows), rows)

        @pl.when(k > 0)
        def _():
            send_dp(rq.at[source], rq.at[source], q_send.at[source], q_recv.at[source], me).wait_recv()

        query = rq[source]
        by_row, by_col = shifts(rows, source * group + g)
        along_rows = skew(nn(tables[0], query) * (1.0 / SCALE), by_row)
        along_cols = skew(nn(tables[1], query) * (1.0 / SCALE), by_col)
        qaug[pl.ds(0, HEAD), span] = query
        cols = parts_of(along_cols, 2)
        qaug[pl.ds(COLS_AT, 2 * SIDE), span] = jnp.concatenate(cols, axis=0).astype(LOW)
        high, rest = parts_of(along_rows, 2)
        for at in range(SIDE // 8):
            pair = jnp.concatenate([high[8 * at : 8 * at + 8], rest[8 * at : 8 * at + 8]], axis=0)
            bias_rows[at, :, span] = pair.astype(LOW)
        return carry

    lax.fori_loop(0, heads, prepare, 0)

    def chunk(source, mate):
        dev = source * group + mate
        cols, in_group = key_onehots(rows, dev)
        kaug_t[pl.ds(0, HEAD), :] = rkv[source, mate, 0]
        kaug_t[pl.ds(COLS_AT, 2 * SIDE), :] = cols.astype(LOW)
        kaug_t[pl.ds(ROWS_AT, 16), :] = in_group.astype(LOW)
        kaug[...] = kaug_t[...].T
        vaug[pl.ds(0, HEAD), :] = rkv[source, mate, 1]
        qaug[pl.ds(ROWS_AT, 16), :] = bias_rows[(dev * (rows // SIDE)) // 8]

        def one(i, carry):
            span = pl.ds(pl.multiple_of(i * block, block), block)
            logits = nn(kaug[:, :HEAD], qaug[pl.ds(0, HEAD), span])
            lpk[...] = jnp.maximum(lpk[...], jnp.max(logits.reshape(rows // 8, 8, block), axis=0))
            scores = nn(kaug[...], qaug[:, span])
            before = mrow[:, span]
            top = jnp.maximum(before, jnp.max(scores, axis=0, keepdims=True))
            mrow[:, span] = top
            weights = jnp.exp2(scores * EXP2_SCALE - top * EXP2_SCALE).astype(LOW)
            keep = jnp.exp2((before - top) * EXP2_SCALE)
            oacc[:, span] = oacc[:, span] * keep + nn(vaug[...], weights)
            return carry

        lax.fori_loop(0, shape.queries // block, one, 0)

    def column_step(k, carry):
        source = paired(z, k, heads)

        @pl.when(k > 0)
        def _():
            send_dp(rkv.at[source, g], rkv.at[source, g], k_send.at[source], k_recv.at[source], me).wait_recv()
            for n, mate in enumerate(mates):
                send_dp(
                    rkv.at[source, g], rkv.at[source, g], x_send.at[source, n], x_recv.at[source, g],
                    z * group + mate,
                ).start()

        chunk(source, g)

        def mate_step(n, inner):
            mate = lax.rem(g + n, group)
            send_dp(
                rkv.at[source, mate], rkv.at[source, mate], x_send.at[source, 0], x_recv.at[source, mate], me
            ).wait_recv()
            chunk(source, mate)
            return inner

        lax.fori_loop(1, group, mate_step, 0)
        return carry

    lax.fori_loop(0, heads, column_step, 0)
    keep_kv = pltpu.make_async_copy(rkv, kv_out, o_sem)
    keep_kv.start()

    def finish(k, carry):
        source = paired(z, lax.rem(k, heads), heads)
        span = pl.ds(pl.multiple_of(source * rows, rows), rows)
        total = oacc[pl.ds(HEAD, 1), span]
        attended = oacc[pl.ds(0, HEAD), span] / total
        o_out[:, span] = attended
        lse_out[:, span] = mrow[:, span] + jnp.log2(total) * (1.0 / EXP2_SCALE)
        att_s[source] = attended.astype(LOW)

        @pl.when(source != z)
        def _():
            send_dp(
                att_s.at[source], att_r.at[z], r_send.at[source], r_recv.at[z], source * group + g
            ).start()

        return carry

    lax.fori_loop(1, heads + 1, finish, 0)
    att[z] = att_s[z]
    peak_out[...] = jnp.full(peak_out.shape, jnp.max(lpk[...]) * SCALE, F32)
    for h in column:
        send_dp(att_s.at[h], att_r.at[h], r_send.at[h], r_recv.at[h], h * group + g).wait()
        att[h] = att_r[h]
    for copy in sends:
        copy.wait_send()
    for source in range(heads):
        for n, mate in enumerate(mates):
            send_dp(
                rkv.at[source, g], rkv.at[source, g], x_send.at[source, n], x_recv.at[source, g],
                z * group + mate,
            ).wait_send()
    keep_kv.wait()


def attend(shape, tokens, weights, listed, rows_t, cols_t):
    heads, group, rows, queries = shape.heads, shape.group, shape.rows, shape.queries
    width, local = tokens.shape[1], heads * HEAD
    args = (tokens, weights, *listed, rows_t, cols_t)
    vmem = pl.BlockSpec(memory_space=pltpu.VMEM)
    hbm = pl.BlockSpec(memory_space=pl.ANY)
    dma = pltpu.SemaphoreType.DMA
    return pl.pallas_call(
        functools.partial(forward_kernel, shape, len(args), 10),
        out_shape=(
            jax.ShapeDtypeStruct((heads, HEAD, rows), LOW),
            jax.ShapeDtypeStruct((AUG, queries), LOW),
            jax.ShapeDtypeStruct((SIDE // 8, 16, queries), LOW),
            jax.ShapeDtypeStruct((heads, group, 2, HEAD, rows), LOW),
            jax.ShapeDtypeStruct((HEAD, queries), F32),
            jax.ShapeDtypeStruct((1, queries), F32),
            jax.ShapeDtypeStruct((8, 128), F32),
            jax.ShapeDtypeStruct((width, rows), LOW),
            jax.ShapeDtypeStruct((2, 2 * SIDE, HEAD), LOW),
            jax.ShapeDtypeStruct((16, width), F32),
        ),
        in_specs=[pl.BlockSpec(memory_space=pltpu.HBM)] * len(args),
        out_specs=(vmem, vmem, vmem, hbm, vmem, vmem, vmem, vmem, vmem, vmem),
        scratch_shapes=[
            *[pltpu.VMEM(each.shape, each.dtype) for each in args],
            dma((len(args),)),
            pltpu.VMEM((rows, width), LOW),
            pltpu.VMEM((3, local, rows), LOW),
            pltpu.VMEM((2, 128, 2 * SIDE), LOW),
            pltpu.VMEM((heads, HEAD, rows), LOW),
            pltpu.VMEM((heads, group, 2, HEAD, rows), LOW),
            pltpu.VMEM((AUG, rows), LOW),
            pltpu.VMEM((rows, AUG), LOW),
            pltpu.VMEM((HEAD + 16, rows), LOW),
            pltpu.VMEM((HEAD + 16, queries), F32),
            pltpu.VMEM((1, queries), F32),
            pltpu.VMEM((8, shape.block), F32),
            pltpu.VMEM((heads, HEAD, rows), LOW),
            pltpu.VMEM((heads, HEAD, rows), LOW),
            dma((heads,)), dma((heads,)), dma((heads,)), dma((heads,)),
            dma((heads, group)), dma((heads, group)), dma((heads,)), dma((heads,)),
            dma,
        ],
        compiler_params=pltpu.CompilerParams(
            collective_id=1, has_side_effects=True, vmem_limit_bytes=VMEM_LIMIT["attend"]
        ),
        name="attend",
    )(*args)


def backward_kernel(
    shape, ga, tables, qaug_in, bias_rows, rkv, o_in, lse_in, fc2_state, fc2_more, fc1, proj,
    grads, table_grads, fc1_out, fc2_out, fc1_state, proj_state,
    rdo, qaug, q_tok, do_aug, do_tok, kaug_t, kaug, vaug_t, vaug, kacc, vacc, dq, drow, dcol,
    part, xr, summed, gq_s, gq_r, gkv_r,
    d_send, d_recv, x_send, x_recv, kv_send, kv_recv, q_send, q_recv, *rest,
):
    chunks = fc1.shape[1]
    rest = list(rest)

    def taken(number):
        found, rest[:] = rest[:number], rest[number:]
        return found

    whole_bufs = 2 + 3 * halve_bits()
    bits = halve_bits()
    moved2 = [Halve(near_first(), fc2_state, taken(3 * (bits - 2)), first=2)]
    if chunks > 1:
        moved2 += [Halve(near_first(), fc2_more, taken(3 * (bits - 1)), first=1)]
    moved0 = Halve(near_first(), proj, taken(3), last=0)
    moved1 = [Halve(near_first(), fc1.at[:, 0], taken(whole_bufs), own=True)]
    if chunks > 1:
        moved1 += [Halve(near_first(), fc1.at[:, 1], taken(5), last=0, own=True)]
    heads, group, rows, block = shape.heads, shape.group, shape.rows, shape.block
    queries = shape.queries
    me = lax.axis_index("dp")
    z, g = me // group, lax.rem(me, group)
    column = [paired(z, k, heads) for k in range(1, heads)]
    mates = [lax.rem(g + k, group) for k in range(1, group)]
    greet([h * group + g for h in column] + [z * group + o for o in mates])
    sends = []
    for h in column:
        copy = send_dp(ga.at[h], rdo.at[z], d_send.at[h], d_recv.at[z], h * group + g)
        copy.start()
        sends.append(copy)
    moved1[0].start()
    for each in moved2:
        each.start()
    for each in moved1:
        each.load()
    rdo[z] = ga[z]
    qaug[...] = qaug_in[...]
    ones = jnp.where(lax.broadcasted_iota(jnp.int32, (16, rows), 0) < 3, 1.0, 0.0).astype(LOW)
    kaug_t[pl.ds(LSE_AT, 16), :] = ones
    vaug_t[pl.ds(HEAD, 16), :] = ones
    vaug_t[pl.ds(HEAD + 16, 32), :] = jnp.zeros((32, rows), LOW)
    low_lse = parts_of(-lse_in[...], 3)
    qaug[pl.ds(LSE_AT, 16), :] = jnp.concatenate(
        low_lse + [jnp.zeros((13, queries), F32)], axis=0
    ).astype(LOW)
    dq[...] = jnp.zeros_like(dq)
    dcol[...] = jnp.zeros_like(dcol)
    drow[...] = jnp.zeros_like(drow)

    def prepare(k, carry):
        source = paired(z, k, heads)
        span = pl.ds(pl.multiple_of(source * rows, rows), rows)

        @pl.when(k > 0)
        def _():
            send_dp(rdo.at[source], rdo.at[source], d_send.at[source], d_recv.at[source], me).wait_recv()

        upstream = rdo[source]
        dots = jnp.sum(upstream.astype(F32) * o_in[:, span], axis=0, keepdims=True)
        low_dots = parts_of(-dots, 3)
        do_aug[pl.ds(0, HEAD), span] = upstream
        do_aug[pl.ds(HEAD, 16), span] = jnp.concatenate(
            low_dots + [jnp.zeros((13, rows), F32)], axis=0
        ).astype(LOW)
        do_aug[pl.ds(HEAD + 16, 32), span] = jnp.zeros((32, rows), LOW)
        do_tok[span, :] = do_aug[:, span].T
        q_tok[span, :] = qaug[pl.ds(0, 128), span].T
        return carry

    lax.fori_loop(0, heads, prepare, 0)

    def chunk(source, mate):
        dev = source * group + mate
        at = (dev * (rows // SIDE)) // 8
        cols, in_group = key_onehots(rows, dev)
        kaug_t[pl.ds(0, HEAD), :] = rkv[source, mate, 0]
        kaug_t[pl.ds(COLS_AT, 2 * SIDE), :] = cols.astype(LOW)
        kaug_t[pl.ds(ROWS_AT, 16), :] = in_group.astype(LOW)
        kaug[...] = kaug_t[...].T
        vaug_t[pl.ds(0, HEAD), :] = rkv[source, mate, 1]
        vaug[...] = vaug_t[...].T
        qaug[pl.ds(ROWS_AT, 16), :] = bias_rows[at]
        kacc[...] = jnp.zeros_like(kacc)
        vacc[...] = jnp.zeros_like(vacc)
        back = jnp.concatenate(
            [kaug_t[pl.ds(0, COLS_AT + SIDE), :], kaug_t[pl.ds(ROWS_AT, 16), :]], axis=0
        )

        def one(i, carry):
            span = pl.ds(pl.multiple_of(i * block, block), block)
            probs = jnp.exp2(nn(kaug[...], qaug[:, span]) * EXP2_SCALE)
            pulled = nn(vaug[...], do_aug[:, span])
            low_grads = (probs * pulled).astype(LOW)
            vacc[...] += nn(probs.astype(LOW), do_tok[span, :])
            kacc[...] += nn(low_grads, q_tok[span, :])
            found = nn(back, low_grads)
            dq[:, span] += found[:HEAD]
            dcol[:, span] += found[COLS_AT : COLS_AT + SIDE]
            drow[at, :, span] += found[COLS_AT + SIDE : COLS_AT + SIDE + 8]
            return carry

        lax.fori_loop(0, queries // block, one, 0)

    def put(where, extra):
        key_part = (kacc[...] * SCALE).T[:HEAD]
        value_part = vacc[...].T[:HEAD]
        for other in extra:
            key_part = key_part + other[0].astype(F32)
            value_part = value_part + other[1].astype(F32)
        where[0] = key_part.astype(LOW)
        where[1] = value_part.astype(LOW)

    def mate_copy(source, mate):
        return send_dp(
            part.at[source, mate], xr.at[source, g], x_send.at[source, mate], x_recv.at[source, g],
            z * group + mate,
        )

    def mates_step(k, carry):
        source = paired(z, lax.rem(k, heads), heads)

        def mate_step(n, inner):
            mate = lax.rem(g + n, group)
            chunk(source, mate)
            put(part.at[source, mate], [])
            mate_copy(source, mate).start()
            return inner

        lax.fori_loop(1, group, mate_step, 0)

        return carry

    lax.fori_loop(1, heads + 1, mates_step, 0)
    moved0.start()
    if chunks > 1:
        moved1[1].start()
        moved2[1].run(1)
    moved1[0].loaded()
    moved1[0].run(0)

    def own_step(k, carry):
        source = paired(z, lax.rem(k, heads), heads)
        chunk(source, g)
        extra = []
        for mate in mates:
            send_dp(
                xr.at[source, mate], xr.at[source, mate], x_send.at[source, mate], x_recv.at[source, mate], me
            ).wait_recv()
            extra.append(xr.at[source, mate])
        put(summed.at[source], extra)

        @pl.when(source != z)
        def _():
            send_dp(
                summed.at[source], gkv_r.at[z], kv_send.at[source], kv_recv.at[z], source * group + g
            ).start()

        return carry

    lax.fori_loop(1, heads + 1, own_step, 0)
    table_grads[...] = jnp.zeros_like(table_grads)

    def finish(k, carry):
        source = paired(z, lax.rem(k, heads), heads)
        span = pl.ds(pl.multiple_of(source * rows, rows), rows)
        by_row, by_col = shifts(rows, source * group + g)
        total = dq[:, span] * SCALE
        for n, held in enumerate((drow[:, :, span].reshape(SIDE, rows), dcol[:, span])):
            spread = unskew(held, by_col if n else by_row)
            for piece in parts_of(spread, 2):
                low_piece = piece.astype(LOW)
                total = total + tn(tables[n], low_piece)
                table_grads[n] += nn(low_piece, q_tok[span, :])
        gq_s[source] = total.astype(LOW)

        @pl.when(source != z)
        def _():
            send_dp(
                gq_s.at[source], gq_r.at[z], q_send.at[source], q_recv.at[z], source * group + g
            ).start()

        return carry

    lax.fori_loop(1, heads + 1, finish, 0)
    moved1[0].run(1)
    for stage in range(2, halve_bits() - 1):
        for each in moved2 + moved1[:1]:
            each.run(stage)
    found = [each.total() for each in moved2]
    fc2_out[...] = jnp.concatenate(found, axis=0) if chunks > 1 else found[0]
    fc1_out[...] = moved1[0].total()
    if chunks > 1:
        moved1[1].loaded()
        moved1[1].run(0)
        fc1_state[...] = moved1[1].stages[0][0][...]
    moved0.run(0)
    proj_state[...] = moved0.stages[0][0][...]
    grads[z, 0] = gq_s[z]
    grads[z, pl.ds(1, 2)] = summed[z]
    for h in column:
        send_dp(summed.at[h], gkv_r.at[h], kv_send.at[h], kv_recv.at[h], h * group + g).wait()
        grads[h, pl.ds(1, 2)] = gkv_r[h]
    for h in column:
        send_dp(gq_s.at[h], gq_r.at[h], q_send.at[h], q_recv.at[h], h * group + g).wait()
        grads[h, 0] = gq_r[h]
    for copy in sends:
        copy.wait_send()
    for source in range(heads):
        for mate in mates:
            mate_copy(source, mate).wait_send()
    for each in moved1 + moved2 + [moved0]:
        each.finish()


def attend_back(shape, ga, tables, qaug, bias_rows, kv, o_rows, lse, fc2_state, fc2_more, fc1, proj):
    local = proj.shape[2]
    devices, chunks, owned, hidden = fc1.shape
    hbm = pl.BlockSpec(memory_space=pl.ANY)
    moving = halve_bufs(owned, hidden, first=2)
    if chunks > 1:
        moving += halve_bufs(owned, hidden, first=1)
    moving += halve_bufs(chunks * owned, local, last=0)
    moving += halve_bufs(owned, hidden, own=True)
    if chunks > 1:
        moving += halve_bufs(owned, hidden, last=0, own=True)
    heads, group, rows, queries = shape.heads, shape.group, shape.rows, shape.queries
    vmem = pl.BlockSpec(memory_space=pltpu.VMEM)
    dma = pltpu.SemaphoreType.DMA
    return pl.pallas_call(
        functools.partial(backward_kernel, shape),
        out_shape=(
            jax.ShapeDtypeStruct((heads, 3, HEAD, rows), LOW),
            jax.ShapeDtypeStruct((2, 2 * SIDE, 128), F32),
            jax.ShapeDtypeStruct((owned, hidden), F32),
            jax.ShapeDtypeStruct((chunks * owned, hidden), F32),
            jax.ShapeDtypeStruct((devices // 2, owned, hidden), LOW),
            jax.ShapeDtypeStruct((devices // 2, chunks * owned, local), LOW),
        ),
        in_specs=[vmem] * 9 + [hbm, vmem],
        out_specs=(vmem,) * 6,
        scratch_shapes=[
            pltpu.VMEM((heads, HEAD, rows), LOW),
            pltpu.VMEM((AUG, queries), LOW),
            pltpu.VMEM((queries, 128), LOW),
            pltpu.VMEM((128, queries), LOW),
            pltpu.VMEM((queries, 128), LOW),
            pltpu.VMEM((AUG, rows), LOW),
            pltpu.VMEM((rows, AUG), LOW),
            pltpu.VMEM((128, rows), LOW),
            pltpu.VMEM((rows, 128), LOW),
            pltpu.VMEM((rows, 128), F32),
            pltpu.VMEM((rows, 128), F32),
            pltpu.VMEM((HEAD, queries), F32),
            pltpu.VMEM((SIDE // 8, 8, queries), F32),
            pltpu.VMEM((SIDE, queries), F32),
            pltpu.VMEM((heads, group, 2, HEAD, rows), LOW),
            pltpu.VMEM((heads, group, 2, HEAD, rows), LOW),
            pltpu.VMEM((heads, 2, HEAD, rows), LOW),
            pltpu.VMEM((heads, HEAD, rows), LOW),
            pltpu.VMEM((heads, HEAD, rows), LOW),
            pltpu.VMEM((heads, 2, HEAD, rows), LOW),
            dma((heads,)), dma((heads,)), dma((heads, group)), dma((heads, group)),
            dma((heads,)), dma((heads,)), dma((heads,)), dma((heads,)),
        ] + moving,
        compiler_params=pltpu.CompilerParams(
            collective_id=2, has_side_effects=True, vmem_limit_bytes=VMEM_LIMIT["attend_back"]
        ),
        name="attend_back",
    )(ga, tables, qaug, bias_rows, kv, o_rows, lse, fc2_state, fc2_more, fc1, proj)


def send_tensor(src, dst, send_sem, recv_sem, dev):
    return pltpu.make_async_remote_copy(
        src_ref=src,
        dst_ref=dst,
        send_sem=send_sem,
        recv_sem=recv_sem,
        device_id={"tensor": dev},
        device_id_type=MESH,
    )


def tensor_place():
    me = lax.axis_index("tensor")
    return lax.rem(me, 2), me // 2, lax.axis_size("tensor") // 2


def tensor_peers():
    core, line, lines = tensor_place()
    far = [lax.rem(line + k, lines) * 2 + core for k in range(1, lines)]
    return far + [line * 2 + 1 - core]


def part_bufs(lines, share, width, dtype=LOW):
    dma = pltpu.SemaphoreType.DMA
    return [pltpu.VMEM((lines, share, width), dtype)] * 3 + [dma((lines,))] * 4


class Reduce:
    def __init__(self, part, mate_in, passed, line_in, m_send, m_recv, l_send, l_recv):
        self.part, self.mate_in, self.passed, self.line_in = part, mate_in, passed, line_in
        self.sems = m_send, m_recv, l_send, l_recv
        self.core, self.line, self.lines = tensor_place()

    def mate_copy(self, to):
        m_send, m_recv, _, _ = self.sems
        return send_tensor(
            self.part.at[to * 2 + 1 - self.core], self.mate_in.at[to],
            m_send.at[to], m_recv.at[to], self.line * 2 + 1 - self.core,
        )

    def line_copy(self, to, slot):
        _, _, l_send, l_recv = self.sems
        return send_tensor(
            self.passed.at[to], self.line_in.at[slot], l_send.at[to], l_recv.at[slot],
            to * 2 + self.core,
        )

    def give(self, to):
        self.mate_copy(to).start()

    def pass_on(self, to):
        self.mate_copy(to).wait_recv()
        both = self.part[to * 2 + self.core].astype(F32) + self.mate_in[to].astype(F32)
        self.passed[to] = both.astype(self.passed.dtype)
        self.line_copy(to, self.line).start()

    def others(self):
        return [lax.rem(self.line + k, self.lines) for k in range(1, self.lines)]

    def total(self):
        self.mate_copy(self.line).wait_recv()
        total = self.part[self.line * 2 + self.core].astype(F32) + self.mate_in[self.line].astype(F32)
        for other in self.others():
            self.line_copy(other, other).wait_recv()
            total = total + self.line_in[other].astype(F32)
        return total

    def finish(self):
        self.mate_copy(self.line).wait_send()
        for other in self.others():
            self.mate_copy(other).wait_send()
            self.line_copy(other, self.line).wait_send()


def gather_sems(lines):
    dma = pltpu.SemaphoreType.DMA
    return [dma((lines,)), dma((lines,)), dma((2 * lines,))]


class Gather:
    def __init__(self, whole, l_send, m_send, recv):
        self.whole, self.sems = whole, (l_send, m_send, recv)
        self.core, self.line, self.lines = tensor_place()

    def line_copy(self, to):
        l_send, _, recv = self.sems
        own = self.line * 2 + self.core
        return send_tensor(
            self.whole.at[own], self.whole.at[own], l_send.at[to], recv.at[own], to * 2 + self.core
        )

    def mate_copy(self, at):
        _, m_send, recv = self.sems
        part = at * 2 + self.core
        return send_tensor(
            self.whole.at[part], self.whole.at[part], m_send.at[at], recv.at[part],
            self.line * 2 + 1 - self.core,
        )

    def arrived(self, part):
        l_send, _, recv = self.sems
        send_tensor(
            self.whole.at[part], self.whole.at[part], l_send.at[0], recv.at[part], part
        ).wait_recv()

    def others(self):
        return [lax.rem(self.line + k, self.lines) for k in range(1, self.lines)]

    def start(self):
        for other in self.others():
            self.line_copy(other).start()
        self.mate_copy(self.line).start()

    def forward(self, at):
        self.arrived(at * 2 + self.core)
        self.mate_copy(at).start()

    def take(self, at):
        self.arrived(at * 2 + 1 - self.core)

    def finish(self):
        self.mate_copy(self.line).wait_send()
        for other in self.others():
            self.mate_copy(other).wait_send()
            self.line_copy(other).wait_send()


def normed(values):
    center = values - jnp.mean(values, axis=-1, keepdims=True)
    variance = jnp.mean(center * center, axis=-1, keepdims=True)
    inverse = lax.rsqrt(variance + EPSILON)
    return center * inverse, inverse


def normed_back(upstream, scaled, inverse, gain):
    weighted = upstream * gain
    centered = weighted - jnp.mean(weighted, axis=-1, keepdims=True)
    return (centered - scaled * jnp.mean(weighted * scaled, axis=-1, keepdims=True)) * inverse


def tile_of(width):
    return 256 if width % 256 == 0 else 128


class Ring:
    def __init__(self, heads):
        self.heads, self.group = heads, lax.axis_size("dp") // heads
        me = lax.axis_index("dp")
        self.z, self.g = me // self.group, lax.rem(me, self.group)

    def column(self):
        return [paired(self.z, k, self.heads) for k in range(1, self.heads)]

    def mates(self):
        return [lax.rem(self.g + k, self.group) for k in range(1, self.group)]

    def peers(self):
        far = [h * self.group + self.g for h in self.column()]
        return far + [self.z * self.group + o for o in self.mates()]


def greet_all(ring):
    barrier = pltpu.get_barrier_semaphore()
    near, far = tensor_peers(), ring.peers()
    for peer in near:
        pl.semaphore_signal(barrier, inc=1, device_id={"tensor": peer}, device_id_type=MESH)
    for peer in far:
        pl.semaphore_signal(barrier, inc=1, device_id={"dp": peer}, device_id_type=MESH)
    pl.semaphore_wait(barrier, len(near) + len(far))


def halve_bits():
    return (lax.axis_size("dp") - 1).bit_length()


def near_first():
    return tuple(range(halve_bits()))


def far_first(group):
    first = group.bit_length() - 1
    return (first,) + tuple(bit for bit in range(halve_bits()) if bit != first)


def halve_bufs(share, width, first=0, last=None, own=False):
    bits = halve_bits()
    last = bits - 1 if last is None else last
    dma = pltpu.SemaphoreType.DMA
    found = []
    if own:
        found += [pltpu.VMEM((1 << (bits - 1), share, width), LOW), dma]
    for stage in range(first, last + 1):
        count = 1 << (bits - 1 - stage)
        found += [pltpu.VMEM((count, share, width), LOW), dma((count,)), dma((count,))]
    return found


class Halve:
    def __init__(self, order, source, bufs, first=0, last=None, own=False):
        self.order, self.source, self.first = order, source, first
        self.last = len(order) - 1 if last is None else last
        bufs = list(bufs)
        self.own = bufs[0:2] if own else None
        bufs = bufs[2:] if own else bufs
        self.stages = {first + n: bufs[3 * n : 3 * n + 3] for n in range(len(bufs) // 3)}
        self.me = lax.axis_index("dp")

    def bit(self, stage):
        return lax.rem(self.me // (1 << self.order[stage]), 2)

    def count(self, stage):
        return 1 << (len(self.order) - 1 - stage)

    def index(self, stage, at, bit):
        if stage > 0:
            return at * 2 + bit
        place = bit * (1 << self.order[0])
        for n, other in enumerate(self.order[1:]):
            place = place + lax.rem(at // (1 << n), 2) * (1 << other)
        return place

    def held(self, stage):
        return self.source if stage == self.first else self.stages[stage - 1][0]

    def copy(self, stage, at):
        bit = self.bit(stage)
        into, send, recv = self.stages[stage]
        return send_dp(
            self.held(stage).at[self.index(stage, at, 1 - bit)], into.at[at],
            send.at[at], recv.at[at], self.me + (1 - 2 * bit) * (1 << self.order[stage]),
        )

    def spots(self, stage):
        if stage == len(self.order) - 1:
            return [0]
        bit, half = self.bit(stage + 1), self.count(stage) // 2
        return [n * 2 + 1 - bit for n in range(half)] + [n * 2 + bit for n in range(half)]

    def load(self):
        for at in range(self.count(0)):
            pltpu.make_async_copy(
                self.source.at[self.index(0, at, self.bit(0))], self.own[0].at[at], self.own[1]
            ).start()

    def loaded(self):
        pltpu.make_async_copy(
            self.source.at[pl.ds(0, self.count(0))], self.own[0], self.own[1]
        ).wait()

    def start(self, only=slice(None)):
        for at in self.spots(self.first)[only]:
            self.copy(self.first, at).start()

    def kept(self, stage, at):
        if stage == self.first and self.own is not None:
            return self.own[0][at].astype(F32)
        return self.held(stage)[self.index(stage, at, self.bit(stage))].astype(F32)

    def sum_at(self, stage, at):
        self.copy(stage, at).wait_recv()
        return self.kept(stage, at) + self.stages[stage][0][at].astype(F32)

    def run(self, stage):
        for n, at in enumerate(self.spots(stage)):
            self.stages[stage][0][at] = self.sum_at(stage, at).astype(LOW)
            if stage < self.last and n < self.count(stage) // 2:
                self.copy(stage + 1, n).start()

    def total(self):
        return self.sum_at(self.last, 0)

    def finish(self):
        for stage in self.stages:
            for at in range(self.count(stage)):
                self.copy(stage, at).wait_send()


def middle_kernel(
    heads, att, proj_w, tokens, cot, fc1_hbm, fc2_hbm, vectors,
    output, middle_out, fc1_out, proj_out, ga_out, fc1_bias_out, sums_out, fc2_state, fc2_more,
    fc1, fc2, att_tok, branch, mlp, back, n2, act, gu, gb, outs, held, spread,
    wide, load1, load2, *rest,
):
    core, line, lines = tensor_place()
    me = lax.axis_index("tensor")
    _, share, width = tokens.shape
    rows = tokens.shape[0] * share
    local, hidden = proj_w.shape[0], fc1_hbm.shape[1]
    step, dstep = tile_of(hidden), tile_of(width)
    in_fc1 = pltpu.make_async_copy(fc1_hbm, fc1, load1)
    in_fc2 = pltpu.make_async_copy(fc2_hbm, fc2, load2)
    in_fc1.start()
    in_fc2.start()
    greet_all(Ring(heads))
    sum_branch = Reduce(branch, *rest[0:7])
    sum_mlp = Reduce(mlp, *rest[7:14])
    sum_back = Reduce(back, *rest[14:21])
    all_n2 = Gather(n2, *rest[21:24])
    all_gb = Gather(gb, *rest[24:27])
    all_out = Gather(outs, *rest[27:30])
    blocks2, blocks1, fc1_sem = rest[30:33]
    devices, chunks, owned, _ = blocks2.shape
    moved = [
        Halve(near_first(), blocks2.at[:, n], rest[36 + 3 * n : 39 + 3 * n], last=0)
        for n in range(1, chunks)
    ]
    moved = [Halve(near_first(), blocks2.at[:, 0], rest[33:39], last=1)] + moved
    att_tok[...] = att[...].T.reshape(att_tok.shape)

    def project(k, carry):
        to = lax.rem(line + 1 + lax.rem(k, lines), lines)
        part = to * 2 + jnp.where(k < lines, 1 - core, core)
        branch[part] = nn(att_tok[part], proj_w[...]).astype(LOW)

        @pl.when(k < lines)
        def _():
            sum_branch.give(to)

        return carry

    lax.fori_loop(0, 2 * lines, project, 0)
    for other in sum_branch.others():
        sum_branch.pass_on(other)
    middle = tokens[me].astype(F32) + vectors[0:1]
    middle = middle + sum_branch.total()
    scaled, inverse = normed(middle)
    n2[me] = (scaled * vectors[1:2] + vectors[2:3]).astype(LOW)
    all_n2.start()
    held[0] = middle
    held[1] = scaled
    spread[...] = jnp.broadcast_to(inverse, spread.shape)
    fc1_bias_out[...] = jnp.zeros_like(fc1_bias_out)
    in_fc1.wait()
    in_fc2.wait()

    def hidden_part(k, carry):
        at = lax.rem(line + k, lines)

        @pl.when(k > 0)
        def _():
            all_n2.forward(at)

        all_n2.take(at)
        pair = pl.ds(at * 2, 2)
        inputs = n2[pair].reshape(2 * share, width)
        pulls = cot[pair].reshape(2 * share, width)

        def tile(n, inner):
            span = pl.ds(pl.multiple_of(n * step, step), step)
            up = nn(inputs, fc1[:, span]) + vectors[6:7, span]
            phi = 0.5 + 0.5 * lax.erf(up * math.sqrt(0.5))
            slope = phi + up * (jnp.exp(-0.5 * up * up) * (2 * math.pi) ** -0.5)
            act[pair, :, span] = (up * phi).astype(LOW).reshape(2, share, step)
            grad_up = (nt(pulls, fc2[span, :]) * slope).astype(LOW)
            gu[pair, :, span] = grad_up.reshape(2, share, step)
            fc1_bias_out[:, span] += jnp.sum(grad_up.astype(F32), axis=0, keepdims=True)
            return inner

        lax.fori_loop(0, hidden // step, tile, 0)

        def tile_back(n, inner):
            span = pl.ds(pl.multiple_of(n * dstep, dstep), dstep)
            found = nt(gu[pair].reshape(2 * share, hidden), fc1[span, :])
            back[pair, :, span] = found.astype(LOW).reshape(2, share, dstep)
            return inner

        lax.fori_loop(0, width // dstep, tile_back, 0)
        sum_back.give(at)

        return carry

    lax.fori_loop(0, lines, hidden_part, 0)

    def weights2(n, carry):
        span = pl.ds(pl.multiple_of(n * dstep, dstep), dstep)
        found = tn(cot[:, :, span].reshape(rows, dstep), act[...].reshape(rows, hidden))
        wide[span, :] = found.astype(LOW)
        return carry

    lax.fori_loop(0, width // dstep, weights2, 0)
    for dev in range(devices):
        for chunk in range(chunks):
            at = (dev * chunks + chunk) * owned
            blocks2[dev, chunk] = wide[pl.ds(at, owned), :]
    for each in moved:
        each.start()
    for other in sum_back.others():
        sum_back.pass_on(other)

    def out_part(k, carry):
        at = lax.rem(line + 1 + k, lines)
        pair = pl.ds(at * 2, 2)

        def tile_out(n, inner):
            span = pl.ds(pl.multiple_of(n * dstep, dstep), dstep)
            found = nn(act[pair].reshape(2 * share, hidden), fc2[:, span])
            mlp[pair, :, span] = found.astype(LOW).reshape(2, share, dstep)
            return inner

        lax.fori_loop(0, width // dstep, tile_out, 0)
        sum_mlp.give(at)
        return carry

    lax.fori_loop(0, lines, out_part, 0)

    def weights1(n, carry):
        span = pl.ds(pl.multiple_of(n * dstep, dstep), dstep)
        found = tn(n2[:, :, span].reshape(rows, dstep), gu[...].reshape(rows, hidden))
        wide[span, :] = found.astype(LOW)
        return carry

    lax.fori_loop(0, width // dstep, weights1, 0)
    for dev in range(devices):
        for chunk in range(chunks):
            at = (dev * chunks + chunk) * owned
            blocks1[dev, chunk] = wide[pl.ds(at, owned), :]
    keep_fc1 = pltpu.make_async_copy(blocks1, fc1_out, fc1_sem)
    keep_fc1.start()
    upstream = sum_back.total()
    sums_out[0:1] = jnp.sum(upstream * held[1], axis=0, keepdims=True)
    sums_out[1:2] = jnp.sum(upstream, axis=0, keepdims=True)
    grad_middle = cot[me].astype(F32) + normed_back(
        upstream, held[1], spread[:, :1], vectors[1:2]
    )
    middle_out[...] = grad_middle
    gb[me] = grad_middle.astype(LOW)
    all_gb.start()
    for other in sum_mlp.others():
        sum_mlp.pass_on(other)
    outs[me] = (held[0] + sum_mlp.total() + vectors[3:4]).astype(LOW)
    all_out.start()

    sums_out[2:3] = jnp.sum(cot[...].astype(F32).reshape(rows, width), axis=0, keepdims=True)
    for other in all_gb.others():
        all_gb.forward(other)
    all_gb.take(line)
    for other in all_gb.others():
        all_gb.take(other)
    whole = gb[...].reshape(rows, width)
    sums_out[3:4] = jnp.sum(whole.astype(F32), axis=0, keepdims=True)
    ga_out[...] = nt(proj_w[...], whole).astype(LOW)

    def weights0(n, carry):
        span = pl.ds(pl.multiple_of(n * dstep, dstep), dstep)
        found = tn(gb[:, :, span].reshape(rows, dstep), att_tok[...].reshape(rows, -1))
        wide[span, :local] = found.astype(LOW)
        return carry

    lax.fori_loop(0, width // dstep, weights0, 0)
    for dev in range(devices):
        proj_out[dev] = wide[pl.ds(dev * chunks * owned, chunks * owned), :local]
    moved[0].run(0)
    for other in all_out.others():
        all_out.forward(other)
    all_out.take(line)
    for other in all_out.others():
        all_out.take(other)
    output[...] = outs[...]
    moved[0].run(1)
    fc2_state[...] = moved[0].stages[1][0][...]
    for n, each in enumerate(moved[1:]):
        each.run(0)
        fc2_more[...] = each.stages[0][0][...]
    keep_fc1.wait()
    for each in (sum_branch, sum_mlp, sum_back, all_n2, all_gb, all_out, *moved):
        each.finish()


def middle_block(heads, att, proj_w, tokens, cot, fc1, fc2, vectors):
    count = lax.axis_size("tensor")
    lines = count // 2
    local, width = proj_w.shape
    rows = tokens.shape[0]
    share = rows // count
    hidden = fc1.shape[1]
    vmem = pl.BlockSpec(memory_space=pltpu.VMEM)
    hbm = pl.BlockSpec(memory_space=pl.ANY)
    dma = pltpu.SemaphoreType.DMA
    whole = (count, share, width)
    devices = lax.axis_size("dp")
    owned = width // devices
    chunks = 2 if owned % 32 == 0 else 1
    weights = (devices, chunks, owned // chunks, hidden)
    scratch = [
        pltpu.VMEM((width, hidden), LOW),
        pltpu.VMEM((hidden, width), LOW),
        pltpu.VMEM((count, share, local), LOW),
        pltpu.VMEM(whole, LOW),
        pltpu.VMEM(whole, LOW),
        pltpu.VMEM(whole, LOW),
        pltpu.VMEM(whole, LOW),
        pltpu.VMEM((count, share, hidden), LOW),
        pltpu.VMEM((count, share, hidden), LOW),
        pltpu.VMEM(whole, LOW),
        pltpu.VMEM(whole, LOW),
        pltpu.VMEM((2, share, width), F32),
        pltpu.VMEM((share, 128), F32),
        pltpu.VMEM((width, hidden), LOW),
        dma,
        dma,
    ]
    scratch += part_bufs(lines, share, width) * 3 + gather_sems(lines) * 3
    scratch += [pltpu.VMEM(weights, LOW), pltpu.VMEM(weights, LOW), dma]
    scratch += halve_bufs(owned // chunks, hidden, last=1)
    scratch += halve_bufs(owned // chunks, hidden, last=0) * (chunks - 1)
    return pl.pallas_call(
        functools.partial(middle_kernel, heads),
        out_shape=(
            jax.ShapeDtypeStruct(whole, LOW),
            jax.ShapeDtypeStruct((share, width), F32),
            jax.ShapeDtypeStruct(weights, LOW),
            jax.ShapeDtypeStruct((devices, owned, local), LOW),
            jax.ShapeDtypeStruct((local, rows), LOW),
            jax.ShapeDtypeStruct((1, hidden), F32),
            jax.ShapeDtypeStruct((8, width), F32),
            jax.ShapeDtypeStruct((devices // 4, owned // chunks, hidden), LOW),
            jax.ShapeDtypeStruct((devices // 2, owned // chunks, hidden), LOW),
        ),
        in_specs=[vmem] * 4 + [hbm] * 2 + [vmem],
        out_specs=(vmem,) * 2 + (hbm,) + (vmem,) * 6,
        scratch_shapes=scratch,
        compiler_params=pltpu.CompilerParams(
            collective_id=3, has_side_effects=True, vmem_limit_bytes=VMEM_LIMIT["middle"]
        ),
        name="middle",
    )(
        att, proj_w, tokens.reshape(whole), cot.reshape(whole), fc1, fc2, vectors,
    )


def small_bufs(heads, stages, shape):
    group, lines = lax.axis_size("dp") // heads, lax.axis_size("tensor") // 2
    dma = pltpu.SemaphoreType.DMA
    found = []
    for stage in stages:
        count = {"core": 2, "line": lines, "mate": group, "far": heads}[stage]
        found += [
            pltpu.VMEM(shape, F32), pltpu.VMEM((count,) + shape, F32), dma((count,)), dma((count,))
        ]
    return found


class Small:
    def __init__(self, ring, stages, merge, *bufs):
        self.ring, self.stages, self.merge = ring, stages, merge
        self.bufs = [bufs[4 * n : 4 * n + 4] for n in range(len(stages))]
        core, line, lines = tensor_place()
        self.peers = {
            "core": (core, [(1 - core, line * 2 + 1 - core)]),
            "line": (line, [(o, o * 2 + core) for o in [lax.rem(line + k, lines) for k in range(1, lines)]]),
            "mate": (ring.g, [(o, ring.z * ring.group + o) for o in ring.mates()]),
            "far": (ring.z, [(o, o * ring.group + ring.g) for o in ring.column()]),
        }

    def copy(self, n, slot, other, dev):
        value, held, send, recv = self.bufs[n]
        call = send_tensor if self.stages[n] in ("core", "line") else send_dp
        return call(value, held.at[slot], send.at[other], recv.at[slot], dev)

    def start(self, n, value):
        own, peers = self.peers[self.stages[n]]
        self.bufs[n][0][...] = value
        for other, dev in peers:
            self.copy(n, own, other, dev).start()

    def take(self, n):
        _, peers = self.peers[self.stages[n]]
        total = self.bufs[n][0][...]
        for other, dev in peers:
            self.copy(n, other, other, dev).wait_recv()
            total = self.merge(total, self.bufs[n][1][other])
        return total

    def step(self, n):
        self.start(n + 1, self.take(n))

    def finish(self):
        for n in range(len(self.stages)):
            own, peers = self.peers[self.stages[n]]
            for other, dev in peers:
                self.copy(n, own, other, dev).wait_send()


EVERY = ("core", "line", "mate", "far")
OVER_DP = ("mate", "far")


def add_peaks(a, b):
    row = lax.broadcasted_iota(jnp.int32, a.shape, 0)
    return jnp.where(row == 2, jnp.maximum(a, b), a + b)


def widen(row, width):
    if row.shape[1] == width:
        return row
    return jnp.concatenate([row, jnp.zeros((1, width - row.shape[1]), F32)], axis=1)


def tail_kernel(
    heads, grads, qkv_w, n1_t, tokens, grad_middle, vectors, tables, sums, fc1_bias, peak,
    proj_state, fc1_half, fc1_state,
    tokens_out, proj_out, fc1_out, qkv_out, tables_out, rows_out, clip_out,
    g_all, g_tok, part, gt, *rest,
):
    ring = Ring(heads)
    core, line, lines = tensor_place()
    me = lax.axis_index("tensor")
    count, share, width = tokens.shape
    rows = count * share
    local = heads * HEAD
    dstep = tile_of(width)
    devices, chunks, _, _ = n1_t.shape
    rest = list(rest)

    def taken(number):
        found, rest[:] = rest[:number], rest[number:]
        return found

    greet_all(ring)
    blocks = [taken(1)[0] for _ in range(chunks)]
    orders = [near_first(), far_first(ring.group)]
    moved3 = [Halve(orders[n], blocks[n], taken(3 * halve_bits())) for n in range(chunks)]
    moved0 = Halve(near_first(), proj_state, taken(3 * (halve_bits() - 1)), first=1)
    moved1 = []
    if chunks > 1:
        moved1 = [Halve(near_first(), fc1_state, taken(3 * (halve_bits() - 1)), first=1)]
    sum_part = Reduce(part, *taken(7))
    all_gt = Gather(gt, *taken(3))
    pool, pooled = taken(2)
    sum_pool = Reduce(pool, *taken(7))
    all_pool = Gather(pooled, *taken(3))
    small_pool = Small(ring, OVER_DP, lax.add, *taken(8))
    small_late = Small(ring, EVERY, lax.add, *taken(16))
    small_dp = Small(ring, OVER_DP, add_peaks, *taken(8))
    pool[...] = tables[...].reshape(pool.shape)
    for other in sum_pool.others() + [line]:
        sum_pool.give(other)
    for each in moved1:
        each.start()
    moved0.start()
    for t in range(3):
        for h in range(heads):
            g_all[pl.ds(t * local + h * HEAD, HEAD), :] = grads[h, t]
    g_tok[...] = g_all[...].T.reshape(g_tok.shape)
    for other in sum_pool.others():
        sum_pool.pass_on(other)
    whole = g_tok[...].reshape(rows, 3 * local)
    lane = lax.broadcasted_iota(jnp.int32, (1, width), 1)
    peaks = jnp.where(lane == ring.z, peak[0:1, 0:1], -jnp.inf)
    bias_sums = jnp.sum(whole.astype(F32), axis=0, keepdims=True)
    dp_rows = [widen(fc1_bias[...], width), widen(bias_sums, width), peaks]
    small_dp.start(0, jnp.concatenate(dp_rows + [jnp.zeros((5, width), F32)], axis=0))

    for n in range(chunks):

        def weight_part(dev, carry):
            found = nn(n1_t[dev, n], g_tok[...].reshape(rows, 3 * local))
            blocks[n][dev] = found.astype(LOW)
            return carry

        lax.fori_loop(0, devices, weight_part, 0)
        if n == 0:
            small_pool.start(0, sum_pool.total())
        if n == chunks - 1:
            small_pool.step(0)
            small_dp.step(0)
        moved3[n].start()

    def norm_part(k, carry):
        at = lax.rem(line + 1 + k, lines)
        pair = pl.ds(at * 2, 2)

        def tile(n, inner):
            span = pl.ds(pl.multiple_of(n * dstep, dstep), dstep)
            found = nn(g_tok[pair].reshape(2 * share, 3 * local), qkv_w[:, span])
            part[pair, :, span] = found.astype(LOW).reshape(2, share, dstep)
            return inner

        lax.fori_loop(0, width // dstep, tile, 0)
        sum_part.give(at)
        return carry

    lax.fori_loop(0, lines, norm_part, 0)
    for other in sum_part.others():
        sum_part.pass_on(other)
    scaled, inverse = normed(tokens[me].astype(F32))
    moved0.run(1)
    for each in moved1:
        each.run(1)
    upstream = sum_part.total()
    late = [
        sums[0:4],
        jnp.sum(upstream * scaled, axis=0, keepdims=True),
        jnp.sum(upstream, axis=0, keepdims=True),
        jnp.zeros((2, width), F32),
    ]
    small_late.start(0, jnp.concatenate(late, axis=0))
    found = grad_middle[...] + normed_back(upstream, scaled, inverse, vectors[4:5])
    gt[me] = found.astype(LOW)
    all_gt.start()
    pooled[me] = small_pool.take(1)
    all_pool.start()
    moved3[0].run(0)
    small_late.step(0)
    for each in moved3[1:]:
        each.run(0)
    small_late.step(1)
    for other in all_gt.others():
        all_gt.forward(other)
    for other in all_pool.others():
        all_pool.forward(other)
    dp_sum = small_dp.take(1)
    limit = vectors[9:10]
    factors = jnp.sqrt(limit / jnp.maximum(dp_sum[2:3], limit))
    lane = lax.broadcasted_iota(jnp.int32, (1, width), 1)
    clipped_bias = vectors[7:8]
    for h in range(heads):
        factor = factors[:, h : h + 1]
        own = (lane >= h * HEAD) & (lane < (h + 1) * HEAD)
        clipped_bias = jnp.where(own, clipped_bias * factor, clipped_bias)
        for t in range(2):
            span = pl.ds(t * local + h * HEAD, HEAD)
            clip_out[span, :] = (qkv_w[span, :].astype(F32) * factor).astype(LOW)
    rows_out[8:11] = dp_sum[0:3]
    rows_out[11:12] = factors
    rows_out[12:13] = clipped_bias
    rows_out[13:16] = jnp.zeros((3, width), F32)
    moved3[0].run(1)
    small_late.step(2)
    for each in moved3[1:]:
        each.run(1)
    for stage in range(2, halve_bits() - 1):
        for each in moved3 + [moved0] + moved1:
            each.run(stage)
    for other in all_gt.others() + [line]:
        all_gt.take(other)
    for other in all_pool.others() + [line]:
        all_pool.take(other)
    tokens_out[...] = gt[...]
    for n in range(2):
        turned_sums = pooled[...].reshape(2, 2 * SIDE, 128)[n].T[:HEAD]
        found = jnp.zeros((HEAD, 2 * SIDE), F32)
        for piece in parts_of(turned_sums, 3):
            found = found + nn(piece.astype(LOW), turned(2 * SIDE))
        tables_out[n] = found
    late = small_late.take(3)
    row = lax.broadcasted_iota(jnp.int32, late.shape, 0)
    rows_out[0:8] = jnp.where((row == 2) | (row == 3), late * (1.0 / count), late)
    owned = fc1_half.shape[0]
    fc1_out[0:owned] = fc1_half[...]
    for each in moved1:
        fc1_out[pl.ds(owned, owned), :] = each.total()
    proj_out[...] = moved0.total()
    for n, each in enumerate(moved3):
        total = each.total()
        owned = total.shape[0]
        for t in range(3):
            qkv_out[t, pl.ds(n * owned, owned), :] = total[:, t * local : (t + 1) * local]
    for each in [
        moved0, sum_part, all_gt, sum_pool, all_pool, small_pool, small_late, small_dp,
    ] + moved3 + moved1:

        each.finish()


def tail(heads, grads, qkv_w, n1_t, tokens, grad_middle, vectors, tables, sums, fc1_bias, peak, proj_state, fc1_half, fc1_state):
    hidden = fc1_half.shape[1]
    count = lax.axis_size("tensor")
    lines = count // 2
    local = heads * HEAD
    devices, chunks, owned, rows = n1_t.shape
    width = devices * chunks * owned
    share = rows // count
    vmem = pl.BlockSpec(memory_space=pltpu.VMEM)
    whole = (count, share, width)
    scratch = [
        pltpu.VMEM((3 * local, rows), LOW),
        pltpu.VMEM((count, share, 3 * local), LOW),
        pltpu.VMEM(whole, LOW),
        pltpu.VMEM(whole, LOW),
    ]
    scratch += [pltpu.VMEM((devices, owned, 3 * local), LOW)] * chunks
    scratch += halve_bufs(owned, 3 * local) * chunks
    scratch += halve_bufs(chunks * owned, local, first=1)
    if chunks > 1:
        scratch += halve_bufs(owned, hidden, first=1)
    scratch += part_bufs(lines, share, width) + gather_sems(lines)
    pool = (count, 4 * SIDE // count, 128)
    scratch += [pltpu.VMEM(pool, F32)] * 2
    scratch += part_bufs(lines, *pool[1:], F32) + gather_sems(lines)
    scratch += small_bufs(heads, OVER_DP, pool[1:])
    scratch += small_bufs(heads, EVERY, (8, width))
    scratch += small_bufs(heads, OVER_DP, (8, width))
    return pl.pallas_call(
        functools.partial(tail_kernel, heads),
        out_shape=(
            jax.ShapeDtypeStruct(whole, LOW),
            jax.ShapeDtypeStruct((chunks * owned, local), F32),
            jax.ShapeDtypeStruct((chunks * owned, hidden), F32),
            jax.ShapeDtypeStruct((3, chunks * owned, local), F32),
            jax.ShapeDtypeStruct((2, HEAD, 2 * SIDE), F32),
            jax.ShapeDtypeStruct((16, width), F32),
            jax.ShapeDtypeStruct((2 * local, width), LOW),
        ),
        in_specs=[vmem] * 13,
        out_specs=(vmem,) * 7,
        scratch_shapes=scratch,
        compiler_params=pltpu.CompilerParams(
            collective_id=4, has_side_effects=True, vmem_limit_bytes=VMEM_LIMIT["tail"]
        ),
        name="tail",
    )(
        grads, qkv_w, n1_t, tokens.reshape(whole), grad_middle, vectors, tables, sums, fc1_bias,
        peak, proj_state, fc1_half, fc1_state,
    )


def finish_kernel(count, *refs):
    large, (rows, tables), refs = refs[:count], refs[count : count + 2], refs[count + 2 :]
    outs, smalls, stage = refs[:count], refs[count : count + 13], refs[count + 13 :]
    sems_in, sems_out = stage[count], stage[count + 1]
    into = [pltpu.make_async_copy(a, b, sems_in.at[n]) for n, (a, b) in enumerate(zip(large, stage))]
    out = [pltpu.make_async_copy(b, c, sems_out.at[n]) for n, (b, c) in enumerate(zip(stage, outs))]
    for copy in into:
        copy.start()
    gain1, shift1, qv, proj, by_row, by_col, gain2, shift2, fc1, fc2, clip_bias, peaks, factors = smalls
    picks = (
        (gain2, 0), (shift2, 1), (fc2, 2), (proj, 3), (gain1, 4), (shift1, 5), (fc1, 8),
        (peaks, 10), (factors, 11), (clip_bias, 12),
    )
    for ref, at in picks:
        ref[...] = rows[at : at + 1, : ref.shape[0]].reshape(ref.shape)
    local = qv.shape[1]
    qv[0:1] = rows[9:10, :local]
    qv[1:2] = rows[9:10, 2 * local : 3 * local]
    by_row[...] = tables[0, :, : by_row.shape[1]]
    by_col[...] = tables[1, :, : by_col.shape[1]]
    for copy, after in zip(into, out):
        copy.wait()
        after.start()
    for copy in out:
        copy.wait()


def finish(large, rows, tables, hidden, local):
    width = rows.shape[1]
    heads = local // HEAD
    vmem = pl.BlockSpec(memory_space=pltpu.VMEM)
    hbm = pl.BlockSpec(memory_space=pl.ANY)
    count = len(large)
    shapes = [
        (width,), (width,), (2, local), (width,), (HEAD, 2 * SIDE - 1), (HEAD, 2 * SIDE - 1),
        (width,), (width,), (hidden,), (width,), (local,), (heads,), (heads,),
    ]
    return pl.pallas_call(
        functools.partial(finish_kernel, count),
        out_shape=[jax.ShapeDtypeStruct(each.shape, each.dtype) for each in large]
        + [jax.ShapeDtypeStruct(each, F32) for each in shapes],
        in_specs=[hbm] * count + [vmem] * 2,
        out_specs=[hbm] * count + [vmem] * len(shapes),
        scratch_shapes=[pltpu.VMEM(each.shape, each.dtype) for each in large]
        + [pltpu.SemaphoreType.DMA((count,))] * 2,
        compiler_params=pltpu.CompilerParams(vmem_limit_bytes=VMEM_LIMIT["finish"]),
        name="finish",
    )(*large, rows, tables)


def on_device(
    tokens,
    cotangent,
    norm1_gain,
    norm1_shift,
    qkv_weight,
    qv_bias,
    proj_weight,
    proj_bias,
    table_rows,
    table_cols,
    norm2_gain,
    norm2_shift,
    fc1_weight,
    fc1_bias,
    fc2_weight,
    fc2_bias,
    threshold,
):
    images, row_count, model_width = tokens.shape
    token_count = images * row_count
    local_width = qkv_weight.shape[2]
    local_heads = local_width // HEAD
    shape = Shape(local_heads, lax.axis_size("dp") // local_heads, row_count)
    flat = tokens.reshape(token_count, model_width)

    listed = (
        proj_bias, norm2_gain, norm2_shift, fc2_bias, norm1_gain, norm1_shift, fc1_bias, qv_bias,
        threshold,
    )
    weights = qkv_weight.transpose(1, 2, 0).reshape(3 * local_width, model_width)
    attended, qaug, bias_rows, kv, o_rows, lse, peak, normed1, tables, vectors = attend(
        shape, flat, weights, listed, table_rows.T, table_cols.T
    )
    (
        output,
        grad_middle,
        grad_fc1,
        grad_proj,
        grad_attended,
        grad_fc1_bias,
        sums,
        fc2_state,
        fc2_more,
    ) = middle_block(
        local_heads,
        attended.reshape(local_width, token_count),
        proj_weight,
        flat,
        cotangent.reshape(token_count, model_width),
        fc1_weight,
        fc2_weight,
        vectors,
    )
    grad_heads = grad_attended.reshape(local_heads, HEAD, row_count)
    devices, chunks, owned, _ = grad_fc1.shape
    grad_triple, table_terms, fc1_half, grad_fc2, fc1_state, proj_state = attend_back(
        shape, grad_heads, tables, qaug, bias_rows, kv, o_rows, lse, fc2_state, fc2_more, grad_fc1,
        grad_proj,
    )
    grad_tokens, grad_proj, grad_fc1, grad_qkv, table_sums, rows, clipped = tail(
        local_heads,
        grad_triple,
        weights,
        normed1.reshape(devices, chunks, owned, token_count),
        flat,
        grad_middle,
        vectors,
        table_terms,
        sums,
        grad_fc1_bias,
        peak,
        proj_state,
        fc1_half,
        fc1_state,
    )
    large = (output, grad_tokens, grad_fc1, grad_fc2, grad_qkv, clipped, grad_proj)
    (
        output,
        grad_tokens,
        grad_fc1,
        grad_fc2,
        grad_qkv,
        clipped,
        grad_proj,
        grad_norm1_gain,
        grad_norm1_shift,
        grad_qv_bias,
        grad_proj_bias,
        grad_rows_t,
        grad_cols_t,
        grad_norm2_gain,
        grad_norm2_shift,
        grad_fc1_bias,
        grad_fc2_bias,
        clipped_q_bias,
        head_peaks,
        clip_factors,
    ) = finish(large, rows, table_sums, fc1_bias.shape[0], local_width)
    output = output.reshape(images, row_count, model_width)
    grad_tokens = grad_tokens.reshape(images, row_count, model_width)
    grad_qkv = grad_qkv.transpose(1, 0, 2)
    grad_fc2, grad_proj = grad_fc2.T, grad_proj.T
    grad_table_rows, grad_table_cols = grad_rows_t.T, grad_cols_t.T
    clipped_qk = clipped.reshape(2, local_width, model_width).transpose(2, 0, 1)
    return (
        output,
        grad_tokens,
        grad_norm1_gain,
        grad_norm1_shift,
        grad_qkv,
        grad_qv_bias,
        grad_proj,
        grad_proj_bias,
        grad_table_rows,
        grad_table_cols,
        grad_norm2_gain,
        grad_norm2_shift,
        grad_fc1,
        grad_fc1_bias,
        grad_fc2,
        grad_fc2_bias,
        clipped_qk,
        clipped_q_bias,
        head_peaks,
        clip_factors,
    )


def solution(mesh):
    in_specs = (
        P(None, "dp", None),
        P(None, "dp", None),
        P(),
        P(),
        P(None, None, "tensor"),
        P(None, "tensor"),
        P("tensor", None),
        P(),
        P(),
        P(),
        P(),
        P(),
        P(None, "tensor"),
        P("tensor"),
        P("tensor", None),
        P(),
        P(),
    )
    out_specs = (
        P(None, "dp", None),
        P(None, "dp", None),
        P(),
        P(),
        P("dp", None, "tensor"),
        P(None, "tensor"),
        P("tensor", "dp"),
        P(),
        P(),
        P(),
        P(),
        P(),
        P("dp", "tensor"),
        P("tensor"),
        P("tensor", "dp"),
        P(),
        P(None, None, "tensor"),
        P("tensor"),
        P("tensor"),
        P("tensor"),
    )
    return jax.shard_map(
        on_device, mesh=mesh, in_specs=in_specs, out_specs=out_specs, check_vma=False
    )
```

```python
import functools
import math

import jax
import jax.numpy as jnp
from jax import lax
from jax.experimental import pallas as pl
from jax.experimental.pallas import tpu as pltpu
from jax.sharding import PartitionSpec as P

HEAD = 80
SIDE = 64

MESH = pl.DeviceIdType.MESH
LOW = jnp.bfloat16
F32 = jnp.float32
EPSILON = 1e-06
SCALE = HEAD**-0.5
EXP2_SCALE = SCALE * math.log2(math.e)
COLS_AT = HEAD
ROWS_AT = COLS_AT + 2 * SIDE
LSE_AT = ROWS_AT + 16
AUG = LSE_AT + 16
VMEM_LIMIT = {
    "attend": 60 * 2**20,
    "middle": 40 * 2**20,
    "attend_back": 24 * 2**20,
    "tail": 24 * 2**20,
    "finish": 12 * 2**20,
}


def nn(a, b):
    return lax.dot_general(a, b, (((1,), (0,)), ((), ())), preferred_element_type=F32)


def tn(a, b):
    return lax.dot_general(a, b, (((0,), (0,)), ((), ())), preferred_element_type=F32)


def nt(a, b):
    return lax.dot_general(a, b, (((1,), (1,)), ((), ())), preferred_element_type=F32)


def parts_of(values, count):
    pieces = []
    for _ in range(count):
        piece = values.astype(LOW).astype(F32)
        pieces.append(piece)
        values = values - piece
    return pieces


def send_dp(src, dst, send_sem, recv_sem, dev):
    return pltpu.make_async_remote_copy(
        src_ref=src,
        dst_ref=dst,
        send_sem=send_sem,
        recv_sem=recv_sem,
        device_id={"dp": dev},
        device_id_type=MESH,
    )


def paired(place, k, count):
    found, bit = 0, 1
    while bit < count:
        found = found + bit * lax.rem(place // bit + k // bit, 2)
        bit *= 2
    return found


def turned(count):
    row = lax.broadcasted_iota(jnp.int32, (count, count), 0)
    column = lax.broadcasted_iota(jnp.int32, (count, count), 1)
    return jnp.where(row + column == count - 2, 1.0, 0.0).astype(LOW)


def shifts(rows, dev):
    spot = lax.broadcasted_iota(jnp.int32, (2 * SIDE, rows), 1)
    by_row = SIDE - 1 - (dev * (rows // SIDE) + lax.shift_right_logical(spot, 6))
    by_col = SIDE - 1 - (spot & (SIDE - 1))
    return by_row, by_col


def skew(values, shift):
    for bit in (32, 16, 8, 4, 2, 1):
        moved = pltpu.roll(values, 2 * SIDE - bit, 0)
        values = jnp.where((shift & bit) != 0, moved, values)
    return values[:SIDE]


def unskew(values, shift):
    values = jnp.concatenate([values, jnp.zeros_like(values)], axis=0)
    for bit in (32, 16, 8, 4, 2, 1):
        moved = pltpu.roll(values, bit, 0)
        values = jnp.where((shift & bit) != 0, moved, values)
    return values


def greet(peers):
    barrier = pltpu.get_barrier_semaphore()
    for peer in peers:
        pl.semaphore_signal(barrier, inc=1, device_id={"dp": peer}, device_id_type=MESH)
    pl.semaphore_wait(barrier, len(peers))


def key_onehots(rows, dev):
    spot = lax.broadcasted_iota(jnp.int32, (2 * SIDE, rows), 1)
    index = lax.broadcasted_iota(jnp.int32, (2 * SIDE, rows), 0)
    cols = jnp.where((index & (SIDE - 1)) == (spot & (SIDE - 1)), 1.0, 0.0)
    spot, index = spot[:16], index[:16]
    offset = lax.rem(dev * (rows // SIDE), 8)
    in_group = jnp.where((index & 7) == offset + lax.shift_right_logical(spot, 6), 1.0, 0.0)
    return cols, in_group


class Shape:
    def __init__(self, heads, group, rows):
        self.heads, self.group, self.rows = heads, group, rows
        self.queries = heads * rows
        self.block = min(1024, self.queries)


def forward_kernel(shape, count, outs, *refs):
    held = refs[count + outs : 2 * count + outs]
    load = refs[2 * count + outs]
    copies = [
        pltpu.make_async_copy(a, b, load.at[n]) for n, (a, b) in enumerate(zip(refs[:count], held))
    ]
    for copy in copies[2:] + copies[:2]:
        copy.start()
    forward_body(
        shape, copies, *held, *refs[count : count + outs], *refs[2 * count + outs + 1 :]
    )


def forward_body(
    shape, copies, tokens, weights, proj_bias, gain2, shift2, fc2_bias, gain1, shift1, fc1_bias,
    qv_bias, threshold, rows_t, cols_t,
    att, qaug, bias_rows, kv_out, o_out, lse_out, peak_out, n1_out, tables, vectors,
    n1, qkv, wide_t, rq, rkv, kaug_t, kaug, vaug, oacc, mrow, lpk, att_s, att_r,
    q_send, q_recv, k_send, k_recv, x_send, x_recv, r_send, r_recv, o_sem,
):
    heads, group, rows, block = shape.heads, shape.group, shape.rows, shape.block
    local = heads * HEAD
    me = lax.axis_index("dp")
    z, g = me // group, lax.rem(me, group)
    column = [paired(z, k, heads) for k in range(1, heads)]
    mates = [lax.rem(g + k, group) for k in range(1, group)]
    greet([h * group + g for h in column] + [z * group + o for o in mates])
    width = tokens.shape[1]
    vectors[...] = jnp.zeros_like(vectors)
    for copy in copies[2:] + copies[:1]:
        copy.wait()
    listed = (proj_bias, gain2, shift2, fc2_bias, gain1, shift1, fc1_bias)
    for n, each in enumerate(listed):
        vectors[n : n + 1, : each.shape[0]] = each[...].reshape(1, each.shape[0])
    vectors[7:9, :local] = qv_bias[...]
    vectors[9:10] = jnp.broadcast_to(threshold[...].reshape(1, 1), (1, width))
    scaled, _ = normed(tokens[...].astype(F32))
    n1[...] = (scaled * vectors[4:5] + vectors[5:6]).astype(LOW)
    biases = vectors[7:9].astype(F32)
    biases = jnp.concatenate([biases, jnp.zeros((6, biases.shape[1]), F32)], axis=0).T

    def project(t):
        found = nt(weights[pl.ds(t * local, local), :], n1[...])
        if t != 1:
            found = found + biases[:local, t // 2 : t // 2 + 1]
        qkv[t] = found.astype(LOW)

    sends = []
    copies[1].wait()
    project(0)
    for h in column:
        mine = pl.ds(pl.multiple_of(h * HEAD, 16), HEAD)
        copy = send_dp(qkv.at[0, mine], rq.at[z], q_send.at[h], q_recv.at[z], h * group + g)
        copy.start()
        sends.append(copy)
    project(1)
    project(2)
    for h in column:
        mine = pl.ds(pl.multiple_of(h * HEAD, 16), HEAD)
        copy = send_dp(
            qkv.at[pl.ds(1, 2), mine], rkv.at[z, g], k_send.at[h], k_recv.at[z], h * group + g
        )
        copy.start()
        sends.append(copy)
    mine = pl.ds(pl.multiple_of(z * HEAD, 16), HEAD)
    rq[z] = qkv[0, mine]
    rkv[z, g] = qkv[pl.ds(1, 2), mine]
    for n, mate in enumerate(mates):
        send_dp(
            rkv.at[z, g], rkv.at[z, g], x_send.at[z, n], x_recv.at[z, g], z * group + mate
        ).start()
    n1_t = n1[...].T
    pieces, devices, piece, _ = n1_out.shape
    for dev in range(devices):
        for at in range(pieces):
            start = (dev * pieces + at) * piece
            n1_out[at, dev] = n1_t[start : start + piece]
    wide_t[...] = jnp.zeros_like(wide_t)
    for n, held in enumerate((rows_t, cols_t)):
        wide_t[n, :HEAD, : held.shape[1]] = held[...]
        tables[n] = nn(wide_t[n], turned(2 * SIDE)).T[:, :HEAD].astype(LOW)
    qaug[pl.ds(LSE_AT, 16), :] = jnp.zeros((16, shape.queries), LOW)
    kaug_t[pl.ds(LSE_AT, 16), :] = jnp.zeros((16, rows), LOW)
    vaug[pl.ds(HEAD, 16), :] = jnp.where(
        lax.broadcasted_iota(jnp.int32, (16, rows), 0) == 0, 1.0, 0.0
    ).astype(LOW)
    oacc[...] = jnp.zeros_like(oacc)
    mrow[...] = jnp.full_like(mrow, -jnp.inf)
    lpk[...] = jnp.full_like(lpk, -jnp.inf)

    def prepare(k, carry):
        source = paired(z, k, heads)
        span = pl.ds(pl.multiple_of(source * rows, rows), rows)

        @pl.when(k > 0)
        def _():
            send_dp(rq.at[source], rq.at[source], q_send.at[source], q_recv.at[source], me).wait_recv()

        query = rq[source]
        by_row, by_col = shifts(rows, source * group + g)
        along_rows = skew(nn(tables[0], query) * (1.0 / SCALE), by_row)
        along_cols = skew(nn(tables[1], query) * (1.0 / SCALE), by_col)
        qaug[pl.ds(0, HEAD), span] = query
        cols = parts_of(along_cols, 2)
        qaug[pl.ds(COLS_AT, 2 * SIDE), span] = jnp.concatenate(cols, axis=0).astype(LOW)
        high, rest = parts_of(along_rows, 2)
        for at in range(SIDE // 8):
            pair = jnp.concatenate([high[8 * at : 8 * at + 8], rest[8 * at : 8 * at + 8]], axis=0)
            bias_rows[at, :, span] = pair.astype(LOW)
        return carry

    lax.fori_loop(0, heads, prepare, 0)

    def chunk(source, mate):
        dev = source * group + mate
        cols, in_group = key_onehots(rows, dev)
        kaug_t[pl.ds(0, HEAD), :] = rkv[source, mate, 0]
        kaug_t[pl.ds(COLS_AT, 2 * SIDE), :] = cols.astype(LOW)
        kaug_t[pl.ds(ROWS_AT, 16), :] = in_group.astype(LOW)
        kaug[...] = kaug_t[...].T
        vaug[pl.ds(0, HEAD), :] = rkv[source, mate, 1]
        qaug[pl.ds(ROWS_AT, 16), :] = bias_rows[(dev * (rows // SIDE)) // 8]

        def one(i, carry):
            span = pl.ds(pl.multiple_of(i * block, block), block)
            logits = nn(kaug[:, :HEAD], qaug[pl.ds(0, HEAD), span])
            lpk[...] = jnp.maximum(lpk[...], jnp.max(logits.reshape(rows // 8, 8, block), axis=0))
            scores = nn(kaug[...], qaug[:, span])
            before = mrow[:, span]
            top = jnp.maximum(before, jnp.max(scores, axis=0, keepdims=True))
            mrow[:, span] = top
            weights = jnp.exp2(scores * EXP2_SCALE - top * EXP2_SCALE).astype(LOW)
            keep = jnp.exp2((before - top) * EXP2_SCALE)
            oacc[:, span] = oacc[:, span] * keep + nn(vaug[...], weights)
            return carry

        lax.fori_loop(0, shape.queries // block, one, 0)

    def column_step(k, carry):
        source = paired(z, k, heads)

        @pl.when(k > 0)
        def _():
            send_dp(rkv.at[source, g], rkv.at[source, g], k_send.at[source], k_recv.at[source], me).wait_recv()
            for n, mate in enumerate(mates):
                send_dp(
                    rkv.at[source, g], rkv.at[source, g], x_send.at[source, n], x_recv.at[source, g],
                    z * group + mate,
                ).start()

        chunk(source, g)

        def mate_step(n, inner):
            mate = lax.rem(g + n, group)
            send_dp(
                rkv.at[source, mate], rkv.at[source, mate], x_send.at[source, 0], x_recv.at[source, mate], me
            ).wait_recv()
            chunk(source, mate)
            return inner

        lax.fori_loop(1, group, mate_step, 0)
        return carry

    lax.fori_loop(0, heads, column_step, 0)
    keep_kv = pltpu.make_async_copy(rkv, kv_out, o_sem)
    keep_kv.start()

    def finish(k, carry):
        source = paired(z, lax.rem(k, heads), heads)
        span = pl.ds(pl.multiple_of(source * rows, rows), rows)
        total = oacc[pl.ds(HEAD, 1), span]
        attended = oacc[pl.ds(0, HEAD), span] / total
        o_out[:, span] = attended
        lse_out[:, span] = mrow[:, span] + jnp.log2(total) * (1.0 / EXP2_SCALE)
        att_s[source] = attended.astype(LOW)

        @pl.when(source != z)
        def _():
            send_dp(
                att_s.at[source], att_r.at[z], r_send.at[source], r_recv.at[z], source * group + g
            ).start()

        return carry

    lax.fori_loop(1, heads + 1, finish, 0)
    att[z] = att_s[z]
    peak_out[...] = jnp.full(peak_out.shape, jnp.max(lpk[...]) * SCALE, F32)
    for h in column:
        send_dp(att_s.at[h], att_r.at[h], r_send.at[h], r_recv.at[h], h * group + g).wait()
        att[h] = att_r[h]
    for copy in sends:
        copy.wait_send()
    for source in range(heads):
        for n, mate in enumerate(mates):
            send_dp(
                rkv.at[source, g], rkv.at[source, g], x_send.at[source, n], x_recv.at[source, g],
                z * group + mate,
            ).wait_send()
    keep_kv.wait()


def attend(shape, tokens, weights, listed, rows_t, cols_t):
    heads, group, rows, queries = shape.heads, shape.group, shape.rows, shape.queries
    width, local = tokens.shape[1], heads * HEAD
    args = (tokens, weights, *listed, rows_t, cols_t)
    devices = heads * group
    owned = width // devices
    piece = 32 if owned % 32 == 0 else owned
    vmem = pl.BlockSpec(memory_space=pltpu.VMEM)
    hbm = pl.BlockSpec(memory_space=pl.ANY)
    dma = pltpu.SemaphoreType.DMA
    return pl.pallas_call(
        functools.partial(forward_kernel, shape, len(args), 10),
        out_shape=(
            jax.ShapeDtypeStruct((heads, HEAD, rows), LOW),
            jax.ShapeDtypeStruct((AUG, queries), LOW),
            jax.ShapeDtypeStruct((SIDE // 8, 16, queries), LOW),
            jax.ShapeDtypeStruct((heads, group, 2, HEAD, rows), LOW),
            jax.ShapeDtypeStruct((HEAD, queries), F32),
            jax.ShapeDtypeStruct((1, queries), F32),
            jax.ShapeDtypeStruct((8, 128), F32),
            jax.ShapeDtypeStruct((owned // piece, devices, piece, rows), LOW),
            jax.ShapeDtypeStruct((2, 2 * SIDE, HEAD), LOW),
            jax.ShapeDtypeStruct((16, width), F32),
        ),
        in_specs=[pl.BlockSpec(memory_space=pltpu.HBM)] * len(args),
        out_specs=(vmem, vmem, vmem, hbm, vmem, vmem, vmem, vmem, vmem, vmem),
        scratch_shapes=[
            *[pltpu.VMEM(each.shape, each.dtype) for each in args],
            dma((len(args),)),
            pltpu.VMEM((rows, width), LOW),
            pltpu.VMEM((3, local, rows), LOW),
            pltpu.VMEM((2, 128, 2 * SIDE), LOW),
            pltpu.VMEM((heads, HEAD, rows), LOW),
            pltpu.VMEM((heads, group, 2, HEAD, rows), LOW),
            pltpu.VMEM((AUG, rows), LOW),
            pltpu.VMEM((rows, AUG), LOW),
            pltpu.VMEM((HEAD + 16, rows), LOW),
            pltpu.VMEM((HEAD + 16, queries), F32),
            pltpu.VMEM((1, queries), F32),
            pltpu.VMEM((8, shape.block), F32),
            pltpu.VMEM((heads, HEAD, rows), LOW),
            pltpu.VMEM((heads, HEAD, rows), LOW),
            dma((heads,)), dma((heads,)), dma((heads,)), dma((heads,)),
            dma((heads, group)), dma((heads, group)), dma((heads,)), dma((heads,)),
            dma,
        ],
        compiler_params=pltpu.CompilerParams(
            collective_id=1, has_side_effects=True, vmem_limit_bytes=VMEM_LIMIT["attend"]
        ),
        name="attend",
    )(*args)


def backward_kernel(
    shape, ga, tables, qaug_in, bias_rows, rkv, o_in, lse_in, fc2_state, fc1, mlp, values, vectors, proj,
    grads, table_grads, fc1_out, fc2_out, fc1_state, output, proj_state,
    rdo, qaug, q_tok, do_aug, do_tok, kaug_t, kaug, vaug_t, vaug, kacc, vacc, dq, drow, dcol,
    part, xr, summed, gq_s, gq_r, gkv_r,
    d_send, d_recv, x_send, x_recv, kv_send, kv_recv, q_send, q_recv, *rest,
):
    chunks = fc1.shape[1]
    rest = list(rest)

    def taken(number):
        found, rest[:] = rest[:number], rest[number:]
        return found

    whole_bufs = 2 + 3 * halve_bits()
    bits = halve_bits()
    orders = [near_first(), far_first(shape.group)]
    moved2 = [
        Halve(orders[n], fc2_state.at[n], taken(3 * (bits - 2)), first=2) for n in range(chunks)
    ]
    moved0 = Halve(far_first(shape.group), proj, taken(3), last=0)
    outs = taken(1)[0]
    lines = lax.axis_size("tensor") // 2
    sum_mlp = Reduce(mlp, *taken(7))
    all_out = Gather(outs, *taken(3))
    line = tensor_place()[1]
    moved1 = [Halve(near_first(), fc1.at[:, 0], taken(whole_bufs), own=True)]
    if chunks > 1:
        moved1 += [Halve(near_first(), fc1.at[:, 1], taken(5), last=0, own=True)]
    heads, group, rows, block = shape.heads, shape.group, shape.rows, shape.block
    queries = shape.queries
    me = lax.axis_index("dp")
    z, g = me // group, lax.rem(me, group)
    column = [paired(z, k, heads) for k in range(1, heads)]
    mates = [lax.rem(g + k, group) for k in range(1, group)]
    greet_all(Ring(heads))
    for other in sum_mlp.others() + [line]:
        sum_mlp.give(other)
    sends = []
    for h in column:
        copy = send_dp(ga.at[h], rdo.at[z], d_send.at[h], d_recv.at[z], h * group + g)
        copy.start()
        sends.append(copy)
    moved1[0].start()
    for each in moved2:
        each.start()
    for each in moved1:
        each.load()
    rdo[z] = ga[z]
    qaug[...] = qaug_in[...]
    ones = jnp.where(lax.broadcasted_iota(jnp.int32, (16, rows), 0) < 3, 1.0, 0.0).astype(LOW)
    kaug_t[pl.ds(LSE_AT, 16), :] = ones
    vaug_t[pl.ds(HEAD, 16), :] = ones
    vaug_t[pl.ds(HEAD + 16, 32), :] = jnp.zeros((32, rows), LOW)
    low_lse = parts_of(-lse_in[...], 3)
    qaug[pl.ds(LSE_AT, 16), :] = jnp.concatenate(
        low_lse + [jnp.zeros((13, queries), F32)], axis=0
    ).astype(LOW)
    dq[...] = jnp.zeros_like(dq)
    dcol[...] = jnp.zeros_like(dcol)
    drow[...] = jnp.zeros_like(drow)

    def prepare(k, carry):
        source = paired(z, k, heads)
        span = pl.ds(pl.multiple_of(source * rows, rows), rows)

        @pl.when(k > 0)
        def _():
            send_dp(rdo.at[source], rdo.at[source], d_send.at[source], d_recv.at[source], me).wait_recv()

        upstream = rdo[source]
        dots = jnp.sum(upstream.astype(F32) * o_in[:, span], axis=0, keepdims=True)
        low_dots = parts_of(-dots, 3)
        do_aug[pl.ds(0, HEAD), span] = upstream
        do_aug[pl.ds(HEAD, 16), span] = jnp.concatenate(
            low_dots + [jnp.zeros((13, rows), F32)], axis=0
        ).astype(LOW)
        do_aug[pl.ds(HEAD + 16, 32), span] = jnp.zeros((32, rows), LOW)
        do_tok[span, :] = do_aug[:, span].T
        q_tok[span, :] = qaug[pl.ds(0, 128), span].T
        return carry

    lax.fori_loop(0, heads, prepare, 0)
    for other in sum_mlp.others():
        sum_mlp.pass_on(other)
    moved0.start()

    def chunk(source, mate):
        dev = source * group + mate
        at = (dev * (rows // SIDE)) // 8
        cols, in_group = key_onehots(rows, dev)
        kaug_t[pl.ds(0, HEAD), :] = rkv[source, mate, 0]
        kaug_t[pl.ds(COLS_AT, 2 * SIDE), :] = cols.astype(LOW)
        kaug_t[pl.ds(ROWS_AT, 16), :] = in_group.astype(LOW)
        kaug[...] = kaug_t[...].T
        vaug_t[pl.ds(0, HEAD), :] = rkv[source, mate, 1]
        vaug[...] = vaug_t[...].T
        qaug[pl.ds(ROWS_AT, 16), :] = bias_rows[at]
        kacc[...] = jnp.zeros_like(kacc)
        vacc[...] = jnp.zeros_like(vacc)
        back = jnp.concatenate(
            [kaug_t[pl.ds(0, COLS_AT + SIDE), :], kaug_t[pl.ds(ROWS_AT, 16), :]], axis=0
        )

        def one(i, carry):
            span = pl.ds(pl.multiple_of(i * block, block), block)
            probs = jnp.exp2(nn(kaug[...], qaug[:, span]) * EXP2_SCALE)
            pulled = nn(vaug[...], do_aug[:, span])
            low_grads = (probs * pulled).astype(LOW)
            vacc[...] += nn(probs.astype(LOW), do_tok[span, :])
            kacc[...] += nn(low_grads, q_tok[span, :])
            found = nn(back, low_grads)
            dq[:, span] += found[:HEAD]
            dcol[:, span] += found[COLS_AT : COLS_AT + SIDE]
            drow[at, :, span] += found[COLS_AT + SIDE : COLS_AT + SIDE + 8]
            return carry

        lax.fori_loop(0, queries // block, one, 0)

    def put(where, extra):
        key_part = (kacc[...] * SCALE).T[:HEAD]
        value_part = vacc[...].T[:HEAD]
        for other in extra:
            key_part = key_part + other[0].astype(F32)
            value_part = value_part + other[1].astype(F32)
        where[0] = key_part.astype(LOW)
        where[1] = value_part.astype(LOW)

    def mate_copy(source, mate):
        return send_dp(
            part.at[source, mate], xr.at[source, g], x_send.at[source, mate], x_recv.at[source, g],
            z * group + mate,
        )

    def mates_step(k, carry):
        source = paired(z, lax.rem(k, heads), heads)

        def mate_step(n, inner):
            mate = lax.rem(g + n, group)
            chunk(source, mate)
            put(part.at[source, mate], [])
            mate_copy(source, mate).start()
            return inner

        lax.fori_loop(1, group, mate_step, 0)

        return carry

    lax.fori_loop(1, heads + 1, mates_step, 0)
    if chunks > 1:
        moved1[1].start()
    spot = lax.axis_index("tensor")
    outs[spot] = (values[...] + sum_mlp.total() + vectors[3:4]).astype(LOW)
    all_out.start()
    moved1[0].loaded()
    moved1[0].run(0)

    def own_step(k, carry):
        source = paired(z, lax.rem(k, heads), heads)
        chunk(source, g)
        extra = []
        for mate in mates:
            send_dp(
                xr.at[source, mate], xr.at[source, mate], x_send.at[source, mate], x_recv.at[source, mate], me
            ).wait_recv()
            extra.append(xr.at[source, mate])
        put(summed.at[source], extra)

        @pl.when(source != z)
        def _():
            send_dp(
                summed.at[source], gkv_r.at[z], kv_send.at[source], kv_recv.at[z], source * group + g
            ).start()

        return carry

    lax.fori_loop(1, heads + 1, own_step, 0)
    for other in all_out.others():
        all_out.forward(other)
    table_grads[...] = jnp.zeros_like(table_grads)

    def finish(k, carry):
        source = paired(z, lax.rem(k, heads), heads)
        span = pl.ds(pl.multiple_of(source * rows, rows), rows)
        by_row, by_col = shifts(rows, source * group + g)
        total = dq[:, span] * SCALE
        for n, held in enumerate((drow[:, :, span].reshape(SIDE, rows), dcol[:, span])):
            spread = unskew(held, by_col if n else by_row)
            for piece in parts_of(spread, 2):
                low_piece = piece.astype(LOW)
                total = total + tn(tables[n], low_piece)
                table_grads[n] += nn(low_piece, q_tok[span, :])
        gq_s[source] = total.astype(LOW)

        @pl.when(source != z)
        def _():
            send_dp(
                gq_s.at[source], gq_r.at[z], q_send.at[source], q_recv.at[z], source * group + g
            ).start()

        return carry

    lax.fori_loop(1, heads + 1, finish, 0)
    moved1[0].run(1)
    for stage in range(2, halve_bits() - 1):
        for each in moved2 + moved1[:1]:
            each.run(stage)
    found = [each.total() for each in moved2]
    fc2_out[...] = jnp.concatenate(found, axis=0) if chunks > 1 else found[0]
    fc1_out[...] = moved1[0].total()
    if chunks > 1:
        moved1[1].loaded()
        moved1[1].run(0)
        fc1_state[...] = moved1[1].stages[0][0][...]
    moved0.run(0)
    proj_state[...] = moved0.stages[0][0][...]
    for other in all_out.others() + [line]:
        all_out.take(other)
    output[...] = outs[...]
    grads[z, 0] = gq_s[z]
    grads[z, pl.ds(1, 2)] = summed[z]
    for h in column:
        send_dp(summed.at[h], gkv_r.at[h], kv_send.at[h], kv_recv.at[h], h * group + g).wait()
        grads[h, pl.ds(1, 2)] = gkv_r[h]
    for h in column:
        send_dp(gq_s.at[h], gq_r.at[h], q_send.at[h], q_recv.at[h], h * group + g).wait()
        grads[h, 0] = gq_r[h]
    for copy in sends:
        copy.wait_send()
    for source in range(heads):
        for mate in mates:
            mate_copy(source, mate).wait_send()
    for each in moved1 + moved2 + [sum_mlp, all_out, moved0]:
        each.finish()


def attend_back(shape, ga, tables, qaug, bias_rows, kv, o_rows, lse, fc2_state, fc1, mlp, values, vectors, proj):
    count, share, width = mlp.shape
    devices, chunks, owned, hidden = fc1.shape
    hbm = pl.BlockSpec(memory_space=pl.ANY)
    moving = halve_bufs(owned, hidden, first=2) * chunks
    moving += halve_bufs(chunks * owned, proj.shape[2], last=0)
    moving += [pltpu.VMEM((count, share, width), LOW)]
    moving += part_bufs(count // 2, share, width) + gather_sems(count // 2)
    moving += halve_bufs(owned, hidden, own=True)
    if chunks > 1:
        moving += halve_bufs(owned, hidden, last=0, own=True)
    heads, group, rows, queries = shape.heads, shape.group, shape.rows, shape.queries
    vmem = pl.BlockSpec(memory_space=pltpu.VMEM)
    dma = pltpu.SemaphoreType.DMA
    return pl.pallas_call(
        functools.partial(backward_kernel, shape),
        out_shape=(
            jax.ShapeDtypeStruct((heads, 3, HEAD, rows), LOW),
            jax.ShapeDtypeStruct((2, 2 * SIDE, 128), F32),
            jax.ShapeDtypeStruct((owned, hidden), F32),
            jax.ShapeDtypeStruct((chunks * owned, hidden), F32),
            jax.ShapeDtypeStruct((devices // 2, owned, hidden), LOW),
            jax.ShapeDtypeStruct((count, share, width), LOW),
            jax.ShapeDtypeStruct((devices // 2,) + proj.shape[1:], LOW),
        ),
        in_specs=[vmem] * 8 + [hbm] + [vmem] * 4,
        out_specs=(vmem,) * 7,
        scratch_shapes=[
            pltpu.VMEM((heads, HEAD, rows), LOW),
            pltpu.VMEM((AUG, queries), LOW),
            pltpu.VMEM((queries, 128), LOW),
            pltpu.VMEM((128, queries), LOW),
            pltpu.VMEM((queries, 128), LOW),
            pltpu.VMEM((AUG, rows), LOW),
            pltpu.VMEM((rows, AUG), LOW),
            pltpu.VMEM((128, rows), LOW),
            pltpu.VMEM((rows, 128), LOW),
            pltpu.VMEM((rows, 128), F32),
            pltpu.VMEM((rows, 128), F32),
            pltpu.VMEM((HEAD, queries), F32),
            pltpu.VMEM((SIDE // 8, 8, queries), F32),
            pltpu.VMEM((SIDE, queries), F32),
            pltpu.VMEM((heads, group, 2, HEAD, rows), LOW),
            pltpu.VMEM((heads, group, 2, HEAD, rows), LOW),
            pltpu.VMEM((heads, 2, HEAD, rows), LOW),
            pltpu.VMEM((heads, HEAD, rows), LOW),
            pltpu.VMEM((heads, HEAD, rows), LOW),
            pltpu.VMEM((heads, 2, HEAD, rows), LOW),
            dma((heads,)), dma((heads,)), dma((heads, group)), dma((heads, group)),
            dma((heads,)), dma((heads,)), dma((heads,)), dma((heads,)),
        ] + moving,
        compiler_params=pltpu.CompilerParams(
            collective_id=2, has_side_effects=True, vmem_limit_bytes=VMEM_LIMIT["attend_back"]
        ),
        name="attend_back",
    )(ga, tables, qaug, bias_rows, kv, o_rows, lse, fc2_state, fc1, mlp, values, vectors, proj)


def send_tensor(src, dst, send_sem, recv_sem, dev):
    return pltpu.make_async_remote_copy(
        src_ref=src,
        dst_ref=dst,
        send_sem=send_sem,
        recv_sem=recv_sem,
        device_id={"tensor": dev},
        device_id_type=MESH,
    )


def tensor_place():
    me = lax.axis_index("tensor")
    return lax.rem(me, 2), me // 2, lax.axis_size("tensor") // 2


def tensor_peers():
    core, line, lines = tensor_place()
    far = [lax.rem(line + k, lines) * 2 + core for k in range(1, lines)]
    return far + [line * 2 + 1 - core]


def part_bufs(lines, share, width, dtype=LOW):
    dma = pltpu.SemaphoreType.DMA
    return [pltpu.VMEM((lines, share, width), dtype)] * 3 + [dma((lines,))] * 4


class Reduce:
    def __init__(self, part, mate_in, passed, line_in, m_send, m_recv, l_send, l_recv):
        self.part, self.mate_in, self.passed, self.line_in = part, mate_in, passed, line_in
        self.sems = m_send, m_recv, l_send, l_recv
        self.core, self.line, self.lines = tensor_place()

    def mate_copy(self, to):
        m_send, m_recv, _, _ = self.sems
        return send_tensor(
            self.part.at[to * 2 + 1 - self.core], self.mate_in.at[to],
            m_send.at[to], m_recv.at[to], self.line * 2 + 1 - self.core,
        )

    def line_copy(self, to, slot):
        _, _, l_send, l_recv = self.sems
        return send_tensor(
            self.passed.at[to], self.line_in.at[slot], l_send.at[to], l_recv.at[slot],
            to * 2 + self.core,
        )

    def give(self, to):
        self.mate_copy(to).start()

    def pass_on(self, to):
        self.mate_copy(to).wait_recv()
        both = self.part[to * 2 + self.core].astype(F32) + self.mate_in[to].astype(F32)
        self.passed[to] = both.astype(self.passed.dtype)
        self.line_copy(to, self.line).start()

    def others(self):
        return [lax.rem(self.line + k, self.lines) for k in range(1, self.lines)]

    def total(self):
        self.mate_copy(self.line).wait_recv()
        total = self.part[self.line * 2 + self.core].astype(F32) + self.mate_in[self.line].astype(F32)
        for other in self.others():
            self.line_copy(other, other).wait_recv()
            total = total + self.line_in[other].astype(F32)
        return total

    def finish(self):
        self.mate_copy(self.line).wait_send()
        for other in self.others():
            self.mate_copy(other).wait_send()
            self.line_copy(other, self.line).wait_send()


def gather_sems(lines):
    dma = pltpu.SemaphoreType.DMA
    return [dma((lines,)), dma((lines,)), dma((2 * lines,))]


class Gather:
    def __init__(self, whole, l_send, m_send, recv):
        self.whole, self.sems = whole, (l_send, m_send, recv)
        self.core, self.line, self.lines = tensor_place()

    def line_copy(self, to):
        l_send, _, recv = self.sems
        own = self.line * 2 + self.core
        return send_tensor(
            self.whole.at[own], self.whole.at[own], l_send.at[to], recv.at[own], to * 2 + self.core
        )

    def mate_copy(self, at):
        _, m_send, recv = self.sems
        part = at * 2 + self.core
        return send_tensor(
            self.whole.at[part], self.whole.at[part], m_send.at[at], recv.at[part],
            self.line * 2 + 1 - self.core,
        )

    def arrived(self, part):
        l_send, _, recv = self.sems
        send_tensor(
            self.whole.at[part], self.whole.at[part], l_send.at[0], recv.at[part], part
        ).wait_recv()

    def others(self):
        return [lax.rem(self.line + k, self.lines) for k in range(1, self.lines)]

    def start(self):
        for other in self.others():
            self.line_copy(other).start()
        self.mate_copy(self.line).start()

    def forward(self, at):
        self.arrived(at * 2 + self.core)
        self.mate_copy(at).start()

    def take(self, at):
        self.arrived(at * 2 + 1 - self.core)

    def finish(self):
        self.mate_copy(self.line).wait_send()
        for other in self.others():
            self.mate_copy(other).wait_send()
            self.line_copy(other).wait_send()


def normed(values):
    center = values - jnp.mean(values, axis=-1, keepdims=True)
    variance = jnp.mean(center * center, axis=-1, keepdims=True)
    inverse = lax.rsqrt(variance + EPSILON)
    return center * inverse, inverse


def normed_back(upstream, scaled, inverse, gain):
    weighted = upstream * gain
    centered = weighted - jnp.mean(weighted, axis=-1, keepdims=True)
    return (centered - scaled * jnp.mean(weighted * scaled, axis=-1, keepdims=True)) * inverse


def tile_of(width):
    return 256 if width % 256 == 0 else 128


class Ring:
    def __init__(self, heads):
        self.heads, self.group = heads, lax.axis_size("dp") // heads
        me = lax.axis_index("dp")
        self.z, self.g = me // self.group, lax.rem(me, self.group)

    def column(self):
        return [paired(self.z, k, self.heads) for k in range(1, self.heads)]

    def mates(self):
        return [lax.rem(self.g + k, self.group) for k in range(1, self.group)]

    def peers(self):
        far = [h * self.group + self.g for h in self.column()]
        return far + [self.z * self.group + o for o in self.mates()]


def greet_all(ring):
    barrier = pltpu.get_barrier_semaphore()
    near, far = tensor_peers(), ring.peers()
    for peer in near:
        pl.semaphore_signal(barrier, inc=1, device_id={"tensor": peer}, device_id_type=MESH)
    for peer in far:
        pl.semaphore_signal(barrier, inc=1, device_id={"dp": peer}, device_id_type=MESH)
    pl.semaphore_wait(barrier, len(near) + len(far))


def halve_bits():
    return (lax.axis_size("dp") - 1).bit_length()


def near_first():
    return tuple(range(halve_bits()))


def far_first(group):
    first = group.bit_length() - 1
    return (first,) + tuple(bit for bit in range(halve_bits()) if bit != first)


def halve_bufs(share, width, first=0, last=None, own=False):
    bits = halve_bits()
    last = bits - 1 if last is None else last
    dma = pltpu.SemaphoreType.DMA
    found = []
    if own:
        found += [pltpu.VMEM((1 << (bits - 1), share, width), LOW), dma]
    for stage in range(first, last + 1):
        count = 1 << (bits - 1 - stage)
        found += [pltpu.VMEM((count, share, width), LOW), dma((count,)), dma((count,))]
    return found


class Halve:
    def __init__(self, order, source, bufs, first=0, last=None, own=False):
        self.order, self.source, self.first = order, source, first
        self.last = len(order) - 1 if last is None else last
        bufs = list(bufs)
        self.own = bufs[0:2] if own else None
        bufs = bufs[2:] if own else bufs
        self.stages = {first + n: bufs[3 * n : 3 * n + 3] for n in range(len(bufs) // 3)}
        self.me = lax.axis_index("dp")

    def bit(self, stage):
        return lax.rem(self.me // (1 << self.order[stage]), 2)

    def count(self, stage):
        return 1 << (len(self.order) - 1 - stage)

    def index(self, stage, at, bit):
        if stage > 0:
            return at * 2 + bit
        place = bit * (1 << self.order[0])
        for n, other in enumerate(self.order[1:]):
            place = place + lax.rem(at // (1 << n), 2) * (1 << other)
        return place

    def held(self, stage):
        return self.source if stage == self.first else self.stages[stage - 1][0]

    def copy(self, stage, at):
        bit = self.bit(stage)
        into, send, recv = self.stages[stage]
        return send_dp(
            self.held(stage).at[self.index(stage, at, 1 - bit)], into.at[at],
            send.at[at], recv.at[at], self.me + (1 - 2 * bit) * (1 << self.order[stage]),
        )

    def spots(self, stage):
        if stage == len(self.order) - 1:
            return [0]
        bit, half = self.bit(stage + 1), self.count(stage) // 2
        return [n * 2 + 1 - bit for n in range(half)] + [n * 2 + bit for n in range(half)]

    def load(self):
        for at in range(self.count(0)):
            pltpu.make_async_copy(
                self.source.at[self.index(0, at, self.bit(0))], self.own[0].at[at], self.own[1]
            ).start()

    def loaded(self):
        pltpu.make_async_copy(
            self.source.at[pl.ds(0, self.count(0))], self.own[0], self.own[1]
        ).wait()

    def start(self, only=slice(None)):
        for at in self.spots(self.first)[only]:
            self.copy(self.first, at).start()

    def kept(self, stage, at):
        if stage == self.first and self.own is not None:
            return self.own[0][at].astype(F32)
        return self.held(stage)[self.index(stage, at, self.bit(stage))].astype(F32)

    def sum_at(self, stage, at):
        self.copy(stage, at).wait_recv()
        return self.kept(stage, at) + self.stages[stage][0][at].astype(F32)

    def run(self, stage):
        for n, at in enumerate(self.spots(stage)):
            self.stages[stage][0][at] = self.sum_at(stage, at).astype(LOW)
            if stage < self.last and n < self.count(stage) // 2:
                self.copy(stage + 1, n).start()

    def total(self):
        return self.sum_at(self.last, 0)

    def finish(self):
        for stage in self.stages:
            for at in range(self.count(stage)):
                self.copy(stage, at).wait_send()


def middle_kernel(
    heads, att, proj_w, tokens, cot, fc1_hbm, fc2_hbm, vectors,
    mlp, values_out, middle_out, fc1_out, proj_out, ga_out, fc1_bias_out, sums_out, fc2_state,
    fc1, fc2, att_tok, branch, back, n2, act, gu, gb, held, spread,
    wide, load1, load2, *rest,
):
    core, line, lines = tensor_place()
    me = lax.axis_index("tensor")
    _, share, width = tokens.shape
    rows = tokens.shape[0] * share
    local, hidden = proj_w.shape[0], fc1_hbm.shape[1]
    step, dstep = tile_of(hidden), tile_of(width)
    in_fc1 = pltpu.make_async_copy(fc1_hbm, fc1, load1)
    in_fc2 = pltpu.make_async_copy(fc2_hbm, fc2, load2)
    in_fc1.start()
    in_fc2.start()
    greet_all(Ring(heads))
    sum_branch = Reduce(branch, *rest[0:7])
    sum_back = Reduce(back, *rest[7:14])
    all_n2 = Gather(n2, *rest[14:17])
    all_gb = Gather(gb, *rest[17:20])
    blocks2, blocks1, fc1_sem = rest[20:23]
    devices, chunks, owned, _ = blocks2.shape
    orders = [near_first(), far_first(lax.axis_size("dp") // heads)]
    moved = [
        Halve(orders[n], blocks2.at[:, n], rest[23 + 6 * n : 29 + 6 * n], last=1)
        for n in range(chunks)
    ]
    att_tok[...] = att[...].T.reshape(att_tok.shape)

    def project(k, carry):
        to = lax.rem(line + 1 + lax.rem(k, lines), lines)
        part = to * 2 + jnp.where(k < lines, 1 - core, core)
        branch[part] = nn(att_tok[part], proj_w[...]).astype(LOW)

        @pl.when(k < lines)
        def _():
            sum_branch.give(to)

        return carry

    lax.fori_loop(0, 2 * lines, project, 0)
    for other in sum_branch.others():
        sum_branch.pass_on(other)
    middle = tokens[me].astype(F32) + vectors[0:1]
    middle = middle + sum_branch.total()
    scaled, inverse = normed(middle)
    n2[me] = (scaled * vectors[1:2] + vectors[2:3]).astype(LOW)
    all_n2.start()
    values_out[...] = middle
    held[...] = scaled
    spread[...] = jnp.broadcast_to(inverse, spread.shape)
    fc1_bias_out[...] = jnp.zeros_like(fc1_bias_out)
    in_fc1.wait()
    in_fc2.wait()

    def hidden_part(k, carry):
        at = lax.rem(line + k, lines)

        @pl.when(k > 0)
        def _():
            all_n2.forward(at)

        all_n2.take(at)
        pair = pl.ds(at * 2, 2)
        inputs = n2[pair].reshape(2 * share, width)
        pulls = cot[pair].reshape(2 * share, width)

        def tile(n, inner):
            span = pl.ds(pl.multiple_of(n * step, step), step)
            up = nn(inputs, fc1[:, span]) + vectors[6:7, span]
            phi = 0.5 + 0.5 * lax.erf(up * math.sqrt(0.5))
            slope = phi + up * (jnp.exp(-0.5 * up * up) * (2 * math.pi) ** -0.5)
            act[pair, :, span] = (up * phi).astype(LOW).reshape(2, share, step)
            grad_up = (nt(pulls, fc2[span, :]) * slope).astype(LOW)
            gu[pair, :, span] = grad_up.reshape(2, share, step)
            fc1_bias_out[:, span] += jnp.sum(grad_up.astype(F32), axis=0, keepdims=True)
            return inner

        lax.fori_loop(0, hidden // step, tile, 0)

        def tile_back(n, inner):
            span = pl.ds(pl.multiple_of(n * dstep, dstep), dstep)
            found = nt(gu[pair].reshape(2 * share, hidden), fc1[span, :])
            back[pair, :, span] = found.astype(LOW).reshape(2, share, dstep)
            return inner

        lax.fori_loop(0, width // dstep, tile_back, 0)
        sum_back.give(at)

        return carry

    lax.fori_loop(0, lines, hidden_part, 0)

    def weights2(n, carry):
        span = pl.ds(pl.multiple_of(n * dstep, dstep), dstep)
        found = tn(cot[:, :, span].reshape(rows, dstep), act[...].reshape(rows, hidden))
        wide[span, :] = found.astype(LOW)
        return carry

    lax.fori_loop(0, width // dstep, weights2, 0)
    for dev in range(devices):
        for chunk in range(chunks):
            at = (dev * chunks + chunk) * owned
            blocks2[dev, chunk] = wide[pl.ds(at, owned), :]
    for each in moved:
        each.start()
    for other in sum_back.others():
        sum_back.pass_on(other)

    def out_part(k, carry):
        at = lax.rem(line + 1 + k, lines)
        pair = pl.ds(at * 2, 2)

        def tile_out(n, inner):
            span = pl.ds(pl.multiple_of(n * dstep, dstep), dstep)
            found = nn(act[pair].reshape(2 * share, hidden), fc2[:, span])
            mlp[pair, :, span] = found.astype(LOW).reshape(2, share, dstep)
            return inner

        lax.fori_loop(0, width // dstep, tile_out, 0)
        return carry

    lax.fori_loop(0, lines, out_part, 0)

    def weights1(n, carry):
        span = pl.ds(pl.multiple_of(n * dstep, dstep), dstep)
        found = tn(n2[:, :, span].reshape(rows, dstep), gu[...].reshape(rows, hidden))
        wide[span, :] = found.astype(LOW)
        return carry

    lax.fori_loop(0, width // dstep, weights1, 0)
    for dev in range(devices):
        for chunk in range(chunks):
            at = (dev * chunks + chunk) * owned
            blocks1[dev, chunk] = wide[pl.ds(at, owned), :]
    keep_fc1 = pltpu.make_async_copy(blocks1, fc1_out, fc1_sem)
    keep_fc1.start()
    upstream = sum_back.total()
    sums_out[0:1] = jnp.sum(upstream * held[...], axis=0, keepdims=True)
    sums_out[1:2] = jnp.sum(upstream, axis=0, keepdims=True)
    grad_middle = cot[me].astype(F32) + normed_back(
        upstream, held[...], spread[:, :1], vectors[1:2]
    )
    middle_out[...] = grad_middle
    gb[me] = grad_middle.astype(LOW)
    all_gb.start()
    for each in moved:
        each.run(0)
    sums_out[2:3] = jnp.sum(cot[...].astype(F32).reshape(rows, width), axis=0, keepdims=True)
    for other in all_gb.others():
        all_gb.forward(other)
    all_gb.take(line)
    for other in all_gb.others():
        all_gb.take(other)
    whole = gb[...].reshape(rows, width)
    sums_out[3:4] = jnp.sum(whole.astype(F32), axis=0, keepdims=True)
    ga_out[...] = nt(proj_w[...], whole).astype(LOW)

    def weights0(n, carry):
        span = pl.ds(pl.multiple_of(n * dstep, dstep), dstep)
        found = tn(gb[:, :, span].reshape(rows, dstep), att_tok[...].reshape(rows, -1))
        wide[span, :local] = found.astype(LOW)
        return carry

    lax.fori_loop(0, width // dstep, weights0, 0)
    for dev in range(devices):
        proj_out[dev] = wide[pl.ds(dev * chunks * owned, chunks * owned), :local]
    for n, each in enumerate(moved):
        each.run(1)
        fc2_state[n] = each.stages[1][0][...]
    keep_fc1.wait()
    for each in (sum_branch, sum_back, all_n2, all_gb, *moved):
        each.finish()


def middle_block(heads, att, proj_w, tokens, cot, fc1, fc2, vectors):
    count = lax.axis_size("tensor")
    lines = count // 2
    local, width = proj_w.shape
    rows = tokens.shape[0]
    share = rows // count
    hidden = fc1.shape[1]
    vmem = pl.BlockSpec(memory_space=pltpu.VMEM)
    hbm = pl.BlockSpec(memory_space=pl.ANY)
    dma = pltpu.SemaphoreType.DMA
    whole = (count, share, width)
    devices = lax.axis_size("dp")
    owned = width // devices
    chunks = 2 if owned % 32 == 0 else 1
    weights = (devices, chunks, owned // chunks, hidden)
    scratch = [
        pltpu.VMEM((width, hidden), LOW),
        pltpu.VMEM((hidden, width), LOW),
        pltpu.VMEM((count, share, local), LOW),
        pltpu.VMEM(whole, LOW),
        pltpu.VMEM(whole, LOW),
        pltpu.VMEM(whole, LOW),
        pltpu.VMEM((count, share, hidden), LOW),
        pltpu.VMEM((count, share, hidden), LOW),
        pltpu.VMEM(whole, LOW),
        pltpu.VMEM((share, width), F32),
        pltpu.VMEM((share, 128), F32),
        pltpu.VMEM((width, hidden), LOW),
        dma,
        dma,
    ]
    scratch += part_bufs(lines, share, width) * 2 + gather_sems(lines) * 2
    scratch += [pltpu.VMEM(weights, LOW), pltpu.VMEM(weights, LOW), dma]
    scratch += halve_bufs(owned // chunks, hidden, last=1) * chunks
    return pl.pallas_call(
        functools.partial(middle_kernel, heads),
        out_shape=(
            jax.ShapeDtypeStruct(whole, LOW),
            jax.ShapeDtypeStruct((share, width), F32),
            jax.ShapeDtypeStruct((share, width), F32),
            jax.ShapeDtypeStruct(weights, LOW),
            jax.ShapeDtypeStruct((devices, owned, local), LOW),
            jax.ShapeDtypeStruct((local, rows), LOW),
            jax.ShapeDtypeStruct((1, hidden), F32),
            jax.ShapeDtypeStruct((8, width), F32),
            jax.ShapeDtypeStruct((chunks, devices // 4, owned // chunks, hidden), LOW),
        ),
        in_specs=[vmem] * 4 + [hbm] * 2 + [vmem],
        out_specs=(vmem,) * 3 + (hbm,) + (vmem,) * 5,
        scratch_shapes=scratch,
        compiler_params=pltpu.CompilerParams(
            collective_id=3, has_side_effects=True, vmem_limit_bytes=VMEM_LIMIT["middle"]
        ),
        name="middle",
    )(
        att, proj_w, tokens.reshape(whole), cot.reshape(whole), fc1, fc2, vectors,
    )


def small_bufs(heads, stages, shape):
    group, lines = lax.axis_size("dp") // heads, lax.axis_size("tensor") // 2
    dma = pltpu.SemaphoreType.DMA
    found = []
    for stage in stages:
        count = {"core": 2, "line": lines, "mate": group, "far": heads}[stage]
        found += [
            pltpu.VMEM(shape, F32), pltpu.VMEM((count,) + shape, F32), dma((count,)), dma((count,))
        ]
    return found


class Small:
    def __init__(self, ring, stages, merge, *bufs):
        self.ring, self.stages, self.merge = ring, stages, merge
        self.bufs = [bufs[4 * n : 4 * n + 4] for n in range(len(stages))]
        core, line, lines = tensor_place()
        self.peers = {
            "core": (core, [(1 - core, line * 2 + 1 - core)]),
            "line": (line, [(o, o * 2 + core) for o in [lax.rem(line + k, lines) for k in range(1, lines)]]),
            "mate": (ring.g, [(o, ring.z * ring.group + o) for o in ring.mates()]),
            "far": (ring.z, [(o, o * ring.group + ring.g) for o in ring.column()]),
        }

    def copy(self, n, slot, other, dev):
        value, held, send, recv = self.bufs[n]
        call = send_tensor if self.stages[n] in ("core", "line") else send_dp
        return call(value, held.at[slot], send.at[other], recv.at[slot], dev)

    def start(self, n, value):
        own, peers = self.peers[self.stages[n]]
        self.bufs[n][0][...] = value
        for other, dev in peers:
            self.copy(n, own, other, dev).start()

    def take(self, n):
        _, peers = self.peers[self.stages[n]]
        total = self.bufs[n][0][...]
        for other, dev in peers:
            self.copy(n, other, other, dev).wait_recv()
            total = self.merge(total, self.bufs[n][1][other])
        return total

    def step(self, n):
        self.start(n + 1, self.take(n))

    def finish(self):
        for n in range(len(self.stages)):
            own, peers = self.peers[self.stages[n]]
            for other, dev in peers:
                self.copy(n, own, other, dev).wait_send()


EVERY = ("core", "line", "far", "mate")
OVER_DP = ("mate", "far")


def add_peaks(a, b):
    row = lax.broadcasted_iota(jnp.int32, a.shape, 0)
    return jnp.where(row == 2, jnp.maximum(a, b), a + b)


def widen(row, width):
    if row.shape[1] == width:
        return row
    return jnp.concatenate([row, jnp.zeros((1, width - row.shape[1]), F32)], axis=1)


def tail_kernel(
    heads, grads, qkv_w, n1_t, tokens, grad_middle, vectors, tables, sums, fc1_bias, peak,
    proj, fc1_half, fc1_state,
    tokens_out, proj_out, fc1_out, qkv_out, tables_out, rows_out, clip_out,
    g_all, g_tok, part, gt, *rest,
):
    ring = Ring(heads)
    core, line, lines = tensor_place()
    me = lax.axis_index("tensor")
    count, share, width = tokens.shape
    rows = count * share
    local = heads * HEAD
    dstep = tile_of(width)
    pieces, devices, piece, _ = n1_t.shape
    chunks = 1 if pieces == 1 else 2
    rest = list(rest)

    def taken(number):
        found, rest[:] = rest[:number], rest[number:]
        return found

    greet_all(ring)
    blocks = [taken(1)[0] for _ in range(pieces)]
    moved3 = [Halve(near_first(), each, taken(3 * halve_bits())) for each in blocks]
    moved0 = Halve(far_first(ring.group), proj, taken(3 * (halve_bits() - 1)), first=1)
    moved1 = []
    if chunks > 1:
        moved1 = [Halve(near_first(), fc1_state, taken(3 * (halve_bits() - 1)), first=1)]
    sum_part = Reduce(part, *taken(7))
    all_gt = Gather(gt, *taken(3))
    pool, pooled = taken(2)
    sum_pool = Reduce(pool, *taken(7))
    all_pool = Gather(pooled, *taken(3))
    small_pool = Small(ring, OVER_DP, lax.add, *taken(8))
    small_late = Small(ring, EVERY, lax.add, *taken(16))
    small_dp = Small(ring, OVER_DP, add_peaks, *taken(8))
    pool[...] = tables[...].reshape(pool.shape)
    for other in sum_pool.others() + [line]:
        sum_pool.give(other)
    for each in moved1:
        each.start()
    moved0.start()
    for t in range(3):
        for h in range(heads):
            g_all[pl.ds(t * local + h * HEAD, HEAD), :] = grads[h, t]
    g_tok[...] = g_all[...].T.reshape(g_tok.shape)
    for other in sum_pool.others():
        sum_pool.pass_on(other)
    whole = g_tok[...].reshape(rows, 3 * local)
    lane = lax.broadcasted_iota(jnp.int32, (1, width), 1)
    peaks = jnp.where(lane == ring.z, peak[0:1, 0:1], -jnp.inf)
    bias_sums = nn(jnp.ones((8, rows), LOW), whole)[0:1]
    dp_rows = [widen(fc1_bias[...], width), widen(bias_sums, width), peaks]
    small_dp.start(0, jnp.concatenate(dp_rows + [jnp.zeros((5, width), F32)], axis=0))

    for n in range(pieces):
        found = nn(
            n1_t[n].reshape(devices * piece, rows), g_tok[...].reshape(rows, 3 * local)
        )
        blocks[n][...] = found.astype(LOW).reshape(devices, piece, 3 * local)
        if n == min(1, pieces - 1):
            small_pool.start(0, sum_pool.total())
        moved3[n].start()

    def norm_part(k, carry):
        at = lax.rem(line + 1 + k, lines)
        pair = pl.ds(at * 2, 2)

        def tile(n, inner):
            span = pl.ds(pl.multiple_of(n * dstep, dstep), dstep)
            found = nn(g_tok[pair].reshape(2 * share, 3 * local), qkv_w[:, span])
            part[pair, :, span] = found.astype(LOW).reshape(2, share, dstep)
            return inner

        lax.fori_loop(0, width // dstep, tile, 0)
        sum_part.give(at)
        return carry

    lax.fori_loop(0, lines, norm_part, 0)
    for other in sum_part.others():
        sum_part.pass_on(other)
    scaled, inverse = normed(tokens[me].astype(F32))
    small_pool.step(0)
    moved0.run(1)
    for each in moved1:
        each.run(1)
    moved3[0].run(0)
    for each in moved3[1:2]:
        each.run(0)
    moved3[0].run(1)
    upstream = sum_part.total()
    late = [
        sums[0:4],
        jnp.sum(upstream * scaled, axis=0, keepdims=True),
        jnp.sum(upstream, axis=0, keepdims=True),
        jnp.zeros((2, width), F32),
    ]
    small_late.start(0, jnp.concatenate(late, axis=0))
    found = grad_middle[...] + normed_back(upstream, scaled, inverse, vectors[4:5])
    gt[me] = found.astype(LOW)
    all_gt.start()
    pooled[me] = small_pool.take(1)
    all_pool.start()
    small_dp.step(0)
    for n, each in enumerate(moved3[2:]):
        each.run(0)
        if n == 0:
            small_late.step(0)
        if n == 1:
            small_late.step(1)
            for other in all_gt.others():
                all_gt.forward(other)
            for other in all_pool.others():
                all_pool.forward(other)
        moved3[n + 1].run(1)
    if pieces < 4:
        for n in range(max(pieces - 2, 0), 2):
            small_late.step(n)
        for other in all_gt.others():
            all_gt.forward(other)
        for other in all_pool.others():
            all_pool.forward(other)
    small_late.step(2)
    dp_sum = small_dp.take(1)
    limit = vectors[9:10]
    factors = jnp.sqrt(limit / jnp.maximum(dp_sum[2:3], limit))
    lane = lax.broadcasted_iota(jnp.int32, (1, width), 1)
    clipped_bias = vectors[7:8]
    for h in range(heads):
        factor = factors[:, h : h + 1]
        own = (lane >= h * HEAD) & (lane < (h + 1) * HEAD)
        clipped_bias = jnp.where(own, clipped_bias * factor, clipped_bias)
        for t in range(2):
            span = pl.ds(t * local + h * HEAD, HEAD)
            clip_out[span, :] = (qkv_w[span, :].astype(F32) * factor).astype(LOW)
    rows_out[8:11] = dp_sum[0:3]
    rows_out[11:12] = factors
    rows_out[12:13] = clipped_bias
    rows_out[13:16] = jnp.zeros((3, width), F32)
    if pieces > 1:
        moved3[-1].run(1)
    for stage in range(2, halve_bits() - 1):
        for each in moved3 + [moved0] + moved1:
            each.run(stage)
    for other in all_gt.others() + [line]:
        all_gt.take(other)
    for other in all_pool.others() + [line]:
        all_pool.take(other)
    tokens_out[...] = gt[...]
    for n in range(2):
        turned_sums = pooled[...].reshape(2, 2 * SIDE, 128)[n].T[:HEAD]
        found = jnp.zeros((HEAD, 2 * SIDE), F32)
        for piece in parts_of(turned_sums, 3):
            found = found + nn(piece.astype(LOW), turned(2 * SIDE))
        tables_out[n] = found
    late = small_late.take(3)
    row = lax.broadcasted_iota(jnp.int32, late.shape, 0)
    rows_out[0:8] = jnp.where((row == 2) | (row == 3), late * (1.0 / count), late)
    owned = fc1_half.shape[0]
    fc1_out[0:owned] = fc1_half[...]
    for each in moved1:
        fc1_out[pl.ds(owned, owned), :] = each.total()
    proj_out[...] = moved0.total()
    for n, each in enumerate(moved3):
        total = each.total()
        owned = total.shape[0]
        for t in range(3):
            qkv_out[t, pl.ds(n * owned, owned), :] = total[:, t * local : (t + 1) * local]
    for each in [
        moved0, sum_part, all_gt, sum_pool, all_pool, small_pool, small_late, small_dp,
    ] + moved3 + moved1:
        each.finish()


def tail(heads, grads, qkv_w, n1_t, tokens, grad_middle, vectors, tables, sums, fc1_bias, peak, proj, fc1_half, fc1_state):
    hidden = fc1_half.shape[1]
    count = lax.axis_size("tensor")
    lines = count // 2
    local = heads * HEAD
    pieces, devices, piece, rows = n1_t.shape
    width = devices * pieces * piece
    owned = fc1_half.shape[0]
    chunks = pieces * piece // owned
    share = rows // count
    vmem = pl.BlockSpec(memory_space=pltpu.VMEM)
    whole = (count, share, width)
    scratch = [
        pltpu.VMEM((3 * local, rows), LOW),
        pltpu.VMEM((count, share, 3 * local), LOW),
        pltpu.VMEM(whole, LOW),
        pltpu.VMEM(whole, LOW),
    ]
    scratch += [pltpu.VMEM((devices, piece, 3 * local), LOW)] * pieces
    scratch += halve_bufs(piece, 3 * local) * pieces
    scratch += halve_bufs(chunks * owned, local, first=1)
    if chunks > 1:
        scratch += halve_bufs(owned, hidden, first=1)
    scratch += part_bufs(lines, share, width) + gather_sems(lines)
    pool = (count, 4 * SIDE // count, 128)
    scratch += [pltpu.VMEM(pool, F32)] * 2
    scratch += part_bufs(lines, *pool[1:], F32) + gather_sems(lines)
    scratch += small_bufs(heads, OVER_DP, pool[1:])
    scratch += small_bufs(heads, EVERY, (8, width))
    scratch += small_bufs(heads, OVER_DP, (8, width))
    return pl.pallas_call(
        functools.partial(tail_kernel, heads),
        out_shape=(
            jax.ShapeDtypeStruct(whole, LOW),
            jax.ShapeDtypeStruct((chunks * owned, local), F32),
            jax.ShapeDtypeStruct((chunks * owned, hidden), F32),
            jax.ShapeDtypeStruct((3, chunks * owned, local), F32),
            jax.ShapeDtypeStruct((2, HEAD, 2 * SIDE), F32),
            jax.ShapeDtypeStruct((16, width), F32),
            jax.ShapeDtypeStruct((2 * local, width), LOW),
        ),
        in_specs=[vmem] * 13,
        out_specs=(vmem,) * 7,
        scratch_shapes=scratch,
        compiler_params=pltpu.CompilerParams(
            collective_id=4, has_side_effects=True, vmem_limit_bytes=VMEM_LIMIT["tail"]
        ),
        name="tail",
    )(
        grads, qkv_w, n1_t, tokens.reshape(whole), grad_middle, vectors, tables, sums, fc1_bias,
        peak, proj, fc1_half, fc1_state,
    )


def finish_kernel(count, *refs):
    large, (rows, tables), refs = refs[:count], refs[count : count + 2], refs[count + 2 :]
    outs, smalls, stage = refs[:count], refs[count : count + 13], refs[count + 13 :]
    sems_in, sems_out = stage[count], stage[count + 1]
    into = [pltpu.make_async_copy(a, b, sems_in.at[n]) for n, (a, b) in enumerate(zip(large, stage))]
    out = [pltpu.make_async_copy(b, c, sems_out.at[n]) for n, (b, c) in enumerate(zip(stage, outs))]
    for copy in into:
        copy.start()
    gain1, shift1, qv, proj, by_row, by_col, gain2, shift2, fc1, fc2, clip_bias, peaks, factors = smalls
    picks = (
        (gain2, 0), (shift2, 1), (fc2, 2), (proj, 3), (gain1, 4), (shift1, 5), (fc1, 8),
        (peaks, 10), (factors, 11), (clip_bias, 12),
    )
    for ref, at in picks:
        ref[...] = rows[at : at + 1, : ref.shape[0]].reshape(ref.shape)
    local = qv.shape[1]
    qv[0:1] = rows[9:10, :local]
    qv[1:2] = rows[9:10, 2 * local : 3 * local]
    by_row[...] = tables[0, :, : by_row.shape[1]]
    by_col[...] = tables[1, :, : by_col.shape[1]]
    for copy, after in zip(into, out):
        copy.wait()
        after.start()
    for copy in out:
        copy.wait()


def finish(large, rows, tables, hidden, local):
    width = rows.shape[1]
    heads = local // HEAD
    vmem = pl.BlockSpec(memory_space=pltpu.VMEM)
    hbm = pl.BlockSpec(memory_space=pl.ANY)
    count = len(large)
    shapes = [
        (width,), (width,), (2, local), (width,), (HEAD, 2 * SIDE - 1), (HEAD, 2 * SIDE - 1),
        (width,), (width,), (hidden,), (width,), (local,), (heads,), (heads,),
    ]
    return pl.pallas_call(
        functools.partial(finish_kernel, count),
        out_shape=[jax.ShapeDtypeStruct(each.shape, each.dtype) for each in large]
        + [jax.ShapeDtypeStruct(each, F32) for each in shapes],
        in_specs=[hbm] * count + [vmem] * 2,
        out_specs=[hbm] * count + [vmem] * len(shapes),
        scratch_shapes=[pltpu.VMEM(each.shape, each.dtype) for each in large]
        + [pltpu.SemaphoreType.DMA((count,))] * 2,
        compiler_params=pltpu.CompilerParams(vmem_limit_bytes=VMEM_LIMIT["finish"]),
        name="finish",
    )(*large, rows, tables)


def on_device(
    tokens,
    cotangent,
    norm1_gain,
    norm1_shift,
    qkv_weight,
    qv_bias,
    proj_weight,
    proj_bias,
    table_rows,
    table_cols,
    norm2_gain,
    norm2_shift,
    fc1_weight,
    fc1_bias,
    fc2_weight,
    fc2_bias,
    threshold,
):
    images, row_count, model_width = tokens.shape
    token_count = images * row_count
    local_width = qkv_weight.shape[2]
    local_heads = local_width // HEAD
    shape = Shape(local_heads, lax.axis_size("dp") // local_heads, row_count)
    flat = tokens.reshape(token_count, model_width)

    listed = (
        proj_bias, norm2_gain, norm2_shift, fc2_bias, norm1_gain, norm1_shift, fc1_bias, qv_bias,
        threshold,
    )
    weights = qkv_weight.transpose(1, 2, 0).reshape(3 * local_width, model_width)
    attended, qaug, bias_rows, kv, o_rows, lse, peak, normed1, tables, vectors = attend(
        shape, flat, weights, listed, table_rows.T, table_cols.T
    )
    (
        mlp_part,
        values,
        grad_middle,
        grad_fc1,
        grad_proj,
        grad_attended,
        grad_fc1_bias,
        sums,
        fc2_state,
    ) = middle_block(
        local_heads,
        attended.reshape(local_width, token_count),
        proj_weight,
        flat,
        cotangent.reshape(token_count, model_width),
        fc1_weight,
        fc2_weight,
        vectors,
    )
    grad_heads = grad_attended.reshape(local_heads, HEAD, row_count)
    grad_triple, table_terms, fc1_half, grad_fc2, fc1_state, output, proj_state = attend_back(
        shape, grad_heads, tables, qaug, bias_rows, kv, o_rows, lse, fc2_state, grad_fc1,
        mlp_part, values, vectors, grad_proj,
    )
    grad_tokens, grad_proj, grad_fc1, grad_qkv, table_sums, rows, clipped = tail(
        local_heads,
        grad_triple,
        weights,
        normed1,
        flat,
        grad_middle,
        vectors,
        table_terms,
        sums,
        grad_fc1_bias,
        peak,
        proj_state,
        fc1_half,
        fc1_state,
    )
    large = (output, grad_tokens, grad_fc1, grad_fc2, grad_qkv, clipped, grad_proj)
    (
        output,
        grad_tokens,
        grad_fc1,
        grad_fc2,
        grad_qkv,
        clipped,
        grad_proj,
        grad_norm1_gain,
        grad_norm1_shift,
        grad_qv_bias,
        grad_proj_bias,
        grad_rows_t,
        grad_cols_t,
        grad_norm2_gain,
        grad_norm2_shift,
        grad_fc1_bias,
        grad_fc2_bias,
        clipped_q_bias,
        head_peaks,
        clip_factors,
    ) = finish(large, rows, table_sums, fc1_bias.shape[0], local_width)
    output = output.reshape(images, row_count, model_width)
    grad_tokens = grad_tokens.reshape(images, row_count, model_width)
    grad_qkv = grad_qkv.transpose(1, 0, 2)
    grad_fc2, grad_proj = grad_fc2.T, grad_proj.T
    grad_table_rows, grad_table_cols = grad_rows_t.T, grad_cols_t.T
    clipped_qk = clipped.reshape(2, local_width, model_width).transpose(2, 0, 1)
    return (
        output,
        grad_tokens,
        grad_norm1_gain,
        grad_norm1_shift,
        grad_qkv,
        grad_qv_bias,
        grad_proj,
        grad_proj_bias,
        grad_table_rows,
        grad_table_cols,
        grad_norm2_gain,
        grad_norm2_shift,
        grad_fc1,
        grad_fc1_bias,
        grad_fc2,
        grad_fc2_bias,
        clipped_qk,
        clipped_q_bias,
        head_peaks,
        clip_factors,
    )


def solution(mesh):
    in_specs = (
        P(None, "dp", None),
        P(None, "dp", None),
        P(),
        P(),
        P(None, None, "tensor"),
        P(None, "tensor"),
        P("tensor", None),
        P(),
        P(),
        P(),
        P(),
        P(),
        P(None, "tensor"),
        P("tensor"),
        P("tensor", None),
        P(),
        P(),
    )
    out_specs = (
        P(None, "dp", None),
        P(None, "dp", None),
        P(),
        P(),
        P("dp", None, "tensor"),
        P(None, "tensor"),
        P("tensor", "dp"),
        P(),
        P(),
        P(),
        P(),
        P(),
        P("dp", "tensor"),
        P("tensor"),
        P("tensor", "dp"),
        P(),
        P(None, None, "tensor"),
        P("tensor"),
        P("tensor"),
        P("tensor"),
    )
    return jax.shard_map(
        on_device, mesh=mesh, in_specs=in_specs, out_specs=out_specs, check_vma=False
    )
```

```python
import functools
import math

import jax
import jax.numpy as jnp
from jax import lax
from jax.experimental import pallas as pl
from jax.experimental.pallas import tpu as pltpu
from jax.sharding import PartitionSpec as P

HEAD = 80
SIDE = 64

MESH = pl.DeviceIdType.MESH
LOW = jnp.bfloat16
F32 = jnp.float32
EPSILON = 1e-06
SCALE = HEAD**-0.5
EXP2_SCALE = SCALE * math.log2(math.e)
COLS_AT = HEAD
ROWS_AT = COLS_AT + 2 * SIDE
LSE_AT = ROWS_AT + 16
AUG = LSE_AT + 16
VMEM_LIMIT = {
    "attend": 60 * 2**20,
    "middle": 40 * 2**20,
    "attend_back": 32 * 2**20,
    "tail": 24 * 2**20,
    "finish": 12 * 2**20,
}


def nn(a, b):
    return lax.dot_general(a, b, (((1,), (0,)), ((), ())), preferred_element_type=F32)


def tn(a, b):
    return lax.dot_general(a, b, (((0,), (0,)), ((), ())), preferred_element_type=F32)


def nt(a, b):
    return lax.dot_general(a, b, (((1,), (1,)), ((), ())), preferred_element_type=F32)


def parts_of(values, count):
    pieces = []
    for _ in range(count):
        piece = values.astype(LOW).astype(F32)
        pieces.append(piece)
        values = values - piece
    return pieces


def send_dp(src, dst, send_sem, recv_sem, dev):
    return pltpu.make_async_remote_copy(
        src_ref=src,
        dst_ref=dst,
        send_sem=send_sem,
        recv_sem=recv_sem,
        device_id={"dp": dev},
        device_id_type=MESH,
    )


def paired(place, k, count):
    found, bit = 0, 1
    while bit < count:
        found = found + bit * lax.rem(place // bit + k // bit, 2)
        bit *= 2
    return found


def turned(count):
    row = lax.broadcasted_iota(jnp.int32, (count, count), 0)
    column = lax.broadcasted_iota(jnp.int32, (count, count), 1)
    return jnp.where(row + column == count - 2, 1.0, 0.0).astype(LOW)


def shifts(rows, dev):
    spot = lax.broadcasted_iota(jnp.int32, (2 * SIDE, rows), 1)
    by_row = SIDE - 1 - (dev * (rows // SIDE) + lax.shift_right_logical(spot, 6))
    by_col = SIDE - 1 - (spot & (SIDE - 1))
    return by_row, by_col


def skew(values, shift):
    for bit in (32, 16, 8, 4, 2, 1):
        moved = pltpu.roll(values, 2 * SIDE - bit, 0)
        values = jnp.where((shift & bit) != 0, moved, values)
    return values[:SIDE]


def unskew(values, shift):
    values = jnp.concatenate([values, jnp.zeros_like(values)], axis=0)
    for bit in (32, 16, 8, 4, 2, 1):
        moved = pltpu.roll(values, bit, 0)
        values = jnp.where((shift & bit) != 0, moved, values)
    return values


def greet(peers):
    barrier = pltpu.get_barrier_semaphore()
    for peer in peers:
        pl.semaphore_signal(barrier, inc=1, device_id={"dp": peer}, device_id_type=MESH)
    pl.semaphore_wait(barrier, len(peers))


def key_onehots(rows, dev):
    spot = lax.broadcasted_iota(jnp.int32, (2 * SIDE, rows), 1)
    index = lax.broadcasted_iota(jnp.int32, (2 * SIDE, rows), 0)
    cols = jnp.where((index & (SIDE - 1)) == (spot & (SIDE - 1)), 1.0, 0.0)
    spot, index = spot[:16], index[:16]
    offset = lax.rem(dev * (rows // SIDE), 8)
    in_group = jnp.where((index & 7) == offset + lax.shift_right_logical(spot, 6), 1.0, 0.0)
    return cols, in_group


class Shape:
    def __init__(self, heads, group, rows):
        self.heads, self.group, self.rows = heads, group, rows
        self.queries = heads * rows
        self.block = min(2048, self.queries)


def forward_kernel(shape, count, outs, *refs):
    results = refs[count : count + outs]
    held, refs_left = refs[count + outs : 2 * count + outs], refs[2 * count + outs :]
    load, save, inner, refs_left = refs_left[0], refs_left[1], refs_left[2 : 1 + outs], refs_left[1 + outs :]
    inner = list(inner[:3]) + [results[3]] + list(inner[3:])
    saves = [
        None if n == 3 else pltpu.make_async_copy(a, b, save.at[n])
        for n, (a, b) in enumerate(zip(inner, results))
    ]
    copies = [
        pltpu.make_async_copy(a, b, load.at[n]) for n, (a, b) in enumerate(zip(refs[:count], held))
    ]
    for copy in copies[2:] + copies[:2]:
        copy.start()
    forward_body(shape, copies, saves, *held, *inner, *refs_left)
    for copy in saves:
        if copy is not None:
            copy.wait()


def forward_body(
    shape, copies, saves, tokens, weights, proj_bias, gain2, shift2, fc2_bias, gain1, shift1, fc1_bias,
    qv_bias, threshold, rows_t, cols_t,
    att, qaug, bias_rows, kv_out, o_out, lse_out, peak_out, n1_out, tables, vectors,
    n1, qkv, wide_t, rq, rkv, kaug_t, kaug, vaug, oacc, mrow, lpk, att_s, att_r,
    q_send, q_recv, k_send, k_recv, x_send, x_recv, r_send, r_recv, o_sem,
):
    heads, group, rows, block = shape.heads, shape.group, shape.rows, shape.block
    local = heads * HEAD
    me = lax.axis_index("dp")
    z, g = me // group, lax.rem(me, group)
    column = [paired(z, k, heads) for k in range(1, heads)]
    mates = [lax.rem(g + k, group) for k in range(1, group)]
    greet([h * group + g for h in column] + [z * group + o for o in mates])
    width = tokens.shape[1]
    vectors[...] = jnp.zeros_like(vectors)
    for copy in copies[2:] + copies[:1]:
        copy.wait()
    listed = (proj_bias, gain2, shift2, fc2_bias, gain1, shift1, fc1_bias)
    for n, each in enumerate(listed):
        vectors[n : n + 1, : each.shape[0]] = each[...].reshape(1, each.shape[0])
    vectors[7:9, :local] = qv_bias[...]
    vectors[9:10] = jnp.broadcast_to(threshold[...].reshape(1, 1), (1, width))
    scaled, _ = normed(tokens[...].astype(F32))
    n1[...] = (scaled * vectors[4:5] + vectors[5:6]).astype(LOW)
    biases = vectors[7:9].astype(F32)
    biases = jnp.concatenate([biases, jnp.zeros((6, biases.shape[1]), F32)], axis=0).T

    def project(t):
        found = nt(weights[pl.ds(t * local, local), :], n1[...])
        if t != 1:
            found = found + biases[:local, t // 2 : t // 2 + 1]
        qkv[t] = found.astype(LOW)

    sends = []
    copies[1].wait()
    project(0)
    for h in column:
        mine = pl.ds(pl.multiple_of(h * HEAD, 16), HEAD)
        copy = send_dp(qkv.at[0, mine], rq.at[z], q_send.at[h], q_recv.at[z], h * group + g)
        copy.start()
        sends.append(copy)
    project(1)
    project(2)
    for h in column:
        mine = pl.ds(pl.multiple_of(h * HEAD, 16), HEAD)
        copy = send_dp(
            qkv.at[pl.ds(1, 2), mine], rkv.at[z, g], k_send.at[h], k_recv.at[z], h * group + g
        )
        copy.start()
        sends.append(copy)
    mine = pl.ds(pl.multiple_of(z * HEAD, 16), HEAD)
    rq[z] = qkv[0, mine]
    rkv[z, g] = qkv[pl.ds(1, 2), mine]
    for n, mate in enumerate(mates):
        send_dp(
            rkv.at[z, g], rkv.at[z, g], x_send.at[z, n], x_recv.at[z, g], z * group + mate
        ).start()
    n1_t = n1[...].T
    pieces, devices, piece, _ = n1_out.shape
    for dev in range(devices):
        for at in range(pieces):
            start = (dev * pieces + at) * piece
            n1_out[at, dev] = n1_t[start : start + piece]
    saves[7].start()
    wide_t[...] = jnp.zeros_like(wide_t)
    for n, held in enumerate((rows_t, cols_t)):
        wide_t[n, :HEAD, : held.shape[1]] = held[...]
        tables[n] = nn(wide_t[n], turned(2 * SIDE)).T[:, :HEAD].astype(LOW)
    saves[8].start()
    saves[9].start()
    qaug[pl.ds(LSE_AT, 16), :] = jnp.zeros((16, shape.queries), LOW)
    kaug_t[pl.ds(LSE_AT, 16), :] = jnp.zeros((16, rows), LOW)
    vaug[pl.ds(HEAD, 16), :] = jnp.where(
        lax.broadcasted_iota(jnp.int32, (16, rows), 0) == 0, 1.0, 0.0
    ).astype(LOW)
    oacc[...] = jnp.zeros_like(oacc)
    mrow[...] = jnp.full_like(mrow, -jnp.inf)
    lpk[...] = jnp.full_like(lpk, -jnp.inf)

    def prepare(k, carry):
        source = paired(z, k, heads)
        span = pl.ds(pl.multiple_of(source * rows, rows), rows)

        @pl.when(k > 0)
        def _():
            send_dp(rq.at[source], rq.at[source], q_send.at[source], q_recv.at[source], me).wait_recv()

        query = rq[source]
        by_row, by_col = shifts(rows, source * group + g)
        along_rows = skew(nn(tables[0], query) * (1.0 / SCALE), by_row)
        along_cols = skew(nn(tables[1], query) * (1.0 / SCALE), by_col)
        qaug[pl.ds(0, HEAD), span] = query
        cols = parts_of(along_cols, 2)
        qaug[pl.ds(COLS_AT, 2 * SIDE), span] = jnp.concatenate(cols, axis=0).astype(LOW)
        high, rest = parts_of(along_rows, 2)
        for at in range(SIDE // 8):
            pair = jnp.concatenate([high[8 * at : 8 * at + 8], rest[8 * at : 8 * at + 8]], axis=0)
            bias_rows[at, :, span] = pair.astype(LOW)
        return carry

    lax.fori_loop(0, heads, prepare, 0)
    saves[2].start()

    def chunk(source, mate):
        dev = source * group + mate
        cols, in_group = key_onehots(rows, dev)
        kaug_t[pl.ds(0, HEAD), :] = rkv[source, mate, 0]
        kaug_t[pl.ds(COLS_AT, 2 * SIDE), :] = cols.astype(LOW)
        kaug_t[pl.ds(ROWS_AT, 16), :] = in_group.astype(LOW)
        kaug[...] = kaug_t[...].T
        vaug[pl.ds(0, HEAD), :] = rkv[source, mate, 1]
        qaug[pl.ds(ROWS_AT, 16), :] = bias_rows[(dev * (rows // SIDE)) // 8]

        def one(i, carry):
            span = pl.ds(pl.multiple_of(i * block, block), block)
            logits = nn(kaug[:, :HEAD], qaug[pl.ds(0, HEAD), span])
            lpk[...] = jnp.maximum(lpk[...], jnp.max(logits.reshape(rows // 8, 8, block), axis=0))
            scores = nn(kaug[...], qaug[:, span])
            before = mrow[:, span]
            top = jnp.maximum(before, jnp.max(scores, axis=0, keepdims=True))
            mrow[:, span] = top
            weights = jnp.exp2(scores * EXP2_SCALE - top * EXP2_SCALE).astype(LOW)
            keep = jnp.exp2((before - top) * EXP2_SCALE)
            oacc[:, span] = oacc[:, span] * keep + nn(vaug[...], weights)
            return carry

        lax.fori_loop(0, shape.queries // block, one, 0)

    def column_step(k, carry):
        source = paired(z, k, heads)

        @pl.when(k > 0)
        def _():
            send_dp(rkv.at[source, g], rkv.at[source, g], k_send.at[source], k_recv.at[source], me).wait_recv()
            for n, mate in enumerate(mates):
                send_dp(
                    rkv.at[source, g], rkv.at[source, g], x_send.at[source, n], x_recv.at[source, g],
                    z * group + mate,
                ).start()

        chunk(source, g)

        @pl.when(k != 1)
        def _():
            mates_of(jnp.maximum(k - 1, 0))

        return carry

    def mates_of(k):
        source = paired(z, k, heads)

        def mate_step(n, inner):
            mate = lax.rem(g + n, group)
            send_dp(
                rkv.at[source, mate], rkv.at[source, mate], x_send.at[source, 0], x_recv.at[source, mate], me
            ).wait_recv()
            chunk(source, mate)
            return inner

        lax.fori_loop(1, group, mate_step, 0)

    lax.fori_loop(0, heads, column_step, 0)
    if heads > 1:
        mates_of(heads - 1)
    keep_kv = pltpu.make_async_copy(rkv, kv_out, o_sem)
    keep_kv.start()

    def finish(k, carry):
        source = paired(z, lax.rem(k, heads), heads)
        span = pl.ds(pl.multiple_of(source * rows, rows), rows)
        total = oacc[pl.ds(HEAD, 1), span]
        attended = oacc[pl.ds(0, HEAD), span] / total
        o_out[:, span] = attended
        lse_out[:, span] = mrow[:, span] + jnp.log2(total) * (1.0 / EXP2_SCALE)
        att_s[source] = attended.astype(LOW)

        @pl.when(source != z)
        def _():
            send_dp(
                att_s.at[source], att_r.at[z], r_send.at[source], r_recv.at[z], source * group + g
            ).start()

        return carry

    saves[1].start()
    lax.fori_loop(1, heads + 1, finish, 0)
    saves[4].start()
    saves[5].start()
    att[z] = att_s[z]
    peak_out[...] = jnp.full(peak_out.shape, jnp.max(lpk[...]) * SCALE, F32)
    saves[6].start()
    for h in column:
        send_dp(att_s.at[h], att_r.at[h], r_send.at[h], r_recv.at[h], h * group + g).wait()
        att[h] = att_r[h]
    saves[0].start()
    for copy in sends:
        copy.wait_send()
    for source in range(heads):
        for n, mate in enumerate(mates):
            send_dp(
                rkv.at[source, g], rkv.at[source, g], x_send.at[source, n], x_recv.at[source, g],
                z * group + mate,
            ).wait_send()
    keep_kv.wait()


def attend(shape, tokens, weights, listed, rows_t, cols_t):
    heads, group, rows, queries = shape.heads, shape.group, shape.rows, shape.queries
    width, local = tokens.shape[1], heads * HEAD
    args = (tokens, weights, *listed, rows_t, cols_t)
    devices = heads * group
    owned = width // devices
    piece = 32 if owned % 32 == 0 else owned
    vmem = pl.BlockSpec(memory_space=pltpu.VMEM)
    hbm = pl.BlockSpec(memory_space=pl.ANY)
    dma = pltpu.SemaphoreType.DMA
    outs = (
        jax.ShapeDtypeStruct((heads, HEAD, rows), LOW),
        jax.ShapeDtypeStruct((AUG, queries), LOW),
        jax.ShapeDtypeStruct((SIDE // 8, 16, queries), LOW),
        jax.ShapeDtypeStruct((heads, group, 2, HEAD, rows), LOW),
        jax.ShapeDtypeStruct((HEAD, queries), F32),
        jax.ShapeDtypeStruct((1, queries), F32),
        jax.ShapeDtypeStruct((8, 128), F32),
        jax.ShapeDtypeStruct((owned // piece, devices, piece, rows), LOW),
        jax.ShapeDtypeStruct((2, 2 * SIDE, HEAD), LOW),
        jax.ShapeDtypeStruct((16, width), F32),
    )
    return pl.pallas_call(
        functools.partial(forward_kernel, shape, len(args), len(outs)),
        out_shape=outs,
        in_specs=[pl.BlockSpec(memory_space=pltpu.HBM)] * len(args),
        out_specs=(hbm,) * len(outs),
        scratch_shapes=[
            *[pltpu.VMEM(each.shape, each.dtype) for each in args],
            dma((len(args),)),
            dma((len(outs),)),
            *[pltpu.VMEM(each.shape, each.dtype) for n, each in enumerate(outs) if n != 3],
            pltpu.VMEM((rows, width), LOW),
            pltpu.VMEM((3, local, rows), LOW),
            pltpu.VMEM((2, 128, 2 * SIDE), LOW),
            pltpu.VMEM((heads, HEAD, rows), LOW),
            pltpu.VMEM((heads, group, 2, HEAD, rows), LOW),
            pltpu.VMEM((AUG, rows), LOW),
            pltpu.VMEM((rows, AUG), LOW),
            pltpu.VMEM((HEAD + 16, rows), LOW),
            pltpu.VMEM((HEAD + 16, queries), F32),
            pltpu.VMEM((1, queries), F32),
            pltpu.VMEM((8, shape.block), F32),
            pltpu.VMEM((heads, HEAD, rows), LOW),
            pltpu.VMEM((heads, HEAD, rows), LOW),
            dma((heads,)), dma((heads,)), dma((heads,)), dma((heads,)),
            dma((heads, group)), dma((heads, group)), dma((heads,)), dma((heads,)),
            dma,
        ],
        compiler_params=pltpu.CompilerParams(
            collective_id=1, has_side_effects=True, vmem_limit_bytes=VMEM_LIMIT["attend"]
        ),
        name="attend",
    )(*args)


def backward_kernel(
    shape, ga, tables, qaug_in, bias_rows, rkv, o_in, lse_in, fc2_state, fc1, mlp, values, vectors, proj,
    grads, table_grads, first_state, fc2_out, fc1_state, output, proj_state,
    rdo, qaug, q_tok, do_aug, do_tok, kaug_t, kaug, vaug_t, vaug, kacc, vacc, dq, drow, dcol,
    part, xr, summed, gq_s, gq_r, gkv_r,
    d_send, d_recv, x_send, x_recv, kv_send, kv_recv, q_send, q_recv, *rest,
):
    chunks = fc1.shape[1]
    rest = list(rest)

    def taken(number):
        found, rest[:] = rest[:number], rest[number:]
        return found

    bits = halve_bits()
    orders = [near_first(), far_first(shape.group)]
    moved2 = [
        Halve(orders[n], fc2_state.at[n], taken(3 * (bits - 2)), first=2) for n in range(chunks)
    ]
    moved0 = Halve(far_first(shape.group), proj, taken(3), last=0)
    outs = taken(1)[0]
    lines = lax.axis_size("tensor") // 2
    sum_mlp = Reduce(mlp, *taken(7))
    all_out = Gather(outs, *taken(3))
    line = tensor_place()[1]
    moved1 = [Halve(near_first(), fc1.at[:, 0], taken(8), last=1, own=True)]
    if chunks > 1:
        moved1 += [Halve(near_first(), fc1.at[:, 1], taken(5), last=0, own=True)]
    heads, group, rows, block = shape.heads, shape.group, shape.rows, shape.block
    queries = shape.queries
    me = lax.axis_index("dp")
    z, g = me // group, lax.rem(me, group)
    column = [paired(z, k, heads) for k in range(1, heads)]
    mates = [lax.rem(g + k, group) for k in range(1, group)]
    greet_all(Ring(heads))
    for other in sum_mlp.others() + [line]:
        sum_mlp.give(other)
    sends = []
    for h in column:
        copy = send_dp(ga.at[h], rdo.at[z], d_send.at[h], d_recv.at[z], h * group + g)
        copy.start()
        sends.append(copy)
    moved1[0].start()
    for each in moved1:
        each.load()
    rdo[z] = ga[z]
    qaug[...] = qaug_in[...]
    ones = jnp.where(lax.broadcasted_iota(jnp.int32, (16, rows), 0) < 3, 1.0, 0.0).astype(LOW)
    kaug_t[pl.ds(LSE_AT, 16), :] = ones
    vaug_t[pl.ds(HEAD, 16), :] = ones
    vaug_t[pl.ds(HEAD + 16, 32), :] = jnp.zeros((32, rows), LOW)
    low_lse = parts_of(-lse_in[...], 3)
    qaug[pl.ds(LSE_AT, 16), :] = jnp.concatenate(
        low_lse + [jnp.zeros((13, queries), F32)], axis=0
    ).astype(LOW)
    dq[...] = jnp.zeros_like(dq)
    dcol[...] = jnp.zeros_like(dcol)
    drow[...] = jnp.zeros_like(drow)

    def prepare(k, carry):
        source = paired(z, k, heads)
        span = pl.ds(pl.multiple_of(source * rows, rows), rows)

        @pl.when(k > 0)
        def _():
            send_dp(rdo.at[source], rdo.at[source], d_send.at[source], d_recv.at[source], me).wait_recv()

        upstream = rdo[source]
        dots = jnp.sum(upstream.astype(F32) * o_in[:, span], axis=0, keepdims=True)
        low_dots = parts_of(-dots, 3)
        do_aug[pl.ds(0, HEAD), span] = upstream
        do_aug[pl.ds(HEAD, 16), span] = jnp.concatenate(
            low_dots + [jnp.zeros((13, rows), F32)], axis=0
        ).astype(LOW)
        do_aug[pl.ds(HEAD + 16, 32), span] = jnp.zeros((32, rows), LOW)
        do_tok[span, :] = do_aug[:, span].T
        q_tok[span, :] = qaug[pl.ds(0, 128), span].T
        return carry

    lax.fori_loop(0, heads, prepare, 0)
    for other in sum_mlp.others():
        sum_mlp.pass_on(other)
    moved0.start()
    for each in moved2:
        each.start()

    def chunk(source, mate):
        dev = source * group + mate
        at = (dev * (rows // SIDE)) // 8
        cols, in_group = key_onehots(rows, dev)
        kaug_t[pl.ds(0, HEAD), :] = rkv[source, mate, 0]
        kaug_t[pl.ds(COLS_AT, 2 * SIDE), :] = cols.astype(LOW)
        kaug_t[pl.ds(ROWS_AT, 16), :] = in_group.astype(LOW)
        kaug[...] = kaug_t[...].T
        vaug_t[pl.ds(0, HEAD), :] = rkv[source, mate, 1]
        vaug[...] = vaug_t[...].T
        qaug[pl.ds(ROWS_AT, 16), :] = bias_rows[at]
        kacc[...] = jnp.zeros_like(kacc)
        vacc[...] = jnp.zeros_like(vacc)
        back = jnp.concatenate(
            [kaug_t[pl.ds(0, COLS_AT + SIDE), :], kaug_t[pl.ds(ROWS_AT, 16), :]], axis=0
        )

        def one(i, carry):
            span = pl.ds(pl.multiple_of(i * block, block), block)
            probs = jnp.exp2(nn(kaug[...], qaug[:, span]) * EXP2_SCALE)
            pulled = nn(vaug[...], do_aug[:, span])
            low_grads = (probs * pulled).astype(LOW)
            vacc[...] += nn(probs.astype(LOW), do_tok[span, :])
            kacc[...] += nn(low_grads, q_tok[span, :])
            found = nn(back, low_grads)
            dq[:, span] += found[:HEAD]
            dcol[:, span] += found[COLS_AT : COLS_AT + SIDE]
            drow[at, :, span] += found[COLS_AT + SIDE : COLS_AT + SIDE + 8]
            return carry

        lax.fori_loop(0, queries // block, one, 0)

    def put(where, extra):
        key_part = (kacc[...] * SCALE).T[:HEAD]
        value_part = vacc[...].T[:HEAD]
        for other in extra:
            key_part = key_part + other[0].astype(F32)
            value_part = value_part + other[1].astype(F32)
        where[0] = key_part.astype(LOW)
        where[1] = value_part.astype(LOW)

    def mate_copy(source, mate):
        return send_dp(
            part.at[source, mate], xr.at[source, g], x_send.at[source, mate], x_recv.at[source, g],
            z * group + mate,
        )

    def mates_step(k, carry):
        source = paired(z, lax.rem(k, heads), heads)

        def mate_step(n, inner):
            mate = lax.rem(g + n, group)
            chunk(source, mate)
            put(part.at[source, mate], [])
            mate_copy(source, mate).start()
            return inner

        lax.fori_loop(1, group, mate_step, 0)

        return carry

    lax.fori_loop(1, heads + 1, mates_step, 0)
    if chunks > 1:
        moved1[1].start()
    spot = lax.axis_index("tensor")
    outs[spot] = (values[...] + sum_mlp.total() + vectors[3:4]).astype(LOW)
    all_out.start()
    moved1[0].loaded()
    moved1[0].run(0)

    def own_step(k, carry):
        source = paired(z, lax.rem(k, heads), heads)
        chunk(source, g)
        extra = []
        for mate in mates:
            send_dp(
                xr.at[source, mate], xr.at[source, mate], x_send.at[source, mate], x_recv.at[source, mate], me
            ).wait_recv()
            extra.append(xr.at[source, mate])
        put(summed.at[source], extra)

        @pl.when(source != z)
        def _():
            send_dp(
                summed.at[source], gkv_r.at[z], kv_send.at[source], kv_recv.at[z], source * group + g
            ).start()

        return carry

    lax.fori_loop(1, heads + 1, own_step, 0)
    for other in all_out.others():
        all_out.forward(other)
    table_grads[...] = jnp.zeros_like(table_grads)

    def finish(k, carry):
        source = paired(z, lax.rem(k, heads), heads)
        span = pl.ds(pl.multiple_of(source * rows, rows), rows)
        by_row, by_col = shifts(rows, source * group + g)
        total = dq[:, span] * SCALE
        for n, held in enumerate((drow[:, :, span].reshape(SIDE, rows), dcol[:, span])):
            spread = unskew(held, by_col if n else by_row)
            for piece in parts_of(spread, 2):
                low_piece = piece.astype(LOW)
                total = total + tn(tables[n], low_piece)
                table_grads[n] += nn(low_piece, q_tok[span, :])
        gq_s[source] = total.astype(LOW)

        @pl.when(source != z)
        def _():
            send_dp(
                gq_s.at[source], gq_r.at[z], q_send.at[source], q_recv.at[z], source * group + g
            ).start()

        return carry

    lax.fori_loop(1, heads + 1, finish, 0)
    moved1[0].run(1)
    for stage in range(2, halve_bits() - 1):
        for each in moved2:
            each.run(stage)
    found = [each.total() for each in moved2]
    fc2_out[...] = jnp.concatenate(found, axis=0) if chunks > 1 else found[0]
    first_state[...] = moved1[0].stages[1][0][...]
    if chunks > 1:
        moved1[1].loaded()
        moved1[1].run(0)
        fc1_state[...] = moved1[1].stages[0][0][...]
    moved0.run(0)
    proj_state[...] = moved0.stages[0][0][...]
    for other in all_out.others() + [line]:
        all_out.take(other)
    output[...] = outs[...]
    grads[z, 0] = gq_s[z]
    grads[z, pl.ds(1, 2)] = summed[z]
    for h in column:
        send_dp(summed.at[h], gkv_r.at[h], kv_send.at[h], kv_recv.at[h], h * group + g).wait()
        grads[h, pl.ds(1, 2)] = gkv_r[h]
    for h in column:
        send_dp(gq_s.at[h], gq_r.at[h], q_send.at[h], q_recv.at[h], h * group + g).wait()
        grads[h, 0] = gq_r[h]
    for copy in sends:
        copy.wait_send()
    for source in range(heads):
        for mate in mates:
            mate_copy(source, mate).wait_send()
    for each in moved1 + moved2 + [sum_mlp, all_out, moved0]:
        each.finish()


def attend_back(shape, ga, tables, qaug, bias_rows, kv, o_rows, lse, fc2_state, fc1, mlp, values, vectors, proj):
    count, share, width = mlp.shape
    devices, chunks, owned, hidden = fc1.shape
    hbm = pl.BlockSpec(memory_space=pl.ANY)
    moving = halve_bufs(owned, hidden, first=2) * chunks
    moving += halve_bufs(chunks * owned, proj.shape[2], last=0)
    moving += [pltpu.VMEM((count, share, width), LOW)]
    moving += part_bufs(count // 2, share, width) + gather_sems(count // 2)
    moving += halve_bufs(owned, hidden, last=1, own=True)
    if chunks > 1:
        moving += halve_bufs(owned, hidden, last=0, own=True)
    heads, group, rows, queries = shape.heads, shape.group, shape.rows, shape.queries
    vmem = pl.BlockSpec(memory_space=pltpu.VMEM)
    dma = pltpu.SemaphoreType.DMA
    return pl.pallas_call(
        functools.partial(backward_kernel, shape),
        out_shape=(
            jax.ShapeDtypeStruct((heads, 3, HEAD, rows), LOW),
            jax.ShapeDtypeStruct((2, 2 * SIDE, 128), F32),
            jax.ShapeDtypeStruct((devices // 4, owned, hidden), LOW),
            jax.ShapeDtypeStruct((chunks * owned, hidden), F32),
            jax.ShapeDtypeStruct((devices // 2, owned, hidden), LOW),
            jax.ShapeDtypeStruct((count, share, width), LOW),
            jax.ShapeDtypeStruct((devices // 2,) + proj.shape[1:], LOW),
        ),
        in_specs=[vmem] * 8 + [hbm] + [vmem] * 4,
        out_specs=(vmem,) * 7,
        scratch_shapes=[
            pltpu.VMEM((heads, HEAD, rows), LOW),
            pltpu.VMEM((AUG, queries), LOW),
            pltpu.VMEM((queries, 128), LOW),
            pltpu.VMEM((128, queries), LOW),
            pltpu.VMEM((queries, 128), LOW),
            pltpu.VMEM((AUG, rows), LOW),
            pltpu.VMEM((rows, AUG), LOW),
            pltpu.VMEM((128, rows), LOW),
            pltpu.VMEM((rows, 128), LOW),
            pltpu.VMEM((rows, 128), F32),
            pltpu.VMEM((rows, 128), F32),
            pltpu.VMEM((HEAD, queries), F32),
            pltpu.VMEM((SIDE // 8, 8, queries), F32),
            pltpu.VMEM((SIDE, queries), F32),
            pltpu.VMEM((heads, group, 2, HEAD, rows), LOW),
            pltpu.VMEM((heads, group, 2, HEAD, rows), LOW),
            pltpu.VMEM((heads, 2, HEAD, rows), LOW),
            pltpu.VMEM((heads, HEAD, rows), LOW),
            pltpu.VMEM((heads, HEAD, rows), LOW),
            pltpu.VMEM((heads, 2, HEAD, rows), LOW),
            dma((heads,)), dma((heads,)), dma((heads, group)), dma((heads, group)),
            dma((heads,)), dma((heads,)), dma((heads,)), dma((heads,)),
        ] + moving,
        compiler_params=pltpu.CompilerParams(
            collective_id=2, has_side_effects=True, vmem_limit_bytes=VMEM_LIMIT["attend_back"]
        ),
        name="attend_back",
    )(ga, tables, qaug, bias_rows, kv, o_rows, lse, fc2_state, fc1, mlp, values, vectors, proj)


def send_tensor(src, dst, send_sem, recv_sem, dev):
    return pltpu.make_async_remote_copy(
        src_ref=src,
        dst_ref=dst,
        send_sem=send_sem,
        recv_sem=recv_sem,
        device_id={"tensor": dev},
        device_id_type=MESH,
    )


def tensor_place():
    me = lax.axis_index("tensor")
    return lax.rem(me, 2), me // 2, lax.axis_size("tensor") // 2


def tensor_peers():
    core, line, lines = tensor_place()
    far = [lax.rem(line + k, lines) * 2 + core for k in range(1, lines)]
    return far + [line * 2 + 1 - core]


def part_bufs(lines, share, width, dtype=LOW):
    dma = pltpu.SemaphoreType.DMA
    return [pltpu.VMEM((lines, share, width), dtype)] * 3 + [dma((lines,))] * 4


class Reduce:
    def __init__(self, part, mate_in, passed, line_in, m_send, m_recv, l_send, l_recv):
        self.part, self.mate_in, self.passed, self.line_in = part, mate_in, passed, line_in
        self.sems = m_send, m_recv, l_send, l_recv
        self.core, self.line, self.lines = tensor_place()

    def mate_copy(self, to):
        m_send, m_recv, _, _ = self.sems
        return send_tensor(
            self.part.at[to * 2 + 1 - self.core], self.mate_in.at[to],
            m_send.at[to], m_recv.at[to], self.line * 2 + 1 - self.core,
        )

    def line_copy(self, to, slot):
        _, _, l_send, l_recv = self.sems
        return send_tensor(
            self.passed.at[to], self.line_in.at[slot], l_send.at[to], l_recv.at[slot],
            to * 2 + self.core,
        )

    def give(self, to):
        self.mate_copy(to).start()

    def pass_on(self, to):
        self.mate_copy(to).wait_recv()
        both = self.part[to * 2 + self.core].astype(F32) + self.mate_in[to].astype(F32)
        self.passed[to] = both.astype(self.passed.dtype)
        self.line_copy(to, self.line).start()

    def others(self):
        return [lax.rem(self.line + k, self.lines) for k in range(1, self.lines)]

    def total(self):
        self.mate_copy(self.line).wait_recv()
        total = self.part[self.line * 2 + self.core].astype(F32) + self.mate_in[self.line].astype(F32)
        for other in self.others():
            self.line_copy(other, other).wait_recv()
            total = total + self.line_in[other].astype(F32)
        return total

    def finish(self):
        self.mate_copy(self.line).wait_send()
        for other in self.others():
            self.mate_copy(other).wait_send()
            self.line_copy(other, self.line).wait_send()


def gather_sems(lines):
    dma = pltpu.SemaphoreType.DMA
    return [dma((lines,)), dma((lines,)), dma((2 * lines,))]


class Gather:
    def __init__(self, whole, l_send, m_send, recv):
        self.whole, self.sems = whole, (l_send, m_send, recv)
        self.core, self.line, self.lines = tensor_place()

    def line_copy(self, to):
        l_send, _, recv = self.sems
        own = self.line * 2 + self.core
        return send_tensor(
            self.whole.at[own], self.whole.at[own], l_send.at[to], recv.at[own], to * 2 + self.core
        )

    def mate_copy(self, at):
        _, m_send, recv = self.sems
        part = at * 2 + self.core
        return send_tensor(
            self.whole.at[part], self.whole.at[part], m_send.at[at], recv.at[part],
            self.line * 2 + 1 - self.core,
        )

    def arrived(self, part):
        l_send, _, recv = self.sems
        send_tensor(
            self.whole.at[part], self.whole.at[part], l_send.at[0], recv.at[part], part
        ).wait_recv()

    def others(self):
        return [lax.rem(self.line + k, self.lines) for k in range(1, self.lines)]

    def start(self):
        for other in self.others():
            self.line_copy(other).start()
        self.mate_copy(self.line).start()

    def forward(self, at):
        self.arrived(at * 2 + self.core)
        self.mate_copy(at).start()

    def take(self, at):
        self.arrived(at * 2 + 1 - self.core)

    def finish(self):
        self.mate_copy(self.line).wait_send()
        for other in self.others():
            self.mate_copy(other).wait_send()
            self.line_copy(other).wait_send()


def normed(values):
    center = values - jnp.mean(values, axis=-1, keepdims=True)
    variance = jnp.mean(center * center, axis=-1, keepdims=True)
    inverse = lax.rsqrt(variance + EPSILON)
    return center * inverse, inverse


def normed_back(upstream, scaled, inverse, gain):
    weighted = upstream * gain
    centered = weighted - jnp.mean(weighted, axis=-1, keepdims=True)
    return (centered - scaled * jnp.mean(weighted * scaled, axis=-1, keepdims=True)) * inverse


def tile_of(width):
    return 256 if width % 256 == 0 else 128


class Ring:
    def __init__(self, heads):
        self.heads, self.group = heads, lax.axis_size("dp") // heads
        me = lax.axis_index("dp")
        self.z, self.g = me // self.group, lax.rem(me, self.group)

    def column(self):
        return [paired(self.z, k, self.heads) for k in range(1, self.heads)]

    def mates(self):
        return [lax.rem(self.g + k, self.group) for k in range(1, self.group)]

    def peers(self):
        far = [h * self.group + self.g for h in self.column()]
        return far + [self.z * self.group + o for o in self.mates()]


def greet_all(ring):
    barrier = pltpu.get_barrier_semaphore()
    near, far = tensor_peers(), ring.peers()
    for peer in near:
        pl.semaphore_signal(barrier, inc=1, device_id={"tensor": peer}, device_id_type=MESH)
    for peer in far:
        pl.semaphore_signal(barrier, inc=1, device_id={"dp": peer}, device_id_type=MESH)
    pl.semaphore_wait(barrier, len(near) + len(far))


def halve_bits():
    return (lax.axis_size("dp") - 1).bit_length()


def near_first():
    return tuple(range(halve_bits()))


def far_first(group):
    first = group.bit_length() - 1
    return (first,) + tuple(bit for bit in range(halve_bits()) if bit != first)


def halve_bufs(share, width, first=0, last=None, own=False):
    bits = halve_bits()
    last = bits - 1 if last is None else last
    dma = pltpu.SemaphoreType.DMA
    found = []
    if own:
        found += [pltpu.VMEM((1 << (bits - 1), share, width), LOW), dma]
    for stage in range(first, last + 1):
        count = 1 << (bits - 1 - stage)
        found += [pltpu.VMEM((count, share, width), LOW), dma((count,)), dma((count,))]
    return found


class Halve:
    def __init__(self, order, source, bufs, first=0, last=None, own=False):
        self.order, self.source, self.first = order, source, first
        self.last = len(order) - 1 if last is None else last
        bufs = list(bufs)
        self.own = bufs[0:2] if own else None
        bufs = bufs[2:] if own else bufs
        self.stages = {first + n: bufs[3 * n : 3 * n + 3] for n in range(len(bufs) // 3)}
        self.me = lax.axis_index("dp")

    def bit(self, stage):
        return lax.rem(self.me // (1 << self.order[stage]), 2)

    def count(self, stage):
        return 1 << (len(self.order) - 1 - stage)

    def index(self, stage, at, bit):
        if stage > 0:
            return at * 2 + bit
        place = bit * (1 << self.order[0])
        for n, other in enumerate(self.order[1:]):
            place = place + lax.rem(at // (1 << n), 2) * (1 << other)
        return place

    def held(self, stage):
        return self.source if stage == self.first else self.stages[stage - 1][0]

    def copy(self, stage, at):
        bit = self.bit(stage)
        into, send, recv = self.stages[stage]
        return send_dp(
            self.held(stage).at[self.index(stage, at, 1 - bit)], into.at[at],
            send.at[at], recv.at[at], self.me + (1 - 2 * bit) * (1 << self.order[stage]),
        )

    def spots(self, stage):
        if stage == len(self.order) - 1:
            return [0]
        bit, half = self.bit(stage + 1), self.count(stage) // 2
        return [n * 2 + 1 - bit for n in range(half)] + [n * 2 + bit for n in range(half)]

    def load(self):
        for at in range(self.count(0)):
            pltpu.make_async_copy(
                self.source.at[self.index(0, at, self.bit(0))], self.own[0].at[at], self.own[1]
            ).start()

    def loaded(self):
        pltpu.make_async_copy(
            self.source.at[pl.ds(0, self.count(0))], self.own[0], self.own[1]
        ).wait()

    def start(self, only=slice(None)):
        for at in self.spots(self.first)[only]:
            self.copy(self.first, at).start()

    def kept(self, stage, at):
        if stage == self.first and self.own is not None:
            return self.own[0][at].astype(F32)
        return self.held(stage)[self.index(stage, at, self.bit(stage))].astype(F32)

    def sum_at(self, stage, at):
        self.copy(stage, at).wait_recv()
        return self.kept(stage, at) + self.stages[stage][0][at].astype(F32)

    def run(self, stage):
        for n, at in enumerate(self.spots(stage)):
            self.stages[stage][0][at] = self.sum_at(stage, at).astype(LOW)
            if stage < self.last and n < self.count(stage) // 2:
                self.copy(stage + 1, n).start()

    def total(self):
        return self.sum_at(self.last, 0)

    def finish(self):
        for stage in self.stages:
            for at in range(self.count(stage)):
                self.copy(stage, at).wait_send()


def middle_kernel(
    heads, att, proj_w, tokens, cot, fc1_hbm, fc2_hbm, vectors,
    mlp, values_out, middle_out, fc1_out, proj_out, ga_out, fc1_bias_out, sums_out, fc2_state,
    fc1, fc2, att_tok, branch, back, n2, act, gu, gb, held, spread,
    wide, load1, load2, *rest,
):
    core, line, lines = tensor_place()
    me = lax.axis_index("tensor")
    _, share, width = tokens.shape
    rows = tokens.shape[0] * share
    local, hidden = proj_w.shape[0], fc1_hbm.shape[1]
    step, dstep = tile_of(hidden), tile_of(width)
    in_fc1 = pltpu.make_async_copy(fc1_hbm, fc1, load1)
    in_fc2 = pltpu.make_async_copy(fc2_hbm, fc2, load2)
    in_fc1.start()
    in_fc2.start()
    greet_all(Ring(heads))
    sum_branch = Reduce(branch, *rest[0:7])
    sum_back = Reduce(back, *rest[7:14])
    all_n2 = Gather(n2, *rest[14:17])
    all_gb = Gather(gb, *rest[17:20])
    blocks2, blocks1, fc1_sem = rest[20:23]
    devices, chunks, owned, _ = blocks2.shape
    orders = [near_first(), far_first(lax.axis_size("dp") // heads)]
    moved = [
        Halve(orders[n], blocks2.at[:, n], rest[23 + 6 * n : 29 + 6 * n], last=1)
        for n in range(chunks)
    ]
    att_tok[...] = att[...].T.reshape(att_tok.shape)

    def project(k, carry):
        to = lax.rem(line + 1 + lax.rem(k, lines), lines)
        part = to * 2 + jnp.where(k < lines, 1 - core, core)
        branch[part] = nn(att_tok[part], proj_w[...]).astype(LOW)

        @pl.when(k < lines)
        def _():
            sum_branch.give(to)

        return carry

    lax.fori_loop(0, 2 * lines, project, 0)
    for other in sum_branch.others():
        sum_branch.pass_on(other)
    middle = tokens[me].astype(F32) + vectors[0:1]
    middle = middle + sum_branch.total()
    scaled, inverse = normed(middle)
    n2[me] = (scaled * vectors[1:2] + vectors[2:3]).astype(LOW)
    all_n2.start()
    values_out[...] = middle
    held[...] = scaled
    spread[...] = jnp.broadcast_to(inverse, spread.shape)
    fc1_bias_out[...] = jnp.zeros_like(fc1_bias_out)
    in_fc1.wait()
    in_fc2.wait()

    def hidden_part(k, carry):
        at = lax.rem(line + k, lines)

        @pl.when(k > 0)
        def _():
            all_n2.forward(at)

        all_n2.take(at)
        pair = pl.ds(at * 2, 2)
        inputs = n2[pair].reshape(2 * share, width)
        pulls = cot[pair].reshape(2 * share, width)

        def tile(n, inner):
            span = pl.ds(pl.multiple_of(n * step, step), step)
            up = nn(inputs, fc1[:, span]) + vectors[6:7, span]
            phi = 0.5 + 0.5 * lax.erf(up * math.sqrt(0.5))
            slope = phi + up * (jnp.exp(-0.5 * up * up) * (2 * math.pi) ** -0.5)
            act[pair, :, span] = (up * phi).astype(LOW).reshape(2, share, step)
            grad_up = (nt(pulls, fc2[span, :]) * slope).astype(LOW)
            gu[pair, :, span] = grad_up.reshape(2, share, step)
            fc1_bias_out[:, span] += jnp.sum(grad_up.astype(F32), axis=0, keepdims=True)
            return inner

        lax.fori_loop(0, hidden // step, tile, 0)

        def tile_back(n, inner):
            span = pl.ds(pl.multiple_of(n * dstep, dstep), dstep)
            found = nt(gu[pair].reshape(2 * share, hidden), fc1[span, :])
            back[pair, :, span] = found.astype(LOW).reshape(2, share, dstep)
            return inner

        lax.fori_loop(0, width // dstep, tile_back, 0)
        sum_back.give(at)

        return carry

    lax.fori_loop(0, lines, hidden_part, 0)

    def weights2(n, carry):
        span = pl.ds(pl.multiple_of(n * dstep, dstep), dstep)
        found = tn(cot[:, :, span].reshape(rows, dstep), act[...].reshape(rows, hidden))
        wide[span, :] = found.astype(LOW)
        return carry

    lax.fori_loop(0, width // dstep, weights2, 0)
    for dev in range(devices):
        for chunk in range(chunks):
            at = (dev * chunks + chunk) * owned
            blocks2[dev, chunk] = wide[pl.ds(at, owned), :]
    for each in moved:
        each.start()
    for other in sum_back.others():
        sum_back.pass_on(other)

    def out_part(k, carry):
        at = lax.rem(line + 1 + k, lines)
        pair = pl.ds(at * 2, 2)

        def tile_out(n, inner):
            span = pl.ds(pl.multiple_of(n * dstep, dstep), dstep)
            found = nn(act[pair].reshape(2 * share, hidden), fc2[:, span])
            mlp[pair, :, span] = found.astype(LOW).reshape(2, share, dstep)
            return inner

        lax.fori_loop(0, width // dstep, tile_out, 0)
        return carry

    lax.fori_loop(0, lines, out_part, 0)

    def weights1(n, carry):
        span = pl.ds(pl.multiple_of(n * dstep, dstep), dstep)
        found = tn(n2[:, :, span].reshape(rows, dstep), gu[...].reshape(rows, hidden))
        wide[span, :] = found.astype(LOW)
        return carry

    lax.fori_loop(0, width // dstep, weights1, 0)
    for dev in range(devices):
        for chunk in range(chunks):
            at = (dev * chunks + chunk) * owned
            blocks1[dev, chunk] = wide[pl.ds(at, owned), :]
    keep_fc1 = pltpu.make_async_copy(blocks1, fc1_out, fc1_sem)
    keep_fc1.start()
    upstream = sum_back.total()
    sums_out[0:1] = jnp.sum(upstream * held[...], axis=0, keepdims=True)
    sums_out[1:2] = jnp.sum(upstream, axis=0, keepdims=True)
    grad_middle = cot[me].astype(F32) + normed_back(
        upstream, held[...], spread[:, :1], vectors[1:2]
    )
    middle_out[...] = grad_middle
    gb[me] = grad_middle.astype(LOW)
    all_gb.start()
    for each in moved:
        each.run(0)
    sums_out[2:3] = jnp.sum(cot[...].astype(F32).reshape(rows, width), axis=0, keepdims=True)
    for other in all_gb.others():
        all_gb.forward(other)
    all_gb.take(line)
    for other in all_gb.others():
        all_gb.take(other)
    whole = gb[...].reshape(rows, width)
    sums_out[3:4] = jnp.sum(whole.astype(F32), axis=0, keepdims=True)
    ga_out[...] = nt(proj_w[...], whole).astype(LOW)

    def weights0(n, carry):
        span = pl.ds(pl.multiple_of(n * dstep, dstep), dstep)
        found = tn(gb[:, :, span].reshape(rows, dstep), att_tok[...].reshape(rows, -1))
        wide[span, :local] = found.astype(LOW)
        return carry

    lax.fori_loop(0, width // dstep, weights0, 0)
    for dev in range(devices):
        proj_out[dev] = wide[pl.ds(dev * chunks * owned, chunks * owned), :local]
    for n, each in enumerate(moved):
        each.run(1)
        fc2_state[n] = each.stages[1][0][...]
    keep_fc1.wait()
    for each in (sum_branch, sum_back, all_n2, all_gb, *moved):
        each.finish()


def middle_block(heads, att, proj_w, tokens, cot, fc1, fc2, vectors):
    count = lax.axis_size("tensor")
    lines = count // 2
    local, width = proj_w.shape
    rows = tokens.shape[0]
    share = rows // count
    hidden = fc1.shape[1]
    vmem = pl.BlockSpec(memory_space=pltpu.VMEM)
    hbm = pl.BlockSpec(memory_space=pl.ANY)
    dma = pltpu.SemaphoreType.DMA
    whole = (count, share, width)
    devices = lax.axis_size("dp")
    owned = width // devices
    chunks = 2 if owned % 32 == 0 else 1
    weights = (devices, chunks, owned // chunks, hidden)
    scratch = [
        pltpu.VMEM((width, hidden), LOW),
        pltpu.VMEM((hidden, width), LOW),
        pltpu.VMEM((count, share, local), LOW),
        pltpu.VMEM(whole, LOW),
        pltpu.VMEM(whole, LOW),
        pltpu.VMEM(whole, LOW),
        pltpu.VMEM((count, share, hidden), LOW),
        pltpu.VMEM((count, share, hidden), LOW),
        pltpu.VMEM(whole, LOW),
        pltpu.VMEM((share, width), F32),
        pltpu.VMEM((share, 128), F32),
        pltpu.VMEM((width, hidden), LOW),
        dma,
        dma,
    ]
    scratch += part_bufs(lines, share, width) * 2 + gather_sems(lines) * 2
    scratch += [pltpu.VMEM(weights, LOW), pltpu.VMEM(weights, LOW), dma]
    scratch += halve_bufs(owned // chunks, hidden, last=1) * chunks
    return pl.pallas_call(
        functools.partial(middle_kernel, heads),
        out_shape=(
            jax.ShapeDtypeStruct(whole, LOW),
            jax.ShapeDtypeStruct((share, width), F32),
            jax.ShapeDtypeStruct((share, width), F32),
            jax.ShapeDtypeStruct(weights, LOW),
            jax.ShapeDtypeStruct((devices, owned, local), LOW),
            jax.ShapeDtypeStruct((local, rows), LOW),
            jax.ShapeDtypeStruct((1, hidden), F32),
            jax.ShapeDtypeStruct((8, width), F32),
            jax.ShapeDtypeStruct((chunks, devices // 4, owned // chunks, hidden), LOW),
        ),
        in_specs=[vmem] * 4 + [hbm] * 2 + [vmem],
        out_specs=(vmem,) * 3 + (hbm,) + (vmem,) * 5,
        scratch_shapes=scratch,
        compiler_params=pltpu.CompilerParams(
            collective_id=3, has_side_effects=True, vmem_limit_bytes=VMEM_LIMIT["middle"]
        ),
        name="middle",
    )(
        att, proj_w, tokens.reshape(whole), cot.reshape(whole), fc1, fc2, vectors,
    )


def small_bufs(heads, stages, shape):
    group, lines = lax.axis_size("dp") // heads, lax.axis_size("tensor") // 2
    dma = pltpu.SemaphoreType.DMA
    found = []
    for stage in stages:
        count = {"core": 2, "line": lines, "mate": group, "far": heads}[stage]
        found += [
            pltpu.VMEM(shape, F32), pltpu.VMEM((count,) + shape, F32), dma((count,)), dma((count,))
        ]
    return found


class Small:
    def __init__(self, ring, stages, merge, *bufs):
        self.ring, self.stages, self.merge = ring, stages, merge
        self.bufs = [bufs[4 * n : 4 * n + 4] for n in range(len(stages))]
        core, line, lines = tensor_place()
        self.peers = {
            "core": (core, [(1 - core, line * 2 + 1 - core)]),
            "line": (line, [(o, o * 2 + core) for o in [lax.rem(line + k, lines) for k in range(1, lines)]]),
            "mate": (ring.g, [(o, ring.z * ring.group + o) for o in ring.mates()]),
            "far": (ring.z, [(o, o * ring.group + ring.g) for o in ring.column()]),
        }

    def copy(self, n, slot, other, dev):
        value, held, send, recv = self.bufs[n]
        call = send_tensor if self.stages[n] in ("core", "line") else send_dp
        return call(value, held.at[slot], send.at[other], recv.at[slot], dev)

    def start(self, n, value):
        own, peers = self.peers[self.stages[n]]
        self.bufs[n][0][...] = value
        for other, dev in peers:
            self.copy(n, own, other, dev).start()

    def take(self, n):
        _, peers = self.peers[self.stages[n]]
        total = self.bufs[n][0][...]
        for other, dev in peers:
            self.copy(n, other, other, dev).wait_recv()
            total = self.merge(total, self.bufs[n][1][other])
        return total

    def step(self, n):
        self.start(n + 1, self.take(n))

    def finish(self):
        for n in range(len(self.stages)):
            own, peers = self.peers[self.stages[n]]
            for other, dev in peers:
                self.copy(n, own, other, dev).wait_send()


EVERY = ("core", "line", "far", "mate")
OVER_DP = ("mate", "far")


def add_peaks(a, b):
    row = lax.broadcasted_iota(jnp.int32, a.shape, 0)
    return jnp.where(row == 2, jnp.maximum(a, b), a + b)


def widen(row, width):
    if row.shape[1] == width:
        return row
    return jnp.concatenate([row, jnp.zeros((1, width - row.shape[1]), F32)], axis=1)


def tail_kernel(
    heads, grads, qkv_w, n1_t, tokens, grad_middle, vectors, tables, sums, fc1_bias, peak,
    proj, first_state, fc1_state,
    tokens_out, proj_out, fc1_out, qkv_out, tables_out, rows_out, clip_out,
    g_all, g_tok, part, gt, *rest,
):
    ring = Ring(heads)
    core, line, lines = tensor_place()
    me = lax.axis_index("tensor")
    count, share, width = tokens.shape
    rows = count * share
    local = heads * HEAD
    dstep = tile_of(width)
    pieces, devices, piece, _ = n1_t.shape
    chunks = 1 if pieces == 1 else 2
    rest = list(rest)

    def taken(number):
        found, rest[:] = rest[:number], rest[number:]
        return found

    greet_all(ring)
    blocks = [taken(1)[0] for _ in range(pieces)]
    moved3 = [Halve(near_first(), each, taken(3 * halve_bits())) for each in blocks]
    moved0 = Halve(far_first(ring.group), proj, taken(3 * (halve_bits() - 1)), first=1)
    moved1 = [Halve(near_first(), first_state, taken(3 * (halve_bits() - 2)), first=2)]
    if chunks > 1:
        moved1 += [Halve(near_first(), fc1_state, taken(3 * (halve_bits() - 1)), first=1)]
    sum_part = Reduce(part, *taken(7))
    all_gt = Gather(gt, *taken(3))
    pool, pooled = taken(2)
    sum_pool = Reduce(pool, *taken(7))
    all_pool = Gather(pooled, *taken(3))
    small_pool = Small(ring, OVER_DP, lax.add, *taken(8))
    small_late = Small(ring, EVERY, lax.add, *taken(16))
    small_dp = Small(ring, OVER_DP, add_peaks, *taken(8))
    pool[...] = tables[...].reshape(pool.shape)
    for other in sum_pool.others() + [line]:
        sum_pool.give(other)
    for each in moved1:
        each.start()
    moved0.start()
    for t in range(3):
        for h in range(heads):
            g_all[pl.ds(t * local + h * HEAD, HEAD), :] = grads[h, t]
    g_tok[...] = g_all[...].T.reshape(g_tok.shape)
    for other in sum_pool.others():
        sum_pool.pass_on(other)
    whole = g_tok[...].reshape(rows, 3 * local)
    lane = lax.broadcasted_iota(jnp.int32, (1, width), 1)
    peaks = jnp.where(lane == ring.z, peak[0:1, 0:1], -jnp.inf)
    bias_sums = nn(jnp.ones((8, rows), LOW), whole)[0:1]
    dp_rows = [widen(fc1_bias[...], width), widen(bias_sums, width), peaks]
    small_dp.start(0, jnp.concatenate(dp_rows + [jnp.zeros((5, width), F32)], axis=0))

    for n in range(pieces):
        found = nn(
            n1_t[n].reshape(devices * piece, rows), g_tok[...].reshape(rows, 3 * local)
        )
        blocks[n][...] = found.astype(LOW).reshape(devices, piece, 3 * local)
        if n == min(1, pieces - 1):
            small_pool.start(0, sum_pool.total())
        moved3[n].start()

    def norm_part(k, carry):
        at = lax.rem(line + 1 + k, lines)
        pair = pl.ds(at * 2, 2)

        def tile(n, inner):
            span = pl.ds(pl.multiple_of(n * dstep, dstep), dstep)
            found = nn(g_tok[pair].reshape(2 * share, 3 * local), qkv_w[:, span])
            part[pair, :, span] = found.astype(LOW).reshape(2, share, dstep)
            return inner

        lax.fori_loop(0, width // dstep, tile, 0)
        sum_part.give(at)
        return carry

    lax.fori_loop(0, lines, norm_part, 0)
    for other in sum_part.others():
        sum_part.pass_on(other)
    scaled, inverse = normed(tokens[me].astype(F32))
    small_pool.step(0)
    moved0.run(1)
    for each in moved1[1:]:
        each.run(1)
    moved3[0].run(0)
    for each in moved3[1:2]:
        each.run(0)
    moved3[0].run(1)
    upstream = sum_part.total()
    late = [
        sums[0:4],
        jnp.sum(upstream * scaled, axis=0, keepdims=True),
        jnp.sum(upstream, axis=0, keepdims=True),
        jnp.zeros((2, width), F32),
    ]
    small_late.start(0, jnp.concatenate(late, axis=0))
    found = grad_middle[...] + normed_back(upstream, scaled, inverse, vectors[4:5])
    gt[me] = found.astype(LOW)
    all_gt.start()
    pooled[me] = small_pool.take(1)
    all_pool.start()
    small_dp.step(0)
    for n, each in enumerate(moved3[2:]):
        each.run(0)
        if n == 0:
            small_late.step(0)
        if n == 1:
            small_late.step(1)
            for other in all_gt.others():
                all_gt.forward(other)
            for other in all_pool.others():
                all_pool.forward(other)
        moved3[n + 1].run(1)
    if pieces < 4:
        for n in range(max(pieces - 2, 0), 2):
            small_late.step(n)
        for other in all_gt.others():
            all_gt.forward(other)
        for other in all_pool.others():
            all_pool.forward(other)
    small_late.step(2)
    dp_sum = small_dp.take(1)
    limit = vectors[9:10]
    factors = jnp.sqrt(limit / jnp.maximum(dp_sum[2:3], limit))
    lane = lax.broadcasted_iota(jnp.int32, (1, width), 1)
    clipped_bias = vectors[7:8]
    for h in range(heads):
        factor = factors[:, h : h + 1]
        own = (lane >= h * HEAD) & (lane < (h + 1) * HEAD)
        clipped_bias = jnp.where(own, clipped_bias * factor, clipped_bias)
        for t in range(2):
            span = pl.ds(t * local + h * HEAD, HEAD)
            clip_out[span, :] = (qkv_w[span, :].astype(F32) * factor).astype(LOW)
    rows_out[8:11] = dp_sum[0:3]
    rows_out[11:12] = factors
    rows_out[12:13] = clipped_bias
    rows_out[13:16] = jnp.zeros((3, width), F32)
    if pieces > 1:
        moved3[-1].run(1)
    for stage in range(2, halve_bits() - 1):
        for each in moved3 + [moved0] + moved1:
            each.run(stage)
    for other in all_gt.others() + [line]:
        all_gt.take(other)
    for other in all_pool.others() + [line]:
        all_pool.take(other)
    tokens_out[...] = gt[...]
    for n in range(2):
        turned_sums = pooled[...].reshape(2, 2 * SIDE, 128)[n].T[:HEAD]
        found = jnp.zeros((HEAD, 2 * SIDE), F32)
        for piece in parts_of(turned_sums, 3):
            found = found + nn(piece.astype(LOW), turned(2 * SIDE))
        tables_out[n] = found
    late = small_late.take(3)
    row = lax.broadcasted_iota(jnp.int32, late.shape, 0)
    rows_out[0:8] = jnp.where((row == 2) | (row == 3), late * (1.0 / count), late)
    owned = first_state.shape[1]
    for n, each in enumerate(moved1):
        fc1_out[pl.ds(n * owned, owned), :] = each.total()
    proj_out[...] = moved0.total()
    for n, each in enumerate(moved3):
        total = each.total()
        owned = total.shape[0]
        for t in range(3):
            qkv_out[t, pl.ds(n * owned, owned), :] = total[:, t * local : (t + 1) * local]
    for each in [
        moved0, sum_part, all_gt, sum_pool, all_pool, small_pool, small_late, small_dp,
    ] + moved3 + moved1:
        each.finish()


def tail(heads, grads, qkv_w, n1_t, tokens, grad_middle, vectors, tables, sums, fc1_bias, peak, proj, first_state, fc1_state):
    hidden = first_state.shape[2]
    count = lax.axis_size("tensor")
    lines = count // 2
    local = heads * HEAD
    pieces, devices, piece, rows = n1_t.shape
    width = devices * pieces * piece
    owned = first_state.shape[1]
    chunks = pieces * piece // owned
    share = rows // count
    vmem = pl.BlockSpec(memory_space=pltpu.VMEM)
    whole = (count, share, width)
    scratch = [
        pltpu.VMEM((3 * local, rows), LOW),
        pltpu.VMEM((count, share, 3 * local), LOW),
        pltpu.VMEM(whole, LOW),
        pltpu.VMEM(whole, LOW),
    ]
    scratch += [pltpu.VMEM((devices, piece, 3 * local), LOW)] * pieces
    scratch += halve_bufs(piece, 3 * local) * pieces
    scratch += halve_bufs(chunks * owned, local, first=1)
    scratch += halve_bufs(owned, hidden, first=2)
    if chunks > 1:
        scratch += halve_bufs(owned, hidden, first=1)
    scratch += part_bufs(lines, share, width) + gather_sems(lines)
    pool = (count, 4 * SIDE // count, 128)
    scratch += [pltpu.VMEM(pool, F32)] * 2
    scratch += part_bufs(lines, *pool[1:], F32) + gather_sems(lines)
    scratch += small_bufs(heads, OVER_DP, pool[1:])
    scratch += small_bufs(heads, EVERY, (8, width))
    scratch += small_bufs(heads, OVER_DP, (8, width))
    return pl.pallas_call(
        functools.partial(tail_kernel, heads),
        out_shape=(
            jax.ShapeDtypeStruct(whole, LOW),
            jax.ShapeDtypeStruct((chunks * owned, local), F32),
            jax.ShapeDtypeStruct((chunks * owned, hidden), F32),
            jax.ShapeDtypeStruct((3, chunks * owned, local), F32),
            jax.ShapeDtypeStruct((2, HEAD, 2 * SIDE), F32),
            jax.ShapeDtypeStruct((16, width), F32),
            jax.ShapeDtypeStruct((2 * local, width), LOW),
        ),
        in_specs=[vmem] * 13,
        out_specs=(vmem,) * 7,
        scratch_shapes=scratch,
        compiler_params=pltpu.CompilerParams(
            collective_id=4, has_side_effects=True, vmem_limit_bytes=VMEM_LIMIT["tail"]
        ),
        name="tail",
    )(
        grads, qkv_w, n1_t, tokens.reshape(whole), grad_middle, vectors, tables, sums, fc1_bias,
        peak, proj, first_state, fc1_state,
    )


def finish_kernel(count, *refs):
    large, (rows, tables), refs = refs[:count], refs[count : count + 2], refs[count + 2 :]
    outs, smalls_out, refs = refs[:count], refs[count : count + 13], refs[count + 13 :]
    stage, smalls, (sems_in, sems_out, sems_small) = refs[:count], refs[count : count + 13], refs[count + 13 :]
    into = [pltpu.make_async_copy(a, b, sems_in.at[n]) for n, (a, b) in enumerate(zip(large, stage))]
    out = [pltpu.make_async_copy(b, c, sems_out.at[n]) for n, (b, c) in enumerate(zip(stage, outs))]
    for copy in into:
        copy.start()
    gain1, shift1, qv, proj, by_row, by_col, gain2, shift2, fc1, fc2, clip_bias, peaks, factors = smalls
    picks = (
        (gain2, 0), (shift2, 1), (fc2, 2), (proj, 3), (gain1, 4), (shift1, 5), (fc1, 8),
        (peaks, 10), (factors, 11), (clip_bias, 12),
    )
    for ref, at in picks:
        ref[...] = rows[at : at + 1, : ref.shape[0]].reshape(ref.shape)
    local = qv.shape[1]
    qv[0:1] = rows[9:10, :local]
    qv[1:2] = rows[9:10, 2 * local : 3 * local]
    by_row[...] = tables[0, :, : by_row.shape[1]]
    by_col[...] = tables[1, :, : by_col.shape[1]]
    small = [
        pltpu.make_async_copy(a, b, sems_small.at[n]) for n, (a, b) in enumerate(zip(smalls, smalls_out))
    ]
    for copy, after in zip(into, out):
        copy.wait()
        after.start()
    for copy in small:
        copy.start()
    for copy in out + small:
        copy.wait()


def finish(large, rows, tables, hidden, local):
    width = rows.shape[1]
    heads = local // HEAD
    vmem = pl.BlockSpec(memory_space=pltpu.VMEM)
    hbm = pl.BlockSpec(memory_space=pl.ANY)
    count = len(large)
    shapes = [
        (width,), (width,), (2, local), (width,), (HEAD, 2 * SIDE - 1), (HEAD, 2 * SIDE - 1),
        (width,), (width,), (hidden,), (width,), (local,), (heads,), (heads,),
    ]
    return pl.pallas_call(
        functools.partial(finish_kernel, count),
        out_shape=[jax.ShapeDtypeStruct(each.shape, each.dtype) for each in large]
        + [jax.ShapeDtypeStruct(each, F32) for each in shapes],
        in_specs=[hbm] * count + [vmem] * 2,
        out_specs=[hbm] * (count + len(shapes)),
        scratch_shapes=[pltpu.VMEM(each.shape, each.dtype) for each in large]
        + [pltpu.VMEM(each, F32) for each in shapes]
        + [pltpu.SemaphoreType.DMA((count,))] * 2
        + [pltpu.SemaphoreType.DMA((len(shapes),))],
        compiler_params=pltpu.CompilerParams(vmem_limit_bytes=VMEM_LIMIT["finish"]),
        name="finish",
    )(*large, rows, tables)


def on_device(
    tokens,
    cotangent,
    norm1_gain,
    norm1_shift,
    qkv_weight,
    qv_bias,
    proj_weight,
    proj_bias,
    table_rows,
    table_cols,
    norm2_gain,
    norm2_shift,
    fc1_weight,
    fc1_bias,
    fc2_weight,
    fc2_bias,
    threshold,
):
    images, row_count, model_width = tokens.shape
    token_count = images * row_count
    local_width = qkv_weight.shape[2]
    local_heads = local_width // HEAD
    shape = Shape(local_heads, lax.axis_size("dp") // local_heads, row_count)
    flat = tokens.reshape(token_count, model_width)

    listed = (
        proj_bias, norm2_gain, norm2_shift, fc2_bias, norm1_gain, norm1_shift, fc1_bias, qv_bias,
        threshold,
    )
    weights = qkv_weight.transpose(1, 2, 0).reshape(3 * local_width, model_width)
    attended, qaug, bias_rows, kv, o_rows, lse, peak, normed1, tables, vectors = attend(
        shape, flat, weights, listed, table_rows.T, table_cols.T
    )
    (
        mlp_part,
        values,
        grad_middle,
        grad_fc1,
        grad_proj,
        grad_attended,
        grad_fc1_bias,
        sums,
        fc2_state,
    ) = middle_block(
        local_heads,
        attended.reshape(local_width, token_count),
        proj_weight,
        flat,
        cotangent.reshape(token_count, model_width),
        fc1_weight,
        fc2_weight,
        vectors,
    )
    grad_heads = grad_attended.reshape(local_heads, HEAD, row_count)
    grad_triple, table_terms, first_state, grad_fc2, fc1_state, output, proj_state = attend_back(
        shape, grad_heads, tables, qaug, bias_rows, kv, o_rows, lse, fc2_state, grad_fc1,
        mlp_part, values, vectors, grad_proj,
    )
    grad_tokens, grad_proj, grad_fc1, grad_qkv, table_sums, rows, clipped = tail(
        local_heads,
        grad_triple,
        weights,
        normed1,
        flat,
        grad_middle,
        vectors,
        table_terms,
        sums,
        grad_fc1_bias,
        peak,
        proj_state,
        first_state,
        fc1_state,
    )
    large = (output, grad_tokens, grad_fc1, grad_fc2, grad_qkv, clipped, grad_proj)
    (
        output,
        grad_tokens,
        grad_fc1,
        grad_fc2,
        grad_qkv,
        clipped,
        grad_proj,
        grad_norm1_gain,
        grad_norm1_shift,
        grad_qv_bias,
        grad_proj_bias,
        grad_rows_t,
        grad_cols_t,
        grad_norm2_gain,
        grad_norm2_shift,
        grad_fc1_bias,
        grad_fc2_bias,
        clipped_q_bias,
        head_peaks,
        clip_factors,
    ) = finish(large, rows, table_sums, fc1_bias.shape[0], local_width)
    output = output.reshape(images, row_count, model_width)
    grad_tokens = grad_tokens.reshape(images, row_count, model_width)
    grad_qkv = grad_qkv.transpose(1, 0, 2)
    grad_fc2, grad_proj = grad_fc2.T, grad_proj.T
    grad_table_rows, grad_table_cols = grad_rows_t.T, grad_cols_t.T
    clipped_qk = clipped.reshape(2, local_width, model_width).transpose(2, 0, 1)
    return (
        output,
        grad_tokens,
        grad_norm1_gain,
        grad_norm1_shift,
        grad_qkv,
        grad_qv_bias,
        grad_proj,
        grad_proj_bias,
        grad_table_rows,
        grad_table_cols,
        grad_norm2_gain,
        grad_norm2_shift,
        grad_fc1,
        grad_fc1_bias,
        grad_fc2,
        grad_fc2_bias,
        clipped_qk,
        clipped_q_bias,
        head_peaks,
        clip_factors,
    )


def solution(mesh):
    in_specs = (
        P(None, "dp", None),
        P(None, "dp", None),
        P(),
        P(),
        P(None, None, "tensor"),
        P(None, "tensor"),
        P("tensor", None),
        P(),
        P(),
        P(),
        P(),
        P(),
        P(None, "tensor"),
        P("tensor"),
        P("tensor", None),
        P(),
        P(),
    )
    out_specs = (
        P(None, "dp", None),
        P(None, "dp", None),
        P(),
        P(),
        P("dp", None, "tensor"),
        P(None, "tensor"),
        P("tensor", "dp"),
        P(),
        P(),
        P(),
        P(),
        P(),
        P("dp", "tensor"),
        P("tensor"),
        P("tensor", "dp"),
        P(),
        P(None, None, "tensor"),
        P("tensor"),
        P("tensor"),
        P("tensor"),
    )
    return jax.shard_map(
        on_device, mesh=mesh, in_specs=in_specs, out_specs=out_specs, check_vma=False
    )
```

```python
import functools
import math

import jax
import jax.numpy as jnp
from jax import lax
from jax.experimental import pallas as pl
from jax.experimental.pallas import tpu as pltpu
from jax.sharding import PartitionSpec as P

HEAD = 80
SIDE = 64

MESH = pl.DeviceIdType.MESH
LOW = jnp.bfloat16
F32 = jnp.float32
EPSILON = 1e-06
SCALE = HEAD**-0.5
EXP2_SCALE = SCALE * math.log2(math.e)
COLS_AT = HEAD
ROWS_AT = COLS_AT + 2 * SIDE
LSE_AT = ROWS_AT + 16
AUG = LSE_AT + 16
VMEM_LIMIT = {
    "attend": 60 * 2**20,
    "middle": 40 * 2**20,
    "attend_back": 32 * 2**20,
    "tail": 24 * 2**20,
    "finish": 12 * 2**20,
}


def nn(a, b):
    return lax.dot_general(a, b, (((1,), (0,)), ((), ())), preferred_element_type=F32)


def tn(a, b):
    return lax.dot_general(a, b, (((0,), (0,)), ((), ())), preferred_element_type=F32)


def nt(a, b):
    return lax.dot_general(a, b, (((1,), (1,)), ((), ())), preferred_element_type=F32)


def parts_of(values, count):
    pieces = []
    for _ in range(count):
        piece = values.astype(LOW).astype(F32)
        pieces.append(piece)
        values = values - piece
    return pieces


def send_dp(src, dst, send_sem, recv_sem, dev):
    return pltpu.make_async_remote_copy(
        src_ref=src,
        dst_ref=dst,
        send_sem=send_sem,
        recv_sem=recv_sem,
        device_id={"dp": dev},
        device_id_type=MESH,
    )


def paired(place, k, count):
    found, bit = 0, 1
    while bit < count:
        found = found + bit * lax.rem(place // bit + k // bit, 2)
        bit *= 2
    return found


def turned(count):
    row = lax.broadcasted_iota(jnp.int32, (count, count), 0)
    column = lax.broadcasted_iota(jnp.int32, (count, count), 1)
    return jnp.where(row + column == count - 2, 1.0, 0.0).astype(LOW)


def shifts(rows, dev):
    spot = lax.broadcasted_iota(jnp.int32, (2 * SIDE, rows), 1)
    by_row = SIDE - 1 - (dev * (rows // SIDE) + lax.shift_right_logical(spot, 6))
    by_col = SIDE - 1 - (spot & (SIDE - 1))
    return by_row, by_col


def skew(values, shift):
    for bit in (32, 16, 8, 4, 2, 1):
        moved = pltpu.roll(values, 2 * SIDE - bit, 0)
        values = jnp.where((shift & bit) != 0, moved, values)
    return values[:SIDE]


def unskew(values, shift):
    values = jnp.concatenate([values, jnp.zeros_like(values)], axis=0)
    for bit in (32, 16, 8, 4, 2, 1):
        moved = pltpu.roll(values, bit, 0)
        values = jnp.where((shift & bit) != 0, moved, values)
    return values


def greet(peers):
    barrier = pltpu.get_barrier_semaphore()
    for peer in peers:
        pl.semaphore_signal(barrier, inc=1, device_id={"dp": peer}, device_id_type=MESH)
    pl.semaphore_wait(barrier, len(peers))


def key_onehots(rows, dev):
    spot = lax.broadcasted_iota(jnp.int32, (2 * SIDE, rows), 1)
    index = lax.broadcasted_iota(jnp.int32, (2 * SIDE, rows), 0)
    cols = jnp.where((index & (SIDE - 1)) == (spot & (SIDE - 1)), 1.0, 0.0)
    spot, index = spot[:16], index[:16]
    offset = lax.rem(dev * (rows // SIDE), 8)
    in_group = jnp.where((index & 7) == offset + lax.shift_right_logical(spot, 6), 1.0, 0.0)
    return cols, in_group


class Shape:
    def __init__(self, heads, group, rows):
        self.heads, self.group, self.rows = heads, group, rows
        self.queries = heads * rows
        self.block = min(2048, self.queries)


def forward_kernel(shape, count, outs, *refs):
    results = refs[count : count + outs]
    held, refs_left = refs[count + outs : 2 * count + outs], refs[2 * count + outs :]
    load, save, inner, refs_left = refs_left[0], refs_left[1], refs_left[2 : 1 + outs], refs_left[1 + outs :]
    inner = list(inner[:3]) + [results[3]] + list(inner[3:])
    saves = [
        None if n == 3 else pltpu.make_async_copy(a, b, save.at[n])
        for n, (a, b) in enumerate(zip(inner, results))
    ]
    copies = [
        pltpu.make_async_copy(a, b, load.at[n]) for n, (a, b) in enumerate(zip(refs[:count], held))
    ]
    for copy in copies[2:] + copies[:2]:
        copy.start()
    forward_body(shape, copies, saves, *held, *inner, *refs_left)
    for copy in saves:
        if copy is not None:
            copy.wait()


def forward_body(
    shape, copies, saves, tokens, weights, proj_bias, gain2, shift2, fc2_bias, gain1, shift1, fc1_bias,
    qv_bias, threshold, rows_t, cols_t,
    att, qaug, bias_rows, kv_out, o_out, lse_out, peak_out, n1_out, tables, vectors,
    n1, qkv, wide_t, rq, rkv, kaug_t, kaug, vaug, oacc, mrow, lpk, att_s, att_r,
    q_send, q_recv, k_send, k_recv, x_send, x_recv, r_send, r_recv, o_sem,
):
    heads, group, rows, block = shape.heads, shape.group, shape.rows, shape.block
    local = heads * HEAD
    me = lax.axis_index("dp")
    z, g = me // group, lax.rem(me, group)
    column = [paired(z, k, heads) for k in range(1, heads)]
    mates = [lax.rem(g + k, group) for k in range(1, group)]
    greet([h * group + g for h in column] + [z * group + o for o in mates])
    width = tokens.shape[1]
    vectors[...] = jnp.zeros_like(vectors)
    for copy in copies[2:] + copies[:1]:
        copy.wait()
    listed = (proj_bias, gain2, shift2, fc2_bias, gain1, shift1, fc1_bias)
    for n, each in enumerate(listed):
        vectors[n : n + 1, : each.shape[0]] = each[...].reshape(1, each.shape[0])
    vectors[7:9, :local] = qv_bias[...]
    vectors[9:10] = jnp.broadcast_to(threshold[...].reshape(1, 1), (1, width))
    scaled, _ = normed(tokens[...].astype(F32))
    n1[...] = (scaled * vectors[4:5] + vectors[5:6]).astype(LOW)
    biases = vectors[7:9].astype(F32)
    biases = jnp.concatenate([biases, jnp.zeros((6, biases.shape[1]), F32)], axis=0).T

    def project(t):
        found = nt(weights[pl.ds(t * local, local), :], n1[...])
        if t != 1:
            found = found + biases[:local, t // 2 : t // 2 + 1]
        qkv[t] = found.astype(LOW)

    sends = []
    copies[1].wait()
    project(0)
    for h in column:
        mine = pl.ds(pl.multiple_of(h * HEAD, 16), HEAD)
        copy = send_dp(qkv.at[0, mine], rq.at[z], q_send.at[h], q_recv.at[z], h * group + g)
        copy.start()
        sends.append(copy)
    project(1)
    project(2)
    for h in column:
        mine = pl.ds(pl.multiple_of(h * HEAD, 16), HEAD)
        copy = send_dp(
            qkv.at[pl.ds(1, 2), mine], rkv.at[z, g], k_send.at[h], k_recv.at[z], h * group + g
        )
        copy.start()
        sends.append(copy)
    mine = pl.ds(pl.multiple_of(z * HEAD, 16), HEAD)
    rq[z] = qkv[0, mine]
    rkv[z, g] = qkv[pl.ds(1, 2), mine]
    for n, mate in enumerate(mates):
        send_dp(
            rkv.at[z, g], rkv.at[z, g], x_send.at[z, n], x_recv.at[z, g], z * group + mate
        ).start()
    n1_t = n1[...].T
    pieces, devices, piece, _ = n1_out.shape
    for dev in range(devices):
        for at in range(pieces):
            start = (dev * pieces + at) * piece
            n1_out[at, dev] = n1_t[start : start + piece]
    saves[7].start()
    wide_t[...] = jnp.zeros_like(wide_t)
    for n, held in enumerate((rows_t, cols_t)):
        wide_t[n, :HEAD, : held.shape[1]] = held[...]
        tables[n] = nn(wide_t[n], turned(2 * SIDE)).T[:, :HEAD].astype(LOW)
    saves[8].start()
    saves[9].start()
    qaug[pl.ds(LSE_AT, 16), :] = jnp.zeros((16, shape.queries), LOW)
    kaug_t[pl.ds(LSE_AT, 16), :] = jnp.zeros((16, rows), LOW)
    vaug[pl.ds(HEAD, 16), :] = jnp.where(
        lax.broadcasted_iota(jnp.int32, (16, rows), 0) == 0, 1.0, 0.0
    ).astype(LOW)
    oacc[...] = jnp.zeros_like(oacc)
    mrow[...] = jnp.full_like(mrow, -jnp.inf)
    lpk[...] = jnp.full_like(lpk, -jnp.inf)

    def prepare(k, carry):
        source = paired(z, k, heads)
        span = pl.ds(pl.multiple_of(source * rows, rows), rows)

        @pl.when(k > 0)
        def _():
            send_dp(rq.at[source], rq.at[source], q_send.at[source], q_recv.at[source], me).wait_recv()

        query = rq[source]
        by_row, by_col = shifts(rows, source * group + g)
        along_rows = skew(nn(tables[0], query) * (1.0 / SCALE), by_row)
        along_cols = skew(nn(tables[1], query) * (1.0 / SCALE), by_col)
        qaug[pl.ds(0, HEAD), span] = query
        cols = parts_of(along_cols, 2)
        qaug[pl.ds(COLS_AT, 2 * SIDE), span] = jnp.concatenate(cols, axis=0).astype(LOW)
        high, rest = parts_of(along_rows, 2)
        for at in range(SIDE // 8):
            pair = jnp.concatenate([high[8 * at : 8 * at + 8], rest[8 * at : 8 * at + 8]], axis=0)
            bias_rows[at, :, span] = pair.astype(LOW)
        return carry

    lax.fori_loop(0, heads, prepare, 0)
    saves[2].start()

    def chunk(source, mate):
        dev = source * group + mate
        cols, in_group = key_onehots(rows, dev)
        kaug_t[pl.ds(0, HEAD), :] = rkv[source, mate, 0]
        kaug_t[pl.ds(COLS_AT, 2 * SIDE), :] = cols.astype(LOW)
        kaug_t[pl.ds(ROWS_AT, 16), :] = in_group.astype(LOW)
        kaug[...] = kaug_t[...].T
        vaug[pl.ds(0, HEAD), :] = rkv[source, mate, 1]
        qaug[pl.ds(ROWS_AT, 16), :] = bias_rows[(dev * (rows // SIDE)) // 8]

        def one(i, carry):
            span = pl.ds(pl.multiple_of(i * block, block), block)
            logits = nn(kaug[:, :HEAD], qaug[pl.ds(0, HEAD), span])
            lpk[...] = jnp.maximum(lpk[...], jnp.max(logits.reshape(rows // 8, 8, block), axis=0))
            scores = nn(kaug[...], qaug[:, span])
            before = mrow[:, span]
            top = jnp.maximum(before, jnp.max(scores, axis=0, keepdims=True))
            mrow[:, span] = top
            weights = jnp.exp2(scores * EXP2_SCALE - top * EXP2_SCALE).astype(LOW)
            keep = jnp.exp2((before - top) * EXP2_SCALE)
            oacc[:, span] = oacc[:, span] * keep + nn(vaug[...], weights)
            return carry

        lax.fori_loop(0, shape.queries // block, one, 0)

    def column_step(k, carry):
        source = paired(z, k, heads)

        @pl.when(k > 0)
        def _():
            send_dp(rkv.at[source, g], rkv.at[source, g], k_send.at[source], k_recv.at[source], me).wait_recv()
            for n, mate in enumerate(mates):
                send_dp(
                    rkv.at[source, g], rkv.at[source, g], x_send.at[source, n], x_recv.at[source, g],
                    z * group + mate,
                ).start()

        chunk(source, g)

        @pl.when(k != 1)
        def _():
            mates_of(jnp.maximum(k - 1, 0))

        return carry

    def mates_of(k):
        source = paired(z, k, heads)

        def mate_step(n, inner):
            mate = lax.rem(g + n, group)
            send_dp(
                rkv.at[source, mate], rkv.at[source, mate], x_send.at[source, 0], x_recv.at[source, mate], me
            ).wait_recv()
            chunk(source, mate)
            return inner

        lax.fori_loop(1, group, mate_step, 0)

    lax.fori_loop(0, heads, column_step, 0)
    if heads > 1:
        mates_of(heads - 1)
    keep_kv = pltpu.make_async_copy(rkv, kv_out, o_sem)
    keep_kv.start()

    def finish(k, carry):
        source = paired(z, lax.rem(k, heads), heads)
        span = pl.ds(pl.multiple_of(source * rows, rows), rows)
        total = oacc[pl.ds(HEAD, 1), span]
        attended = oacc[pl.ds(0, HEAD), span] / total
        o_out[:, span] = attended
        lse_out[:, span] = mrow[:, span] + jnp.log2(total) * (1.0 / EXP2_SCALE)
        att_s[source] = attended.astype(LOW)

        @pl.when(source != z)
        def _():
            send_dp(
                att_s.at[source], att_r.at[z], r_send.at[source], r_recv.at[z], source * group + g
            ).start()

        return carry

    saves[1].start()
    lax.fori_loop(1, heads + 1, finish, 0)
    saves[4].start()
    saves[5].start()
    att[z] = att_s[z]
    peak_out[...] = jnp.full(peak_out.shape, jnp.max(lpk[...]) * SCALE, F32)
    saves[6].start()
    for h in column:
        send_dp(att_s.at[h], att_r.at[h], r_send.at[h], r_recv.at[h], h * group + g).wait()
        att[h] = att_r[h]
    saves[0].start()
    for copy in sends:
        copy.wait_send()
    for source in range(heads):
        for n, mate in enumerate(mates):
            send_dp(
                rkv.at[source, g], rkv.at[source, g], x_send.at[source, n], x_recv.at[source, g],
                z * group + mate,
            ).wait_send()
    keep_kv.wait()


def attend(shape, tokens, weights, listed, rows_t, cols_t):
    heads, group, rows, queries = shape.heads, shape.group, shape.rows, shape.queries
    width, local = tokens.shape[1], heads * HEAD
    args = (tokens, weights, *listed, rows_t, cols_t)
    devices = heads * group
    owned = width // devices
    piece = 32 if owned % 32 == 0 else owned
    vmem = pl.BlockSpec(memory_space=pltpu.VMEM)
    hbm = pl.BlockSpec(memory_space=pl.ANY)
    dma = pltpu.SemaphoreType.DMA
    outs = (
        jax.ShapeDtypeStruct((heads, HEAD, rows), LOW),
        jax.ShapeDtypeStruct((AUG, queries), LOW),
        jax.ShapeDtypeStruct((SIDE // 8, 16, queries), LOW),
        jax.ShapeDtypeStruct((heads, group, 2, HEAD, rows), LOW),
        jax.ShapeDtypeStruct((HEAD, queries), F32),
        jax.ShapeDtypeStruct((1, queries), F32),
        jax.ShapeDtypeStruct((8, 128), F32),
        jax.ShapeDtypeStruct((owned // piece, devices, piece, rows), LOW),
        jax.ShapeDtypeStruct((2, 2 * SIDE, HEAD), LOW),
        jax.ShapeDtypeStruct((16, width), F32),
    )
    return pl.pallas_call(
        functools.partial(forward_kernel, shape, len(args), len(outs)),
        out_shape=outs,
        in_specs=[pl.BlockSpec(memory_space=pltpu.HBM)] * len(args),
        out_specs=(hbm,) * len(outs),
        scratch_shapes=[
            *[pltpu.VMEM(each.shape, each.dtype) for each in args],
            dma((len(args),)),
            dma((len(outs),)),
            *[pltpu.VMEM(each.shape, each.dtype) for n, each in enumerate(outs) if n != 3],
            pltpu.VMEM((rows, width), LOW),
            pltpu.VMEM((3, local, rows), LOW),
            pltpu.VMEM((2, 128, 2 * SIDE), LOW),
            pltpu.VMEM((heads, HEAD, rows), LOW),
            pltpu.VMEM((heads, group, 2, HEAD, rows), LOW),
            pltpu.VMEM((AUG, rows), LOW),
            pltpu.VMEM((rows, AUG), LOW),
            pltpu.VMEM((HEAD + 16, rows), LOW),
            pltpu.VMEM((HEAD + 16, queries), F32),
            pltpu.VMEM((1, queries), F32),
            pltpu.VMEM((8, shape.block), F32),
            pltpu.VMEM((heads, HEAD, rows), LOW),
            pltpu.VMEM((heads, HEAD, rows), LOW),
            dma((heads,)), dma((heads,)), dma((heads,)), dma((heads,)),
            dma((heads, group)), dma((heads, group)), dma((heads,)), dma((heads,)),
            dma,
        ],
        compiler_params=pltpu.CompilerParams(
            collective_id=1, has_side_effects=True, vmem_limit_bytes=VMEM_LIMIT["attend"]
        ),
        name="attend",
    )(*args)


def backward_kernel(
    shape, ga, tables, qaug_in, bias_rows, rkv, o_in, lse_in, fc2_state, fc1, mlp, values, vectors, proj,
    grads, table_grads, first_state, fc2_out, fc1_state, output, proj_state,
    rdo, qaug, q_tok, do_aug, do_tok, kaug_t, kaug, vaug_t, vaug, kacc, vacc, dq, drow, dcol,
    part, xr, summed, gq_s, gq_r, gkv_r,
    d_send, d_recv, x_send, x_recv, kv_send, kv_recv, q_send, q_recv, *rest,
):
    chunks = fc1.shape[1]
    rest = list(rest)

    def taken(number):
        found, rest[:] = rest[:number], rest[number:]
        return found

    bits = halve_bits()
    orders = [near_first(), far_first(shape.group)]
    moved2 = [
        Halve(orders[n], fc2_state.at[n], taken(3 * (bits - 2)), first=2) for n in range(chunks)
    ]
    moved0 = Halve(far_first(shape.group), proj, taken(3), last=0)
    outs = taken(1)[0]
    lines = lax.axis_size("tensor") // 2
    sum_mlp = Reduce(mlp, *taken(7))
    all_out = Gather(outs, *taken(3))
    line = tensor_place()[1]
    moved1 = [Halve(near_first(), fc1.at[:, 0], taken(8), last=1, own=True)]
    if chunks > 1:
        moved1 += [Halve(near_first(), fc1.at[:, 1], taken(5), last=0, own=True)]
    heads, group, rows, block = shape.heads, shape.group, shape.rows, shape.block
    queries = shape.queries
    me = lax.axis_index("dp")
    z, g = me // group, lax.rem(me, group)
    column = [paired(z, k, heads) for k in range(1, heads)]
    mates = [lax.rem(g + k, group) for k in range(1, group)]
    greet_all(Ring(heads))
    for other in sum_mlp.others() + [line]:
        sum_mlp.give(other)
    sends = []
    for h in column:
        copy = send_dp(ga.at[h], rdo.at[z], d_send.at[h], d_recv.at[z], h * group + g)
        copy.start()
        sends.append(copy)
    moved1[0].start()
    for each in moved1:
        each.load()
    rdo[z] = ga[z]
    qaug[...] = qaug_in[...]
    ones = jnp.where(lax.broadcasted_iota(jnp.int32, (16, rows), 0) < 3, 1.0, 0.0).astype(LOW)
    kaug_t[pl.ds(LSE_AT, 16), :] = ones
    vaug_t[pl.ds(HEAD, 16), :] = ones
    vaug_t[pl.ds(HEAD + 16, 32), :] = jnp.zeros((32, rows), LOW)
    low_lse = parts_of(-lse_in[...], 3)
    qaug[pl.ds(LSE_AT, 16), :] = jnp.concatenate(
        low_lse + [jnp.zeros((13, queries), F32)], axis=0
    ).astype(LOW)
    dq[...] = jnp.zeros_like(dq)
    dcol[...] = jnp.zeros_like(dcol)
    drow[...] = jnp.zeros_like(drow)

    def prepare(k, carry):
        source = paired(z, k, heads)
        span = pl.ds(pl.multiple_of(source * rows, rows), rows)

        @pl.when(k > 0)
        def _():
            send_dp(rdo.at[source], rdo.at[source], d_send.at[source], d_recv.at[source], me).wait_recv()

        upstream = rdo[source]
        dots = jnp.sum(upstream.astype(F32) * o_in[:, span], axis=0, keepdims=True)
        low_dots = parts_of(-dots, 3)
        do_aug[pl.ds(0, HEAD), span] = upstream
        do_aug[pl.ds(HEAD, 16), span] = jnp.concatenate(
            low_dots + [jnp.zeros((13, rows), F32)], axis=0
        ).astype(LOW)
        do_aug[pl.ds(HEAD + 16, 32), span] = jnp.zeros((32, rows), LOW)
        do_tok[span, :] = do_aug[:, span].T
        q_tok[span, :] = qaug[pl.ds(0, 128), span].T
        return carry

    lax.fori_loop(0, heads, prepare, 0)
    for other in sum_mlp.others():
        sum_mlp.pass_on(other)
    moved0.start()
    for each in moved2:
        each.start()

    def chunk(source, mate):
        dev = source * group + mate
        at = (dev * (rows // SIDE)) // 8
        cols, in_group = key_onehots(rows, dev)
        kaug_t[pl.ds(0, HEAD), :] = rkv[source, mate, 0]
        kaug_t[pl.ds(COLS_AT, 2 * SIDE), :] = cols.astype(LOW)
        kaug_t[pl.ds(ROWS_AT, 16), :] = in_group.astype(LOW)
        kaug[...] = kaug_t[...].T
        vaug_t[pl.ds(0, HEAD), :] = rkv[source, mate, 1]
        vaug[...] = vaug_t[...].T
        qaug[pl.ds(ROWS_AT, 16), :] = bias_rows[at]
        kacc[...] = jnp.zeros_like(kacc)
        vacc[...] = jnp.zeros_like(vacc)
        back = jnp.concatenate(
            [kaug_t[pl.ds(0, COLS_AT + SIDE), :], kaug_t[pl.ds(ROWS_AT, 16), :]], axis=0
        )

        def one(i, carry):
            span = pl.ds(pl.multiple_of(i * block, block), block)
            probs = jnp.exp2(nn(kaug[...], qaug[:, span]) * EXP2_SCALE)
            pulled = nn(vaug[...], do_aug[:, span])
            low_grads = (probs * pulled).astype(LOW)
            vacc[...] += nn(probs.astype(LOW), do_tok[span, :])
            kacc[...] += nn(low_grads, q_tok[span, :])
            found = nn(back, low_grads)
            dq[:, span] += found[:HEAD]
            dcol[:, span] += found[COLS_AT : COLS_AT + SIDE]
            drow[at, :, span] += found[COLS_AT + SIDE : COLS_AT + SIDE + 8]
            return carry

        lax.fori_loop(0, queries // block, one, 0)

    def put(where, extra):
        key_part = (kacc[...] * SCALE).T[:HEAD]
        value_part = vacc[...].T[:HEAD]
        for other in extra:
            key_part = key_part + other[0].astype(F32)
            value_part = value_part + other[1].astype(F32)
        where[0] = key_part.astype(LOW)
        where[1] = value_part.astype(LOW)

    def mate_copy(source, mate):
        return send_dp(
            part.at[source, mate], xr.at[source, g], x_send.at[source, mate], x_recv.at[source, g],
            z * group + mate,
        )

    def mates_step(k, carry):
        source = paired(z, lax.rem(k, heads), heads)

        def mate_step(n, inner):
            mate = lax.rem(g + n, group)
            chunk(source, mate)
            put(part.at[source, mate], [])
            mate_copy(source, mate).start()
            return inner

        lax.fori_loop(1, group, mate_step, 0)

        return carry

    lax.fori_loop(1, heads + 1, mates_step, 0)
    if chunks > 1:
        moved1[1].start()
    spot = lax.axis_index("tensor")
    outs[spot] = (values[...] + sum_mlp.total() + vectors[3:4]).astype(LOW)
    all_out.start()
    moved1[0].loaded()
    moved1[0].run(0)

    def own_step(k, carry):
        source = paired(z, lax.rem(k, heads), heads)
        chunk(source, g)
        extra = []
        for mate in mates:
            send_dp(
                xr.at[source, mate], xr.at[source, mate], x_send.at[source, mate], x_recv.at[source, mate], me
            ).wait_recv()
            extra.append(xr.at[source, mate])
        put(summed.at[source], extra)

        @pl.when(source != z)
        def _():
            send_dp(
                summed.at[source], gkv_r.at[z], kv_send.at[source], kv_recv.at[z], source * group + g
            ).start()

        return carry

    lax.fori_loop(1, heads + 1, own_step, 0)
    for other in all_out.others():
        all_out.forward(other)
    table_grads[...] = jnp.zeros_like(table_grads)

    def finish(k, carry):
        source = paired(z, lax.rem(k, heads), heads)
        span = pl.ds(pl.multiple_of(source * rows, rows), rows)
        by_row, by_col = shifts(rows, source * group + g)
        total = dq[:, span] * SCALE
        for n, held in enumerate((drow[:, :, span].reshape(SIDE, rows), dcol[:, span])):
            spread = unskew(held, by_col if n else by_row)
            for piece in parts_of(spread, 2):
                low_piece = piece.astype(LOW)
                total = total + tn(tables[n], low_piece)
                table_grads[n] += nn(low_piece, q_tok[span, :])
        gq_s[source] = total.astype(LOW)

        @pl.when(source != z)
        def _():
            send_dp(
                gq_s.at[source], gq_r.at[z], q_send.at[source], q_recv.at[z], source * group + g
            ).start()

        return carry

    lax.fori_loop(1, heads + 1, finish, 0)
    moved1[0].run(1)
    for stage in range(2, halve_bits() - 1):
        for each in moved2:
            each.run(stage)
    found = [each.total() for each in moved2]
    fc2_out[...] = jnp.concatenate(found, axis=0) if chunks > 1 else found[0]
    first_state[...] = moved1[0].stages[1][0][...]
    if chunks > 1:
        moved1[1].loaded()
        moved1[1].run(0)
        fc1_state[...] = moved1[1].stages[0][0][...]
    moved0.run(0)
    proj_state[...] = moved0.stages[0][0][...]
    for other in all_out.others() + [line]:
        all_out.take(other)
    output[...] = outs[...]
    grads[z, 0] = gq_s[z]
    grads[z, pl.ds(1, 2)] = summed[z]
    for h in column:
        send_dp(summed.at[h], gkv_r.at[h], kv_send.at[h], kv_recv.at[h], h * group + g).wait()
        grads[h, pl.ds(1, 2)] = gkv_r[h]
    for h in column:
        send_dp(gq_s.at[h], gq_r.at[h], q_send.at[h], q_recv.at[h], h * group + g).wait()
        grads[h, 0] = gq_r[h]
    for copy in sends:
        copy.wait_send()
    for source in range(heads):
        for mate in mates:
            mate_copy(source, mate).wait_send()
    for each in moved1 + moved2 + [sum_mlp, all_out, moved0]:
        each.finish()


def attend_back(shape, ga, tables, qaug, bias_rows, kv, o_rows, lse, fc2_state, fc1, mlp, values, vectors, proj):
    count, share, width = mlp.shape
    devices, chunks, owned, hidden = fc1.shape
    hbm = pl.BlockSpec(memory_space=pl.ANY)
    moving = halve_bufs(owned, hidden, first=2) * chunks
    moving += halve_bufs(chunks * owned, proj.shape[2], last=0)
    moving += [pltpu.VMEM((count, share, width), LOW)]
    moving += part_bufs(count // 2, share, width) + gather_sems(count // 2)
    moving += halve_bufs(owned, hidden, last=1, own=True)
    if chunks > 1:
        moving += halve_bufs(owned, hidden, last=0, own=True)
    heads, group, rows, queries = shape.heads, shape.group, shape.rows, shape.queries
    vmem = pl.BlockSpec(memory_space=pltpu.VMEM)
    dma = pltpu.SemaphoreType.DMA
    return pl.pallas_call(
        functools.partial(backward_kernel, shape),
        out_shape=(
            jax.ShapeDtypeStruct((heads, 3, HEAD, rows), LOW),
            jax.ShapeDtypeStruct((2, 2 * SIDE, 128), F32),
            jax.ShapeDtypeStruct((devices // 4, owned, hidden), LOW),
            jax.ShapeDtypeStruct((chunks * owned, hidden), F32),
            jax.ShapeDtypeStruct((devices // 2, owned, hidden), LOW),
            jax.ShapeDtypeStruct((count, share, width), LOW),
            jax.ShapeDtypeStruct((devices // 2,) + proj.shape[1:], LOW),
        ),
        in_specs=[vmem] * 8 + [hbm] + [vmem] * 4,
        out_specs=(vmem,) * 7,
        scratch_shapes=[
            pltpu.VMEM((heads, HEAD, rows), LOW),
            pltpu.VMEM((AUG, queries), LOW),
            pltpu.VMEM((queries, 128), LOW),
            pltpu.VMEM((128, queries), LOW),
            pltpu.VMEM((queries, 128), LOW),
            pltpu.VMEM((AUG, rows), LOW),
            pltpu.VMEM((rows, AUG), LOW),
            pltpu.VMEM((128, rows), LOW),
            pltpu.VMEM((rows, 128), LOW),
            pltpu.VMEM((rows, 128), F32),
            pltpu.VMEM((rows, 128), F32),
            pltpu.VMEM((HEAD, queries), F32),
            pltpu.VMEM((SIDE // 8, 8, queries), F32),
            pltpu.VMEM((SIDE, queries), F32),
            pltpu.VMEM((heads, group, 2, HEAD, rows), LOW),
            pltpu.VMEM((heads, group, 2, HEAD, rows), LOW),
            pltpu.VMEM((heads, 2, HEAD, rows), LOW),
            pltpu.VMEM((heads, HEAD, rows), LOW),
            pltpu.VMEM((heads, HEAD, rows), LOW),
            pltpu.VMEM((heads, 2, HEAD, rows), LOW),
            dma((heads,)), dma((heads,)), dma((heads, group)), dma((heads, group)),
            dma((heads,)), dma((heads,)), dma((heads,)), dma((heads,)),
        ] + moving,
        compiler_params=pltpu.CompilerParams(
            collective_id=2, has_side_effects=True, vmem_limit_bytes=VMEM_LIMIT["attend_back"]
        ),
        name="attend_back",
    )(ga, tables, qaug, bias_rows, kv, o_rows, lse, fc2_state, fc1, mlp, values, vectors, proj)


def send_tensor(src, dst, send_sem, recv_sem, dev):
    return pltpu.make_async_remote_copy(
        src_ref=src,
        dst_ref=dst,
        send_sem=send_sem,
        recv_sem=recv_sem,
        device_id={"tensor": dev},
        device_id_type=MESH,
    )


def tensor_place():
    me = lax.axis_index("tensor")
    return lax.rem(me, 2), me // 2, lax.axis_size("tensor") // 2


def tensor_peers():
    core, line, lines = tensor_place()
    far = [lax.rem(line + k, lines) * 2 + core for k in range(1, lines)]
    return far + [line * 2 + 1 - core]


def part_bufs(lines, share, width, dtype=LOW):
    dma = pltpu.SemaphoreType.DMA
    return [pltpu.VMEM((lines, share, width), dtype)] * 3 + [dma((lines,))] * 4


class Reduce:
    def __init__(self, part, mate_in, passed, line_in, m_send, m_recv, l_send, l_recv):
        self.part, self.mate_in, self.passed, self.line_in = part, mate_in, passed, line_in
        self.sems = m_send, m_recv, l_send, l_recv
        self.core, self.line, self.lines = tensor_place()

    def mate_copy(self, to):
        m_send, m_recv, _, _ = self.sems
        return send_tensor(
            self.part.at[to * 2 + 1 - self.core], self.mate_in.at[to],
            m_send.at[to], m_recv.at[to], self.line * 2 + 1 - self.core,
        )

    def line_copy(self, to, slot):
        _, _, l_send, l_recv = self.sems
        return send_tensor(
            self.passed.at[to], self.line_in.at[slot], l_send.at[to], l_recv.at[slot],
            to * 2 + self.core,
        )

    def give(self, to):
        self.mate_copy(to).start()

    def pass_on(self, to):
        self.mate_copy(to).wait_recv()
        both = self.part[to * 2 + self.core].astype(F32) + self.mate_in[to].astype(F32)
        self.passed[to] = both.astype(self.passed.dtype)
        self.line_copy(to, self.line).start()

    def others(self):
        return [lax.rem(self.line + k, self.lines) for k in range(1, self.lines)]

    def total(self):
        self.mate_copy(self.line).wait_recv()
        total = self.part[self.line * 2 + self.core].astype(F32) + self.mate_in[self.line].astype(F32)
        for other in self.others():
            self.line_copy(other, other).wait_recv()
            total = total + self.line_in[other].astype(F32)
        return total

    def finish(self):
        self.mate_copy(self.line).wait_send()
        for other in self.others():
            self.mate_copy(other).wait_send()
            self.line_copy(other, self.line).wait_send()


def gather_sems(lines):
    dma = pltpu.SemaphoreType.DMA
    return [dma((lines,)), dma((lines,)), dma((2 * lines,))]


class Gather:
    def __init__(self, whole, l_send, m_send, recv):
        self.whole, self.sems = whole, (l_send, m_send, recv)
        self.core, self.line, self.lines = tensor_place()

    def line_copy(self, to):
        l_send, _, recv = self.sems
        own = self.line * 2 + self.core
        return send_tensor(
            self.whole.at[own], self.whole.at[own], l_send.at[to], recv.at[own], to * 2 + self.core
        )

    def mate_copy(self, at):
        _, m_send, recv = self.sems
        part = at * 2 + self.core
        return send_tensor(
            self.whole.at[part], self.whole.at[part], m_send.at[at], recv.at[part],
            self.line * 2 + 1 - self.core,
        )

    def arrived(self, part):
        l_send, _, recv = self.sems
        send_tensor(
            self.whole.at[part], self.whole.at[part], l_send.at[0], recv.at[part], part
        ).wait_recv()

    def others(self):
        return [lax.rem(self.line + k, self.lines) for k in range(1, self.lines)]

    def start(self):
        for other in self.others():
            self.line_copy(other).start()
        self.mate_copy(self.line).start()

    def forward(self, at):
        self.arrived(at * 2 + self.core)
        self.mate_copy(at).start()

    def take(self, at):
        self.arrived(at * 2 + 1 - self.core)

    def finish(self):
        self.mate_copy(self.line).wait_send()
        for other in self.others():
            self.mate_copy(other).wait_send()
            self.line_copy(other).wait_send()


def normed(values):
    center = values - jnp.mean(values, axis=-1, keepdims=True)
    variance = jnp.mean(center * center, axis=-1, keepdims=True)
    inverse = lax.rsqrt(variance + EPSILON)
    return center * inverse, inverse


def normed_back(upstream, scaled, inverse, gain):
    weighted = upstream * gain
    centered = weighted - jnp.mean(weighted, axis=-1, keepdims=True)
    return (centered - scaled * jnp.mean(weighted * scaled, axis=-1, keepdims=True)) * inverse


def tile_of(width):
    return 256 if width % 256 == 0 else 128


class Ring:
    def __init__(self, heads):
        self.heads, self.group = heads, lax.axis_size("dp") // heads
        me = lax.axis_index("dp")
        self.z, self.g = me // self.group, lax.rem(me, self.group)

    def column(self):
        return [paired(self.z, k, self.heads) for k in range(1, self.heads)]

    def mates(self):
        return [lax.rem(self.g + k, self.group) for k in range(1, self.group)]

    def peers(self):
        far = [h * self.group + self.g for h in self.column()]
        return far + [self.z * self.group + o for o in self.mates()]


def greet_all(ring):
    barrier = pltpu.get_barrier_semaphore()
    near, far = tensor_peers(), ring.peers()
    for peer in near:
        pl.semaphore_signal(barrier, inc=1, device_id={"tensor": peer}, device_id_type=MESH)
    for peer in far:
        pl.semaphore_signal(barrier, inc=1, device_id={"dp": peer}, device_id_type=MESH)
    pl.semaphore_wait(barrier, len(near) + len(far))


def halve_bits():
    return (lax.axis_size("dp") - 1).bit_length()


def near_first():
    return tuple(range(halve_bits()))


def far_first(group):
    first = group.bit_length() - 1
    return (first,) + tuple(bit for bit in range(halve_bits()) if bit != first)


def halve_bufs(share, width, first=0, last=None, own=False):
    bits = halve_bits()
    last = bits - 1 if last is None else last
    dma = pltpu.SemaphoreType.DMA
    found = []
    if own:
        found += [pltpu.VMEM((1 << (bits - 1), share, width), LOW), dma]
    for stage in range(first, last + 1):
        count = 1 << (bits - 1 - stage)
        found += [pltpu.VMEM((count, share, width), LOW), dma((count,)), dma((count,))]
    return found


class Halve:
    def __init__(self, order, source, bufs, first=0, last=None, own=False):
        self.order, self.source, self.first = order, source, first
        self.last = len(order) - 1 if last is None else last
        bufs = list(bufs)
        self.own = bufs[0:2] if own else None
        bufs = bufs[2:] if own else bufs
        self.stages = {first + n: bufs[3 * n : 3 * n + 3] for n in range(len(bufs) // 3)}
        self.me = lax.axis_index("dp")

    def bit(self, stage):
        return lax.rem(self.me // (1 << self.order[stage]), 2)

    def count(self, stage):
        return 1 << (len(self.order) - 1 - stage)

    def index(self, stage, at, bit):
        if stage > 0:
            return at * 2 + bit
        place = bit * (1 << self.order[0])
        for n, other in enumerate(self.order[1:]):
            place = place + lax.rem(at // (1 << n), 2) * (1 << other)
        return place

    def held(self, stage):
        return self.source if stage == self.first else self.stages[stage - 1][0]

    def copy(self, stage, at):
        bit = self.bit(stage)
        into, send, recv = self.stages[stage]
        return send_dp(
            self.held(stage).at[self.index(stage, at, 1 - bit)], into.at[at],
            send.at[at], recv.at[at], self.me + (1 - 2 * bit) * (1 << self.order[stage]),
        )

    def spots(self, stage):
        if stage == len(self.order) - 1:
            return [0]
        bit, half = self.bit(stage + 1), self.count(stage) // 2
        return [n * 2 + 1 - bit for n in range(half)] + [n * 2 + bit for n in range(half)]

    def load(self):
        for at in range(self.count(0)):
            pltpu.make_async_copy(
                self.source.at[self.index(0, at, self.bit(0))], self.own[0].at[at], self.own[1]
            ).start()

    def loaded(self):
        pltpu.make_async_copy(
            self.source.at[pl.ds(0, self.count(0))], self.own[0], self.own[1]
        ).wait()

    def start(self, only=slice(None)):
        for at in self.spots(self.first)[only]:
            self.copy(self.first, at).start()

    def kept(self, stage, at):
        if stage == self.first and self.own is not None:
            return self.own[0][at].astype(F32)
        return self.held(stage)[self.index(stage, at, self.bit(stage))].astype(F32)

    def sum_at(self, stage, at):
        self.copy(stage, at).wait_recv()
        return self.kept(stage, at) + self.stages[stage][0][at].astype(F32)

    def run(self, stage):
        for n, at in enumerate(self.spots(stage)):
            self.stages[stage][0][at] = self.sum_at(stage, at).astype(LOW)
            if stage < self.last and n < self.count(stage) // 2:
                self.copy(stage + 1, n).start()

    def total(self):
        return self.sum_at(self.last, 0)

    def finish(self):
        for stage in self.stages:
            for at in range(self.count(stage)):
                self.copy(stage, at).wait_send()


def middle_kernel(
    heads, att, proj_w, tokens, cot, fc1_hbm, fc2_hbm, vectors,
    mlp, values_out, middle_out, fc1_out, proj_out, ga_out, fc1_bias_out, sums_out, fc2_state,
    fc1, fc2, att_tok, branch, back, n2, act, gu, gb, held, spread,
    wide, load1, load2, *rest,
):
    core, line, lines = tensor_place()
    me = lax.axis_index("tensor")
    _, share, width = tokens.shape
    rows = tokens.shape[0] * share
    local, hidden = proj_w.shape[0], fc1_hbm.shape[1]
    step, dstep = tile_of(hidden), tile_of(width)
    in_fc1 = pltpu.make_async_copy(fc1_hbm, fc1, load1)
    in_fc2 = pltpu.make_async_copy(fc2_hbm, fc2, load2)
    in_fc1.start()
    in_fc2.start()
    greet_all(Ring(heads))
    sum_branch = Reduce(branch, *rest[0:7])
    sum_back = Reduce(back, *rest[7:14])
    all_n2 = Gather(n2, *rest[14:17])
    all_gb = Gather(gb, *rest[17:20])
    blocks2, blocks1, fc1_sem = rest[20:23]
    devices, chunks, owned, _ = blocks2.shape
    orders = [near_first(), far_first(lax.axis_size("dp") // heads)]
    moved = [
        Halve(orders[n], blocks2.at[:, n], rest[23 + 6 * n : 29 + 6 * n], last=1)
        for n in range(chunks)
    ]
    att_tok[...] = att[...].T.reshape(att_tok.shape)

    def project(k, carry):
        to = lax.rem(line + 1 + lax.rem(k, lines), lines)
        part = to * 2 + jnp.where(k < lines, 1 - core, core)
        branch[part] = nn(att_tok[part], proj_w[...]).astype(LOW)

        @pl.when(k < lines)
        def _():
            sum_branch.give(to)

        return carry

    lax.fori_loop(0, 2 * lines, project, 0)
    for other in sum_branch.others():
        sum_branch.pass_on(other)
    middle = tokens[me].astype(F32) + vectors[0:1]
    middle = middle + sum_branch.total()
    scaled, inverse = normed(middle)
    n2[me] = (scaled * vectors[1:2] + vectors[2:3]).astype(LOW)
    all_n2.start()
    values_out[...] = middle
    held[...] = scaled
    spread[...] = jnp.broadcast_to(inverse, spread.shape)
    fc1_bias_out[...] = jnp.zeros_like(fc1_bias_out)
    in_fc1.wait()
    in_fc2.wait()

    def hidden_part(k, carry):
        at = lax.rem(line + k, lines)

        @pl.when(k > 0)
        def _():
            all_n2.forward(at)

        all_n2.take(at)
        pair = pl.ds(at * 2, 2)
        inputs = n2[pair].reshape(2 * share, width)
        pulls = cot[pair].reshape(2 * share, width)

        def tile(n, inner):
            span = pl.ds(pl.multiple_of(n * step, step), step)
            up = nn(inputs, fc1[:, span]) + vectors[6:7, span]
            phi = 0.5 + 0.5 * lax.erf(up * math.sqrt(0.5))
            slope = phi + up * (jnp.exp(-0.5 * up * up) * (2 * math.pi) ** -0.5)
            act[pair, :, span] = (up * phi).astype(LOW).reshape(2, share, step)
            grad_up = (nt(pulls, fc2[span, :]) * slope).astype(LOW)
            gu[pair, :, span] = grad_up.reshape(2, share, step)
            fc1_bias_out[:, span] += jnp.sum(grad_up.astype(F32), axis=0, keepdims=True)
            return inner

        lax.fori_loop(0, hidden // step, tile, 0)

        def tile_back(n, inner):
            span = pl.ds(pl.multiple_of(n * dstep, dstep), dstep)
            found = nt(gu[pair].reshape(2 * share, hidden), fc1[span, :])
            back[pair, :, span] = found.astype(LOW).reshape(2, share, dstep)
            return inner

        lax.fori_loop(0, width // dstep, tile_back, 0)
        sum_back.give(at)

        return carry

    lax.fori_loop(0, lines, hidden_part, 0)

    def weights2(n, carry):
        span = pl.ds(pl.multiple_of(n * dstep, dstep), dstep)
        found = tn(cot[:, :, span].reshape(rows, dstep), act[...].reshape(rows, hidden))
        wide[span, :] = found.astype(LOW)
        return carry

    lax.fori_loop(0, width // dstep, weights2, 0)
    for dev in range(devices):
        for chunk in range(chunks):
            at = (dev * chunks + chunk) * owned
            blocks2[dev, chunk] = wide[pl.ds(at, owned), :]
    for each in moved:
        each.start()
    for other in sum_back.others():
        sum_back.pass_on(other)

    def out_part(k, carry):
        at = lax.rem(line + 1 + k, lines)
        pair = pl.ds(at * 2, 2)

        def tile_out(n, inner):
            span = pl.ds(pl.multiple_of(n * dstep, dstep), dstep)
            found = nn(act[pair].reshape(2 * share, hidden), fc2[:, span])
            mlp[pair, :, span] = found.astype(LOW).reshape(2, share, dstep)
            return inner

        lax.fori_loop(0, width // dstep, tile_out, 0)
        return carry

    lax.fori_loop(0, lines, out_part, 0)

    def weights1(n, carry):
        span = pl.ds(pl.multiple_of(n * dstep, dstep), dstep)
        found = tn(n2[:, :, span].reshape(rows, dstep), gu[...].reshape(rows, hidden))
        wide[span, :] = found.astype(LOW)
        return carry

    lax.fori_loop(0, width // dstep, weights1, 0)
    for dev in range(devices):
        for chunk in range(chunks):
            at = (dev * chunks + chunk) * owned
            blocks1[dev, chunk] = wide[pl.ds(at, owned), :]
    keep_fc1 = pltpu.make_async_copy(blocks1, fc1_out, fc1_sem)
    keep_fc1.start()
    upstream = sum_back.total()
    sums_out[0:1] = jnp.sum(upstream * held[...], axis=0, keepdims=True)
    sums_out[1:2] = jnp.sum(upstream, axis=0, keepdims=True)
    grad_middle = cot[me].astype(F32) + normed_back(
        upstream, held[...], spread[:, :1], vectors[1:2]
    )
    middle_out[...] = grad_middle
    gb[me] = grad_middle.astype(LOW)
    all_gb.start()
    for each in moved:
        each.run(0)
    sums_out[2:3] = jnp.sum(cot[...].astype(F32).reshape(rows, width), axis=0, keepdims=True)
    for other in all_gb.others():
        all_gb.forward(other)
    all_gb.take(line)
    for other in all_gb.others():
        all_gb.take(other)
    whole = gb[...].reshape(rows, width)
    sums_out[3:4] = jnp.sum(whole.astype(F32), axis=0, keepdims=True)
    ga_out[...] = nt(proj_w[...], whole).astype(LOW)

    def weights0(n, carry):
        span = pl.ds(pl.multiple_of(n * dstep, dstep), dstep)
        found = tn(gb[:, :, span].reshape(rows, dstep), att_tok[...].reshape(rows, -1))
        wide[span, :local] = found.astype(LOW)
        return carry

    lax.fori_loop(0, width // dstep, weights0, 0)
    for dev in range(devices):
        proj_out[dev] = wide[pl.ds(dev * chunks * owned, chunks * owned), :local]
    for n, each in enumerate(moved):
        each.run(1)
        fc2_state[n] = each.stages[1][0][...]
    keep_fc1.wait()
    for each in (sum_branch, sum_back, all_n2, all_gb, *moved):
        each.finish()


def middle_block(heads, att, proj_w, tokens, cot, fc1, fc2, vectors):
    count = lax.axis_size("tensor")
    lines = count // 2
    local, width = proj_w.shape
    rows = tokens.shape[0]
    share = rows // count
    hidden = fc1.shape[1]
    vmem = pl.BlockSpec(memory_space=pltpu.VMEM)
    hbm = pl.BlockSpec(memory_space=pl.ANY)
    dma = pltpu.SemaphoreType.DMA
    whole = (count, share, width)
    devices = lax.axis_size("dp")
    owned = width // devices
    chunks = 2 if owned % 32 == 0 else 1
    weights = (devices, chunks, owned // chunks, hidden)
    scratch = [
        pltpu.VMEM((width, hidden), LOW),
        pltpu.VMEM((hidden, width), LOW),
        pltpu.VMEM((count, share, local), LOW),
        pltpu.VMEM(whole, LOW),
        pltpu.VMEM(whole, LOW),
        pltpu.VMEM(whole, LOW),
        pltpu.VMEM((count, share, hidden), LOW),
        pltpu.VMEM((count, share, hidden), LOW),
        pltpu.VMEM(whole, LOW),
        pltpu.VMEM((share, width), F32),
        pltpu.VMEM((share, 128), F32),
        pltpu.VMEM((width, hidden), LOW),
        dma,
        dma,
    ]
    scratch += part_bufs(lines, share, width) * 2 + gather_sems(lines) * 2
    scratch += [pltpu.VMEM(weights, LOW), pltpu.VMEM(weights, LOW), dma]
    scratch += halve_bufs(owned // chunks, hidden, last=1) * chunks
    return pl.pallas_call(
        functools.partial(middle_kernel, heads),
        out_shape=(
            jax.ShapeDtypeStruct(whole, LOW),
            jax.ShapeDtypeStruct((share, width), F32),
            jax.ShapeDtypeStruct((share, width), F32),
            jax.ShapeDtypeStruct(weights, LOW),
            jax.ShapeDtypeStruct((devices, owned, local), LOW),
            jax.ShapeDtypeStruct((local, rows), LOW),
            jax.ShapeDtypeStruct((1, hidden), F32),
            jax.ShapeDtypeStruct((8, width), F32),
            jax.ShapeDtypeStruct((chunks, devices // 4, owned // chunks, hidden), LOW),
        ),
        in_specs=[vmem] * 4 + [hbm] * 2 + [vmem],
        out_specs=(vmem,) * 3 + (hbm,) + (vmem,) * 5,
        scratch_shapes=scratch,
        compiler_params=pltpu.CompilerParams(
            collective_id=3, has_side_effects=True, vmem_limit_bytes=VMEM_LIMIT["middle"]
        ),
        name="middle",
    )(
        att, proj_w, tokens.reshape(whole), cot.reshape(whole), fc1, fc2, vectors,
    )


def small_bufs(heads, stages, shape):
    group, lines = lax.axis_size("dp") // heads, lax.axis_size("tensor") // 2
    dma = pltpu.SemaphoreType.DMA
    found = []
    for stage in stages:
        count = {"core": 2, "line": lines, "mate": group, "far": heads}[stage]
        found += [
            pltpu.VMEM(shape, F32), pltpu.VMEM((count,) + shape, F32), dma((count,)), dma((count,))
        ]
    return found


class Small:
    def __init__(self, ring, stages, merge, *bufs):
        self.ring, self.stages, self.merge = ring, stages, merge
        self.bufs = [bufs[4 * n : 4 * n + 4] for n in range(len(stages))]
        core, line, lines = tensor_place()
        self.peers = {
            "core": (core, [(1 - core, line * 2 + 1 - core)]),
            "line": (line, [(o, o * 2 + core) for o in [lax.rem(line + k, lines) for k in range(1, lines)]]),
            "mate": (ring.g, [(o, ring.z * ring.group + o) for o in ring.mates()]),
            "far": (ring.z, [(o, o * ring.group + ring.g) for o in ring.column()]),
        }

    def copy(self, n, slot, other, dev):
        value, held, send, recv = self.bufs[n]
        call = send_tensor if self.stages[n] in ("core", "line") else send_dp
        return call(value, held.at[slot], send.at[other], recv.at[slot], dev)

    def start(self, n, value):
        own, peers = self.peers[self.stages[n]]
        self.bufs[n][0][...] = value
        for other, dev in peers:
            self.copy(n, own, other, dev).start()

    def take(self, n):
        _, peers = self.peers[self.stages[n]]
        total = self.bufs[n][0][...]
        for other, dev in peers:
            self.copy(n, other, other, dev).wait_recv()
            total = self.merge(total, self.bufs[n][1][other])
        return total

    def step(self, n):
        self.start(n + 1, self.take(n))

    def finish(self):
        for n in range(len(self.stages)):
            own, peers = self.peers[self.stages[n]]
            for other, dev in peers:
                self.copy(n, own, other, dev).wait_send()


EVERY = ("core", "line", "far", "mate")
OVER_DP = ("mate", "far")


def add_peaks(a, b):
    row = lax.broadcasted_iota(jnp.int32, a.shape, 0)
    return jnp.where(row == 2, jnp.maximum(a, b), a + b)


def widen(row, width):
    if row.shape[1] == width:
        return row
    return jnp.concatenate([row, jnp.zeros((1, width - row.shape[1]), F32)], axis=1)


def tail_kernel(
    heads, grads, qkv_w, n1_t, tokens, grad_middle, vectors, tables, sums, fc1_bias, peak,
    proj, first_state, fc1_state,
    tokens_out, proj_out, fc1_out, qkv_out, tables_out, rows_out, clip_out,
    g_all, g_tok, part, gt, *rest,
):
    ring = Ring(heads)
    core, line, lines = tensor_place()
    me = lax.axis_index("tensor")
    count, share, width = tokens.shape
    rows = count * share
    local = heads * HEAD
    dstep = tile_of(width)
    pieces, devices, piece, _ = n1_t.shape
    chunks = 1 if pieces == 1 else 2
    rest = list(rest)

    def taken(number):
        found, rest[:] = rest[:number], rest[number:]
        return found

    greet_all(ring)
    blocks = [taken(1)[0] for _ in range(pieces)]
    moved3 = [Halve(near_first(), each, taken(3 * halve_bits())) for each in blocks]
    moved0 = Halve(far_first(ring.group), proj, taken(3 * (halve_bits() - 1)), first=1)
    moved1 = [Halve(near_first(), first_state, taken(3 * (halve_bits() - 2)), first=2)]
    if chunks > 1:
        moved1 += [Halve(near_first(), fc1_state, taken(3 * (halve_bits() - 1)), first=1)]
    sum_part = Reduce(part, *taken(7))
    all_gt = Gather(gt, *taken(3))
    pool, pooled = taken(2)
    sum_pool = Reduce(pool, *taken(7))
    all_pool = Gather(pooled, *taken(3))
    small_pool = Small(ring, OVER_DP, lax.add, *taken(8))
    small_late = Small(ring, EVERY, lax.add, *taken(16))
    small_dp = Small(ring, OVER_DP, add_peaks, *taken(8))
    pool[...] = tables[...].reshape(pool.shape)
    for other in sum_pool.others() + [line]:
        sum_pool.give(other)
    for each in moved1:
        each.start()
    moved0.start()
    for t in range(3):
        for h in range(heads):
            g_all[pl.ds(t * local + h * HEAD, HEAD), :] = grads[h, t]
    g_tok[...] = g_all[...].T.reshape(g_tok.shape)
    for other in sum_pool.others():
        sum_pool.pass_on(other)
    whole = g_tok[...].reshape(rows, 3 * local)
    lane = lax.broadcasted_iota(jnp.int32, (1, width), 1)
    peaks = jnp.where(lane == ring.z, peak[0:1, 0:1], -jnp.inf)
    bias_sums = nn(jnp.ones((8, rows), LOW), whole)[0:1]
    dp_rows = [widen(fc1_bias[...], width), widen(bias_sums, width), peaks]
    small_dp.start(0, jnp.concatenate(dp_rows + [jnp.zeros((5, width), F32)], axis=0))

    for n in range(pieces):
        found = nn(
            n1_t[n].reshape(devices * piece, rows), g_tok[...].reshape(rows, 3 * local)
        )
        blocks[n][...] = found.astype(LOW).reshape(devices, piece, 3 * local)
        if n == min(1, pieces - 1):
            small_pool.start(0, sum_pool.total())
        moved3[n].start()

    def norm_part(k, carry):
        at = lax.rem(line + 1 + k, lines)
        pair = pl.ds(at * 2, 2)

        def tile(n, inner):
            span = pl.ds(pl.multiple_of(n * dstep, dstep), dstep)
            found = nn(g_tok[pair].reshape(2 * share, 3 * local), qkv_w[:, span])
            part[pair, :, span] = found.astype(LOW).reshape(2, share, dstep)
            return inner

        lax.fori_loop(0, width // dstep, tile, 0)
        sum_part.give(at)
        return carry

    lax.fori_loop(0, lines, norm_part, 0)
    for other in sum_part.others():
        sum_part.pass_on(other)
    scaled, inverse = normed(tokens[me].astype(F32))
    for each in moved1[1:]:
        each.run(1)
    moved3[0].run(0)
    small_pool.step(0)
    moved0.run(1)
    for each in moved3[1:2]:
        each.run(0)
    moved3[0].run(1)
    upstream = sum_part.total()
    late = [
        sums[0:4],
        jnp.sum(upstream * scaled, axis=0, keepdims=True),
        jnp.sum(upstream, axis=0, keepdims=True),
        jnp.zeros((2, width), F32),
    ]
    small_late.start(0, jnp.concatenate(late, axis=0))
    found = grad_middle[...] + normed_back(upstream, scaled, inverse, vectors[4:5])
    gt[me] = found.astype(LOW)
    all_gt.start()
    pooled[me] = small_pool.take(1)
    all_pool.start()
    small_dp.step(0)
    for n, each in enumerate(moved3[2:]):
        each.run(0)
        if n == 0:
            small_late.step(0)
        if n == 1:
            small_late.step(1)
            for other in all_gt.others():
                all_gt.forward(other)
            for other in all_pool.others():
                all_pool.forward(other)
        moved3[n + 1].run(1)
    if pieces < 4:
        for n in range(max(pieces - 2, 0), 2):
            small_late.step(n)
        for other in all_gt.others():
            all_gt.forward(other)
        for other in all_pool.others():
            all_pool.forward(other)
    small_late.step(2)
    if pieces > 1:
        moved3[-1].run(1)
    dp_sum = small_dp.take(1)
    limit = vectors[9:10]
    factors = jnp.sqrt(limit / jnp.maximum(dp_sum[2:3], limit))
    lane = lax.broadcasted_iota(jnp.int32, (1, width), 1)
    clipped_bias = vectors[7:8]
    for h in range(heads):
        factor = factors[:, h : h + 1]
        own = (lane >= h * HEAD) & (lane < (h + 1) * HEAD)
        clipped_bias = jnp.where(own, clipped_bias * factor, clipped_bias)
        for t in range(2):
            span = pl.ds(t * local + h * HEAD, HEAD)
            clip_out[span, :] = (qkv_w[span, :].astype(F32) * factor).astype(LOW)
    rows_out[8:11] = dp_sum[0:3]
    rows_out[11:12] = factors
    rows_out[12:13] = clipped_bias
    rows_out[13:16] = jnp.zeros((3, width), F32)
    for stage in range(2, halve_bits() - 1):
        for each in moved3 + [moved0] + moved1:
            each.run(stage)
    for other in all_gt.others() + [line]:
        all_gt.take(other)
    for other in all_pool.others() + [line]:
        all_pool.take(other)
    tokens_out[...] = gt[...]
    for n in range(2):
        turned_sums = pooled[...].reshape(2, 2 * SIDE, 128)[n].T[:HEAD]
        found = jnp.zeros((HEAD, 2 * SIDE), F32)
        for piece in parts_of(turned_sums, 3):
            found = found + nn(piece.astype(LOW), turned(2 * SIDE))
        tables_out[n] = found
    late = small_late.take(3)
    row = lax.broadcasted_iota(jnp.int32, late.shape, 0)
    rows_out[0:8] = jnp.where((row == 2) | (row == 3), late * (1.0 / count), late)
    owned = first_state.shape[1]
    for n, each in enumerate(moved1):
        fc1_out[pl.ds(n * owned, owned), :] = each.total()
    proj_out[...] = moved0.total()
    for n, each in enumerate(moved3):
        total = each.total()
        owned = total.shape[0]
        for t in range(3):
            qkv_out[t, pl.ds(n * owned, owned), :] = total[:, t * local : (t + 1) * local]
    for each in [
        moved0, sum_part, all_gt, sum_pool, all_pool, small_pool, small_late, small_dp,
    ] + moved3 + moved1:
        each.finish()


def tail(heads, grads, qkv_w, n1_t, tokens, grad_middle, vectors, tables, sums, fc1_bias, peak, proj, first_state, fc1_state):
    hidden = first_state.shape[2]
    count = lax.axis_size("tensor")
    lines = count // 2
    local = heads * HEAD
    pieces, devices, piece, rows = n1_t.shape
    width = devices * pieces * piece
    owned = first_state.shape[1]
    chunks = pieces * piece // owned
    share = rows // count
    vmem = pl.BlockSpec(memory_space=pltpu.VMEM)
    whole = (count, share, width)
    scratch = [
        pltpu.VMEM((3 * local, rows), LOW),
        pltpu.VMEM((count, share, 3 * local), LOW),
        pltpu.VMEM(whole, LOW),
        pltpu.VMEM(whole, LOW),
    ]
    scratch += [pltpu.VMEM((devices, piece, 3 * local), LOW)] * pieces
    scratch += halve_bufs(piece, 3 * local) * pieces
    scratch += halve_bufs(chunks * owned, local, first=1)
    scratch += halve_bufs(owned, hidden, first=2)
    if chunks > 1:
        scratch += halve_bufs(owned, hidden, first=1)
    scratch += part_bufs(lines, share, width) + gather_sems(lines)
    pool = (count, 4 * SIDE // count, 128)
    scratch += [pltpu.VMEM(pool, F32)] * 2
    scratch += part_bufs(lines, *pool[1:], F32) + gather_sems(lines)
    scratch += small_bufs(heads, OVER_DP, pool[1:])
    scratch += small_bufs(heads, EVERY, (8, width))
    scratch += small_bufs(heads, OVER_DP, (8, width))
    return pl.pallas_call(
        functools.partial(tail_kernel, heads),
        out_shape=(
            jax.ShapeDtypeStruct(whole, LOW),
            jax.ShapeDtypeStruct((chunks * owned, local), F32),
            jax.ShapeDtypeStruct((chunks * owned, hidden), F32),
            jax.ShapeDtypeStruct((3, chunks * owned, local), F32),
            jax.ShapeDtypeStruct((2, HEAD, 2 * SIDE), F32),
            jax.ShapeDtypeStruct((16, width), F32),
            jax.ShapeDtypeStruct((2 * local, width), LOW),
        ),
        in_specs=[vmem] * 13,
        out_specs=(vmem,) * 7,
        scratch_shapes=scratch,
        compiler_params=pltpu.CompilerParams(
            collective_id=4, has_side_effects=True, vmem_limit_bytes=VMEM_LIMIT["tail"]
        ),
        name="tail",
    )(
        grads, qkv_w, n1_t, tokens.reshape(whole), grad_middle, vectors, tables, sums, fc1_bias,
        peak, proj, first_state, fc1_state,
    )


def finish_kernel(count, *refs):
    large, (rows, tables), refs = refs[:count], refs[count : count + 2], refs[count + 2 :]
    outs, smalls_out, refs = refs[:count], refs[count : count + 13], refs[count + 13 :]
    stage, smalls, (sems_in, sems_out, sems_small) = refs[:count], refs[count : count + 13], refs[count + 13 :]
    into = [pltpu.make_async_copy(a, b, sems_in.at[n]) for n, (a, b) in enumerate(zip(large, stage))]
    out = [pltpu.make_async_copy(b, c, sems_out.at[n]) for n, (b, c) in enumerate(zip(stage, outs))]
    for copy in into:
        copy.start()
    gain1, shift1, qv, proj, by_row, by_col, gain2, shift2, fc1, fc2, clip_bias, peaks, factors = smalls
    picks = (
        (gain2, 0), (shift2, 1), (fc2, 2), (proj, 3), (gain1, 4), (shift1, 5), (fc1, 8),
        (peaks, 10), (factors, 11), (clip_bias, 12),
    )
    for ref, at in picks:
        ref[...] = rows[at : at + 1, : ref.shape[0]].reshape(ref.shape)
    local = qv.shape[1]
    qv[0:1] = rows[9:10, :local]
    qv[1:2] = rows[9:10, 2 * local : 3 * local]
    by_row[...] = tables[0, :, : by_row.shape[1]]
    by_col[...] = tables[1, :, : by_col.shape[1]]
    small = [
        pltpu.make_async_copy(a, b, sems_small.at[n]) for n, (a, b) in enumerate(zip(smalls, smalls_out))
    ]
    for copy, after in zip(into, out):
        copy.wait()
        after.start()
    for copy in small:
        copy.start()
    for copy in out + small:
        copy.wait()


def finish(large, rows, tables, hidden, local):
    width = rows.shape[1]
    heads = local // HEAD
    vmem = pl.BlockSpec(memory_space=pltpu.VMEM)
    hbm = pl.BlockSpec(memory_space=pl.ANY)
    count = len(large)
    shapes = [
        (width,), (width,), (2, local), (width,), (HEAD, 2 * SIDE - 1), (HEAD, 2 * SIDE - 1),
        (width,), (width,), (hidden,), (width,), (local,), (heads,), (heads,),
    ]
    return pl.pallas_call(
        functools.partial(finish_kernel, count),
        out_shape=[jax.ShapeDtypeStruct(each.shape, each.dtype) for each in large]
        + [jax.ShapeDtypeStruct(each, F32) for each in shapes],
        in_specs=[hbm] * count + [vmem] * 2,
        out_specs=[hbm] * (count + len(shapes)),
        scratch_shapes=[pltpu.VMEM(each.shape, each.dtype) for each in large]
        + [pltpu.VMEM(each, F32) for each in shapes]
        + [pltpu.SemaphoreType.DMA((count,))] * 2
        + [pltpu.SemaphoreType.DMA((len(shapes),))],
        compiler_params=pltpu.CompilerParams(vmem_limit_bytes=VMEM_LIMIT["finish"]),
        name="finish",
    )(*large, rows, tables)


def on_device(
    tokens,
    cotangent,
    norm1_gain,
    norm1_shift,
    qkv_weight,
    qv_bias,
    proj_weight,
    proj_bias,
    table_rows,
    table_cols,
    norm2_gain,
    norm2_shift,
    fc1_weight,
    fc1_bias,
    fc2_weight,
    fc2_bias,
    threshold,
):
    images, row_count, model_width = tokens.shape
    token_count = images * row_count
    local_width = qkv_weight.shape[2]
    local_heads = local_width // HEAD
    shape = Shape(local_heads, lax.axis_size("dp") // local_heads, row_count)
    flat = tokens.reshape(token_count, model_width)

    listed = (
        proj_bias, norm2_gain, norm2_shift, fc2_bias, norm1_gain, norm1_shift, fc1_bias, qv_bias,
        threshold,
    )
    weights = qkv_weight.transpose(1, 2, 0).reshape(3 * local_width, model_width)
    attended, qaug, bias_rows, kv, o_rows, lse, peak, normed1, tables, vectors = attend(
        shape, flat, weights, listed, table_rows.T, table_cols.T
    )
    (
        mlp_part,
        values,
        grad_middle,
        grad_fc1,
        grad_proj,
        grad_attended,
        grad_fc1_bias,
        sums,
        fc2_state,
    ) = middle_block(
        local_heads,
        attended.reshape(local_width, token_count),
        proj_weight,
        flat,
        cotangent.reshape(token_count, model_width),
        fc1_weight,
        fc2_weight,
        vectors,
    )
    grad_heads = grad_attended.reshape(local_heads, HEAD, row_count)
    grad_triple, table_terms, first_state, grad_fc2, fc1_state, output, proj_state = attend_back(
        shape, grad_heads, tables, qaug, bias_rows, kv, o_rows, lse, fc2_state, grad_fc1,
        mlp_part, values, vectors, grad_proj,
    )
    grad_tokens, grad_proj, grad_fc1, grad_qkv, table_sums, rows, clipped = tail(
        local_heads,
        grad_triple,
        weights,
        normed1,
        flat,
        grad_middle,
        vectors,
        table_terms,
        sums,
        grad_fc1_bias,
        peak,
        proj_state,
        first_state,
        fc1_state,
    )
    large = (output, grad_tokens, grad_fc1, grad_fc2, grad_qkv, clipped, grad_proj)
    (
        output,
        grad_tokens,
        grad_fc1,
        grad_fc2,
        grad_qkv,
        clipped,
        grad_proj,
        grad_norm1_gain,
        grad_norm1_shift,
        grad_qv_bias,
        grad_proj_bias,
        grad_rows_t,
        grad_cols_t,
        grad_norm2_gain,
        grad_norm2_shift,
        grad_fc1_bias,
        grad_fc2_bias,
        clipped_q_bias,
        head_peaks,
        clip_factors,
    ) = finish(large, rows, table_sums, fc1_bias.shape[0], local_width)
    output = output.reshape(images, row_count, model_width)
    grad_tokens = grad_tokens.reshape(images, row_count, model_width)
    grad_qkv = grad_qkv.transpose(1, 0, 2)
    grad_fc2, grad_proj = grad_fc2.T, grad_proj.T
    grad_table_rows, grad_table_cols = grad_rows_t.T, grad_cols_t.T
    clipped_qk = clipped.reshape(2, local_width, model_width).transpose(2, 0, 1)
    return (
        output,
        grad_tokens,
        grad_norm1_gain,
        grad_norm1_shift,
        grad_qkv,
        grad_qv_bias,
        grad_proj,
        grad_proj_bias,
        grad_table_rows,
        grad_table_cols,
        grad_norm2_gain,
        grad_norm2_shift,
        grad_fc1,
        grad_fc1_bias,
        grad_fc2,
        grad_fc2_bias,
        clipped_qk,
        clipped_q_bias,
        head_peaks,
        clip_factors,
    )


def solution(mesh):
    in_specs = (
        P(None, "dp", None),
        P(None, "dp", None),
        P(),
        P(),
        P(None, None, "tensor"),
        P(None, "tensor"),
        P("tensor", None),
        P(),
        P(),
        P(),
        P(),
        P(),
        P(None, "tensor"),
        P("tensor"),
        P("tensor", None),
        P(),
        P(),
    )
    out_specs = (
        P(None, "dp", None),
        P(None, "dp", None),
        P(),
        P(),
        P("dp", None, "tensor"),
        P(None, "tensor"),
        P("tensor", "dp"),
        P(),
        P(),
        P(),
        P(),
        P(),
        P("dp", "tensor"),
        P("tensor"),
        P("tensor", "dp"),
        P(),
        P(None, None, "tensor"),
        P("tensor"),
        P("tensor"),
        P("tensor"),
    )
    return jax.shard_map(
        on_device, mesh=mesh, in_specs=in_specs, out_specs=out_specs, check_vma=False
    )
```

```python
import functools
import math

import jax
import jax.numpy as jnp
from jax import lax
from jax.experimental import pallas as pl
from jax.experimental.pallas import tpu as pltpu
from jax.sharding import PartitionSpec as P

HEAD = 80
SIDE = 64

MESH = pl.DeviceIdType.MESH
LOW = jnp.bfloat16
F32 = jnp.float32
EPSILON = 1e-06
SCALE = HEAD**-0.5
EXP2_SCALE = SCALE * math.log2(math.e)
COLS_AT = HEAD
ROWS_AT = COLS_AT + 2 * SIDE
LSE_AT = ROWS_AT + 16
AUG = LSE_AT + 16
VMEM_LIMIT = {
    "attend": 60 * 2**20,
    "middle": 40 * 2**20,
    "attend_back": 32 * 2**20,
    "tail": 24 * 2**20,
    "finish": 12 * 2**20,
}


def nn(a, b):
    return lax.dot_general(a, b, (((1,), (0,)), ((), ())), preferred_element_type=F32)


def tn(a, b):
    return lax.dot_general(a, b, (((0,), (0,)), ((), ())), preferred_element_type=F32)


def nt(a, b):
    return lax.dot_general(a, b, (((1,), (1,)), ((), ())), preferred_element_type=F32)


def parts_of(values, count):
    pieces = []
    for _ in range(count):
        piece = values.astype(LOW).astype(F32)
        pieces.append(piece)
        values = values - piece
    return pieces


def send_dp(src, dst, send_sem, recv_sem, dev):
    return pltpu.make_async_remote_copy(
        src_ref=src,
        dst_ref=dst,
        send_sem=send_sem,
        recv_sem=recv_sem,
        device_id={"dp": dev},
        device_id_type=MESH,
    )


def paired(place, k, count):
    found, bit = 0, 1
    while bit < count:
        found = found + bit * lax.rem(place // bit + k // bit, 2)
        bit *= 2
    return found


def turned(count):
    row = lax.broadcasted_iota(jnp.int32, (count, count), 0)
    column = lax.broadcasted_iota(jnp.int32, (count, count), 1)
    return jnp.where(row + column == count - 2, 1.0, 0.0).astype(LOW)


def shifts(rows, dev):
    spot = lax.broadcasted_iota(jnp.int32, (2 * SIDE, rows), 1)
    by_row = SIDE - 1 - (dev * (rows // SIDE) + lax.shift_right_logical(spot, 6))
    by_col = SIDE - 1 - (spot & (SIDE - 1))
    return by_row, by_col


def skew(values, shift):
    for bit in (32, 16, 8, 4, 2, 1):
        moved = pltpu.roll(values, 2 * SIDE - bit, 0)
        values = jnp.where((shift & bit) != 0, moved, values)
    return values[:SIDE]


def unskew(values, shift):
    values = jnp.concatenate([values, jnp.zeros_like(values)], axis=0)
    for bit in (32, 16, 8, 4, 2, 1):
        moved = pltpu.roll(values, bit, 0)
        values = jnp.where((shift & bit) != 0, moved, values)
    return values


def greet(peers):
    barrier = pltpu.get_barrier_semaphore()
    for peer in peers:
        pl.semaphore_signal(barrier, inc=1, device_id={"dp": peer}, device_id_type=MESH)
    pl.semaphore_wait(barrier, len(peers))


def key_onehots(rows, dev):
    spot = lax.broadcasted_iota(jnp.int32, (2 * SIDE, rows), 1)
    index = lax.broadcasted_iota(jnp.int32, (2 * SIDE, rows), 0)
    cols = jnp.where((index & (SIDE - 1)) == (spot & (SIDE - 1)), 1.0, 0.0)
    spot, index = spot[:16], index[:16]
    offset = lax.rem(dev * (rows // SIDE), 8)
    in_group = jnp.where((index & 7) == offset + lax.shift_right_logical(spot, 6), 1.0, 0.0)
    return cols, in_group


class Shape:
    def __init__(self, heads, group, rows):
        self.heads, self.group, self.rows = heads, group, rows
        self.queries = heads * rows
        self.block = min(2048, self.queries)


def forward_kernel(shape, count, outs, *refs):
    results = refs[count : count + outs]
    held, refs_left = refs[count + outs : 2 * count + outs], refs[2 * count + outs :]
    load, save, inner, refs_left = refs_left[0], refs_left[1], refs_left[2 : 1 + outs], refs_left[1 + outs :]
    inner = list(inner[:3]) + [results[3]] + list(inner[3:])
    saves = [
        None if n == 3 else pltpu.make_async_copy(a, b, save.at[n])
        for n, (a, b) in enumerate(zip(inner, results))
    ]
    copies = [
        pltpu.make_async_copy(a, b, load.at[n]) for n, (a, b) in enumerate(zip(refs[:count], held))
    ]
    for copy in copies[2:] + copies[:2]:
        copy.start()
    forward_body(shape, copies, saves, *held, *inner, *refs_left)
    for copy in saves:
        if copy is not None:
            copy.wait()


def forward_body(
    shape, copies, saves, tokens, weights, proj_bias, gain2, shift2, fc2_bias, gain1, shift1, fc1_bias,
    qv_bias, threshold, rows_t, cols_t,
    att, qaug, bias_rows, kv_out, o_out, lse_out, peak_out, n1_out, tables, vectors,
    n1, qkv, wide_t, rq, rkv, kaug_t, kaug, vaug, oacc, mrow, lpk, att_s, att_r,
    q_send, q_recv, k_send, k_recv, x_send, x_recv, r_send, r_recv, o_sem,
):
    heads, group, rows, block = shape.heads, shape.group, shape.rows, shape.block
    local = heads * HEAD
    me = lax.axis_index("dp")
    z, g = me // group, lax.rem(me, group)
    column = [paired(z, k, heads) for k in range(1, heads)]
    mates = [lax.rem(g + k, group) for k in range(1, group)]
    greet([h * group + g for h in column] + [z * group + o for o in mates])
    width = tokens.shape[1]
    vectors[...] = jnp.zeros_like(vectors)
    for copy in copies[2:] + copies[:1]:
        copy.wait()
    listed = (proj_bias, gain2, shift2, fc2_bias, gain1, shift1, fc1_bias)
    for n, each in enumerate(listed):
        vectors[n : n + 1, : each.shape[0]] = each[...].reshape(1, each.shape[0])
    vectors[7:9, :local] = qv_bias[...]
    vectors[9:10] = jnp.broadcast_to(threshold[...].reshape(1, 1), (1, width))
    scaled, _ = normed(tokens[...].astype(F32))
    n1[...] = (scaled * vectors[4:5] + vectors[5:6]).astype(LOW)
    biases = vectors[7:9].astype(F32)
    biases = jnp.concatenate([biases, jnp.zeros((6, biases.shape[1]), F32)], axis=0).T

    def project(t):
        found = nt(weights[pl.ds(t * local, local), :], n1[...])
        if t != 1:
            found = found + biases[:local, t // 2 : t // 2 + 1]
        qkv[t] = found.astype(LOW)

    sends = []
    copies[1].wait()
    project(0)
    for h in column:
        mine = pl.ds(pl.multiple_of(h * HEAD, 16), HEAD)
        copy = send_dp(qkv.at[0, mine], rq.at[z], q_send.at[h], q_recv.at[z], h * group + g)
        copy.start()
        sends.append(copy)
    project(1)
    project(2)
    for h in column:
        mine = pl.ds(pl.multiple_of(h * HEAD, 16), HEAD)
        copy = send_dp(
            qkv.at[pl.ds(1, 2), mine], rkv.at[z, g], k_send.at[h], k_recv.at[z], h * group + g
        )
        copy.start()
        sends.append(copy)
    mine = pl.ds(pl.multiple_of(z * HEAD, 16), HEAD)
    rq[z] = qkv[0, mine]
    rkv[z, g] = qkv[pl.ds(1, 2), mine]
    for n, mate in enumerate(mates):
        send_dp(
            rkv.at[z, g], rkv.at[z, g], x_send.at[z, n], x_recv.at[z, g], z * group + mate
        ).start()
    n1_t = n1[...].T
    pieces, devices, piece, _ = n1_out.shape
    for dev in range(devices):
        for at in range(pieces):
            start = (dev * pieces + at) * piece
            n1_out[at, dev] = n1_t[start : start + piece]
    saves[7].start()
    wide_t[...] = jnp.zeros_like(wide_t)
    for n, held in enumerate((rows_t, cols_t)):
        wide_t[n, :HEAD, : held.shape[1]] = held[...]
        tables[n] = nn(wide_t[n], turned(2 * SIDE)).T[:, :HEAD].astype(LOW)
    saves[8].start()
    saves[9].start()
    qaug[pl.ds(LSE_AT, 16), :] = jnp.zeros((16, shape.queries), LOW)
    kaug_t[pl.ds(LSE_AT, 16), :] = jnp.zeros((16, rows), LOW)
    vaug[pl.ds(HEAD, 16), :] = jnp.where(
        lax.broadcasted_iota(jnp.int32, (16, rows), 0) == 0, 1.0, 0.0
    ).astype(LOW)
    oacc[...] = jnp.zeros_like(oacc)
    mrow[...] = jnp.full_like(mrow, -jnp.inf)
    lpk[...] = jnp.full_like(lpk, -jnp.inf)

    def prepare(k, carry):
        source = paired(z, k, heads)
        span = pl.ds(pl.multiple_of(source * rows, rows), rows)

        @pl.when(k > 0)
        def _():
            send_dp(rq.at[source], rq.at[source], q_send.at[source], q_recv.at[source], me).wait_recv()

        query = rq[source]
        by_row, by_col = shifts(rows, source * group + g)
        along_rows = skew(nn(tables[0], query) * (1.0 / SCALE), by_row)
        along_cols = skew(nn(tables[1], query) * (1.0 / SCALE), by_col)
        qaug[pl.ds(0, HEAD), span] = query
        cols = parts_of(along_cols, 2)
        qaug[pl.ds(COLS_AT, 2 * SIDE), span] = jnp.concatenate(cols, axis=0).astype(LOW)
        high, rest = parts_of(along_rows, 2)
        for at in range(SIDE // 8):
            pair = jnp.concatenate([high[8 * at : 8 * at + 8], rest[8 * at : 8 * at + 8]], axis=0)
            bias_rows[at, :, span] = pair.astype(LOW)
        return carry

    lax.fori_loop(0, heads, prepare, 0)
    saves[2].start()

    def chunk(source, mate):
        dev = source * group + mate
        cols, in_group = key_onehots(rows, dev)
        kaug_t[pl.ds(0, HEAD), :] = rkv[source, mate, 0]
        kaug_t[pl.ds(COLS_AT, 2 * SIDE), :] = cols.astype(LOW)
        kaug_t[pl.ds(ROWS_AT, 16), :] = in_group.astype(LOW)
        kaug[...] = kaug_t[...].T
        vaug[pl.ds(0, HEAD), :] = rkv[source, mate, 1]
        qaug[pl.ds(ROWS_AT, 16), :] = bias_rows[(dev * (rows // SIDE)) // 8]

        def one(i, carry):
            span = pl.ds(pl.multiple_of(i * block, block), block)
            logits = nn(kaug[:, :HEAD], qaug[pl.ds(0, HEAD), span])
            lpk[...] = jnp.maximum(lpk[...], jnp.max(logits.reshape(rows // 8, 8, block), axis=0))
            scores = nn(kaug[...], qaug[:, span])
            before = mrow[:, span]
            top = jnp.maximum(before, jnp.max(scores, axis=0, keepdims=True))
            mrow[:, span] = top
            weights = jnp.exp2(scores * EXP2_SCALE - top * EXP2_SCALE).astype(LOW)
            keep = jnp.exp2((before - top) * EXP2_SCALE)
            oacc[:, span] = oacc[:, span] * keep + nn(vaug[...], weights)
            return carry

        lax.fori_loop(0, shape.queries // block, one, 0)

    def column_step(k, carry):
        source = paired(z, k, heads)

        @pl.when(k > 0)
        def _():
            send_dp(rkv.at[source, g], rkv.at[source, g], k_send.at[source], k_recv.at[source], me).wait_recv()
            for n, mate in enumerate(mates):
                send_dp(
                    rkv.at[source, g], rkv.at[source, g], x_send.at[source, n], x_recv.at[source, g],
                    z * group + mate,
                ).start()

        chunk(source, g)

        @pl.when(k != 1)
        def _():
            mates_of(jnp.maximum(k - 1, 0))

        return carry

    def mates_of(k):
        source = paired(z, k, heads)

        def mate_step(n, inner):
            mate = lax.rem(g + n, group)
            send_dp(
                rkv.at[source, mate], rkv.at[source, mate], x_send.at[source, 0], x_recv.at[source, mate], me
            ).wait_recv()
            chunk(source, mate)
            return inner

        lax.fori_loop(1, group, mate_step, 0)

    lax.fori_loop(0, heads, column_step, 0)
    if heads > 1:
        mates_of(heads - 1)
    keep_kv = pltpu.make_async_copy(rkv, kv_out, o_sem)
    keep_kv.start()

    def finish(k, carry):
        source = paired(z, lax.rem(k, heads), heads)
        span = pl.ds(pl.multiple_of(source * rows, rows), rows)
        total = oacc[pl.ds(HEAD, 1), span]
        attended = oacc[pl.ds(0, HEAD), span] / total
        o_out[:, span] = attended
        lse_out[:, span] = mrow[:, span] + jnp.log2(total) * (1.0 / EXP2_SCALE)
        att_s[source] = attended.astype(LOW)

        @pl.when(source != z)
        def _():
            send_dp(
                att_s.at[source], att_r.at[z], r_send.at[source], r_recv.at[z], source * group + g
            ).start()

        return carry

    saves[1].start()
    lax.fori_loop(1, heads + 1, finish, 0)
    saves[4].start()
    saves[5].start()
    att[z] = att_s[z]
    peak_out[...] = jnp.full(peak_out.shape, jnp.max(lpk[...]) * SCALE, F32)
    saves[6].start()
    for h in column:
        send_dp(att_s.at[h], att_r.at[h], r_send.at[h], r_recv.at[h], h * group + g).wait()
        att[h] = att_r[h]
    saves[0].start()
    for copy in sends:
        copy.wait_send()
    for source in range(heads):
        for n, mate in enumerate(mates):
            send_dp(
                rkv.at[source, g], rkv.at[source, g], x_send.at[source, n], x_recv.at[source, g],
                z * group + mate,
            ).wait_send()
    keep_kv.wait()


def attend(shape, tokens, weights, listed, rows_t, cols_t):
    heads, group, rows, queries = shape.heads, shape.group, shape.rows, shape.queries
    width, local = tokens.shape[1], heads * HEAD
    args = (tokens, weights, *listed, rows_t, cols_t)
    devices = heads * group
    owned = width // devices
    piece = 32 if owned % 32 == 0 else owned
    vmem = pl.BlockSpec(memory_space=pltpu.VMEM)
    hbm = pl.BlockSpec(memory_space=pl.ANY)
    dma = pltpu.SemaphoreType.DMA
    outs = (
        jax.ShapeDtypeStruct((heads, HEAD, rows), LOW),
        jax.ShapeDtypeStruct((AUG, queries), LOW),
        jax.ShapeDtypeStruct((SIDE // 8, 16, queries), LOW),
        jax.ShapeDtypeStruct((heads, group, 2, HEAD, rows), LOW),
        jax.ShapeDtypeStruct((HEAD, queries), F32),
        jax.ShapeDtypeStruct((1, queries), F32),
        jax.ShapeDtypeStruct((8, 128), F32),
        jax.ShapeDtypeStruct((owned // piece, devices, piece, rows), LOW),
        jax.ShapeDtypeStruct((2, 2 * SIDE, HEAD), LOW),
        jax.ShapeDtypeStruct((16, width), F32),
    )
    return pl.pallas_call(
        functools.partial(forward_kernel, shape, len(args), len(outs)),
        out_shape=outs,
        in_specs=[pl.BlockSpec(memory_space=pltpu.HBM)] * len(args),
        out_specs=(hbm,) * len(outs),
        scratch_shapes=[
            *[pltpu.VMEM(each.shape, each.dtype) for each in args],
            dma((len(args),)),
            dma((len(outs),)),
            *[pltpu.VMEM(each.shape, each.dtype) for n, each in enumerate(outs) if n != 3],
            pltpu.VMEM((rows, width), LOW),
            pltpu.VMEM((3, local, rows), LOW),
            pltpu.VMEM((2, 128, 2 * SIDE), LOW),
            pltpu.VMEM((heads, HEAD, rows), LOW),
            pltpu.VMEM((heads, group, 2, HEAD, rows), LOW),
            pltpu.VMEM((AUG, rows), LOW),
            pltpu.VMEM((rows, AUG), LOW),
            pltpu.VMEM((HEAD + 16, rows), LOW),
            pltpu.VMEM((HEAD + 16, queries), F32),
            pltpu.VMEM((1, queries), F32),
            pltpu.VMEM((8, shape.block), F32),
            pltpu.VMEM((heads, HEAD, rows), LOW),
            pltpu.VMEM((heads, HEAD, rows), LOW),
            dma((heads,)), dma((heads,)), dma((heads,)), dma((heads,)),
            dma((heads, group)), dma((heads, group)), dma((heads,)), dma((heads,)),
            dma,
        ],
        compiler_params=pltpu.CompilerParams(
            collective_id=1, has_side_effects=True, vmem_limit_bytes=VMEM_LIMIT["attend"]
        ),
        name="attend",
    )(*args)


def backward_kernel(
    shape, ga, tables, qaug_in, bias_rows, rkv, o_in, lse_in, fc2_state, fc1, mlp, values, vectors, proj,
    grads, table_grads, first_state, fc2_out, fc1_state, output, proj_state,
    rdo, qaug, q_tok, do_aug, do_tok, kaug_t, kaug, vaug_t, vaug, kacc, vacc, dq, drow, dcol,
    part, xr, summed, gq_s, gq_r, gkv_r,
    d_send, d_recv, x_send, x_recv, kv_send, kv_recv, q_send, q_recv, *rest,
):
    chunks = fc1.shape[1]
    rest = list(rest)

    def taken(number):
        found, rest[:] = rest[:number], rest[number:]
        return found

    bits = halve_bits()
    orders = [near_first(), far_first(shape.group)]
    moved2 = [
        Halve(orders[n], fc2_state.at[n], taken(3 * (bits - 2)), first=2) for n in range(chunks)
    ]
    moved0 = Halve(far_first(shape.group), proj, taken(3), last=0)
    outs = taken(1)[0]
    lines = lax.axis_size("tensor") // 2
    sum_mlp = Reduce(mlp, *taken(7))
    all_out = Gather(outs, *taken(3))
    line = tensor_place()[1]
    moved1 = [Halve(near_first(), fc1.at[:, 0], taken(8), last=1, own=True)]
    if chunks > 1:
        moved1 += [Halve(near_first(), fc1.at[:, 1], taken(5), last=0, own=True)]
    heads, group, rows, block = shape.heads, shape.group, shape.rows, shape.block
    queries = shape.queries
    me = lax.axis_index("dp")
    z, g = me // group, lax.rem(me, group)
    column = [paired(z, k, heads) for k in range(1, heads)]
    mates = [lax.rem(g + k, group) for k in range(1, group)]
    greet_all(Ring(heads))
    for other in sum_mlp.others() + [line]:
        sum_mlp.give(other)
    sends = []
    for h in column:
        copy = send_dp(ga.at[h], rdo.at[z], d_send.at[h], d_recv.at[z], h * group + g)
        copy.start()
        sends.append(copy)
    moved1[0].start()
    for each in moved1:
        each.load()
    rdo[z] = ga[z]
    qaug[...] = qaug_in[...]
    ones = jnp.where(lax.broadcasted_iota(jnp.int32, (16, rows), 0) < 3, 1.0, 0.0).astype(LOW)
    kaug_t[pl.ds(LSE_AT, 16), :] = ones
    vaug_t[pl.ds(HEAD, 16), :] = ones
    vaug_t[pl.ds(HEAD + 16, 32), :] = jnp.zeros((32, rows), LOW)
    low_lse = parts_of(-lse_in[...], 3)
    qaug[pl.ds(LSE_AT, 16), :] = jnp.concatenate(
        low_lse + [jnp.zeros((13, queries), F32)], axis=0
    ).astype(LOW)
    dq[...] = jnp.zeros_like(dq)
    dcol[...] = jnp.zeros_like(dcol)
    drow[...] = jnp.zeros_like(drow)

    def prepare(k, carry):
        source = paired(z, k, heads)
        span = pl.ds(pl.multiple_of(source * rows, rows), rows)

        @pl.when(k > 0)
        def _():
            send_dp(rdo.at[source], rdo.at[source], d_send.at[source], d_recv.at[source], me).wait_recv()

        upstream = rdo[source]
        dots = jnp.sum(upstream.astype(F32) * o_in[:, span], axis=0, keepdims=True)
        low_dots = parts_of(-dots, 3)
        do_aug[pl.ds(0, HEAD), span] = upstream
        do_aug[pl.ds(HEAD, 16), span] = jnp.concatenate(
            low_dots + [jnp.zeros((13, rows), F32)], axis=0
        ).astype(LOW)
        do_aug[pl.ds(HEAD + 16, 32), span] = jnp.zeros((32, rows), LOW)
        do_tok[span, :] = do_aug[:, span].T
        q_tok[span, :] = qaug[pl.ds(0, 128), span].T
        return carry

    lax.fori_loop(0, heads, prepare, 0)
    for other in sum_mlp.others():
        sum_mlp.pass_on(other)
    moved0.start()
    for each in moved2:
        each.start()

    def chunk(source, mate):
        dev = source * group + mate
        at = (dev * (rows // SIDE)) // 8
        cols, in_group = key_onehots(rows, dev)
        kaug_t[pl.ds(0, HEAD), :] = rkv[source, mate, 0]
        kaug_t[pl.ds(COLS_AT, 2 * SIDE), :] = cols.astype(LOW)
        kaug_t[pl.ds(ROWS_AT, 16), :] = in_group.astype(LOW)
        kaug[...] = kaug_t[...].T
        vaug_t[pl.ds(0, HEAD), :] = rkv[source, mate, 1]
        vaug[...] = vaug_t[...].T
        qaug[pl.ds(ROWS_AT, 16), :] = bias_rows[at]
        kacc[...] = jnp.zeros_like(kacc)
        vacc[...] = jnp.zeros_like(vacc)
        back = jnp.concatenate(
            [kaug_t[pl.ds(0, COLS_AT + SIDE), :], kaug_t[pl.ds(ROWS_AT, 16), :]], axis=0
        )

        def one(i, carry):
            span = pl.ds(pl.multiple_of(i * block, block), block)
            probs = jnp.exp2(nn(kaug[...], qaug[:, span]) * EXP2_SCALE)
            pulled = nn(vaug[...], do_aug[:, span])
            low_grads = (probs * pulled).astype(LOW)
            vacc[...] += nn(probs.astype(LOW), do_tok[span, :])
            kacc[...] += nn(low_grads, q_tok[span, :])
            found = nn(back, low_grads)
            dq[:, span] += found[:HEAD]
            dcol[:, span] += found[COLS_AT : COLS_AT + SIDE]
            drow[at, :, span] += found[COLS_AT + SIDE : COLS_AT + SIDE + 8]
            return carry

        lax.fori_loop(0, queries // block, one, 0)

    def put(where, extra):
        key_part = (kacc[...] * SCALE).T[:HEAD]
        value_part = vacc[...].T[:HEAD]
        for other in extra:
            key_part = key_part + other[0].astype(F32)
            value_part = value_part + other[1].astype(F32)
        where[0] = key_part.astype(LOW)
        where[1] = value_part.astype(LOW)

    def mate_copy(source, mate):
        return send_dp(
            part.at[source, mate], xr.at[source, g], x_send.at[source, mate], x_recv.at[source, g],
            z * group + mate,
        )

    def mates_step(k, carry):
        source = paired(z, lax.rem(k, heads), heads)

        def mate_step(n, inner):
            mate = lax.rem(g + n, group)
            chunk(source, mate)
            put(part.at[source, mate], [])
            mate_copy(source, mate).start()
            return inner

        lax.fori_loop(1, group, mate_step, 0)

        return carry

    lax.fori_loop(1, heads + 1, mates_step, 0)
    if chunks > 1:
        moved1[1].start()
    spot = lax.axis_index("tensor")
    outs[spot] = (values[...] + sum_mlp.total() + vectors[3:4]).astype(LOW)
    all_out.start()
    moved1[0].loaded()
    moved1[0].run(0)

    def own_step(k, carry):
        source = paired(z, lax.rem(k, heads), heads)
        chunk(source, g)
        extra = []
        for mate in mates:
            send_dp(
                xr.at[source, mate], xr.at[source, mate], x_send.at[source, mate], x_recv.at[source, mate], me
            ).wait_recv()
            extra.append(xr.at[source, mate])
        put(summed.at[source], extra)

        @pl.when(source != z)
        def _():
            send_dp(
                summed.at[source], gkv_r.at[z], kv_send.at[source], kv_recv.at[z], source * group + g
            ).start()

        return carry

    lax.fori_loop(1, heads + 1, own_step, 0)
    for other in all_out.others():
        all_out.forward(other)
    table_grads[...] = jnp.zeros_like(table_grads)

    def finish(k, carry):
        source = paired(z, lax.rem(k, heads), heads)
        span = pl.ds(pl.multiple_of(source * rows, rows), rows)
        by_row, by_col = shifts(rows, source * group + g)
        total = dq[:, span] * SCALE
        for n, held in enumerate((drow[:, :, span].reshape(SIDE, rows), dcol[:, span])):
            spread = unskew(held, by_col if n else by_row)
            for piece in parts_of(spread, 2):
                low_piece = piece.astype(LOW)
                total = total + tn(tables[n], low_piece)
                table_grads[n] += nn(low_piece, q_tok[span, :])
        gq_s[source] = total.astype(LOW)

        @pl.when(source != z)
        def _():
            send_dp(
                gq_s.at[source], gq_r.at[z], q_send.at[source], q_recv.at[z], source * group + g
            ).start()

        return carry

    lax.fori_loop(1, heads + 1, finish, 0)
    moved1[0].run(1)
    for stage in range(2, halve_bits() - 1):
        for each in moved2:
            each.run(stage)
    found = [each.total() for each in moved2]
    fc2_out[...] = jnp.concatenate(found, axis=0) if chunks > 1 else found[0]
    first_state[...] = moved1[0].stages[1][0][...]
    if chunks > 1:
        moved1[1].loaded()
        moved1[1].run(0)
        fc1_state[...] = moved1[1].stages[0][0][...]
    moved0.run(0)
    proj_state[...] = moved0.stages[0][0][...]
    for other in all_out.others() + [line]:
        all_out.take(other)
    output[...] = outs[...]
    grads[z, 0] = gq_s[z]
    grads[z, pl.ds(1, 2)] = summed[z]
    for h in column:
        send_dp(summed.at[h], gkv_r.at[h], kv_send.at[h], kv_recv.at[h], h * group + g).wait()
        grads[h, pl.ds(1, 2)] = gkv_r[h]
    for h in column:
        send_dp(gq_s.at[h], gq_r.at[h], q_send.at[h], q_recv.at[h], h * group + g).wait()
        grads[h, 0] = gq_r[h]
    for copy in sends:
        copy.wait_send()
    for source in range(heads):
        for mate in mates:
            mate_copy(source, mate).wait_send()
    for each in moved1 + moved2 + [sum_mlp, all_out, moved0]:
        each.finish()


def attend_back(shape, ga, tables, qaug, bias_rows, kv, o_rows, lse, fc2_state, fc1, mlp, values, vectors, proj):
    count, share, width = mlp.shape
    devices, chunks, owned, hidden = fc1.shape
    hbm = pl.BlockSpec(memory_space=pl.ANY)
    moving = halve_bufs(owned, hidden, first=2) * chunks
    moving += halve_bufs(chunks * owned, proj.shape[2], last=0)
    moving += [pltpu.VMEM((count, share, width), LOW)]
    moving += part_bufs(count // 2, share, width) + gather_sems(count // 2)
    moving += halve_bufs(owned, hidden, last=1, own=True)
    if chunks > 1:
        moving += halve_bufs(owned, hidden, last=0, own=True)
    heads, group, rows, queries = shape.heads, shape.group, shape.rows, shape.queries
    vmem = pl.BlockSpec(memory_space=pltpu.VMEM)
    dma = pltpu.SemaphoreType.DMA
    return pl.pallas_call(
        functools.partial(backward_kernel, shape),
        out_shape=(
            jax.ShapeDtypeStruct((heads, 3, HEAD, rows), LOW),
            jax.ShapeDtypeStruct((2, 2 * SIDE, 128), F32),
            jax.ShapeDtypeStruct((devices // 4, owned, hidden), LOW),
            jax.ShapeDtypeStruct((chunks * owned, hidden), F32),
            jax.ShapeDtypeStruct((devices // 2, owned, hidden), LOW),
            jax.ShapeDtypeStruct((count, share, width), LOW),
            jax.ShapeDtypeStruct((devices // 2,) + proj.shape[1:], LOW),
        ),
        in_specs=[vmem] * 8 + [hbm] + [vmem] * 4,
        out_specs=(vmem,) * 7,
        scratch_shapes=[
            pltpu.VMEM((heads, HEAD, rows), LOW),
            pltpu.VMEM((AUG, queries), LOW),
            pltpu.VMEM((queries, 128), LOW),
            pltpu.VMEM((128, queries), LOW),
            pltpu.VMEM((queries, 128), LOW),
            pltpu.VMEM((AUG, rows), LOW),
            pltpu.VMEM((rows, AUG), LOW),
            pltpu.VMEM((128, rows), LOW),
            pltpu.VMEM((rows, 128), LOW),
            pltpu.VMEM((rows, 128), F32),
            pltpu.VMEM((rows, 128), F32),
            pltpu.VMEM((HEAD, queries), F32),
            pltpu.VMEM((SIDE // 8, 8, queries), F32),
            pltpu.VMEM((SIDE, queries), F32),
            pltpu.VMEM((heads, group, 2, HEAD, rows), LOW),
            pltpu.VMEM((heads, group, 2, HEAD, rows), LOW),
            pltpu.VMEM((heads, 2, HEAD, rows), LOW),
            pltpu.VMEM((heads, HEAD, rows), LOW),
            pltpu.VMEM((heads, HEAD, rows), LOW),
            pltpu.VMEM((heads, 2, HEAD, rows), LOW),
            dma((heads,)), dma((heads,)), dma((heads, group)), dma((heads, group)),
            dma((heads,)), dma((heads,)), dma((heads,)), dma((heads,)),
        ] + moving,
        compiler_params=pltpu.CompilerParams(
            collective_id=2, has_side_effects=True, vmem_limit_bytes=VMEM_LIMIT["attend_back"]
        ),
        name="attend_back",
    )(ga, tables, qaug, bias_rows, kv, o_rows, lse, fc2_state, fc1, mlp, values, vectors, proj)


def send_tensor(src, dst, send_sem, recv_sem, dev):
    return pltpu.make_async_remote_copy(
        src_ref=src,
        dst_ref=dst,
        send_sem=send_sem,
        recv_sem=recv_sem,
        device_id={"tensor": dev},
        device_id_type=MESH,
    )


def tensor_place():
    me = lax.axis_index("tensor")
    return lax.rem(me, 2), me // 2, lax.axis_size("tensor") // 2


def tensor_peers():
    core, line, lines = tensor_place()
    far = [lax.rem(line + k, lines) * 2 + core for k in range(1, lines)]
    return far + [line * 2 + 1 - core]


def part_bufs(lines, share, width, dtype=LOW):
    dma = pltpu.SemaphoreType.DMA
    return [pltpu.VMEM((lines, share, width), dtype)] * 3 + [dma((lines,))] * 4


class Reduce:
    def __init__(self, part, mate_in, passed, line_in, m_send, m_recv, l_send, l_recv):
        self.part, self.mate_in, self.passed, self.line_in = part, mate_in, passed, line_in
        self.sems = m_send, m_recv, l_send, l_recv
        self.core, self.line, self.lines = tensor_place()

    def mate_copy(self, to):
        m_send, m_recv, _, _ = self.sems
        return send_tensor(
            self.part.at[to * 2 + 1 - self.core], self.mate_in.at[to],
            m_send.at[to], m_recv.at[to], self.line * 2 + 1 - self.core,
        )

    def line_copy(self, to, slot):
        _, _, l_send, l_recv = self.sems
        return send_tensor(
            self.passed.at[to], self.line_in.at[slot], l_send.at[to], l_recv.at[slot],
            to * 2 + self.core,
        )

    def give(self, to):
        self.mate_copy(to).start()

    def pass_on(self, to):
        self.mate_copy(to).wait_recv()
        both = self.part[to * 2 + self.core].astype(F32) + self.mate_in[to].astype(F32)
        self.passed[to] = both.astype(self.passed.dtype)
        self.line_copy(to, self.line).start()

    def others(self):
        return [lax.rem(self.line + k, self.lines) for k in range(1, self.lines)]

    def total(self):
        self.mate_copy(self.line).wait_recv()
        total = self.part[self.line * 2 + self.core].astype(F32) + self.mate_in[self.line].astype(F32)
        for other in self.others():
            self.line_copy(other, other).wait_recv()
            total = total + self.line_in[other].astype(F32)
        return total

    def finish(self):
        self.mate_copy(self.line).wait_send()
        for other in self.others():
            self.mate_copy(other).wait_send()
            self.line_copy(other, self.line).wait_send()


def gather_sems(lines):
    dma = pltpu.SemaphoreType.DMA
    return [dma((lines,)), dma((lines,)), dma((2 * lines,))]


class Gather:
    def __init__(self, whole, l_send, m_send, recv):
        self.whole, self.sems = whole, (l_send, m_send, recv)
        self.core, self.line, self.lines = tensor_place()

    def line_copy(self, to):
        l_send, _, recv = self.sems
        own = self.line * 2 + self.core
        return send_tensor(
            self.whole.at[own], self.whole.at[own], l_send.at[to], recv.at[own], to * 2 + self.core
        )

    def mate_copy(self, at):
        _, m_send, recv = self.sems
        part = at * 2 + self.core
        return send_tensor(
            self.whole.at[part], self.whole.at[part], m_send.at[at], recv.at[part],
            self.line * 2 + 1 - self.core,
        )

    def arrived(self, part):
        l_send, _, recv = self.sems
        send_tensor(
            self.whole.at[part], self.whole.at[part], l_send.at[0], recv.at[part], part
        ).wait_recv()

    def others(self):
        return [lax.rem(self.line + k, self.lines) for k in range(1, self.lines)]

    def start(self):
        for other in self.others():
            self.line_copy(other).start()
        self.mate_copy(self.line).start()

    def forward(self, at):
        self.arrived(at * 2 + self.core)
        self.mate_copy(at).start()

    def take(self, at):
        self.arrived(at * 2 + 1 - self.core)

    def finish(self):
        self.mate_copy(self.line).wait_send()
        for other in self.others():
            self.mate_copy(other).wait_send()
            self.line_copy(other).wait_send()


def normed(values):
    center = values - jnp.mean(values, axis=-1, keepdims=True)
    variance = jnp.mean(center * center, axis=-1, keepdims=True)
    inverse = lax.rsqrt(variance + EPSILON)
    return center * inverse, inverse


def normed_back(upstream, scaled, inverse, gain):
    weighted = upstream * gain
    centered = weighted - jnp.mean(weighted, axis=-1, keepdims=True)
    return (centered - scaled * jnp.mean(weighted * scaled, axis=-1, keepdims=True)) * inverse


def tile_of(width):
    return 256 if width % 256 == 0 else 128


class Ring:
    def __init__(self, heads):
        self.heads, self.group = heads, lax.axis_size("dp") // heads
        me = lax.axis_index("dp")
        self.z, self.g = me // self.group, lax.rem(me, self.group)

    def column(self):
        return [paired(self.z, k, self.heads) for k in range(1, self.heads)]

    def mates(self):
        return [lax.rem(self.g + k, self.group) for k in range(1, self.group)]

    def peers(self):
        far = [h * self.group + self.g for h in self.column()]
        return far + [self.z * self.group + o for o in self.mates()]


def greet_all(ring):
    barrier = pltpu.get_barrier_semaphore()
    near, far = tensor_peers(), ring.peers()
    for peer in near:
        pl.semaphore_signal(barrier, inc=1, device_id={"tensor": peer}, device_id_type=MESH)
    for peer in far:
        pl.semaphore_signal(barrier, inc=1, device_id={"dp": peer}, device_id_type=MESH)
    pl.semaphore_wait(barrier, len(near) + len(far))


def halve_bits():
    return (lax.axis_size("dp") - 1).bit_length()


def near_first():
    return tuple(range(halve_bits()))


def far_first(group):
    first = group.bit_length() - 1
    return (first,) + tuple(bit for bit in range(halve_bits()) if bit != first)


def halve_bufs(share, width, first=0, last=None, own=False):
    bits = halve_bits()
    last = bits - 1 if last is None else last
    dma = pltpu.SemaphoreType.DMA
    found = []
    if own:
        found += [pltpu.VMEM((1 << (bits - 1), share, width), LOW), dma]
    for stage in range(first, last + 1):
        count = 1 << (bits - 1 - stage)
        found += [pltpu.VMEM((count, share, width), LOW), dma((count,)), dma((count,))]
    return found


class Halve:
    def __init__(self, order, source, bufs, first=0, last=None, own=False):
        self.order, self.source, self.first = order, source, first
        self.last = len(order) - 1 if last is None else last
        bufs = list(bufs)
        self.own = bufs[0:2] if own else None
        bufs = bufs[2:] if own else bufs
        self.stages = {first + n: bufs[3 * n : 3 * n + 3] for n in range(len(bufs) // 3)}
        self.me = lax.axis_index("dp")

    def bit(self, stage):
        return lax.rem(self.me // (1 << self.order[stage]), 2)

    def count(self, stage):
        return 1 << (len(self.order) - 1 - stage)

    def index(self, stage, at, bit):
        if stage > 0:
            return at * 2 + bit
        place = bit * (1 << self.order[0])
        for n, other in enumerate(self.order[1:]):
            place = place + lax.rem(at // (1 << n), 2) * (1 << other)
        return place

    def held(self, stage):
        return self.source if stage == self.first else self.stages[stage - 1][0]

    def copy(self, stage, at):
        bit = self.bit(stage)
        into, send, recv = self.stages[stage]
        return send_dp(
            self.held(stage).at[self.index(stage, at, 1 - bit)], into.at[at],
            send.at[at], recv.at[at], self.me + (1 - 2 * bit) * (1 << self.order[stage]),
        )

    def spots(self, stage):
        if stage == len(self.order) - 1:
            return [0]
        bit, half = self.bit(stage + 1), self.count(stage) // 2
        return [n * 2 + 1 - bit for n in range(half)] + [n * 2 + bit for n in range(half)]

    def load(self):
        for at in range(self.count(0)):
            pltpu.make_async_copy(
                self.source.at[self.index(0, at, self.bit(0))], self.own[0].at[at], self.own[1]
            ).start()

    def loaded(self):
        pltpu.make_async_copy(
            self.source.at[pl.ds(0, self.count(0))], self.own[0], self.own[1]
        ).wait()

    def start(self, only=slice(None)):
        for at in self.spots(self.first)[only]:
            self.copy(self.first, at).start()

    def kept(self, stage, at):
        if stage == self.first and self.own is not None:
            return self.own[0][at].astype(F32)
        return self.held(stage)[self.index(stage, at, self.bit(stage))].astype(F32)

    def sum_at(self, stage, at):
        self.copy(stage, at).wait_recv()
        return self.kept(stage, at) + self.stages[stage][0][at].astype(F32)

    def run(self, stage):
        for n, at in enumerate(self.spots(stage)):
            self.stages[stage][0][at] = self.sum_at(stage, at).astype(LOW)
            if stage < self.last and n < self.count(stage) // 2:
                self.copy(stage + 1, n).start()

    def total(self):
        return self.sum_at(self.last, 0)

    def finish(self):
        for stage in self.stages:
            for at in range(self.count(stage)):
                self.copy(stage, at).wait_send()


def middle_kernel(
    heads, att, proj_w, tokens, cot, fc1_hbm, fc2_hbm, vectors,
    mlp, values_out, middle_out, fc1_out, proj_out, ga_out, fc1_bias_out, sums_out, fc2_state,
    fc1, fc2, att_tok, branch, back, n2, act, gu, gb, held, spread,
    wide, load1, load2, *rest,
):
    core, line, lines = tensor_place()
    me = lax.axis_index("tensor")
    _, share, width = tokens.shape
    rows = tokens.shape[0] * share
    local, hidden = proj_w.shape[0], fc1_hbm.shape[1]
    step, dstep = tile_of(hidden), tile_of(width)
    in_fc1 = pltpu.make_async_copy(fc1_hbm, fc1, load1)
    in_fc2 = pltpu.make_async_copy(fc2_hbm, fc2, load2)
    in_fc1.start()
    in_fc2.start()
    greet_all(Ring(heads))
    sum_branch = Reduce(branch, *rest[0:7])
    sum_back = Reduce(back, *rest[7:14])
    all_n2 = Gather(n2, *rest[14:17])
    all_gb = Gather(gb, *rest[17:20])
    blocks2, blocks1, fc1_sem = rest[20:23]
    devices, chunks, owned, _ = blocks2.shape
    orders = [near_first(), far_first(lax.axis_size("dp") // heads)]
    moved = [
        Halve(orders[n], blocks2.at[:, n], rest[23 + 6 * n : 29 + 6 * n], last=1)
        for n in range(chunks)
    ]
    att_tok[...] = att[...].T.reshape(att_tok.shape)

    def project(k, carry):
        to = lax.rem(line + 1 + lax.rem(k, lines), lines)
        part = to * 2 + jnp.where(k < lines, 1 - core, core)
        branch[part] = nn(att_tok[part], proj_w[...]).astype(LOW)

        @pl.when(k < lines)
        def _():
            sum_branch.give(to)

        return carry

    lax.fori_loop(0, 2 * lines, project, 0)
    for other in sum_branch.others():
        sum_branch.pass_on(other)
    middle = tokens[me].astype(F32) + vectors[0:1]
    middle = middle + sum_branch.total()
    scaled, inverse = normed(middle)
    n2[me] = (scaled * vectors[1:2] + vectors[2:3]).astype(LOW)
    all_n2.start()
    values_out[...] = middle
    held[...] = scaled
    spread[...] = jnp.broadcast_to(inverse, spread.shape)
    fc1_bias_out[...] = jnp.zeros_like(fc1_bias_out)
    in_fc1.wait()
    in_fc2.wait()

    def hidden_part(k, carry):
        at = lax.rem(line + k, lines)

        @pl.when(k > 0)
        def _():
            all_n2.forward(at)

        all_n2.take(at)
        pair = pl.ds(at * 2, 2)
        inputs = n2[pair].reshape(2 * share, width)
        pulls = cot[pair].reshape(2 * share, width)

        def tile(n, inner):
            span = pl.ds(pl.multiple_of(n * step, step), step)
            up = nn(inputs, fc1[:, span]) + vectors[6:7, span]
            phi = 0.5 + 0.5 * lax.erf(up * math.sqrt(0.5))
            slope = phi + up * (jnp.exp(-0.5 * up * up) * (2 * math.pi) ** -0.5)
            act[pair, :, span] = (up * phi).astype(LOW).reshape(2, share, step)
            grad_up = (nt(pulls, fc2[span, :]) * slope).astype(LOW)
            gu[pair, :, span] = grad_up.reshape(2, share, step)
            fc1_bias_out[:, span] += jnp.sum(grad_up.astype(F32), axis=0, keepdims=True)
            return inner

        lax.fori_loop(0, hidden // step, tile, 0)

        def tile_back(n, inner):
            span = pl.ds(pl.multiple_of(n * dstep, dstep), dstep)
            found = nt(gu[pair].reshape(2 * share, hidden), fc1[span, :])
            back[pair, :, span] = found.astype(LOW).reshape(2, share, dstep)
            return inner

        lax.fori_loop(0, width // dstep, tile_back, 0)
        sum_back.give(at)

        return carry

    lax.fori_loop(0, lines, hidden_part, 0)

    def weights2(n, carry):
        span = pl.ds(pl.multiple_of(n * dstep, dstep), dstep)
        found = tn(cot[:, :, span].reshape(rows, dstep), act[...].reshape(rows, hidden))
        wide[span, :] = found.astype(LOW)
        return carry

    lax.fori_loop(0, width // dstep, weights2, 0)
    for dev in range(devices):
        for chunk in range(chunks):
            at = (dev * chunks + chunk) * owned
            blocks2[dev, chunk] = wide[pl.ds(at, owned), :]
    for each in moved:
        each.start()
    for other in sum_back.others():
        sum_back.pass_on(other)

    def out_part(k, carry):
        at = lax.rem(line + 1 + k, lines)
        pair = pl.ds(at * 2, 2)

        def tile_out(n, inner):
            span = pl.ds(pl.multiple_of(n * dstep, dstep), dstep)
            found = nn(act[pair].reshape(2 * share, hidden), fc2[:, span])
            mlp[pair, :, span] = found.astype(LOW).reshape(2, share, dstep)
            return inner

        lax.fori_loop(0, width // dstep, tile_out, 0)
        return carry

    lax.fori_loop(0, lines, out_part, 0)

    def weights1(n, carry):
        span = pl.ds(pl.multiple_of(n * dstep, dstep), dstep)
        found = tn(n2[:, :, span].reshape(rows, dstep), gu[...].reshape(rows, hidden))
        wide[span, :] = found.astype(LOW)
        return carry

    lax.fori_loop(0, width // dstep, weights1, 0)
    for dev in range(devices):
        for chunk in range(chunks):
            at = (dev * chunks + chunk) * owned
            blocks1[dev, chunk] = wide[pl.ds(at, owned), :]
    keep_fc1 = pltpu.make_async_copy(blocks1, fc1_out, fc1_sem)
    keep_fc1.start()
    upstream = sum_back.total()
    sums_out[0:1] = jnp.sum(upstream * held[...], axis=0, keepdims=True)
    sums_out[1:2] = jnp.sum(upstream, axis=0, keepdims=True)
    grad_middle = cot[me].astype(F32) + normed_back(
        upstream, held[...], spread[:, :1], vectors[1:2]
    )
    middle_out[...] = grad_middle
    gb[me] = grad_middle.astype(LOW)
    all_gb.start()
    for each in moved:
        each.run(0)
    sums_out[2:3] = jnp.sum(cot[...].astype(F32).reshape(rows, width), axis=0, keepdims=True)
    for other in all_gb.others():
        all_gb.forward(other)
    all_gb.take(line)
    for other in all_gb.others():
        all_gb.take(other)
    whole = gb[...].reshape(rows, width)
    sums_out[3:4] = jnp.sum(whole.astype(F32), axis=0, keepdims=True)
    ga_out[...] = nt(proj_w[...], whole).astype(LOW)

    def weights0(n, carry):
        span = pl.ds(pl.multiple_of(n * dstep, dstep), dstep)
        found = tn(gb[:, :, span].reshape(rows, dstep), att_tok[...].reshape(rows, -1))
        wide[span, :local] = found.astype(LOW)
        return carry

    lax.fori_loop(0, width // dstep, weights0, 0)
    for dev in range(devices):
        proj_out[dev] = wide[pl.ds(dev * chunks * owned, chunks * owned), :local]
    for n, each in enumerate(moved):
        each.run(1)
        fc2_state[n] = each.stages[1][0][...]
    keep_fc1.wait()
    for each in (sum_branch, sum_back, all_n2, all_gb, *moved):
        each.finish()


def middle_block(heads, att, proj_w, tokens, cot, fc1, fc2, vectors):
    count = lax.axis_size("tensor")
    lines = count // 2
    local, width = proj_w.shape
    rows = tokens.shape[0]
    share = rows // count
    hidden = fc1.shape[1]
    vmem = pl.BlockSpec(memory_space=pltpu.VMEM)
    hbm = pl.BlockSpec(memory_space=pl.ANY)
    dma = pltpu.SemaphoreType.DMA
    whole = (count, share, width)
    devices = lax.axis_size("dp")
    owned = width // devices
    chunks = 2 if owned % 32 == 0 else 1
    weights = (devices, chunks, owned // chunks, hidden)
    scratch = [
        pltpu.VMEM((width, hidden), LOW),
        pltpu.VMEM((hidden, width), LOW),
        pltpu.VMEM((count, share, local), LOW),
        pltpu.VMEM(whole, LOW),
        pltpu.VMEM(whole, LOW),
        pltpu.VMEM(whole, LOW),
        pltpu.VMEM((count, share, hidden), LOW),
        pltpu.VMEM((count, share, hidden), LOW),
        pltpu.VMEM(whole, LOW),
        pltpu.VMEM((share, width), F32),
        pltpu.VMEM((share, 128), F32),
        pltpu.VMEM((width, hidden), LOW),
        dma,
        dma,
    ]
    scratch += part_bufs(lines, share, width) * 2 + gather_sems(lines) * 2
    scratch += [pltpu.VMEM(weights, LOW), pltpu.VMEM(weights, LOW), dma]
    scratch += halve_bufs(owned // chunks, hidden, last=1) * chunks
    return pl.pallas_call(
        functools.partial(middle_kernel, heads),
        out_shape=(
            jax.ShapeDtypeStruct(whole, LOW),
            jax.ShapeDtypeStruct((share, width), F32),
            jax.ShapeDtypeStruct((share, width), F32),
            jax.ShapeDtypeStruct(weights, LOW),
            jax.ShapeDtypeStruct((devices, owned, local), LOW),
            jax.ShapeDtypeStruct((local, rows), LOW),
            jax.ShapeDtypeStruct((1, hidden), F32),
            jax.ShapeDtypeStruct((8, width), F32),
            jax.ShapeDtypeStruct((chunks, devices // 4, owned // chunks, hidden), LOW),
        ),
        in_specs=[vmem] * 4 + [hbm] * 2 + [vmem],
        out_specs=(vmem,) * 3 + (hbm,) + (vmem,) * 5,
        scratch_shapes=scratch,
        compiler_params=pltpu.CompilerParams(
            collective_id=3, has_side_effects=True, vmem_limit_bytes=VMEM_LIMIT["middle"]
        ),
        name="middle",
    )(
        att, proj_w, tokens.reshape(whole), cot.reshape(whole), fc1, fc2, vectors,
    )


def small_bufs(heads, stages, shape):
    group, lines = lax.axis_size("dp") // heads, lax.axis_size("tensor") // 2
    dma = pltpu.SemaphoreType.DMA
    found = []
    for stage in stages:
        count = {"core": 2, "line": lines, "mate": group, "far": heads}[stage]
        found += [
            pltpu.VMEM(shape, F32), pltpu.VMEM((count,) + shape, F32), dma((count,)), dma((count,))
        ]
    return found


class Small:
    def __init__(self, ring, stages, merge, *bufs):
        self.ring, self.stages, self.merge = ring, stages, merge
        self.bufs = [bufs[4 * n : 4 * n + 4] for n in range(len(stages))]
        core, line, lines = tensor_place()
        self.peers = {
            "core": (core, [(1 - core, line * 2 + 1 - core)]),
            "line": (line, [(o, o * 2 + core) for o in [lax.rem(line + k, lines) for k in range(1, lines)]]),
            "mate": (ring.g, [(o, ring.z * ring.group + o) for o in ring.mates()]),
            "far": (ring.z, [(o, o * ring.group + ring.g) for o in ring.column()]),
        }

    def copy(self, n, slot, other, dev):
        value, held, send, recv = self.bufs[n]
        call = send_tensor if self.stages[n] in ("core", "line") else send_dp
        return call(value, held.at[slot], send.at[other], recv.at[slot], dev)

    def start(self, n, value):
        own, peers = self.peers[self.stages[n]]
        self.bufs[n][0][...] = value
        for other, dev in peers:
            self.copy(n, own, other, dev).start()

    def take(self, n):
        _, peers = self.peers[self.stages[n]]
        total = self.bufs[n][0][...]
        for other, dev in peers:
            self.copy(n, other, other, dev).wait_recv()
            total = self.merge(total, self.bufs[n][1][other])
        return total

    def step(self, n):
        self.start(n + 1, self.take(n))

    def finish(self):
        for n in range(len(self.stages)):
            own, peers = self.peers[self.stages[n]]
            for other, dev in peers:
                self.copy(n, own, other, dev).wait_send()


EVERY = ("core", "line", "far", "mate")
OVER_DP = ("mate", "far")


def add_peaks(a, b):
    row = lax.broadcasted_iota(jnp.int32, a.shape, 0)
    return jnp.where(row == 2, jnp.maximum(a, b), a + b)


def widen(row, width):
    if row.shape[1] == width:
        return row
    return jnp.concatenate([row, jnp.zeros((1, width - row.shape[1]), F32)], axis=1)


def tail_kernel(
    heads, grads, qkv_w, n1_t, tokens, grad_middle, vectors, tables, sums, fc1_bias, peak,
    proj, first_state, fc1_state,
    tokens_out, proj_out, fc1_out, qkv_out, tables_out, rows_out, clip_out,
    g_all, g_tok, part, gt, *rest,
):
    ring = Ring(heads)
    core, line, lines = tensor_place()
    me = lax.axis_index("tensor")
    count, share, width = tokens.shape
    rows = count * share
    local = heads * HEAD
    dstep = tile_of(width)
    pieces, devices, piece, _ = n1_t.shape
    chunks = 1 if pieces == 1 else 2
    rest = list(rest)

    def taken(number):
        found, rest[:] = rest[:number], rest[number:]
        return found

    greet_all(ring)
    blocks = [taken(1)[0] for _ in range(pieces)]
    moved3 = [Halve(near_first(), each, taken(3 * halve_bits())) for each in blocks]
    moved0 = Halve(far_first(ring.group), proj, taken(3 * (halve_bits() - 1)), first=1)
    moved1 = [Halve(near_first(), first_state, taken(3 * (halve_bits() - 2)), first=2)]
    if chunks > 1:
        moved1 += [Halve(near_first(), fc1_state, taken(3 * (halve_bits() - 1)), first=1)]
    sum_part = Reduce(part, *taken(7))
    all_gt = Gather(gt, *taken(3))
    pool, pooled = taken(2)
    sum_pool = Reduce(pool, *taken(7))
    all_pool = Gather(pooled, *taken(3))
    small_pool = Small(ring, OVER_DP, lax.add, *taken(8))
    small_late = Small(ring, EVERY, lax.add, *taken(16))
    small_dp = Small(ring, OVER_DP, add_peaks, *taken(8))
    pool[...] = tables[...].reshape(pool.shape)
    for other in sum_pool.others() + [line]:
        sum_pool.give(other)
    for each in moved1:
        each.start()
    for t in range(3):
        for h in range(heads):
            g_all[pl.ds(t * local + h * HEAD, HEAD), :] = grads[h, t]
    g_tok[...] = g_all[...].T.reshape(g_tok.shape)
    for other in sum_pool.others():
        sum_pool.pass_on(other)
    whole = g_tok[...].reshape(rows, 3 * local)
    lane = lax.broadcasted_iota(jnp.int32, (1, width), 1)
    peaks = jnp.where(lane == ring.z, peak[0:1, 0:1], -jnp.inf)
    bias_sums = nn(jnp.ones((8, rows), LOW), whole)[0:1]
    dp_rows = [widen(fc1_bias[...], width), widen(bias_sums, width), peaks]
    small_dp.start(0, jnp.concatenate(dp_rows + [jnp.zeros((5, width), F32)], axis=0))

    for n in range(pieces):
        found = nn(
            n1_t[n].reshape(devices * piece, rows), g_tok[...].reshape(rows, 3 * local)
        )
        blocks[n][...] = found.astype(LOW).reshape(devices, piece, 3 * local)
        if n == min(1, pieces - 1):
            small_pool.start(0, sum_pool.total())
        moved3[n].start()
        if n == min(1, pieces - 1):
            moved0.start()

    def norm_part(k, carry):
        at = lax.rem(line + 1 + k, lines)
        pair = pl.ds(at * 2, 2)

        def tile(n, inner):
            span = pl.ds(pl.multiple_of(n * dstep, dstep), dstep)
            found = nn(g_tok[pair].reshape(2 * share, 3 * local), qkv_w[:, span])
            part[pair, :, span] = found.astype(LOW).reshape(2, share, dstep)
            return inner

        lax.fori_loop(0, width // dstep, tile, 0)
        sum_part.give(at)
        return carry

    lax.fori_loop(0, lines, norm_part, 0)
    for other in sum_part.others():
        sum_part.pass_on(other)
    scaled, inverse = normed(tokens[me].astype(F32))
    for each in moved1[1:]:
        each.run(1)
    moved3[0].run(0)
    small_pool.step(0)
    for each in moved3[1:2]:
        each.run(0)
    moved3[0].run(1)
    upstream = sum_part.total()
    late = [
        sums[0:4],
        jnp.sum(upstream * scaled, axis=0, keepdims=True),
        jnp.sum(upstream, axis=0, keepdims=True),
        jnp.zeros((2, width), F32),
    ]
    small_late.start(0, jnp.concatenate(late, axis=0))
    found = grad_middle[...] + normed_back(upstream, scaled, inverse, vectors[4:5])
    gt[me] = found.astype(LOW)
    all_gt.start()
    pooled[me] = small_pool.take(1)
    all_pool.start()
    small_dp.step(0)
    for n, each in enumerate(moved3[2:]):
        each.run(0)
        if n == 0:
            small_late.step(0)
            moved0.run(1)
        if n == 1:
            small_late.step(1)
            for other in all_gt.others():
                all_gt.forward(other)
            for other in all_pool.others():
                all_pool.forward(other)
        moved3[n + 1].run(1)
    if pieces < 3:
        moved0.run(1)
    if pieces < 4:
        for n in range(max(pieces - 2, 0), 2):
            small_late.step(n)
        for other in all_gt.others():
            all_gt.forward(other)
        for other in all_pool.others():
            all_pool.forward(other)
    small_late.step(2)
    if pieces > 1:
        moved3[-1].run(1)
    dp_sum = small_dp.take(1)
    limit = vectors[9:10]
    factors = jnp.sqrt(limit / jnp.maximum(dp_sum[2:3], limit))
    lane = lax.broadcasted_iota(jnp.int32, (1, width), 1)
    clipped_bias = vectors[7:8]
    for h in range(heads):
        factor = factors[:, h : h + 1]
        own = (lane >= h * HEAD) & (lane < (h + 1) * HEAD)
        clipped_bias = jnp.where(own, clipped_bias * factor, clipped_bias)
        for t in range(2):
            span = pl.ds(t * local + h * HEAD, HEAD)
            clip_out[span, :] = (qkv_w[span, :].astype(F32) * factor).astype(LOW)
    rows_out[8:11] = dp_sum[0:3]
    rows_out[11:12] = factors
    rows_out[12:13] = clipped_bias
    rows_out[13:16] = jnp.zeros((3, width), F32)
    for stage in range(2, halve_bits() - 1):
        for each in moved3 + [moved0] + moved1:
            each.run(stage)
    for other in all_gt.others() + [line]:
        all_gt.take(other)
    for other in all_pool.others() + [line]:
        all_pool.take(other)
    tokens_out[...] = gt[...]
    for n in range(2):
        turned_sums = pooled[...].reshape(2, 2 * SIDE, 128)[n].T[:HEAD]
        found = jnp.zeros((HEAD, 2 * SIDE), F32)
        for piece in parts_of(turned_sums, 3):
            found = found + nn(piece.astype(LOW), turned(2 * SIDE))
        tables_out[n] = found
    late = small_late.take(3)
    row = lax.broadcasted_iota(jnp.int32, late.shape, 0)
    rows_out[0:8] = jnp.where((row == 2) | (row == 3), late * (1.0 / count), late)
    owned = first_state.shape[1]
    for n, each in enumerate(moved1):
        fc1_out[pl.ds(n * owned, owned), :] = each.total()
    proj_out[...] = moved0.total()
    for n, each in enumerate(moved3):
        total = each.total()
        owned = total.shape[0]
        for t in range(3):
            qkv_out[t, pl.ds(n * owned, owned), :] = total[:, t * local : (t + 1) * local]
    for each in [
        moved0, sum_part, all_gt, sum_pool, all_pool, small_pool, small_late, small_dp,
    ] + moved3 + moved1:
        each.finish()


def tail(heads, grads, qkv_w, n1_t, tokens, grad_middle, vectors, tables, sums, fc1_bias, peak, proj, first_state, fc1_state):
    hidden = first_state.shape[2]
    count = lax.axis_size("tensor")
    lines = count // 2
    local = heads * HEAD
    pieces, devices, piece, rows = n1_t.shape
    width = devices * pieces * piece
    owned = first_state.shape[1]
    chunks = pieces * piece // owned
    share = rows // count
    vmem = pl.BlockSpec(memory_space=pltpu.VMEM)
    whole = (count, share, width)
    scratch = [
        pltpu.VMEM((3 * local, rows), LOW),
        pltpu.VMEM((count, share, 3 * local), LOW),
        pltpu.VMEM(whole, LOW),
        pltpu.VMEM(whole, LOW),
    ]
    scratch += [pltpu.VMEM((devices, piece, 3 * local), LOW)] * pieces
    scratch += halve_bufs(piece, 3 * local) * pieces
    scratch += halve_bufs(chunks * owned, local, first=1)
    scratch += halve_bufs(owned, hidden, first=2)
    if chunks > 1:
        scratch += halve_bufs(owned, hidden, first=1)
    scratch += part_bufs(lines, share, width) + gather_sems(lines)
    pool = (count, 4 * SIDE // count, 128)
    scratch += [pltpu.VMEM(pool, F32)] * 2
    scratch += part_bufs(lines, *pool[1:], F32) + gather_sems(lines)
    scratch += small_bufs(heads, OVER_DP, pool[1:])
    scratch += small_bufs(heads, EVERY, (8, width))
    scratch += small_bufs(heads, OVER_DP, (8, width))
    return pl.pallas_call(
        functools.partial(tail_kernel, heads),
        out_shape=(
            jax.ShapeDtypeStruct(whole, LOW),
            jax.ShapeDtypeStruct((chunks * owned, local), F32),
            jax.ShapeDtypeStruct((chunks * owned, hidden), F32),
            jax.ShapeDtypeStruct((3, chunks * owned, local), F32),
            jax.ShapeDtypeStruct((2, HEAD, 2 * SIDE), F32),
            jax.ShapeDtypeStruct((16, width), F32),
            jax.ShapeDtypeStruct((2 * local, width), LOW),
        ),
        in_specs=[vmem] * 13,
        out_specs=(vmem,) * 7,
        scratch_shapes=scratch,
        compiler_params=pltpu.CompilerParams(
            collective_id=4, has_side_effects=True, vmem_limit_bytes=VMEM_LIMIT["tail"]
        ),
        name="tail",
    )(
        grads, qkv_w, n1_t, tokens.reshape(whole), grad_middle, vectors, tables, sums, fc1_bias,
        peak, proj, first_state, fc1_state,
    )


def finish_kernel(count, *refs):
    large, (rows, tables), refs = refs[:count], refs[count : count + 2], refs[count + 2 :]
    outs, smalls_out, refs = refs[:count], refs[count : count + 13], refs[count + 13 :]
    stage, smalls, (sems_in, sems_out, sems_small) = refs[:count], refs[count : count + 13], refs[count + 13 :]
    into = [pltpu.make_async_copy(a, b, sems_in.at[n]) for n, (a, b) in enumerate(zip(large, stage))]
    out = [pltpu.make_async_copy(b, c, sems_out.at[n]) for n, (b, c) in enumerate(zip(stage, outs))]
    for copy in into:
        copy.start()
    gain1, shift1, qv, proj, by_row, by_col, gain2, shift2, fc1, fc2, clip_bias, peaks, factors = smalls
    picks = (
        (gain2, 0), (shift2, 1), (fc2, 2), (proj, 3), (gain1, 4), (shift1, 5), (fc1, 8),
        (peaks, 10), (factors, 11), (clip_bias, 12),
    )
    for ref, at in picks:
        ref[...] = rows[at : at + 1, : ref.shape[0]].reshape(ref.shape)
    local = qv.shape[1]
    qv[0:1] = rows[9:10, :local]
    qv[1:2] = rows[9:10, 2 * local : 3 * local]
    by_row[...] = tables[0, :, : by_row.shape[1]]
    by_col[...] = tables[1, :, : by_col.shape[1]]
    small = [
        pltpu.make_async_copy(a, b, sems_small.at[n]) for n, (a, b) in enumerate(zip(smalls, smalls_out))
    ]
    for copy, after in zip(into, out):
        copy.wait()
        after.start()
    for copy in small:
        copy.start()
    for copy in out + small:
        copy.wait()


def finish(large, rows, tables, hidden, local):
    width = rows.shape[1]
    heads = local // HEAD
    vmem = pl.BlockSpec(memory_space=pltpu.VMEM)
    hbm = pl.BlockSpec(memory_space=pl.ANY)
    count = len(large)
    shapes = [
        (width,), (width,), (2, local), (width,), (HEAD, 2 * SIDE - 1), (HEAD, 2 * SIDE - 1),
        (width,), (width,), (hidden,), (width,), (local,), (heads,), (heads,),
    ]
    return pl.pallas_call(
        functools.partial(finish_kernel, count),
        out_shape=[jax.ShapeDtypeStruct(each.shape, each.dtype) for each in large]
        + [jax.ShapeDtypeStruct(each, F32) for each in shapes],
        in_specs=[hbm] * count + [vmem] * 2,
        out_specs=[hbm] * (count + len(shapes)),
        scratch_shapes=[pltpu.VMEM(each.shape, each.dtype) for each in large]
        + [pltpu.VMEM(each, F32) for each in shapes]
        + [pltpu.SemaphoreType.DMA((count,))] * 2
        + [pltpu.SemaphoreType.DMA((len(shapes),))],
        compiler_params=pltpu.CompilerParams(vmem_limit_bytes=VMEM_LIMIT["finish"]),
        name="finish",
    )(*large, rows, tables)


def on_device(
    tokens,
    cotangent,
    norm1_gain,
    norm1_shift,
    qkv_weight,
    qv_bias,
    proj_weight,
    proj_bias,
    table_rows,
    table_cols,
    norm2_gain,
    norm2_shift,
    fc1_weight,
    fc1_bias,
    fc2_weight,
    fc2_bias,
    threshold,
):
    images, row_count, model_width = tokens.shape
    token_count = images * row_count
    local_width = qkv_weight.shape[2]
    local_heads = local_width // HEAD
    shape = Shape(local_heads, lax.axis_size("dp") // local_heads, row_count)
    flat = tokens.reshape(token_count, model_width)

    listed = (
        proj_bias, norm2_gain, norm2_shift, fc2_bias, norm1_gain, norm1_shift, fc1_bias, qv_bias,
        threshold,
    )
    weights = qkv_weight.transpose(1, 2, 0).reshape(3 * local_width, model_width)
    attended, qaug, bias_rows, kv, o_rows, lse, peak, normed1, tables, vectors = attend(
        shape, flat, weights, listed, table_rows.T, table_cols.T
    )
    (
        mlp_part,
        values,
        grad_middle,
        grad_fc1,
        grad_proj,
        grad_attended,
        grad_fc1_bias,
        sums,
        fc2_state,
    ) = middle_block(
        local_heads,
        attended.reshape(local_width, token_count),
        proj_weight,
        flat,
        cotangent.reshape(token_count, model_width),
        fc1_weight,
        fc2_weight,
        vectors,
    )
    grad_heads = grad_attended.reshape(local_heads, HEAD, row_count)
    grad_triple, table_terms, first_state, grad_fc2, fc1_state, output, proj_state = attend_back(
        shape, grad_heads, tables, qaug, bias_rows, kv, o_rows, lse, fc2_state, grad_fc1,
        mlp_part, values, vectors, grad_proj,
    )
    grad_tokens, grad_proj, grad_fc1, grad_qkv, table_sums, rows, clipped = tail(
        local_heads,
        grad_triple,
        weights,
        normed1,
        flat,
        grad_middle,
        vectors,
        table_terms,
        sums,
        grad_fc1_bias,
        peak,
        proj_state,
        first_state,
        fc1_state,
    )
    large = (output, grad_tokens, grad_fc1, grad_fc2, grad_qkv, clipped, grad_proj)
    (
        output,
        grad_tokens,
        grad_fc1,
        grad_fc2,
        grad_qkv,
        clipped,
        grad_proj,
        grad_norm1_gain,
        grad_norm1_shift,
        grad_qv_bias,
        grad_proj_bias,
        grad_rows_t,
        grad_cols_t,
        grad_norm2_gain,
        grad_norm2_shift,
        grad_fc1_bias,
        grad_fc2_bias,
        clipped_q_bias,
        head_peaks,
        clip_factors,
    ) = finish(large, rows, table_sums, fc1_bias.shape[0], local_width)
    output = output.reshape(images, row_count, model_width)
    grad_tokens = grad_tokens.reshape(images, row_count, model_width)
    grad_qkv = grad_qkv.transpose(1, 0, 2)
    grad_fc2, grad_proj = grad_fc2.T, grad_proj.T
    grad_table_rows, grad_table_cols = grad_rows_t.T, grad_cols_t.T
    clipped_qk = clipped.reshape(2, local_width, model_width).transpose(2, 0, 1)
    return (
        output,
        grad_tokens,
        grad_norm1_gain,
        grad_norm1_shift,
        grad_qkv,
        grad_qv_bias,
        grad_proj,
        grad_proj_bias,
        grad_table_rows,
        grad_table_cols,
        grad_norm2_gain,
        grad_norm2_shift,
        grad_fc1,
        grad_fc1_bias,
        grad_fc2,
        grad_fc2_bias,
        clipped_qk,
        clipped_q_bias,
        head_peaks,
        clip_factors,
    )


def solution(mesh):
    in_specs = (
        P(None, "dp", None),
        P(None, "dp", None),
        P(),
        P(),
        P(None, None, "tensor"),
        P(None, "tensor"),
        P("tensor", None),
        P(),
        P(),
        P(),
        P(),
        P(),
        P(None, "tensor"),
        P("tensor"),
        P("tensor", None),
        P(),
        P(),
    )
    out_specs = (
        P(None, "dp", None),
        P(None, "dp", None),
        P(),
        P(),
        P("dp", None, "tensor"),
        P(None, "tensor"),
        P("tensor", "dp"),
        P(),
        P(),
        P(),
        P(),
        P(),
        P("dp", "tensor"),
        P("tensor"),
        P("tensor", "dp"),
        P(),
        P(None, None, "tensor"),
        P("tensor"),
        P("tensor"),
        P("tensor"),
    )
    return jax.shard_map(
        on_device, mesh=mesh, in_specs=in_specs, out_specs=out_specs, check_vma=False
    )
```
